32 devices in a mesh: groups: 2 (over y), tiles: 16 (over z, x, core).
Axes of the slice: x: 2, y: 2, z: 4, core: 2. Of those that a mesh axis runs over, the one named last changes fastest.
Arguments:
- node_latent: bfloat16 [8192, 512], P(('groups', 'tiles')), parts along dimension 0, may hold values from -6 to 6
- edge_latent: bfloat16 [49152, 512], P(('groups', 'tiles')), parts along dimension 0, may hold values from -6 to 6
- node_cot: bfloat16 [8192, 512], P(('groups', 'tiles')), parts along dimension 0, may hold values from -6 to 6
- edge_cot: bfloat16 [49152, 512], P(('groups', 'tiles')), parts along dimension 0, may hold values from -6 to 6
- edge_w1: bfloat16 [1536, 512], replicated, may hold values from -0.15625 to 0.15625
- edge_b1: float32 [512], replicated, may hold values from -3 to 3
- edge_w2: bfloat16 [512, 512], replicated, may hold values from -0.25 to 0.25
- edge_b2: float32 [512], replicated, may hold values from -3 to 3
- edge_gain: float32 [512], replicated, may hold values from 0.1 to 1.9
- node_w1: bfloat16 [1024, 512], replicated, may hold values from -0.1875 to 0.1875
- node_b1: float32 [512], replicated, may hold values from -3 to 3
- node_w2: bfloat16 [512, 512], replicated, may hold values from -0.25 to 0.25
- node_b2: float32 [512], replicated, may hold values from -3 to 3
- node_gain: float32 [512], replicated, may hold values from 0.1 to 1.9
- send_index: int32 [32, 16, 2], P(('groups', 'tiles')), parts along dimension 0, may hold values from 0 to 255
- edge_sender: int32 [49152], P(('groups', 'tiles')), parts along dimension 0, may hold values from 0 to 415, as said below
- edge_receiver: int32 [49152], P(('groups', 'tiles')), parts along dimension 0, may hold values from 0 to 255
- edge_count: int32 [32], P('groups'), parts along dimension 0, may hold values from 32 to 1536, as said below
Outputs:
- grad_node: bfloat16 [8192, 512], P(('groups', 'tiles')), parts along dimension 0
- grad_edge: bfloat16 [49152, 512], P(('groups', 'tiles')), parts along dimension 0
- grad_edge_w1: float32 [3072, 512], P(('groups', 'tiles')), parts along dimension 0
- grad_edge_w2: float32 [1024, 512], P(('groups', 'tiles')), parts along dimension 0
- grad_node_w1: float32 [2048, 512], P(('groups', 'tiles')), parts along dimension 0
- grad_node_w2: float32 [1024, 512], P(('groups', 'tiles')), parts along dimension 0
The draws below stay inside these ranges and needn't reach their ends.
There are 2 independent parts, one for each index of `groups`. The reference program is written for one: setup_inputs(seed, part) draws one part's arguments, and reference() takes and returns one part's arrays. A program takes and returns all parts, laid end to end along the dimension named above; an argument that names none is the same for every part. Nothing has to cross between parts.
Inputs may be any that keep to these rules, and one draw needn't show every extreme that they name: `edge_count`: the count of some device is exactly 1536, and that of the device 16 / 2 indices away from it exactly 32. `edge_sender`: an index into the device's sender table: below 64 the previous device's last 64 nodes, then its own 256 nodes, then the next device's first 64 nodes, then the 32 coarse-level rows listed for it; the first device never names the first part and the last never the third; in each device's block of 1536 slots the first 32 name every coarse-level row once.
All inputs are finite; a program needn't handle non-finite values.
Results may differ from the reference program's by a relative error of at most 0.0085.
Values may be sent and summed in bfloat16 or wider, within the bound.
No kernel may reach another device: no remote copies, remote signals or barrier semaphores. Data moves between devices by JAX's collectives and lax.ppermute only.
A program may use at most 128 MiB of HBM per device.

```python
import jax
import jax.numpy as jnp
from jax import lax

D = 512
H = 512
SLOT = 2
NEAR = 64
NODE_DEV = 256
EDGE_DEV = 1536
NODES = 4096
EDGES = 24576
N_TILES = 16


def draw_edge_sender(key, part):
    key = jax.random.fold_in(key, 11)
    far_total = N_TILES * SLOT
    base = NODE_DEV + 2 * NEAR
    rest = EDGE_DEV - far_total
    device_keys = jax.random.split(key, N_TILES)

    def one_device(device_key, device):
        keys = jax.random.split(device_key, 6)
        covered = base + jax.random.permutation(keys[0], far_total).astype(jnp.int32)
        kind = jax.random.randint(keys[1], (rest,), 0, 20, dtype=jnp.int32)
        own = NEAR + jax.random.randint(keys[2], (rest,), 0, NODE_DEV, dtype=jnp.int32)
        side = jax.random.randint(keys[3], (rest,), 0, 2, dtype=jnp.int32)
        side = jnp.where(device == 0, 1, jnp.where(device == N_TILES - 1, 0, side))
        rim_pick = jax.random.randint(keys[4], (rest,), 0, NEAR, dtype=jnp.int32)
        rim = jnp.where(side == 0, rim_pick, NEAR + NODE_DEV + rim_pick)
        far = base + jax.random.randint(keys[5], (rest,), 0, far_total, dtype=jnp.int32)
        others = jnp.where(kind < 12, own, jnp.where(kind < 19, rim, far))
        others = others.at[0].set(jnp.where(device > 0, 0, others[0]))
        return jnp.concatenate([covered, others]).astype(jnp.int32)
    return jax.vmap(one_device)(device_keys, jnp.arange(N_TILES, dtype=jnp.int32)).reshape(-1)


def draw_edge_count(key, part):
    key = jax.random.fold_in(key, 12)
    keys = jax.random.split(key, 4)
    lowest = N_TILES * SLOT
    spread = EDGE_DEV - lowest
    first_draw = jax.random.randint(keys[0], (N_TILES,), 0, spread + 1, dtype=jnp.int32)
    second_draw = jax.random.randint(keys[1], (N_TILES,), 0, spread + 1, dtype=jnp.int32)
    third_draw = jax.random.randint(keys[2], (N_TILES,), 0, spread + 1, dtype=jnp.int32)
    counts = lowest + first_draw * second_draw // spread * third_draw // spread
    busiest = jax.random.randint(keys[3], (), 0, N_TILES, dtype=jnp.int32)
    partner = (busiest + N_TILES // 2) % N_TILES
    ids = jnp.arange(N_TILES, dtype=jnp.int32)
    return jnp.where(ids == busiest, EDGE_DEV, jnp.where(ids == partner, lowest, counts)).astype(jnp.int32)


def set_ends(values, key, smallest, high):
    extent = values.shape
    spot = [jax.random.randint(jax.random.fold_in(key, axis), (), 0, extent[axis]) for axis in range(len(extent))]
    values = values.at[tuple(spot)].set(smallest)
    longest = extent.index(max(extent))
    spot[longest] = (spot[longest] + 1) % extent[longest]
    return values.at[tuple(spot)].set(high)


def steps_of(key, dims, cuts, least, largest):
    loudness = 1.0
    for axis_at, blocks in cuts:
        steps = jax.random.uniform(jax.random.fold_in(jax.random.fold_in(key, 6), axis_at), (blocks,), jnp.float32, least / len(cuts), largest / len(cuts))
        loudness = loudness * jnp.repeat(jnp.exp(steps), dims[axis_at] // blocks).reshape((-1,) + (1,) * (len(dims) - 1 - axis_at))
    return loudness


def normal_values(key, shape, scale, limit, cuts=(), held_as=jnp.bfloat16):
    entries = jax.random.normal(key, shape, jnp.float32) * scale
    if len(cuts) > 0:
        entries = steps_of(key, shape, cuts, -0.22, 0.18) * entries
    return jnp.clip(entries, min=-limit, max=limit).astype(held_as)


def setup_inputs(seed: int = 0, part: int = 0) -> dict:
    streams_of = jax.random.split(jax.random.key(seed), 19)
    part_keys = jax.random.split(jax.random.fold_in(streams_of[18], part), 19)
    node_latent = normal_values(part_keys[0], (NODES, D), 1.0, 6.0, ((0, 16),))
    edge_latent = normal_values(part_keys[1], (EDGES, D), 1.0, 6.0, ((0, 16),))
    node_cot = normal_values(part_keys[2], (NODES, D), 1.0, 6.0, ((0, 16),))
    edge_cot = normal_values(part_keys[3], (EDGES, D), 1.0, 6.0, ((0, 16),))
    edge_w1 = normal_values(streams_of[4], (3 * D, H), (3 * D) ** -0.5, 0.15625)
    edge_b1 = normal_values(streams_of[5], (H,), 0.5, 3.0, (), jnp.float32)
    edge_w2 = normal_values(streams_of[6], (H, D), H ** -0.5, 0.25)
    edge_b2 = normal_values(streams_of[7], (D,), 0.5, 3.0, (), jnp.float32)
    edge_gain = jnp.clip(1.0 + 0.18 * jax.random.normal(streams_of[8], (D,), jnp.float32), 0.1, 1.9)
    node_w1 = normal_values(streams_of[9], (2 * D, H), (2 * D) ** -0.5, 0.1875)
    node_b1 = normal_values(streams_of[10], (H,), 0.5, 3.0, (), jnp.float32)
    node_w2 = normal_values(streams_of[11], (H, D), H ** -0.5, 0.25)
    node_b2 = normal_values(streams_of[12], (D,), 0.5, 3.0, (), jnp.float32)
    node_gain = jnp.clip(1.0 + 0.18 * jax.random.normal(streams_of[13], (D,), jnp.float32), 0.1, 1.9)
    send_index = set_ends(jax.random.randint(part_keys[14], (N_TILES, N_TILES, SLOT), 0, NODE_DEV), jax.random.fold_in(part_keys[14], 1), 0, NODE_DEV - 1).astype(jnp.int32)
    edge_sender = draw_edge_sender(jax.random.fold_in(jax.random.fold_in(streams_of[18], part), 71), part)
    edge_receiver = set_ends(jax.random.randint(part_keys[16], (EDGES,), 0, NODE_DEV), jax.random.fold_in(part_keys[16], 1), 0, NODE_DEV - 1).astype(jnp.int32)
    edge_count = draw_edge_count(jax.random.fold_in(jax.random.fold_in(streams_of[18], part), 71), part)
    return {"node_latent": node_latent, "edge_latent": edge_latent, "node_cot": node_cot, "edge_cot": edge_cot, "edge_w1": edge_w1, "edge_b1": edge_b1, "edge_w2": edge_w2, "edge_b2": edge_b2, "edge_gain": edge_gain, "node_w1": node_w1, "node_b1": node_b1, "node_w2": node_w2, "node_b2": node_b2, "node_gain": node_gain, "send_index": send_index, "edge_sender": edge_sender, "edge_receiver": edge_receiver, "edge_count": edge_count}


EPSILON = 1e-05

def silu_slope(preact):
    sigmoid_value = jax.nn.sigmoid(preact)
    return sigmoid_value * (1.0 + preact * (1.0 - sigmoid_value))

def mlp_forward(inputs, w_first, b_first, w_second, b_second):
    preact = jnp.dot(inputs, w_first, preferred_element_type=jnp.float32) + b_first
    hidden = jax.nn.silu(preact).astype(jnp.bfloat16)
    output_pre = jnp.dot(hidden, w_second, preferred_element_type=jnp.float32) + b_second
    centred = output_pre - lax.optimization_barrier(jnp.mean(output_pre, axis=-1, keepdims=True))
    inverse = lax.rsqrt(lax.optimization_barrier(jnp.mean(centred * centred, axis=-1, keepdims=True)) + EPSILON)
    return (preact, hidden, centred * inverse, inverse)

def mlp_backward(inputs, preact, hidden, normed, inverse, grad_out, gain, w_first, w_second):
    scaled = grad_out * gain
    grad_outer = inverse * (scaled - lax.optimization_barrier(jnp.mean(scaled, axis=-1, keepdims=True)) - normed * lax.optimization_barrier(jnp.mean(scaled * normed, axis=-1, keepdims=True)))
    grad_outer = grad_outer.astype(jnp.bfloat16)
    grad_second = jnp.dot(hidden.T, grad_outer, preferred_element_type=jnp.float32)
    grad_hidden = jnp.dot(grad_outer, w_second.T, preferred_element_type=jnp.float32)
    grad_preact = (grad_hidden * silu_slope(preact)).astype(jnp.bfloat16)
    grad_first = jnp.dot(inputs.T, grad_preact, preferred_element_type=jnp.float32)
    grad_inputs = jnp.dot(grad_preact, w_first.T, preferred_element_type=jnp.float32)
    return (grad_inputs, grad_first, grad_second)

def reference(node_latent, edge_latent, node_cot, edge_cot, edge_w1, edge_b1, edge_w2, edge_b2, edge_gain, node_w1, node_b1, node_w2, node_b2, node_gain, send_index, edge_sender, edge_receiver, edge_count):

    def sender_nodes(device, sender_here):
        lower = (device - 1) * NODE_DEV + NODE_DEV - NEAR + sender_here
        own = device * NODE_DEV + sender_here - NEAR
        upper = (device + 1) * NODE_DEV + sender_here - NEAR - NODE_DEV
        far_slot = jnp.clip(sender_here - (NODE_DEV + 2 * NEAR), 0, N_TILES * SLOT - 1).astype(jnp.int32)
        owner = (far_slot // SLOT).astype(jnp.int32)
        far = owner * NODE_DEV + send_index[owner, device, far_slot % SLOT]
        chosen = jnp.where(sender_here < NEAR, lower, jnp.where(sender_here < NEAR + NODE_DEV, own, jnp.where(sender_here < 2 * NEAR + NODE_DEV, upper, far)))
        return jnp.clip(chosen, 0, NODES - 1).astype(jnp.int32)
    devices = jnp.arange(N_TILES, dtype=jnp.int32)
    node_blocks = node_latent.reshape(N_TILES, NODE_DEV, D)
    edge_blocks = edge_latent.reshape(N_TILES, EDGE_DEV, D)
    cot_blocks = edge_cot.reshape(N_TILES, EDGE_DEV, D)
    sender_blocks = edge_sender.reshape(N_TILES, EDGE_DEV)
    recv_blocks = edge_receiver.reshape(N_TILES, EDGE_DEV)
    positions = jnp.arange(EDGE_DEV, dtype=jnp.int32)

    def edge_forward(pieces):
        edges_here, sender_here, recv_here, live_count, device, nodes_here = pieces
        senders = node_latent[sender_nodes(device, sender_here)]
        receivers = nodes_here[recv_here]
        live_mask = (positions < live_count).astype(jnp.float32)[:, None]
        inputs = jnp.concatenate([edges_here, senders, receivers], axis=1)
        preact, hidden, normed, inverse = mlp_forward(inputs, edge_w1, edge_b1, edge_w2, edge_b2)
        return (inputs, preact, hidden, normed, inverse, live_mask)

    def aggregate(pieces):
        inputs, preact, hidden, normed, inverse, live_mask = edge_forward(pieces)
        update = (normed * edge_gain * live_mask).astype(jnp.bfloat16)
        return jax.ops.segment_sum(update.astype(jnp.float32), pieces[2], num_segments=NODE_DEV)
    pieces_all = (edge_blocks, sender_blocks, recv_blocks, edge_count, devices, node_blocks)
    summed = lax.map(aggregate, pieces_all).reshape(NODES, D).astype(jnp.bfloat16)
    node_inputs = jnp.concatenate([node_latent, summed], axis=1)
    preact_n, hidden_n, normed_n, inverse_n = mlp_forward(node_inputs, node_w1, node_b1, node_w2, node_b2)
    grad_node_inputs, grad_node_w1, grad_node_w2 = mlp_backward(node_inputs, preact_n, hidden_n, normed_n, inverse_n, node_cot.astype(jnp.float32), node_gain, node_w1, node_w2)
    direct = grad_node_inputs[:, :D]
    grad_summed = grad_node_inputs[:, D:].reshape(N_TILES, NODE_DEV, D)

    def edge_step(running, pieces):
        sender_acc, first_acc, second_acc = running
        cot_here, summed_here = (pieces[6], pieces[7])
        inputs, preact, hidden, normed, inverse, live_mask = edge_forward(pieces[:6])
        grad_update = cot_here.astype(jnp.float32) + summed_here[pieces[2]]
        grad_inputs, first_term, second_term = mlp_backward(inputs, preact, hidden, normed, inverse, grad_update, edge_gain[None, :] * live_mask, edge_w1, edge_w2)
        grad_edges = (cot_here.astype(jnp.float32) + grad_inputs[:, :D]).astype(jnp.bfloat16)
        receiver_part = jax.ops.segment_sum(grad_inputs[:, 2 * D:], pieces[2], num_segments=NODE_DEV)
        sender_acc = sender_acc.at[sender_nodes(pieces[4], pieces[1])].add(grad_inputs[:, D:2 * D])
        return ((sender_acc, first_acc + first_term, second_acc + second_term), (grad_edges, receiver_part))
    start_state = (jnp.zeros((NODES, D), jnp.float32), jnp.zeros((3 * D, H), jnp.float32), jnp.zeros((H, D), jnp.float32))
    final_state, outputs = lax.scan(edge_step, start_state, pieces_all + (cot_blocks, grad_summed))
    sender_acc, grad_edge_w1, grad_edge_w2 = final_state
    grad_edge_blocks, receiver_parts = outputs
    grad_node = (node_cot.astype(jnp.float32) + direct + receiver_parts.reshape(NODES, D) + sender_acc).astype(jnp.bfloat16)
    return (grad_node, grad_edge_blocks.reshape(EDGES, D), grad_edge_w1, grad_edge_w2, grad_node_w1, grad_node_w2)
```

```python
import functools

import jax
import jax.numpy as jnp
from jax import lax
from jax.experimental import pallas as pl
from jax.experimental.pallas import tpu as pltpu
from jax.sharding import PartitionSpec as P

NEAR = 64
EPSILON = 1e-05
TILE = 256
LANES = 128
F32 = jnp.float32
BF16 = jnp.bfloat16
MIB = 1024 * 1024

NN = (((1,), (0,)), ((), ()))
NT = (((1,), (1,)), ((), ()))
TN = (((0,), (0,)), ((), ()))


def dot(a, b, dims=NN):
    return lax.dot_general(a, b, dims, preferred_element_type=F32)


def sigmoid(x):
    return 0.5 * jnp.tanh(0.5 * x) + 0.5


def row_mean(x):
    return jnp.sum(x, axis=-1, keepdims=True) * (1.0 / x.shape[-1])


def ones_where(mask):
    return jnp.where(mask, 1.0, 0.0).astype(BF16)


def index_columns(idx_ref, step, tile):
    per = tile // LANES
    parts = []
    for j in range(per):
        row = idx_ref[pl.ds(step * per + j, 1), :]
        parts.append(jnp.transpose(jnp.broadcast_to(row, (LANES, LANES))))
    return jnp.concatenate(parts, axis=0)


def pick_columns(columns, width):
    lane = lax.broadcasted_iota(jnp.int32, columns.shape, 1)
    return [ones_where(columns == lane + c * LANES) for c in range(width // LANES)]


def pick_rows(idx_ref, step, tile, width):
    per = tile // LANES
    row = jnp.concatenate([idx_ref[pl.ds(step * per + j, 1), :] for j in range(per)], axis=1)
    return ones_where(lax.broadcasted_iota(jnp.int32, (width, tile), 0) == row)


def norm_forward(out):
    centred = out - row_mean(out)
    inverse = lax.rsqrt(row_mean(centred * centred) + EPSILON)
    return centred, inverse


def norm_backward(scaled, normed, inverse):
    return (
        inverse * (scaled - row_mean(scaled) - normed * row_mean(scaled * normed))
    ).astype(BF16)


def split_halves(bit, total_ref, at, rows, send_ref, keep_ref, offset):
    half = send_ref.shape[0]
    for q in range(half):
        there = pl.multiple_of((2 * q + 1 - bit) * rows, rows)
        here = pl.multiple_of((2 * q + bit) * rows, rows)
        send_ref[q, offset : offset + rows, :] = total_ref[pl.ds(at + there, rows), :].astype(BF16)
        keep_ref[q, offset : offset + rows, :] = total_ref[pl.ds(at + here, rows), :]


def outgoing_kernel(index_ref, node_ref, far_ref, head_ref, tail_ref):
    tiles, places = index_ref.shape[1], index_ref.shape[2]
    nodes = node_ref.shape[0]
    lane = lax.broadcasted_iota(jnp.int32, (tiles, nodes), 1)
    index = index_ref[0]
    for j in range(places):
        far_ref[j] = dot(ones_where(index[:, j : j + 1] == lane), node_ref[...]).astype(BF16)
    head_ref[...] = node_ref[:NEAR, :]
    tail_ref[...] = node_ref[nodes - NEAR :, :]


def sender_table_index(sender_ref, places, tiles, base):
    raw = sender_ref[...]
    far = raw - base
    moved = base + lax.rem(far, places) * tiles + lax.div(far, places)
    return jnp.where(raw >= base, moved, raw)


def forward_kernel(
    tiles, places, fast,
    count_ref, edge_ref, sender_ref, receiver_ref, node_ref, lower_ref, upper_ref, far_ref,
    w1_ref, b1_ref, w2_ref, b2_ref, gain_ref,
    nw1_ref, nb1_ref, nw2_ref, nb2_ref, ngain_ref, ncot_ref,
    hidden_ref, slope_ref, normed_ref, inverse_ref, table_ref, moved_ref, dsum_ref, base_ref,
    gsend_ref, gkeep_ref,
    weights, summed, grads,
):
    step = pl.program_id(0)
    last = pl.num_programs(0) - 1
    here = lax.axis_index("tiles")
    tile, latent = edge_ref.shape
    nodes = node_ref.shape[0]
    rows = table_ref.shape[0]
    far_base = nodes + 2 * NEAR

    @pl.when(step == 0)
    def _():
        moved_ref[...] = sender_table_index(sender_ref, places, tiles, far_base)
        table_ref[:NEAR, :] = lower_ref[...]
        table_ref[NEAR : NEAR + nodes, :] = node_ref[...]
        table_ref[NEAR + nodes : far_base, :] = upper_ref[...]
        for j in range(places):
            table_ref[far_base + j * tiles : far_base + (j + 1) * tiles, :] = far_ref[j]
        used = far_base + places * tiles
        if used < rows:
            table_ref[used:, :] = jnp.zeros((rows - used, latent), BF16)
        weights[:latent, :] = w1_ref[:latent, :]
        weights[latent : latent + rows, :] = dot(
            table_ref[...], w1_ref[latent : 2 * latent, :]
        ).astype(BF16)
        weights[latent + rows :, :] = dot(node_ref[...], w1_ref[2 * latent :, :]).astype(BF16)
        summed[...] = jnp.zeros_like(summed)

    senders = pick_columns(index_columns(moved_ref, step, tile), rows)
    receivers = pick_columns(index_columns(receiver_ref, step, tile), nodes)
    inputs = jnp.concatenate([edge_ref[...]] + senders + receivers, axis=1)
    preact = dot(inputs, weights[...]) + b1_ref[...]
    sig = sigmoid(preact)
    hidden = (preact * sig).astype(BF16)
    hidden_ref[...] = hidden
    slope_ref[...] = (sig * (1.0 + preact * (1.0 - sig))).astype(BF16)
    centred, inverse = norm_forward(dot(hidden, w2_ref[...]) + b2_ref[...])
    position = step * tile + lax.broadcasted_iota(jnp.int32, inverse.shape, 0)
    inverse = jnp.where(position < count_ref[here], inverse, 0.0)
    normed = centred * inverse
    normed_ref[...] = normed
    inverse_ref[...] = jnp.broadcast_to(inverse, inverse_ref.shape)
    update = (normed * gain_ref[...]).astype(BF16)
    summed[...] += dot(pick_rows(receiver_ref, step, tile, nodes), update)

    @pl.when(step == last)
    def _():
        node_in = jnp.concatenate([node_ref[...], summed[...].astype(BF16)], axis=1)
        preact_n = dot(node_in, nw1_ref[...]) + nb1_ref[...]
        sig_n = sigmoid(preact_n)
        hidden_n = (preact_n * sig_n).astype(BF16)
        centred_n, inverse_n = norm_forward(dot(hidden_n, nw2_ref[...]) + nb2_ref[...])
        cot = ncot_ref[...].astype(F32)
        dout = norm_backward(cot * ngain_ref[...], centred_n * inverse_n, inverse_n)
        slope_n = sig_n * (1.0 + preact_n * (1.0 - sig_n))
        dpre = (dot(dout, nw2_ref[...], NT) * slope_n).astype(BF16)
        grads[: 2 * latent, :] = dot(node_in, dpre, TN)
        grads[2 * latent :, :] = dot(hidden_n, dout, TN)
        base_ref[...] = cot + dot(dpre, nw1_ref[:latent, :], NT)
        dsum_ref[...] = dot(dpre, nw1_ref[latent:, :], NT).astype(BF16)
        if fast:
            bit = lax.rem(here, 2)
            first = 2 * latent // tiles
            split_halves(bit, grads, 0, first, gsend_ref, gkeep_ref, 0)
            split_halves(bit, grads, 2 * latent, latent // tiles, gsend_ref, gkeep_ref, first)
        else:
            gkeep_ref[...] = grads[: 2 * latent, :]
            gsend_ref[...] = grads[2 * latent :, :]


def slope_kernel(
    tiles, fast,
    cot_ref, receiver_ref, dsum_ref, hidden_ref, slope_ref, normed_ref, inverse_ref, w2_ref, gain_ref,
    dpre_ref, gsend_ref, gkeep_ref,
    grads,
):
    step = pl.program_id(0)
    last = pl.num_programs(0) - 1
    here = lax.axis_index("tiles")
    tile, latent = cot_ref.shape
    nodes = dsum_ref.shape[0]

    @pl.when(step == 0)
    def _():
        grads[...] = jnp.zeros_like(grads)

    receivers = jnp.concatenate(
        pick_columns(index_columns(receiver_ref, step, tile), nodes), axis=1
    )
    grad_update = cot_ref[...].astype(F32) + dot(receivers, dsum_ref[...])
    inverse = inverse_ref[:, :1]
    dout = norm_backward(grad_update * gain_ref[...], normed_ref[...], inverse)
    grads[...] += dot(hidden_ref[...], dout, TN)
    dpre_ref[...] = (dot(dout, w2_ref[...], NT) * slope_ref[...].astype(F32)).astype(BF16)

    @pl.when(step == last)
    def _():
        if fast:
            split_halves(lax.rem(here, 2), grads, 0, latent // tiles, gsend_ref, gkeep_ref, 0)
        else:
            gkeep_ref[...] = grads[...]
            gsend_ref[...] = jnp.zeros_like(gsend_ref)


def first_kernel(
    tiles, places, fast,
    dpre_ref, edge_ref, sender_ref, receiver_ref, table_ref, node_ref, w1_ref, base_ref,
    gsend_ref, gkeep_ref, lower_ref, upper_ref, far_ref, partial_ref,
    grads, sums,
):
    step = pl.program_id(0)
    last = pl.num_programs(0) - 1
    here = lax.axis_index("tiles")
    tile, latent = edge_ref.shape
    nodes = node_ref.shape[0]
    rows = table_ref.shape[0]

    @pl.when(step == 0)
    def _():
        grads[:latent, :] = jnp.zeros((latent, latent), F32)
        sums[...] = jnp.zeros_like(sums)

    dpre = dpre_ref[...]
    grads[:latent, :] += dot(edge_ref[...], dpre, TN)
    picks = jnp.concatenate(
        [
            pick_rows(sender_ref, step, tile, rows),
            pick_rows(receiver_ref, step, tile, nodes),
        ],
        axis=0,
    )
    sums[...] += dot(picks, dpre)

    @pl.when(step == last)
    def _():
        by_sender = sums[:rows, :].astype(BF16)
        by_receiver = sums[rows:, :].astype(BF16)
        grads[latent : 2 * latent, :] = dot(table_ref[...], by_sender, TN)
        grads[2 * latent :, :] = dot(node_ref[...], by_receiver, TN)
        if fast:
            split_halves(
                lax.rem(here, 2), grads, 0, 3 * latent // tiles, gsend_ref, gkeep_ref, 0
            )
        else:
            gkeep_ref[...] = grads[...]
            gsend_ref[...] = jnp.zeros_like(gsend_ref)
        back = dot(by_sender, w1_ref[latent : 2 * latent, :], NT)
        lower_ref[...] = back[:NEAR, :].astype(BF16)
        upper_ref[...] = back[NEAR + nodes : 2 * NEAR + nodes, :].astype(BF16)
        for j in range(places):
            at = 2 * NEAR + nodes + j * tiles
            far_ref[j] = back[at : at + tiles, :].astype(BF16)
        partial_ref[...] = (
            base_ref[...]
            + back[NEAR : NEAR + nodes, :]
            + dot(by_receiver, w1_ref[2 * latent :, :], NT)
        )


def edge_kernel(dpre_ref, cot_ref, w1_ref, out_ref):
    latent = cot_ref.shape[1]
    out_ref[...] = (
        cot_ref[...].astype(F32) + dot(dpre_ref[...], w1_ref[...], NT)
    ).astype(BF16)


def node_kernel(index_ref, partial_ref, below_ref, above_ref, far_ref, out_ref):
    tiles, places = index_ref.shape[1], index_ref.shape[2]
    nodes = partial_ref.shape[0]
    lane = lax.broadcasted_iota(jnp.int32, (tiles, nodes), 1)
    index = index_ref[0]
    total = partial_ref[...]
    for j in range(places):
        total = total + dot(ones_where(index[:, j : j + 1] == lane), far_ref[j], TN)
    out_ref[:NEAR, :] = (total[:NEAR, :] + below_ref[...].astype(F32)).astype(BF16)
    out_ref[NEAR : nodes - NEAR, :] = total[NEAR : nodes - NEAR, :].astype(BF16)
    out_ref[nodes - NEAR :, :] = (
        total[nodes - NEAR :, :] + above_ref[...].astype(F32)
    ).astype(BF16)


def halve_kernel(shift, keep_ref, got_ref, send_ref, kept_ref):
    bit = lax.rem(lax.div(lax.axis_index("tiles"), 2**shift), 2)
    send_ref[0] = (keep_ref[1 - bit] + got_ref[1 - bit].astype(F32)).astype(BF16)
    kept_ref[0] = keep_ref[bit] + got_ref[bit].astype(F32)


def spread_kernel(keep_ref, got_ref, own_ref, *send_refs):
    count = keep_ref.shape[0]
    place = lax.div(lax.axis_index("tiles"), 4)
    own_ref[...] = keep_ref[place] + got_ref[place].astype(F32)
    for k, send_ref in enumerate(send_refs):
        there = lax.rem(place + k + 1, count)
        send_ref[...] = (keep_ref[there] + got_ref[there].astype(F32)).astype(BF16)


def whole(shape=None):
    return pl.BlockSpec(memory_space=pltpu.VMEM)


def tiled(shape):
    zeros = (0,) * (len(shape) - 1)
    return pl.BlockSpec(shape, lambda i: (i,) + zeros)


def fixed(shape):
    zeros = (0,) * len(shape)
    return pl.BlockSpec(shape, lambda i: zeros, pipeline_mode=pl.Buffered(1))


def shaped(shape, dtype):
    return jax.ShapeDtypeStruct(shape, dtype)


def flip(tiles, bit):
    return [(i, i ^ bit) for i in range(tiles)]


def fold(send, keep, tiles):
    half, rows, width = keep.shape
    got = lax.ppermute(send, "tiles", flip(tiles, 1))
    quarter = half // 2
    send, keep = pl.pallas_call(
        functools.partial(halve_kernel, 1),
        grid=(quarter,),
        in_specs=[tiled((2, rows, width)), tiled((2, rows, width))],
        out_specs=[tiled((1, rows, width)), tiled((1, rows, width))],
        out_shape=[shaped((quarter, rows, width), BF16), shaped((quarter, rows, width), F32)],
        name="halve",
    )(keep, got)
    got = lax.ppermute(send, "tiles", flip(tiles, 2))
    own, *sends = pl.pallas_call(
        spread_kernel,
        out_shape=[shaped((rows, width), F32)] + [shaped((rows, width), BF16)] * (quarter - 1),
        name="spread",
    )(keep, got)
    total = own
    for k, send in enumerate(sends):
        pairs = [(i, (i // 4 + k + 1) % quarter * 4 + i % 4) for i in range(tiles)]
        total = total + lax.ppermute(send, "tiles", pairs).astype(F32)
    return total


def shards(
    node_latent, edge_latent, node_cot, edge_cot,
    edge_w1, edge_b1, edge_w2, edge_b2, edge_gain,
    node_w1, node_b1, node_w2, node_b2, node_gain,
    send_index, edge_sender, edge_receiver, edge_count,
):
    tiles = lax.axis_size("tiles")
    nodes, latent = node_latent.shape
    edges = edge_latent.shape[0]
    places = send_index.shape[2]
    steps = edges // TILE
    used = nodes + 2 * NEAR + places * tiles
    rows = -(-used // LANES) * LANES
    fast = tiles == 16
    half = tiles // 2
    upward = [(i, i + 1) for i in range(tiles - 1)]
    downward = [(i + 1, i) for i in range(tiles - 1)]
    sender = edge_sender.reshape(edges // LANES, LANES)
    receiver = edge_receiver.reshape(edges // LANES, LANES)
    row = lambda vector: vector.reshape(1, -1)
    params = pltpu.CompilerParams(vmem_limit_bytes=40 * MIB)
    edge_block = tiled((TILE, latent))
    vector = fixed((1, latent))
    square = fixed((latent, latent))

    outgoing, head, tail = pl.pallas_call(
        outgoing_kernel,
        out_shape=[
            shaped((places, tiles, latent), BF16),
            shaped((NEAR, latent), BF16),
            shaped((NEAR, latent), BF16),
        ],
        name="outgoing",
    )(send_index, node_latent)
    lower = lax.ppermute(tail, "tiles", upward)
    upper = lax.ppermute(head, "tiles", downward)
    incoming = lax.all_to_all(outgoing, "tiles", split_axis=1, concat_axis=1, tiled=True)

    if fast:
        grad_shapes = lambda count: [
            shaped((half, count // tiles, latent), BF16),
            shaped((half, count // tiles, latent), F32),
        ]
    else:
        grad_shapes = lambda count: [shaped((latent, latent), F32), shaped((count, latent), F32)]
    node_grads = grad_shapes(3 * latent) if fast else grad_shapes(2 * latent)
    hidden, slope, normed, inverse, table, moved, dsum, base, node_send, node_keep = pl.pallas_call(
        functools.partial(forward_kernel, tiles, places, fast),
        grid=(steps,),
        in_specs=[
            pl.BlockSpec(memory_space=pltpu.SMEM),
            edge_block,
            fixed(sender.shape), fixed(receiver.shape),
            fixed((nodes, latent)), fixed((NEAR, latent)), fixed((NEAR, latent)),
            fixed((places, tiles, latent)),
            fixed(edge_w1.shape), vector, square, vector, vector,
            fixed(node_w1.shape), vector, square, vector, vector,
            fixed((nodes, latent)),
        ],
        out_specs=[
            edge_block, edge_block, edge_block, tiled((TILE, LANES)),
            fixed((rows, latent)), fixed(sender.shape),
            fixed((nodes, latent)), fixed((nodes, latent)),
            fixed(node_grads[0].shape), fixed(node_grads[1].shape),
        ],
        out_shape=[
            shaped((edges, latent), BF16),
            shaped((edges, latent), BF16),
            shaped((edges, latent), F32),
            shaped((edges, LANES), F32),
            shaped((rows, latent), BF16),
            shaped(sender.shape, jnp.int32),
            shaped((nodes, latent), BF16),
            shaped((nodes, latent), F32),
        ] + node_grads,
        scratch_shapes=[
            pltpu.VMEM((latent + rows + nodes, latent), BF16),
            pltpu.VMEM((nodes, latent), F32),
            pltpu.VMEM((3 * latent, latent), F32),
        ],
        compiler_params=params,
        name="forward",
    )(
        edge_count, edge_latent, sender, receiver, node_latent, lower, upper, incoming,
        edge_w1, row(edge_b1), edge_w2, row(edge_b2), row(edge_gain),
        node_w1, row(node_b1), node_w2, row(node_b2), row(node_gain), node_cot,
    )

    second_grads = grad_shapes(latent)
    dpre, second_send, second_keep = pl.pallas_call(
        functools.partial(slope_kernel, tiles, fast),
        grid=(steps,),
        in_specs=[
            edge_block, fixed(receiver.shape), fixed((nodes, latent)),
            edge_block, edge_block, edge_block, tiled((TILE, LANES)), square, vector,
        ],
        out_specs=[edge_block, fixed(second_grads[0].shape), fixed(second_grads[1].shape)],
        out_shape=[shaped((edges, latent), BF16)] + second_grads,
        scratch_shapes=[pltpu.VMEM((latent, latent), F32)],
        compiler_params=params,
        name="slope",
    )(edge_cot, receiver, dsum, hidden, slope, normed, inverse, edge_w2, row(edge_gain))

    first_grads = grad_shapes(3 * latent)
    first_send, first_keep, to_lower, to_upper, to_far, partial = pl.pallas_call(
        functools.partial(first_kernel, tiles, places, fast),
        grid=(steps,),
        in_specs=[
            edge_block, edge_block, fixed(sender.shape), fixed(receiver.shape),
            fixed((rows, latent)), fixed((nodes, latent)), fixed(edge_w1.shape),
            fixed((nodes, latent)),
        ],
        out_specs=[
            fixed(first_grads[0].shape), fixed(first_grads[1].shape),
            fixed((NEAR, latent)), fixed((NEAR, latent)), fixed((places, tiles, latent)),
            fixed((nodes, latent)),
        ],
        out_shape=first_grads + [
            shaped((NEAR, latent), BF16),
            shaped((NEAR, latent), BF16),
            shaped((places, tiles, latent), BF16),
            shaped((nodes, latent), F32),
        ],
        scratch_shapes=[
            pltpu.VMEM((3 * latent, latent), F32),
            pltpu.VMEM((rows + nodes, latent), F32),
        ],
        compiler_params=params,
        name="first",
    )(dpre, edge_latent, moved, receiver, table, node_latent, edge_w1, base)

    grad_edge = pl.pallas_call(
        edge_kernel,
        grid=(steps,),
        in_specs=[edge_block, edge_block, square],
        out_specs=edge_block,
        out_shape=shaped((edges, latent), BF16),
        compiler_params=params,
        name="edge",
    )(dpre, edge_cot, edge_w1)

    above = lax.ppermute(to_lower, "tiles", downward)
    below = lax.ppermute(to_upper, "tiles", upward)
    returned = lax.all_to_all(to_far, "tiles", split_axis=1, concat_axis=1, tiled=True)
    grad_node = pl.pallas_call(
        node_kernel,
        out_shape=shaped((nodes, latent), BF16),
        name="node",
    )(send_index, partial, below, above, returned)

    if fast:
        node_total = fold(node_send, node_keep, tiles)
        cut = 2 * latent // tiles
        grad_node_w1, grad_node_w2 = node_total[:cut], node_total[cut:]
        grad_edge_w2 = fold(second_send, second_keep, tiles)
        grad_edge_w1 = fold(first_send, first_keep, tiles)
    else:
        scatter = functools.partial(
            lax.psum_scatter, axis_name="tiles", scatter_dimension=0, tiled=True
        )
        grad_node_w1, grad_node_w2 = scatter(node_keep), scatter(node_send)
        grad_edge_w1, grad_edge_w2 = scatter(first_keep), scatter(second_keep)
    return (grad_node, grad_edge, grad_edge_w1, grad_edge_w2, grad_node_w1, grad_node_w2)


def solution(mesh):
    split = P(("groups", "tiles"), None)
    return jax.shard_map(
        shards,
        mesh=mesh,
        in_specs=(split,) * 4
        + (P(),) * 10
        + (
            P(("groups", "tiles"), None, None),
            P(("groups", "tiles")),
            P(("groups", "tiles")),
            P("groups"),
        ),
        out_specs=(split,) * 6,
        check_vma=False,
    )
```

```python
import functools

import jax
import jax.numpy as jnp
from jax import lax
from jax.experimental import pallas as pl
from jax.experimental.pallas import tpu as pltpu
from jax.sharding import PartitionSpec as P

NEAR = 64
EPSILON = 1e-05
TILE = 512
LANES = 128
F32 = jnp.float32
BF16 = jnp.bfloat16
MIB = 1024 * 1024

NN = (((1,), (0,)), ((), ()))
NT = (((1,), (1,)), ((), ()))
TN = (((0,), (0,)), ((), ()))


def dot(a, b, dims=NN):
    return lax.dot_general(a, b, dims, preferred_element_type=F32)


def sigmoid(x):
    return 0.5 * jnp.tanh(0.5 * x) + 0.5


def row_mean(x):
    return jnp.sum(x, axis=-1, keepdims=True) * (1.0 / x.shape[-1])


def ones_where(mask):
    return jnp.where(mask, 1.0, 0.0).astype(BF16)


def index_columns(idx_ref, step, tile):
    per = tile // LANES
    parts = []
    for j in range(per):
        row = idx_ref[pl.ds(step * per + j, 1), :]
        parts.append(jnp.transpose(jnp.broadcast_to(row, (LANES, LANES))))
    return jnp.concatenate(parts, axis=0)


def pick_columns(columns, width):
    lane = lax.broadcasted_iota(jnp.int32, columns.shape, 1)
    return [ones_where(columns == lane + c * LANES) for c in range(width // LANES)]


def pick_rows(idx_ref, step, tile, width):
    per = tile // LANES
    row = jnp.concatenate([idx_ref[pl.ds(step * per + j, 1), :] for j in range(per)], axis=1)
    return ones_where(lax.broadcasted_iota(jnp.int32, (width, tile), 0) == row)


def norm_forward(out):
    centred = out - row_mean(out)
    inverse = lax.rsqrt(row_mean(centred * centred) + EPSILON)
    return centred, inverse


def norm_backward(scaled, normed, inverse):
    return (
        inverse * (scaled - row_mean(scaled) - normed * row_mean(scaled * normed))
    ).astype(BF16)


def split_halves(bit, total_ref, at, rows, send_ref, keep_ref, offset):
    half = send_ref.shape[0]
    for q in range(half):
        there = pl.multiple_of((2 * q + 1 - bit) * rows, rows)
        here = pl.multiple_of((2 * q + bit) * rows, rows)
        send_ref[q, offset : offset + rows, :] = total_ref[pl.ds(at + there, rows), :].astype(BF16)
        keep_ref[q, offset : offset + rows, :] = total_ref[pl.ds(at + here, rows), :]


def outgoing_kernel(index_ref, node_ref, far_ref, head_ref, tail_ref):
    places, tiles = index_ref.shape[1], index_ref.shape[2]
    nodes = node_ref.shape[0]
    place = lax.broadcasted_iota(jnp.int32, (nodes, tiles), 0)
    for j in range(places):
        picks = ones_where(place == index_ref[0, j : j + 1, :])
        far_ref[:, j, :] = dot(picks, node_ref[...], TN).astype(BF16)
    head_ref[...] = node_ref[:NEAR, :]
    tail_ref[...] = node_ref[nodes - NEAR :, :]


def sender_table_index(sender_ref, places, tiles, base):
    raw = sender_ref[...]
    far = raw - base
    moved = base + lax.rem(far, places) * tiles + lax.div(far, places)
    return jnp.where(raw >= base, moved, raw)


def forward_kernel(
    tiles, places, fast,
    count_ref, edge_ref, sender_ref, receiver_ref, node_ref, lower_ref, upper_ref, far_ref,
    w1_ref, b1_ref, w2_ref, b2_ref, gain_ref,
    nw1_ref, nb1_ref, nw2_ref, nb2_ref, ngain_ref, ncot_ref,
    hidden_ref, slope_ref, normed_ref, inverse_ref, table_ref, moved_ref, dsum_ref, base_ref,
    gsend_ref, gkeep_ref,
    weights, summed, grads,
):
    step = pl.program_id(0)
    last = pl.num_programs(0) - 1
    here = lax.axis_index("tiles")
    tile, latent = edge_ref.shape
    nodes = node_ref.shape[0]
    rows = table_ref.shape[0]
    far_base = nodes + 2 * NEAR

    @pl.when(step == 0)
    def _():
        moved_ref[...] = sender_table_index(sender_ref, places, tiles, far_base)
        table_ref[:NEAR, :] = lower_ref[...]
        table_ref[NEAR : NEAR + nodes, :] = node_ref[...]
        table_ref[NEAR + nodes : far_base, :] = upper_ref[...]
        for j in range(places):
            table_ref[far_base + j * tiles : far_base + (j + 1) * tiles, :] = far_ref[:, j, :]
        used = far_base + places * tiles
        if used < rows:
            table_ref[used:, :] = jnp.zeros((rows - used, latent), BF16)
        weights[:latent, :] = w1_ref[:latent, :]
        weights[latent : latent + rows, :] = dot(
            table_ref[...], w1_ref[latent : 2 * latent, :]
        ).astype(BF16)
        weights[latent + rows :, :] = dot(node_ref[...], w1_ref[2 * latent :, :]).astype(BF16)
        summed[...] = jnp.zeros_like(summed)

    senders = pick_columns(index_columns(moved_ref, step, tile), rows)
    receivers = pick_columns(index_columns(receiver_ref, step, tile), nodes)
    inputs = jnp.concatenate([edge_ref[...]] + senders + receivers, axis=1)
    preact = dot(inputs, weights[...]) + b1_ref[...]
    sig = sigmoid(preact)
    hidden = (preact * sig).astype(BF16)
    hidden_ref[...] = hidden
    slope_ref[...] = (sig * (1.0 + preact * (1.0 - sig))).astype(BF16)
    centred, inverse = norm_forward(dot(hidden, w2_ref[...]) + b2_ref[...])
    position = step * tile + lax.broadcasted_iota(jnp.int32, inverse.shape, 0)
    inverse = jnp.where(position < count_ref[here], inverse, 0.0)
    normed = centred * inverse
    normed_ref[...] = normed
    inverse_ref[...] = jnp.broadcast_to(inverse, inverse_ref.shape)
    update = (normed * gain_ref[...]).astype(BF16)
    summed[...] += dot(pick_rows(receiver_ref, step, tile, nodes), update)

    @pl.when(step == last)
    def _():
        node_in = jnp.concatenate([node_ref[...], summed[...].astype(BF16)], axis=1)
        preact_n = dot(node_in, nw1_ref[...]) + nb1_ref[...]
        sig_n = sigmoid(preact_n)
        hidden_n = (preact_n * sig_n).astype(BF16)
        centred_n, inverse_n = norm_forward(dot(hidden_n, nw2_ref[...]) + nb2_ref[...])
        cot = ncot_ref[...].astype(F32)
        dout = norm_backward(cot * ngain_ref[...], centred_n * inverse_n, inverse_n)
        slope_n = sig_n * (1.0 + preact_n * (1.0 - sig_n))
        dpre = (dot(dout, nw2_ref[...], NT) * slope_n).astype(BF16)
        grads[: 2 * latent, :] = dot(node_in, dpre, TN)
        grads[2 * latent :, :] = dot(hidden_n, dout, TN)
        base_ref[...] = cot + dot(dpre, nw1_ref[:latent, :], NT)
        dsum_ref[...] = dot(dpre, nw1_ref[latent:, :], NT).astype(BF16)
        if fast:
            bit = lax.rem(here, 2)
            first = 2 * latent // tiles
            split_halves(bit, grads, 0, first, gsend_ref, gkeep_ref, 0)
            split_halves(bit, grads, 2 * latent, latent // tiles, gsend_ref, gkeep_ref, first)
        else:
            gkeep_ref[...] = grads[: 2 * latent, :]
            gsend_ref[...] = grads[2 * latent :, :]


def slope_kernel(
    tiles, fast,
    cot_ref, receiver_ref, dsum_ref, hidden_ref, slope_ref, normed_ref, inverse_ref, w2_ref, gain_ref,
    dpre_ref, gsend_ref, gkeep_ref,
    grads,
):
    step = pl.program_id(0)
    last = pl.num_programs(0) - 1
    here = lax.axis_index("tiles")
    tile, latent = cot_ref.shape
    nodes = dsum_ref.shape[0]

    @pl.when(step == 0)
    def _():
        grads[...] = jnp.zeros_like(grads)

    receivers = jnp.concatenate(
        pick_columns(index_columns(receiver_ref, step, tile), nodes), axis=1
    )
    grad_update = cot_ref[...].astype(F32) + dot(receivers, dsum_ref[...])
    inverse = inverse_ref[:, :1]
    dout = norm_backward(grad_update * gain_ref[...], normed_ref[...], inverse)
    grads[...] += dot(hidden_ref[...], dout, TN)
    dpre_ref[...] = (dot(dout, w2_ref[...], NT) * slope_ref[...].astype(F32)).astype(BF16)

    @pl.when(step == last)
    def _():
        if fast:
            split_halves(lax.rem(here, 2), grads, 0, latent // tiles, gsend_ref, gkeep_ref, 0)
        else:
            gkeep_ref[...] = grads[...]
            gsend_ref[...] = jnp.zeros_like(gsend_ref)


def first_kernel(
    tiles, places, fast,
    dpre_ref, edge_ref, sender_ref, receiver_ref, table_ref, node_ref, w1_ref, base_ref,
    gsend_ref, gkeep_ref, lower_ref, upper_ref, far_ref, partial_ref,
    grads, sums,
):
    step = pl.program_id(0)
    last = pl.num_programs(0) - 1
    here = lax.axis_index("tiles")
    tile, latent = edge_ref.shape
    nodes = node_ref.shape[0]
    rows = table_ref.shape[0]

    @pl.when(step == 0)
    def _():
        grads[:latent, :] = jnp.zeros((latent, latent), F32)
        sums[...] = jnp.zeros_like(sums)

    dpre = dpre_ref[...]
    grads[:latent, :] += dot(edge_ref[...], dpre, TN)
    picks = jnp.concatenate(
        [
            pick_rows(sender_ref, step, tile, rows),
            pick_rows(receiver_ref, step, tile, nodes),
        ],
        axis=0,
    )
    sums[...] += dot(picks, dpre)

    @pl.when(step == last)
    def _():
        by_sender = sums[:rows, :].astype(BF16)
        by_receiver = sums[rows:, :].astype(BF16)
        grads[latent : 2 * latent, :] = dot(table_ref[...], by_sender, TN)
        grads[2 * latent :, :] = dot(node_ref[...], by_receiver, TN)
        if fast:
            split_halves(
                lax.rem(here, 2), grads, 0, 3 * latent // tiles, gsend_ref, gkeep_ref, 0
            )
        else:
            gkeep_ref[...] = grads[...]
            gsend_ref[...] = jnp.zeros_like(gsend_ref)
        back = dot(by_sender, w1_ref[latent : 2 * latent, :], NT)
        lower_ref[...] = back[:NEAR, :].astype(BF16)
        upper_ref[...] = back[NEAR + nodes : 2 * NEAR + nodes, :].astype(BF16)
        for j in range(places):
            at = 2 * NEAR + nodes + j * tiles
            far_ref[:, j, :] = back[at : at + tiles, :].astype(BF16)
        partial_ref[...] = (
            base_ref[...]
            + back[NEAR : NEAR + nodes, :]
            + dot(by_receiver, w1_ref[2 * latent :, :], NT)
        )


def edge_kernel(dpre_ref, cot_ref, w1_ref, out_ref):
    latent = cot_ref.shape[1]
    out_ref[...] = (
        cot_ref[...].astype(F32) + dot(dpre_ref[...], w1_ref[...], NT)
    ).astype(BF16)


def node_kernel(index_ref, partial_ref, below_ref, above_ref, far_ref, out_ref):
    places, tiles = index_ref.shape[1], index_ref.shape[2]
    nodes = partial_ref.shape[0]
    place = lax.broadcasted_iota(jnp.int32, (nodes, tiles), 0)
    total = partial_ref[...]
    for j in range(places):
        picks = ones_where(place == index_ref[0, j : j + 1, :])
        total = total + dot(picks, far_ref[:, j, :])
    out_ref[:NEAR, :] = (total[:NEAR, :] + below_ref[...].astype(F32)).astype(BF16)
    out_ref[NEAR : nodes - NEAR, :] = total[NEAR : nodes - NEAR, :].astype(BF16)
    out_ref[nodes - NEAR :, :] = (
        total[nodes - NEAR :, :] + above_ref[...].astype(F32)
    ).astype(BF16)


def halve_kernel(shift, count, *refs):
    keeps, gots = refs[:count], refs[count : 2 * count]
    send_ref, kept_ref = refs[2 * count :]
    bit = lax.rem(lax.div(lax.axis_index("tiles"), 2**shift), 2)
    at = 0
    for keep_ref, got_ref in zip(keeps, gots):
        rows = keep_ref.shape[1]
        for q in range(keep_ref.shape[0] // 2):
            there, here = 2 * q + 1 - bit, 2 * q + bit
            send_ref[q, at : at + rows, :] = (
                keep_ref[there] + got_ref[there].astype(F32)
            ).astype(BF16)
            kept_ref[q, at : at + rows, :] = keep_ref[here] + got_ref[here].astype(F32)
        at += rows


def spread_kernel(keep_ref, got_ref, own_ref, *send_refs):
    count = keep_ref.shape[0]
    place = lax.div(lax.axis_index("tiles"), 4)
    own_ref[...] = keep_ref[place] + got_ref[place].astype(F32)
    for k, send_ref in enumerate(send_refs):
        there = lax.rem(place + k + 1, count)
        send_ref[...] = (keep_ref[there] + got_ref[there].astype(F32)).astype(BF16)


def finish_kernel(count, own_ref, *refs):
    total = own_ref[...]
    for got_ref in refs[:count]:
        total = total + got_ref[...].astype(F32)
    at = 0
    for out_ref in refs[count:]:
        out_ref[...] = total[at : at + out_ref.shape[0], :]
        at += out_ref.shape[0]


def tiled(shape):
    zeros = (0,) * (len(shape) - 1)
    return pl.BlockSpec(shape, lambda i: (i,) + zeros)


def fixed(shape):
    zeros = (0,) * len(shape)
    return pl.BlockSpec(shape, lambda i: zeros, pipeline_mode=pl.Buffered(1))


def shaped(shape, dtype):
    return jax.ShapeDtypeStruct(shape, dtype)


def swap(tiles, bit, send):
    return lax.ppermute(send, "tiles", [(i, i ^ bit) for i in range(tiles)])


def halve(keeps, gots):
    half, _, width = keeps[0].shape
    rows = sum(keep.shape[1] for keep in keeps)
    return pl.pallas_call(
        functools.partial(halve_kernel, 1, len(keeps)),
        out_shape=[shaped((half // 2, rows, width), BF16), shaped((half // 2, rows, width), F32)],
        compiler_params=pltpu.CompilerParams(vmem_limit_bytes=16 * MIB),
        name="halve",
    )(*keeps, *gots)


def spread(keep, got):
    quarter, rows, width = keep.shape
    return pl.pallas_call(
        spread_kernel,
        out_shape=[shaped((rows, width), F32)] + [shaped((rows, width), BF16)] * (quarter - 1),
        compiler_params=pltpu.CompilerParams(vmem_limit_bytes=16 * MIB),
        name="spread",
    )(keep, got)


def exchange(tiles, sends):
    quarter = len(sends) + 1
    gots = []
    for k, send in enumerate(sends):
        pairs = [(i, (i // 4 + k + 1) % quarter * 4 + i % 4) for i in range(tiles)]
        gots.append(lax.ppermute(send, "tiles", pairs))
    return gots


def finish(own, gots, sizes):
    return pl.pallas_call(
        functools.partial(finish_kernel, len(gots)),
        out_shape=[shaped((size, own.shape[1]), F32) for size in sizes],
        compiler_params=pltpu.CompilerParams(vmem_limit_bytes=16 * MIB),
        name="finish",
    )(own, *gots)


def shards(
    node_latent, edge_latent, node_cot, edge_cot,
    edge_w1, edge_b1, edge_w2, edge_b2, edge_gain,
    node_w1, node_b1, node_w2, node_b2, node_gain,
    send_index, edge_sender, edge_receiver, edge_count,
):
    tiles = lax.axis_size("tiles")
    nodes, latent = node_latent.shape
    edges = edge_latent.shape[0]
    places = send_index.shape[2]
    steps = edges // TILE
    used = nodes + 2 * NEAR + places * tiles
    rows = -(-used // LANES) * LANES
    fast = tiles == 16
    half = tiles // 2
    upward = [(i, i + 1) for i in range(tiles - 1)]
    downward = [(i + 1, i) for i in range(tiles - 1)]
    sender = edge_sender.reshape(edges // LANES, LANES)
    receiver = edge_receiver.reshape(edges // LANES, LANES)
    listed = jnp.swapaxes(send_index, 1, 2)
    row = lambda vector: vector.reshape(1, -1)
    params = pltpu.CompilerParams(vmem_limit_bytes=60 * MIB)
    edge_block = tiled((TILE, latent))
    vector = fixed((1, latent))
    square = fixed((latent, latent))

    outgoing, head, tail = pl.pallas_call(
        outgoing_kernel,
        out_shape=[
            shaped((tiles, places, latent), BF16),
            shaped((NEAR, latent), BF16),
            shaped((NEAR, latent), BF16),
        ],
        compiler_params=pltpu.CompilerParams(vmem_limit_bytes=16 * MIB),
        name="outgoing",
    )(listed, node_latent)
    lower = lax.ppermute(tail, "tiles", upward)
    upper = lax.ppermute(head, "tiles", downward)
    incoming = lax.all_to_all(outgoing, "tiles", split_axis=0, concat_axis=0, tiled=True)

    if fast:
        grad_shapes = lambda count: [
            shaped((half, count // tiles, latent), BF16),
            shaped((half, count // tiles, latent), F32),
        ]
    else:
        grad_shapes = lambda count: [shaped((latent, latent), F32), shaped((count, latent), F32)]
    node_grads = grad_shapes(3 * latent) if fast else grad_shapes(2 * latent)
    hidden, slope, normed, inverse, table, moved, dsum, base, node_send, node_keep = pl.pallas_call(
        functools.partial(forward_kernel, tiles, places, fast),
        grid=(steps,),
        in_specs=[
            pl.BlockSpec(memory_space=pltpu.SMEM),
            edge_block,
            fixed(sender.shape), fixed(receiver.shape),
            fixed((nodes, latent)), fixed((NEAR, latent)), fixed((NEAR, latent)),
            fixed((tiles, places, latent)),
            fixed(edge_w1.shape), vector, square, vector, vector,
            fixed(node_w1.shape), vector, square, vector, vector,
            fixed((nodes, latent)),
        ],
        out_specs=[
            edge_block, edge_block, edge_block, tiled((TILE, LANES)),
            fixed((rows, latent)), fixed(sender.shape),
            fixed((nodes, latent)), fixed((nodes, latent)),
            fixed(node_grads[0].shape), fixed(node_grads[1].shape),
        ],
        out_shape=[
            shaped((edges, latent), BF16),
            shaped((edges, latent), BF16),
            shaped((edges, latent), F32),
            shaped((edges, LANES), F32),
            shaped((rows, latent), BF16),
            shaped(sender.shape, jnp.int32),
            shaped((nodes, latent), BF16),
            shaped((nodes, latent), F32),
        ] + node_grads,
        scratch_shapes=[
            pltpu.VMEM((latent + rows + nodes, latent), BF16),
            pltpu.VMEM((nodes, latent), F32),
            pltpu.VMEM((3 * latent, latent), F32),
        ],
        compiler_params=params,
        name="forward",
    )(
        edge_count, edge_latent, sender, receiver, node_latent, lower, upper, incoming,
        edge_w1, row(edge_b1), edge_w2, row(edge_b2), row(edge_gain),
        node_w1, row(node_b1), node_w2, row(node_b2), row(node_gain), node_cot,
    )

    second_grads = grad_shapes(latent)
    dpre, second_send, second_keep = pl.pallas_call(
        functools.partial(slope_kernel, tiles, fast),
        grid=(steps,),
        in_specs=[
            edge_block, fixed(receiver.shape), fixed((nodes, latent)),
            edge_block, edge_block, edge_block, tiled((TILE, LANES)), square, vector,
        ],
        out_specs=[edge_block, fixed(second_grads[0].shape), fixed(second_grads[1].shape)],
        out_shape=[shaped((edges, latent), BF16)] + second_grads,
        scratch_shapes=[pltpu.VMEM((latent, latent), F32)],
        compiler_params=params,
        name="slope",
    )(edge_cot, receiver, dsum, hidden, slope, normed, inverse, edge_w2, row(edge_gain))

    if fast:
        send, chain = halve(
            [node_keep, second_keep],
            [swap(tiles, 1, node_send), swap(tiles, 1, second_send)],
        )
        dpre, send = lax.optimization_barrier((dpre, send))
        got = swap(tiles, 2, send)

    first_grads = grad_shapes(3 * latent)
    first_send, first_keep, to_lower, to_upper, to_far, partial = pl.pallas_call(
        functools.partial(first_kernel, tiles, places, fast),
        grid=(steps,),
        in_specs=[
            edge_block, edge_block, fixed(sender.shape), fixed(receiver.shape),
            fixed((rows, latent)), fixed((nodes, latent)), fixed(edge_w1.shape),
            fixed((nodes, latent)),
        ],
        out_specs=[
            fixed(first_grads[0].shape), fixed(first_grads[1].shape),
            fixed((NEAR, latent)), fixed((NEAR, latent)), fixed((tiles, places, latent)),
            fixed((nodes, latent)),
        ],
        out_shape=first_grads + [
            shaped((NEAR, latent), BF16),
            shaped((NEAR, latent), BF16),
            shaped((tiles, places, latent), BF16),
            shaped((nodes, latent), F32),
        ],
        scratch_shapes=[
            pltpu.VMEM((3 * latent, latent), F32),
            pltpu.VMEM((rows + nodes, latent), F32),
        ],
        compiler_params=params,
        name="first",
    )(dpre, edge_latent, moved, receiver, table, node_latent, edge_w1, base)

    grad_edge = pl.pallas_call(
        edge_kernel,
        grid=(steps,),
        in_specs=[edge_block, edge_block, square],
        out_specs=edge_block,
        out_shape=shaped((edges, latent), BF16),
        compiler_params=params,
        name="edge",
    )(dpre, edge_cot, edge_w1)

    above = lax.ppermute(to_lower, "tiles", downward)
    below = lax.ppermute(to_upper, "tiles", upward)
    returned = lax.all_to_all(to_far, "tiles", split_axis=0, concat_axis=0, tiled=True)
    grad_node = pl.pallas_call(
        node_kernel,
        out_shape=shaped((nodes, latent), BF16),
        compiler_params=pltpu.CompilerParams(vmem_limit_bytes=16 * MIB),
        name="node",
    )(listed, partial, below, above, returned)

    if fast:
        send, late_chain = halve([first_keep], [swap(tiles, 1, first_send)])
        late_got = swap(tiles, 2, send)
        own, *sends = spread(chain, got)
        per = latent // tiles
        grad_node_w1, grad_node_w2, grad_edge_w2 = finish(
            own, exchange(tiles, sends), [2 * per, per, per]
        )
        own, *sends = spread(late_chain, late_got)
        (grad_edge_w1,) = finish(own, exchange(tiles, sends), [3 * per])
    else:
        scatter = functools.partial(
            lax.psum_scatter, axis_name="tiles", scatter_dimension=0, tiled=True
        )
        grad_node_w1, grad_node_w2 = scatter(node_keep), scatter(node_send)
        grad_edge_w1, grad_edge_w2 = scatter(first_keep), scatter(second_keep)
    return (grad_node, grad_edge, grad_edge_w1, grad_edge_w2, grad_node_w1, grad_node_w2)


def solution(mesh):
    split = P(("groups", "tiles"), None)
    return jax.shard_map(
        shards,
        mesh=mesh,
        in_specs=(split,) * 4
        + (P(),) * 10
        + (
            P(("groups", "tiles"), None, None),
            P(("groups", "tiles")),
            P(("groups", "tiles")),
            P("groups"),
        ),
        out_specs=(split,) * 6,
        check_vma=False,
    )
```

```python
import functools

import jax
import jax.numpy as jnp
from jax import lax
from jax.experimental import pallas as pl
from jax.experimental.pallas import tpu as pltpu
from jax.sharding import PartitionSpec as P

NEAR = 64
EPSILON = 1e-05
TILE = 256
LANES = 128
F32 = jnp.float32
BF16 = jnp.bfloat16
MIB = 1024 * 1024

NN = (((1,), (0,)), ((), ()))
NT = (((1,), (1,)), ((), ()))
TN = (((0,), (0,)), ((), ()))


def dot(a, b, dims=NN):
    return lax.dot_general(a, b, dims, preferred_element_type=F32)


def sigmoid(x):
    return 0.5 * jnp.tanh(0.5 * x) + 0.5


def row_mean(x):
    return jnp.sum(x, axis=-1, keepdims=True) * (1.0 / x.shape[-1])


def ones_where(mask):
    return jnp.where(mask, 1.0, 0.0).astype(BF16)


def index_columns(idx_ref, step, tile):
    per = tile // LANES
    parts = []
    for j in range(per):
        row = idx_ref[pl.ds(step * per + j, 1), :]
        parts.append(jnp.transpose(jnp.broadcast_to(row, (LANES, LANES))))
    return jnp.concatenate(parts, axis=0)


def pick_columns(columns, width):
    lane = lax.broadcasted_iota(jnp.int32, columns.shape, 1)
    return [ones_where(columns == lane + c * LANES) for c in range(width // LANES)]


def pick_rows(idx_ref, step, tile, width):
    per = tile // LANES
    row = jnp.concatenate([idx_ref[pl.ds(step * per + j, 1), :] for j in range(per)], axis=1)
    return ones_where(lax.broadcasted_iota(jnp.int32, (width, tile), 0) == row)


def norm_forward(out):
    centred = out - row_mean(out)
    inverse = lax.rsqrt(row_mean(centred * centred) + EPSILON)
    return centred, inverse


def norm_backward(scaled, normed, inverse):
    return (
        inverse * (scaled - row_mean(scaled) - normed * row_mean(scaled * normed))
    ).astype(BF16)


def split_halves(bit, total_ref, at, rows, send_ref, keep_ref, offset):
    half = send_ref.shape[0]
    for q in range(half):
        there = pl.multiple_of((2 * q + 1 - bit) * rows, rows)
        here = pl.multiple_of((2 * q + bit) * rows, rows)
        send_ref[q, offset : offset + rows, :] = total_ref[pl.ds(at + there, rows), :].astype(BF16)
        keep_ref[q, offset : offset + rows, :] = total_ref[pl.ds(at + here, rows), :]


def fetch(pairs, sems):
    copies = []
    for at, (source, target) in enumerate(pairs):
        copies.append(pltpu.make_async_copy(source, target, sems.at[at]))
    for copy in copies:
        copy.start()
    return copies


def tile_pairs(source, target, tile):
    return [
        (source.at[pl.ds(at, tile)], target.at[pl.ds(at, tile)])
        for at in range(0, source.shape[0], tile)
    ]


def outgoing_kernel(index_hbm, node_hbm, far_ref, head_ref, tail_ref, index_ref, node_ref, sems):
    for copy in fetch([(index_hbm, index_ref), (node_hbm, node_ref)], sems):
        copy.wait()
    places, tiles = index_ref.shape[1], index_ref.shape[2]
    nodes = node_ref.shape[0]
    place = lax.broadcasted_iota(jnp.int32, (nodes, tiles), 0)
    for j in range(places):
        picks = ones_where(place == index_ref[0, j : j + 1, :])
        far_ref[:, j, :] = dot(picks, node_ref[...], TN).astype(BF16)
    head_ref[...] = node_ref[:NEAR, :]
    tail_ref[...] = node_ref[nodes - NEAR :, :]


def sender_table_index(raw, places, tiles, base):
    far = raw - base
    moved = base + lax.rem(far, places) * tiles + lax.div(far, places)
    return jnp.where(raw >= base, moved, raw)


def forward_kernel(
    tiles, places, fast,
    edge_hbm, w1_hbm, w2_hbm, nw1_hbm, nw2_hbm, node_hbm, ncot_hbm,
    sender_hbm, receiver_hbm, b1_hbm, b2_hbm, gain_hbm, nb1_hbm, nb2_hbm, ngain_hbm, count_hbm,
    lower_ref, upper_ref, far_ref,
    edge_ref, w1_ref, w2_ref, node_ref, receiver_ref, gain_ref,
    hidden_ref, slope_ref, normed_ref, inverse_ref, table_ref, moved_ref, dsum_ref, base_ref,
    gsend_ref, gkeep_ref,
    weights, summed, grads, nw1_ref, nw2_ref, ncot_ref, sender_ref,
    b1_ref, b2_ref, nb1_ref, nb2_ref, ngain_ref, count_ref, sems, edge_sems,
):
    here = lax.axis_index("tiles")
    edges, latent = edge_ref.shape
    nodes = node_ref.shape[0]
    rows = table_ref.shape[0]
    far_base = nodes + 2 * NEAR

    early = fetch(
        [
            (node_hbm, node_ref), (w1_hbm, w1_ref), (sender_hbm, sender_ref),
            (receiver_hbm, receiver_ref), (b1_hbm, b1_ref), (b2_hbm, b2_ref),
            (gain_hbm, gain_ref), (count_hbm, count_ref), (w2_hbm, w2_ref),
        ],
        sems,
    )
    edge_copies = fetch(tile_pairs(edge_hbm, edge_ref, TILE), edge_sems)
    late = fetch(
        [
            (nw1_hbm, nw1_ref), (nw2_hbm, nw2_ref), (ncot_hbm, ncot_ref),
            (nb1_hbm, nb1_ref), (nb2_hbm, nb2_ref), (ngain_hbm, ngain_ref),
        ],
        sems.at[pl.ds(len(early), 6)],
    )

    for copy in early:
        copy.wait()
    moved_ref[...] = sender_table_index(sender_ref[...], places, tiles, far_base)
    table_ref[:NEAR, :] = lower_ref[...]
    table_ref[NEAR : NEAR + nodes, :] = node_ref[...]
    table_ref[NEAR + nodes : far_base, :] = upper_ref[...]
    for j in range(places):
        table_ref[far_base + j * tiles : far_base + (j + 1) * tiles, :] = far_ref[:, j, :]
    used = far_base + places * tiles
    if used < rows:
        table_ref[used:, :] = jnp.zeros((rows - used, latent), BF16)
    weights[:latent, :] = w1_ref[:latent, :]
    weights[latent : latent + rows, :] = dot(
        table_ref[...], w1_ref[latent : 2 * latent, :]
    ).astype(BF16)
    weights[latent + rows :, :] = dot(node_ref[...], w1_ref[2 * latent :, :]).astype(BF16)

    for step in range(edges // TILE):
        edge_copies[step].wait()
        tile = slice(step * TILE, (step + 1) * TILE)
        senders = pick_columns(index_columns(moved_ref, step, TILE), rows)
        receivers = pick_columns(index_columns(receiver_ref, step, TILE), nodes)
        inputs = jnp.concatenate([edge_ref[tile, :]] + senders + receivers, axis=1)
        preact = dot(inputs, weights[...]) + b1_ref[...]
        sig = sigmoid(preact)
        hidden = (preact * sig).astype(BF16)
        hidden_ref[tile, :] = hidden
        slope_ref[tile, :] = (sig * (1.0 + preact * (1.0 - sig))).astype(BF16)
        centred, inverse = norm_forward(dot(hidden, w2_ref[...]) + b2_ref[...])
        position = step * TILE + lax.broadcasted_iota(jnp.int32, inverse.shape, 0)
        inverse = jnp.where(position < count_ref[here], inverse, 0.0)
        normed = centred * inverse
        normed_ref[tile, :] = normed
        inverse_ref[tile, :] = jnp.broadcast_to(inverse, (TILE, LANES))
        update = (normed * gain_ref[...]).astype(BF16)
        part = dot(pick_rows(receiver_ref, step, TILE, nodes), update)
        if step == 0:
            summed[...] = part
        else:
            summed[...] += part

    for copy in late:
        copy.wait()
    node_in = jnp.concatenate([node_ref[...], summed[...].astype(BF16)], axis=1)
    preact_n = dot(node_in, nw1_ref[...]) + nb1_ref[...]
    sig_n = sigmoid(preact_n)
    hidden_n = (preact_n * sig_n).astype(BF16)
    centred_n, inverse_n = norm_forward(dot(hidden_n, nw2_ref[...]) + nb2_ref[...])
    cot = ncot_ref[...].astype(F32)
    dout = norm_backward(cot * ngain_ref[...], centred_n * inverse_n, inverse_n)
    slope_n = sig_n * (1.0 + preact_n * (1.0 - sig_n))
    dpre = (dot(dout, nw2_ref[...], NT) * slope_n).astype(BF16)
    grads[: 2 * latent, :] = dot(node_in, dpre, TN)
    grads[2 * latent :, :] = dot(hidden_n, dout, TN)
    base_ref[...] = cot + dot(dpre, nw1_ref[:latent, :], NT)
    dsum_ref[...] = dot(dpre, nw1_ref[latent:, :], NT).astype(BF16)
    if fast:
        bit = lax.rem(here, 2)
        first = 2 * latent // tiles
        split_halves(bit, grads, 0, first, gsend_ref, gkeep_ref, 0)
        split_halves(bit, grads, 2 * latent, latent // tiles, gsend_ref, gkeep_ref, first)
    else:
        gkeep_ref[...] = grads[: 2 * latent, :]
        gsend_ref[...] = grads[2 * latent :, :]


def slope_kernel(
    tiles, fast,
    cot_hbm, receiver_ref, dsum_ref, hidden_ref, slope_ref, normed_ref, inverse_ref, w2_ref, gain_ref,
    cot_ref, dpre_ref, gsend_ref, gkeep_ref,
    grads, sems,
):
    here = lax.axis_index("tiles")
    edges, latent = cot_ref.shape
    nodes = dsum_ref.shape[0]
    copies = fetch(tile_pairs(cot_hbm, cot_ref, TILE), sems)

    for step in range(edges // TILE):
        copies[step].wait()
        tile = slice(step * TILE, (step + 1) * TILE)
        receivers = jnp.concatenate(
            pick_columns(index_columns(receiver_ref, step, TILE), nodes), axis=1
        )
        grad_update = cot_ref[tile, :].astype(F32) + dot(receivers, dsum_ref[...])
        inverse = inverse_ref[tile, :1]
        dout = norm_backward(grad_update * gain_ref[...], normed_ref[tile, :], inverse)
        dpre_ref[tile, :] = (
            dot(dout, w2_ref[...], NT) * slope_ref[tile, :].astype(F32)
        ).astype(BF16)
        part = dot(hidden_ref[tile, :], dout, TN)
        if step == 0:
            grads[...] = part
        else:
            grads[...] += part

    if fast:
        split_halves(lax.rem(here, 2), grads, 0, latent // tiles, gsend_ref, gkeep_ref, 0)
    else:
        gkeep_ref[...] = grads[...]
        gsend_ref[...] = jnp.zeros_like(gsend_ref)


def first_kernel(
    tiles, places, fast,
    dpre_ref, edge_ref, sender_ref, receiver_ref, table_ref, node_ref, w1_ref, base_ref,
    gsend_ref, gkeep_ref, lower_ref, upper_ref, far_ref, partial_ref,
    grads, sums,
):
    here = lax.axis_index("tiles")
    edges, latent = edge_ref.shape
    nodes = node_ref.shape[0]
    rows = table_ref.shape[0]

    for step in range(edges // TILE):
        tile = slice(step * TILE, (step + 1) * TILE)
        dpre = dpre_ref[tile, :]
        part = dot(edge_ref[tile, :], dpre, TN)
        picks = jnp.concatenate(
            [
                pick_rows(sender_ref, step, TILE, rows),
                pick_rows(receiver_ref, step, TILE, nodes),
            ],
            axis=0,
        )
        scattered = dot(picks, dpre)
        if step == 0:
            grads[:latent, :] = part
            sums[...] = scattered
        else:
            grads[:latent, :] += part
            sums[...] += scattered

    by_sender = sums[:rows, :].astype(BF16)
    by_receiver = sums[rows:, :].astype(BF16)
    grads[latent : 2 * latent, :] = dot(table_ref[...], by_sender, TN)
    grads[2 * latent :, :] = dot(node_ref[...], by_receiver, TN)
    if fast:
        split_halves(lax.rem(here, 2), grads, 0, 3 * latent // tiles, gsend_ref, gkeep_ref, 0)
    else:
        gkeep_ref[...] = grads[...]
        gsend_ref[...] = jnp.zeros_like(gsend_ref)
    back = dot(by_sender, w1_ref[latent : 2 * latent, :], NT)
    lower_ref[...] = back[:NEAR, :].astype(BF16)
    upper_ref[...] = back[NEAR + nodes : 2 * NEAR + nodes, :].astype(BF16)
    for j in range(places):
        at = 2 * NEAR + nodes + j * tiles
        far_ref[:, j, :] = back[at : at + tiles, :].astype(BF16)
    partial_ref[...] = (
        base_ref[...]
        + back[NEAR : NEAR + nodes, :]
        + dot(by_receiver, w1_ref[2 * latent :, :], NT)
    )


def edge_kernel(dpre_ref, cot_ref, w1_ref, out_hbm, out_ref, sems):
    edges, latent = cot_ref.shape
    copies = []
    for step in range(edges // TILE):
        tile = pl.ds(step * TILE, TILE)
        out_ref[tile, :] = (
            cot_ref[tile, :].astype(F32) + dot(dpre_ref[tile, :], w1_ref[:latent, :], NT)
        ).astype(BF16)
        copy = pltpu.make_async_copy(out_ref.at[tile], out_hbm.at[tile], sems.at[step])
        copy.start()
        copies.append(copy)
    for copy in copies:
        copy.wait()


def node_kernel(index_ref, partial_ref, below_ref, above_ref, far_ref, out_ref):
    places, tiles = index_ref.shape[1], index_ref.shape[2]
    nodes = partial_ref.shape[0]
    place = lax.broadcasted_iota(jnp.int32, (nodes, tiles), 0)
    total = partial_ref[...]
    for j in range(places):
        picks = ones_where(place == index_ref[0, j : j + 1, :])
        total = total + dot(picks, far_ref[:, j, :])
    out_ref[:NEAR, :] = (total[:NEAR, :] + below_ref[...].astype(F32)).astype(BF16)
    out_ref[NEAR : nodes - NEAR, :] = total[NEAR : nodes - NEAR, :].astype(BF16)
    out_ref[nodes - NEAR :, :] = (
        total[nodes - NEAR :, :] + above_ref[...].astype(F32)
    ).astype(BF16)


def halve_kernel(shift, count, *refs):
    keeps, gots = refs[:count], refs[count : 2 * count]
    send_ref, kept_ref = refs[2 * count :]
    bit = lax.rem(lax.div(lax.axis_index("tiles"), 2**shift), 2)
    at = 0
    for keep_ref, got_ref in zip(keeps, gots):
        rows = keep_ref.shape[1]
        for q in range(keep_ref.shape[0] // 2):
            there, here = 2 * q + 1 - bit, 2 * q + bit
            send_ref[q, at : at + rows, :] = (
                keep_ref[there] + got_ref[there].astype(F32)
            ).astype(BF16)
            kept_ref[q, at : at + rows, :] = keep_ref[here] + got_ref[here].astype(F32)
        at += rows


def spread_kernel(keep_ref, got_ref, own_ref, send_ref):
    place = lax.div(lax.axis_index("tiles"), 4)
    own_ref[...] = keep_ref[place] + got_ref[place].astype(F32)
    for q in range(keep_ref.shape[0]):
        send_ref[q] = (keep_ref[q] + got_ref[q].astype(F32)).astype(BF16)


def finish_kernel(own_ref, got_ref, *out_refs):
    count = got_ref.shape[0]
    place = lax.div(lax.axis_index("tiles"), 4)
    total = own_ref[...]
    for k in range(1, count):
        total = total + got_ref[lax.rem(place + k, count)].astype(F32)
    at = 0
    for out_ref in out_refs:
        out_ref[...] = total[at : at + out_ref.shape[0], :]
        at += out_ref.shape[0]


def shaped(shape, dtype):
    return jax.ShapeDtypeStruct(shape, dtype)


def in_hbm(*arrays):
    return [pltpu.with_memory_space_constraint(array, pltpu.HBM) for array in arrays]


def call(kernel, name, out_shape, args, hbm=0, scratch=(), out_specs=None, flops=0, limit=16):
    vmem = pl.BlockSpec(memory_space=pltpu.VMEM)
    return pl.pallas_call(
        kernel,
        in_specs=[pl.BlockSpec(memory_space=pltpu.HBM)] * hbm + [vmem] * (len(args) - hbm),
        out_specs=out_specs or [vmem] * len(out_shape),
        out_shape=out_shape,
        scratch_shapes=scratch,
        compiler_params=pltpu.CompilerParams(vmem_limit_bytes=limit * MIB),
        cost_estimate=pl.CostEstimate(flops=flops, bytes_accessed=flops // 400, transcendentals=0),
        name=name,
    )(*in_hbm(*args[:hbm]), *args[hbm:])


def swap(tiles, bit, send):
    return lax.ppermute(send, "tiles", [(i, i ^ bit) for i in range(tiles)])


def halve(keeps, gots):
    half, _, width = keeps[0].shape
    rows = sum(keep.shape[1] for keep in keeps)
    shape = (half // 2, rows, width)
    return call(
        functools.partial(halve_kernel, 1, len(keeps)),
        "halve",
        [pltpu.VMEM(shape, BF16), pltpu.VMEM(shape, F32)],
        [*keeps, *gots],
    )


def spread(keep, got):
    return call(
        spread_kernel,
        "spread",
        [pltpu.VMEM(keep.shape[1:], F32), pltpu.VMEM(keep.shape, BF16)],
        [keep, got],
    )


def exchange(tiles, send):
    groups = [[z * 4 + i for z in range(tiles // 4)] for i in range(4)]
    return lax.all_to_all(
        send, "tiles", split_axis=0, concat_axis=0, axis_index_groups=groups, tiled=True
    )


def finish(own, got, sizes):
    return call(
        finish_kernel, "finish", [shaped((size, own.shape[1]), F32) for size in sizes], [own, got]
    )


def shards(
    node_latent, edge_latent, node_cot, edge_cot,
    edge_w1, edge_b1, edge_w2, edge_b2, edge_gain,
    node_w1, node_b1, node_w2, node_b2, node_gain,
    send_index, edge_sender, edge_receiver, edge_count,
):
    tiles = lax.axis_size("tiles")
    nodes, latent = node_latent.shape
    edges = edge_latent.shape[0]
    places = send_index.shape[2]
    steps = edges // TILE
    used = nodes + 2 * NEAR + places * tiles
    rows = -(-used // LANES) * LANES
    fast = tiles == 16
    half = tiles // 2
    upward = [(i, i + 1) for i in range(tiles - 1)]
    downward = [(i + 1, i) for i in range(tiles - 1)]
    sender = edge_sender.reshape(edges // LANES, LANES)
    receiver = edge_receiver.reshape(edges // LANES, LANES)
    listed = jnp.swapaxes(send_index, 1, 2)
    row = lambda vector: vector.reshape(1, -1)
    vmem = pltpu.VMEM
    unit = 2 * edges * latent * latent

    if fast:
        grad_shapes = lambda count: [
            vmem((half, count // tiles, latent), BF16),
            vmem((half, count // tiles, latent), F32),
        ]
    else:
        grad_shapes = lambda count: [shaped((latent, latent), F32), shaped((count, latent), F32)]

    outgoing, head, tail = call(
        outgoing_kernel,
        "outgoing",
        [
            shaped((tiles, places, latent), BF16),
            shaped((NEAR, latent), BF16),
            shaped((NEAR, latent), BF16),
        ],
        [listed, node_latent],
        hbm=2,
        scratch=[vmem(listed.shape, jnp.int32), vmem((nodes, latent), BF16), pltpu.SemaphoreType.DMA((2,))],
    )
    lower = lax.ppermute(tail, "tiles", upward)
    upper = lax.ppermute(head, "tiles", downward)
    incoming = lax.all_to_all(outgoing, "tiles", split_axis=0, concat_axis=0, tiled=True)

    (
        edge_kept, w1_kept, w2_kept, node_kept, receiver_kept, gain_kept,
        hidden, slope, normed, inverse, table, moved, dsum, base, node_send, node_keep,
    ) = call(
        functools.partial(forward_kernel, tiles, places, fast),
        "forward",
        [
            vmem((edges, latent), BF16), vmem(edge_w1.shape, BF16), vmem(edge_w2.shape, BF16),
            vmem((nodes, latent), BF16), vmem(receiver.shape, jnp.int32), vmem((1, latent), F32),
            vmem((edges, latent), BF16), vmem((edges, latent), BF16), vmem((edges, latent), F32),
            vmem((edges, LANES), F32), vmem((rows, latent), BF16), vmem(sender.shape, jnp.int32),
            vmem((nodes, latent), BF16), vmem((nodes, latent), F32),
        ] + grad_shapes(3 * latent if fast else 2 * latent),
        [
            edge_latent, edge_w1, edge_w2, node_w1, node_w2, node_latent, node_cot,
            sender, receiver, row(edge_b1), row(edge_b2), row(edge_gain),
            row(node_b1), row(node_b2), row(node_gain), edge_count,
            lower, upper, incoming,
        ],
        hbm=16,
        scratch=[
            vmem((latent + rows + nodes, latent), BF16), vmem((nodes, latent), F32),
            vmem((3 * latent, latent), F32), vmem(node_w1.shape, BF16), vmem(node_w2.shape, BF16),
            vmem((nodes, latent), BF16), vmem(sender.shape, jnp.int32),
        ] + [vmem((1, latent), F32)] * 5 + [
            pltpu.SMEM(edge_count.shape, jnp.int32),
            pltpu.SemaphoreType.DMA((15,)), pltpu.SemaphoreType.DMA((steps,)),
        ],
        flops=7 * unit,
        limit=24,
    )

    cot_kept, dpre, second_send, second_keep = call(
        functools.partial(slope_kernel, tiles, fast),
        "slope",
        [vmem((edges, latent), BF16), vmem((edges, latent), BF16)] + grad_shapes(latent),
        [edge_cot, receiver_kept, dsum, hidden, slope, normed, inverse, w2_kept, gain_kept],
        hbm=1,
        scratch=[vmem((latent, latent), F32), pltpu.SemaphoreType.DMA((steps,))],
        flops=3 * unit,
    )
    if fast:
        send, chain = halve(
            [node_keep, second_keep],
            [swap(tiles, 1, node_send), swap(tiles, 1, second_send)],
        )
        dpre, send = lax.optimization_barrier((dpre, send))
        got = swap(tiles, 2, send)

    first_send, first_keep, to_lower, to_upper, to_far, partial = call(
        functools.partial(first_kernel, tiles, places, fast),
        "first",
        grad_shapes(3 * latent) + [
            shaped((NEAR, latent), BF16),
            shaped((NEAR, latent), BF16),
            shaped((tiles, places, latent), BF16),
            vmem((nodes, latent), F32),
        ],
        [dpre, edge_kept, moved, receiver_kept, table, node_kept, w1_kept, base],
        scratch=[vmem((3 * latent, latent), F32), vmem((rows + nodes, latent), F32)],
        flops=4 * unit,
    )

    (grad_edge,) = call(
        edge_kernel,
        "edge",
        [shaped((edges, latent), BF16)],
        [dpre, cot_kept, w1_kept],
        out_specs=[pl.BlockSpec(memory_space=pltpu.HBM)],
        scratch=[vmem((edges, latent), BF16), pltpu.SemaphoreType.DMA((steps,))],
        flops=2 * unit,
    )

    above = lax.ppermute(to_lower, "tiles", downward)
    below = lax.ppermute(to_upper, "tiles", upward)
    returned = lax.all_to_all(to_far, "tiles", split_axis=0, concat_axis=0, tiled=True)
    (grad_node,) = call(
        node_kernel,
        "node",
        [shaped((nodes, latent), BF16)],
        [listed, partial, below, above, returned],
    )

    if fast:
        send, late_chain = halve([first_keep], [swap(tiles, 1, first_send)])
        late_got = swap(tiles, 2, send)
        per = latent // tiles
        own, send = spread(chain, got)
        grad_node_w1, grad_node_w2, grad_edge_w2 = finish(
            own, exchange(tiles, send), [2 * per, per, per]
        )
        own, send = spread(late_chain, late_got)
        (grad_edge_w1,) = finish(own, exchange(tiles, send), [3 * per])
    else:
        scatter = functools.partial(
            lax.psum_scatter, axis_name="tiles", scatter_dimension=0, tiled=True
        )
        grad_node_w1, grad_node_w2 = scatter(node_keep), scatter(node_send)
        grad_edge_w1, grad_edge_w2 = scatter(first_keep), scatter(second_keep)
    return (grad_node, grad_edge, grad_edge_w1, grad_edge_w2, grad_node_w1, grad_node_w2)


def solution(mesh):
    split = P(("groups", "tiles"), None)
    return jax.shard_map(
        shards,
        mesh=mesh,
        in_specs=(split,) * 4
        + (P(),) * 10
        + (
            P(("groups", "tiles"), None, None),
            P(("groups", "tiles")),
            P(("groups", "tiles")),
            P("groups"),
        ),
        out_specs=(split,) * 6,
        check_vma=False,
    )
```

```python
import functools

import jax
import jax.numpy as jnp
from jax import lax
from jax.experimental import pallas as pl
from jax.experimental.pallas import tpu as pltpu
from jax.sharding import PartitionSpec as P

NEAR = 64
EPSILON = 1e-05
TILE = 256
LANES = 128
F32 = jnp.float32
BF16 = jnp.bfloat16
MIB = 1024 * 1024

NN = (((1,), (0,)), ((), ()))
NT = (((1,), (1,)), ((), ()))
TN = (((0,), (0,)), ((), ()))


def dot(a, b, dims=NN):
    return lax.dot_general(a, b, dims, preferred_element_type=F32)


def sigmoid(x):
    return 0.5 * jnp.tanh(0.5 * x) + 0.5


def row_mean(x):
    return jnp.sum(x, axis=-1, keepdims=True) * (1.0 / x.shape[-1])


def ones_where(mask):
    return jnp.where(mask, 1.0, 0.0).astype(BF16)


def index_columns(idx_ref, step, tile):
    per = tile // LANES
    parts = []
    for j in range(per):
        row = idx_ref[pl.ds(step * per + j, 1), :]
        parts.append(jnp.transpose(jnp.broadcast_to(row, (LANES, LANES))))
    return jnp.concatenate(parts, axis=0)


def pick_columns(columns, start, stop):
    lane = lax.broadcasted_iota(jnp.int32, columns.shape, 1)
    return [ones_where(columns == lane + at) for at in range(start, stop, LANES)]


def pick_rows(idx_ref, step, tile, width):
    per = tile // LANES
    row = jnp.concatenate([idx_ref[pl.ds(step * per + j, 1), :] for j in range(per)], axis=1)
    return ones_where(lax.broadcasted_iota(jnp.int32, (width, tile), 0) == row)


def norm_forward(out):
    centred = out - row_mean(out)
    inverse = lax.rsqrt(row_mean(centred * centred) + EPSILON)
    return centred, inverse


def norm_backward(scaled, normed, inverse):
    return (
        inverse * (scaled - row_mean(scaled) - normed * row_mean(scaled * normed))
    ).astype(BF16)


def split_halves(bit, total_ref, at, block, first, rows, send_ref, keep_ref, offset):
    half = send_ref.shape[0]
    for q in range(half):
        there = pl.multiple_of(at + first + (2 * q + 1 - bit) * block, 32)
        here = pl.multiple_of(at + first + (2 * q + bit) * block, 32)
        send_ref[q, offset : offset + rows, :] = total_ref[pl.ds(there, rows), :].astype(BF16)
        keep_ref[q, offset : offset + rows, :] = total_ref[pl.ds(here, rows), :]


def fetch(pairs, sems):
    copies = []
    for at, (source, target) in enumerate(pairs):
        copies.append(pltpu.make_async_copy(source, target, sems.at[at]))
    for copy in copies:
        copy.start()
    return copies


def tile_pairs(source, target, tile):
    return [
        (source.at[pl.ds(at, tile)], target.at[pl.ds(at, tile)])
        for at in range(0, source.shape[0], tile)
    ]


def outgoing_kernel(index_hbm, node_hbm, far_ref, head_ref, tail_ref, index_ref, node_ref, sems):
    for copy in fetch([(index_hbm, index_ref), (node_hbm, node_ref)], sems):
        copy.wait()
    places, tiles = index_ref.shape[1], index_ref.shape[2]
    nodes = node_ref.shape[0]
    place = lax.broadcasted_iota(jnp.int32, (nodes, tiles), 0)
    for j in range(places):
        picks = ones_where(place == index_ref[0, j : j + 1, :])
        far_ref[:, j, :] = dot(picks, node_ref[...], TN).astype(BF16)
    head_ref[...] = node_ref[:NEAR, :]
    tail_ref[...] = node_ref[nodes - NEAR :, :]


def table_index(raw, places, tiles, nodes):
    far = raw - (nodes + 2 * NEAR)
    far = nodes + 2 * NEAR + lax.rem(far, places) * tiles + lax.div(far, places)
    rim = jnp.where(raw < NEAR, raw + nodes, raw)
    own = jnp.where((raw >= NEAR) & (raw < NEAR + nodes), raw - NEAR, rim)
    return jnp.where(raw >= nodes + 2 * NEAR, far, own)


def prepare_kernel(
    tiles, places,
    node_hbm, w1_hbm, sender_hbm, receiver_hbm, b1_hbm, edge_hbm,
    edge_ref, w1_ref, node_ref, receiver_ref, moved_ref, partial_ref,
    weights, sender_ref, b1_ref, sems, edge_sems,
):
    edges, latent = edge_ref.shape
    nodes = node_ref.shape[0]
    copies = fetch(
        [
            (node_hbm, node_ref), (w1_hbm, w1_ref), (sender_hbm, sender_ref),
            (receiver_hbm, receiver_ref), (b1_hbm, b1_ref),
        ],
        sems,
    )
    edge_copies = fetch(tile_pairs(edge_hbm, edge_ref, edges // 2), edge_sems)
    for copy in copies:
        copy.wait()
    moved_ref[...] = table_index(sender_ref[...], places, tiles, nodes)
    weights[:latent, :] = w1_ref[:latent, :]
    weights[latent : latent + nodes, :] = dot(
        node_ref[...], w1_ref[latent : 2 * latent, :]
    ).astype(BF16)
    weights[latent + nodes :, :] = dot(node_ref[...], w1_ref[2 * latent :, :]).astype(BF16)
    for copy in edge_copies:
        copy.wait()
    for step in range(edges // TILE):
        tile = slice(step * TILE, (step + 1) * TILE)
        senders = pick_columns(index_columns(moved_ref, step, TILE), 0, nodes)
        receivers = pick_columns(index_columns(receiver_ref, step, TILE), 0, nodes)
        inputs = jnp.concatenate([edge_ref[tile, :]] + senders + receivers, axis=1)
        partial_ref[tile, :] = dot(inputs, weights[...]) + b1_ref[...]


def forward_kernel(
    tiles, places, fast,
    w2_hbm, nw1_hbm, nw2_hbm, ncot_hbm,
    b2_hbm, gain_hbm, nb1_hbm, nb2_hbm, ngain_hbm, count_hbm,
    lower_ref, upper_ref, far_ref, partial_ref, w1_ref, node_ref, receiver_ref, moved_ref,
    w2_ref, gain_ref,
    hidden_ref, slope_ref, normed_ref, inverse_ref, table_ref, dsum_ref, base_ref,
    gsend_ref, gkeep_ref,
    weights, summed, grads, nw1_ref, nw2_ref, ncot_ref,
    b2_ref, nb1_ref, nb2_ref, ngain_ref, count_ref, sems,
):
    here = lax.axis_index("tiles")
    edges, latent = hidden_ref.shape
    nodes = node_ref.shape[0]
    rows = table_ref.shape[0]
    steps = edges // TILE

    early = fetch(
        [(count_hbm, count_ref), (b2_hbm, b2_ref), (gain_hbm, gain_ref), (w2_hbm, w2_ref)], sems
    )
    late = fetch(
        [
            (nw1_hbm, nw1_ref), (nw2_hbm, nw2_ref), (ncot_hbm, ncot_ref),
            (nb1_hbm, nb1_ref), (nb2_hbm, nb2_ref), (ngain_hbm, ngain_ref),
        ],
        sems.at[pl.ds(len(early), 6)],
    )

    table_ref[:nodes, :] = node_ref[...]
    table_ref[nodes : nodes + NEAR, :] = lower_ref[...]
    table_ref[nodes + NEAR : nodes + 2 * NEAR, :] = upper_ref[...]
    for j in range(places):
        at = nodes + 2 * NEAR + j * tiles
        table_ref[at : at + tiles, :] = far_ref[:, j, :]
    used = nodes + 2 * NEAR + places * tiles
    if used < rows:
        table_ref[used:, :] = jnp.zeros((rows - used, latent), BF16)
    weights[...] = dot(table_ref[nodes:, :], w1_ref[latent : 2 * latent, :]).astype(BF16)
    for copy in early:
        copy.wait()
    live = count_ref[here]

    def activate(step):
        tile = slice(step * TILE, (step + 1) * TILE)
        senders = pick_columns(index_columns(moved_ref, step, TILE), nodes, rows)
        preact = partial_ref[tile, :] + dot(jnp.concatenate(senders, axis=1), weights[...])
        sig = sigmoid(preact)
        slope_ref[tile, :] = (sig * (1.0 + preact * (1.0 - sig))).astype(BF16)
        hidden_ref[tile, :] = (preact * sig).astype(BF16)

    def normalize(step):
        tile = slice(step * TILE, (step + 1) * TILE)
        centred, inverse = norm_forward(dot(hidden_ref[tile, :], w2_ref[...]) + b2_ref[...])
        position = step * TILE + lax.broadcasted_iota(jnp.int32, inverse.shape, 0)
        inverse = jnp.where(position < live, inverse, 0.0)
        normed = centred * inverse
        normed_ref[tile, :] = normed
        inverse_ref[tile, :] = jnp.broadcast_to(inverse, (TILE, LANES))
        update = (normed * gain_ref[...]).astype(BF16)
        part = dot(pick_rows(receiver_ref, step, TILE, nodes), update)
        if step == 0:
            summed[...] = part
        else:
            summed[...] += part

    for step in range(steps + 1):
        if step < steps:
            activate(step)
        if step > 0:
            normalize(step - 1)

    for copy in late:
        copy.wait()
    node_in = jnp.concatenate([node_ref[...], summed[...].astype(BF16)], axis=1)
    preact_n = dot(node_in, nw1_ref[...]) + nb1_ref[...]
    sig_n = sigmoid(preact_n)
    hidden_n = (preact_n * sig_n).astype(BF16)
    centred_n, inverse_n = norm_forward(dot(hidden_n, nw2_ref[...]) + nb2_ref[...])
    cot = ncot_ref[...].astype(F32)
    dout = norm_backward(cot * ngain_ref[...], centred_n * inverse_n, inverse_n)
    slope_n = sig_n * (1.0 + preact_n * (1.0 - sig_n))
    dpre = (dot(dout, nw2_ref[...], NT) * slope_n).astype(BF16)
    grads[: 2 * latent, :] = dot(node_in, dpre, TN)
    grads[2 * latent :, :] = dot(hidden_n, dout, TN)
    base_ref[...] = cot + dot(dpre, nw1_ref[:latent, :], NT)
    dsum_ref[...] = dot(dpre, nw1_ref[latent:, :], NT).astype(BF16)
    if fast:
        bit = lax.rem(here, 2)
        first = 2 * latent // tiles
        split_halves(bit, grads, 0, first, 0, first, gsend_ref, gkeep_ref, 0)
        second = latent // tiles
        split_halves(bit, grads, 2 * latent, second, 0, second, gsend_ref, gkeep_ref, first)
    else:
        gkeep_ref[...] = grads[: 2 * latent, :]
        gsend_ref[...] = grads[2 * latent :, :]


def slope_kernel(
    tiles, fast,
    cot_hbm, receiver_ref, dsum_ref, hidden_ref, slope_ref, normed_ref, inverse_ref, w2_ref, gain_ref,
    cot_ref, dpre_ref, gsend_ref, gkeep_ref,
    grads, dout, sems,
):
    here = lax.axis_index("tiles")
    edges, latent = cot_ref.shape
    nodes = dsum_ref.shape[0]
    copies = fetch(tile_pairs(cot_hbm, cot_ref, edges // 2), sems)
    steps = edges // TILE
    for copy in copies:
        copy.wait()

    def outer(step):
        tile = slice(step * TILE, (step + 1) * TILE)
        receivers = jnp.concatenate(
            pick_columns(index_columns(receiver_ref, step, TILE), 0, nodes), axis=1
        )
        grad_update = cot_ref[tile, :].astype(F32) + dot(receivers, dsum_ref[...])
        inverse = inverse_ref[tile, :1]
        dout[tile, :] = norm_backward(grad_update * gain_ref[...], normed_ref[tile, :], inverse)

    def inner(step):
        tile = slice(step * TILE, (step + 1) * TILE)
        dpre_ref[tile, :] = (
            dot(dout[tile, :], w2_ref[...], NT) * slope_ref[tile, :].astype(F32)
        ).astype(BF16)
        part = dot(hidden_ref[tile, :], dout[tile, :], TN)
        if step == 0:
            grads[...] = part
        else:
            grads[...] += part

    for step in range(steps + 1):
        if step < steps:
            outer(step)
        if step > 0:
            inner(step - 1)

    if fast:
        rows = latent // tiles
        split_halves(lax.rem(here, 2), grads, 0, rows, 0, rows, gsend_ref, gkeep_ref, 0)
    else:
        gkeep_ref[...] = grads[...]
        gsend_ref[...] = jnp.zeros_like(gsend_ref)


def first_kernel(
    tiles, places, fast,
    dpre_ref, edge_ref, sender_ref, receiver_ref, table_ref, node_ref, w1_ref, base_ref,
    *refs,
):
    out_refs, (grads, sums) = refs[:-2], refs[-2:]
    lower_ref, upper_ref, far_ref, partial_ref = out_refs[:4]
    here = lax.axis_index("tiles")
    edges, latent = edge_ref.shape
    nodes = node_ref.shape[0]
    rows = table_ref.shape[0]

    for step in range(edges // TILE):
        tile = slice(step * TILE, (step + 1) * TILE)
        dpre = dpre_ref[tile, :]
        part = dot(edge_ref[tile, :], dpre, TN)
        picks = jnp.concatenate(
            [
                pick_rows(sender_ref, step, TILE, rows),
                pick_rows(receiver_ref, step, TILE, nodes),
            ],
            axis=0,
        )
        scattered = dot(picks, dpre)
        if step == 0:
            grads[:latent, :] = part
            sums[...] = scattered
        else:
            grads[:latent, :] += part
            sums[...] += scattered

    by_sender = sums[:rows, :].astype(BF16)
    by_receiver = sums[rows:, :].astype(BF16)
    grads[latent : 2 * latent, :] = dot(table_ref[...], by_sender, TN)
    grads[2 * latent :, :] = dot(node_ref[...], by_receiver, TN)
    if fast:
        bit = lax.rem(here, 2)
        block = 3 * latent // tiles
        at = 0
        for send_ref, keep_ref in (out_refs[4:6], out_refs[6:8]):
            part = send_ref.shape[1]
            split_halves(bit, grads, 0, block, at, part, send_ref, keep_ref, 0)
            at += part
    else:
        out_refs[4][...] = grads[...]
    back = dot(by_sender, w1_ref[latent : 2 * latent, :], NT)
    lower_ref[...] = back[nodes : nodes + NEAR, :].astype(BF16)
    upper_ref[...] = back[nodes + NEAR : nodes + 2 * NEAR, :].astype(BF16)
    for j in range(places):
        at = 2 * NEAR + nodes + j * tiles
        far_ref[:, j, :] = back[at : at + tiles, :].astype(BF16)
    partial_ref[...] = (
        base_ref[...] + back[:nodes, :] + dot(by_receiver, w1_ref[2 * latent :, :], NT)
    )


def edge_kernel(dpre_ref, cot_ref, w1_ref, out_hbm, out_ref, sems):
    edges, latent = cot_ref.shape
    copies = []
    for step in range(edges // TILE):
        tile = pl.ds(step * TILE, TILE)
        out_ref[tile, :] = (
            cot_ref[tile, :].astype(F32) + dot(dpre_ref[tile, :], w1_ref[:latent, :], NT)
        ).astype(BF16)
        copy = pltpu.make_async_copy(out_ref.at[tile], out_hbm.at[tile], sems.at[step])
        copy.start()
        copies.append(copy)
    for copy in copies:
        copy.wait()


def node_kernel(index_ref, partial_ref, below_ref, above_ref, far_ref, out_ref):
    places, tiles = index_ref.shape[1], index_ref.shape[2]
    nodes = partial_ref.shape[0]
    place = lax.broadcasted_iota(jnp.int32, (nodes, tiles), 0)
    total = partial_ref[...]
    for j in range(places):
        picks = ones_where(place == index_ref[0, j : j + 1, :])
        total = total + dot(picks, far_ref[:, j, :])
    out_ref[:NEAR, :] = (total[:NEAR, :] + below_ref[...].astype(F32)).astype(BF16)
    out_ref[NEAR : nodes - NEAR, :] = total[NEAR : nodes - NEAR, :].astype(BF16)
    out_ref[nodes - NEAR :, :] = (
        total[nodes - NEAR :, :] + above_ref[...].astype(F32)
    ).astype(BF16)


def halve_kernel(shift, count, *refs):
    keeps, gots = refs[:count], refs[count : 2 * count]
    send_ref, kept_ref = refs[2 * count :]
    bit = lax.rem(lax.div(lax.axis_index("tiles"), 2**shift), 2)
    at = 0
    for keep_ref, got_ref in zip(keeps, gots):
        rows = keep_ref.shape[1]
        for q in range(keep_ref.shape[0] // 2):
            there, here = 2 * q + 1 - bit, 2 * q + bit
            send_ref[q, at : at + rows, :] = (
                keep_ref[there] + got_ref[there].astype(F32)
            ).astype(BF16)
            kept_ref[q, at : at + rows, :] = keep_ref[here] + got_ref[here].astype(F32)
        at += rows


def finish_kernel(count, splits, *refs):
    out_refs = refs[2 * count :]
    rows = [0] * len(out_refs)
    for keep_ref, got_ref, parts in zip(refs[:count], refs[count : 2 * count], splits):
        at = 0
        for which, size in parts:
            first = rows[which]
            out_refs[which][first : first + size, :] = keep_ref[0, at : at + size, :] + got_ref[
                0, at : at + size, :
            ].astype(F32)
            at += size
            rows[which] += size


def shaped(shape, dtype):
    return jax.ShapeDtypeStruct(shape, dtype)


def in_hbm(*arrays):
    return [pltpu.with_memory_space_constraint(array, pltpu.HBM) for array in arrays]


def call(kernel, name, out_shape, args, hbm=0, scratch=(), out_specs=None, flops=0, limit=16):
    vmem = pl.BlockSpec(memory_space=pltpu.VMEM)
    return pl.pallas_call(
        kernel,
        in_specs=[pl.BlockSpec(memory_space=pltpu.HBM)] * hbm + [vmem] * (len(args) - hbm),
        out_specs=out_specs or [vmem] * len(out_shape),
        out_shape=out_shape,
        scratch_shapes=scratch,
        compiler_params=pltpu.CompilerParams(vmem_limit_bytes=limit * MIB),
        cost_estimate=pl.CostEstimate(flops=flops, bytes_accessed=flops // 400, transcendentals=0),
        name=name,
    )(*in_hbm(*args[:hbm]), *args[hbm:])


def swap(tiles, bit, send):
    return lax.ppermute(send, "tiles", [(i, i ^ bit) for i in range(tiles)])


def halve(shift, keeps, gots):
    half, _, width = keeps[0].shape
    rows = sum(keep.shape[1] for keep in keeps)
    shape = (half // 2, rows, width)
    return call(
        functools.partial(halve_kernel, shift, len(keeps)),
        "halve",
        [pltpu.VMEM(shape, BF16), pltpu.VMEM(shape, F32)],
        [*keeps, *gots],
    )


def finish(keeps, gots, splits, sizes):
    return call(
        functools.partial(finish_kernel, len(keeps), splits),
        "finish",
        [shaped((size, keeps[0].shape[-1]), F32) for size in sizes],
        [*keeps, *gots],
    )


def after(value, *others):
    return lax.optimization_barrier((value, *others))[0]


def shards(
    node_latent, edge_latent, node_cot, edge_cot,
    edge_w1, edge_b1, edge_w2, edge_b2, edge_gain,
    node_w1, node_b1, node_w2, node_b2, node_gain,
    send_index, edge_sender, edge_receiver, edge_count,
):
    tiles = lax.axis_size("tiles")
    nodes, latent = node_latent.shape
    edges = edge_latent.shape[0]
    places = send_index.shape[2]
    steps = edges // TILE
    used = nodes + 2 * NEAR + places * tiles
    rows = -(-used // LANES) * LANES
    fast = tiles == 16
    half = tiles // 2
    upward = [(i, i + 1) for i in range(tiles - 1)]
    downward = [(i + 1, i) for i in range(tiles - 1)]
    sender = edge_sender.reshape(edges // LANES, LANES)
    receiver = edge_receiver.reshape(edges // LANES, LANES)
    listed = jnp.swapaxes(send_index, 1, 2)
    row = lambda vector: vector.reshape(1, -1)
    vmem = pltpu.VMEM
    unit = 2 * edges * latent * latent

    if fast:
        grad_shapes = lambda count: [
            vmem((half, count // tiles, latent), BF16),
            vmem((half, count // tiles, latent), F32),
        ]
    else:
        grad_shapes = lambda count: [shaped((latent, latent), F32), shaped((count, latent), F32)]

    outgoing, head, tail = call(
        outgoing_kernel,
        "outgoing",
        [
            shaped((tiles, places, latent), BF16),
            shaped((NEAR, latent), BF16),
            shaped((NEAR, latent), BF16),
        ],
        [listed, node_latent],
        hbm=2,
        scratch=[vmem(listed.shape, jnp.int32), vmem((nodes, latent), BF16), pltpu.SemaphoreType.DMA((2,))],
    )
    lower = lax.ppermute(tail, "tiles", upward)
    upper = lax.ppermute(head, "tiles", downward)
    incoming = lax.all_to_all(outgoing, "tiles", split_axis=0, concat_axis=0, tiled=True)

    edge_kept, w1_kept, node_kept, receiver_kept, moved, preact = call(
        functools.partial(prepare_kernel, tiles, places),
        "prepare",
        [
            vmem((edges, latent), BF16), vmem(edge_w1.shape, BF16), vmem((nodes, latent), BF16),
            vmem(receiver.shape, jnp.int32), vmem(sender.shape, jnp.int32),
            vmem((edges, latent), F32),
        ],
        [node_latent, edge_w1, after(sender, outgoing), receiver, row(edge_b1), edge_latent],
        hbm=6,
        scratch=[
            vmem((latent + 2 * nodes, latent), BF16), vmem(sender.shape, jnp.int32),
            vmem((1, latent), F32), pltpu.SemaphoreType.DMA((5,)), pltpu.SemaphoreType.DMA((2,)),
        ],
        flops=3 * unit,
    )

    (
        w2_kept, gain_kept,
        hidden, slope, normed, inverse, table, dsum, base, node_send, node_keep,
    ) = call(
        functools.partial(forward_kernel, tiles, places, fast),
        "forward",
        [
            vmem(edge_w2.shape, BF16), vmem((1, latent), F32),
            vmem((edges, latent), BF16), vmem((edges, latent), BF16), vmem((edges, latent), F32),
            vmem((edges, LANES), F32), vmem((rows, latent), BF16),
            vmem((nodes, latent), BF16), vmem((nodes, latent), F32),
        ] + grad_shapes(3 * latent if fast else 2 * latent),
        [
            edge_w2, node_w1, node_w2, node_cot,
            row(edge_b2), row(edge_gain), row(node_b1), row(node_b2), row(node_gain), edge_count,
            lower, upper, incoming, preact, w1_kept, node_kept, receiver_kept, moved,
        ],
        hbm=10,
        scratch=[
            vmem((rows - nodes, latent), BF16), vmem((nodes, latent), F32),
            vmem((3 * latent, latent), F32), vmem(node_w1.shape, BF16), vmem(node_w2.shape, BF16),
            vmem((nodes, latent), BF16),
        ] + [vmem((1, latent), F32)] * 4 + [
            pltpu.SMEM(edge_count.shape, jnp.int32), pltpu.SemaphoreType.DMA((10,)),
        ],
        flops=5 * unit,
    )

    cot_kept, dpre, second_send, second_keep = call(
        functools.partial(slope_kernel, tiles, fast),
        "slope",
        [vmem((edges, latent), BF16), vmem((edges, latent), BF16)] + grad_shapes(latent),
        [edge_cot, receiver_kept, dsum, hidden, slope, normed, inverse, w2_kept, gain_kept],
        hbm=1,
        scratch=[
            vmem((latent, latent), F32), vmem((edges, latent), BF16), pltpu.SemaphoreType.DMA((2,)),
        ],
        flops=3 * unit,
    )
    if fast:
        send, chain = halve(1, [node_keep], [swap(tiles, 1, node_send)])
        dpre = after(dpre, send)
        got = swap(tiles, 2, send)
        got_second = swap(tiles, 1, second_send)

    per = latent // tiles
    to_lower, to_upper, to_far, partial, *first = call(
        functools.partial(first_kernel, tiles, places, fast),
        "first",
        [
            vmem((NEAR, latent), BF16),
            vmem((NEAR, latent), BF16),
            shaped((tiles, places, latent), BF16),
            vmem((nodes, latent), F32),
        ] + (
            [
                vmem((half, 2 * per, latent), BF16), vmem((half, 2 * per, latent), F32),
                vmem((half, per, latent), BF16), vmem((half, per, latent), F32),
            ]
            if fast else [shaped((3 * latent, latent), F32)]
        ),
        [dpre, edge_kept, moved, receiver_kept, table, node_kept, w1_kept, base],
        scratch=[vmem((3 * latent, latent), F32), vmem((rows + nodes, latent), F32)],
        flops=4 * unit,
    )

    (grad_edge,) = call(
        edge_kernel,
        "edge",
        [shaped((edges, latent), BF16)],
        [after(dpre, partial), cot_kept, w1_kept],
        out_specs=[pl.BlockSpec(memory_space=pltpu.HBM)],
        scratch=[vmem((edges, latent), BF16), pltpu.SemaphoreType.DMA((steps,))],
        flops=2 * unit,
    )

    if fast:
        send_a, keep_a, send_b, keep_b = first
        send_a, chain_a = halve(1, [after(keep_a, grad_edge)], [swap(tiles, 1, send_a)])
        got_a = swap(tiles, 2, send_a)
        send_b, chain_b = halve(
            1, [after(keep_b, send_a), second_keep], [swap(tiles, 1, send_b), got_second]
        )
        got_b = swap(tiles, 2, send_b)
        send, chain = halve(2, [after(chain, send_b)], [got])
        got = swap(tiles, 4, send)
        to_far, to_lower, to_upper = lax.optimization_barrier((to_far, to_lower, to_upper, send))[:3]

    above = lax.ppermute(to_lower, "tiles", downward)
    below = lax.ppermute(to_upper, "tiles", upward)
    returned = lax.all_to_all(to_far, "tiles", split_axis=0, concat_axis=0, tiled=True)
    (grad_node,) = call(
        node_kernel,
        "node",
        [shaped((nodes, latent), BF16)],
        [listed, partial, below, above, returned],
    )

    if fast:
        send, chain = halve(3, [chain], [got])
        got = swap(tiles, 8, send)
        send_a, chain_a = halve(2, [after(chain_a, send)], [got_a])
        got_a = swap(tiles, 4, send_a)
        send_a, chain_a = halve(3, [chain_a], [got_a])
        got_a = swap(tiles, 8, send_a)
        send_b, chain_b = halve(2, [after(chain_b, send_a)], [got_b])
        got_b = swap(tiles, 4, send_b)
        grad_node_w1, grad_node_w2 = finish(
            [chain], [got], [[(0, 2 * per), (1, per)]], [2 * per, per]
        )
        send_b, chain_b = halve(3, [chain_b], [got_b])
        got_b = swap(tiles, 8, send_b)
        grad_edge_w1, grad_edge_w2 = finish(
            [chain_a, chain_b], [got_a, got_b], [[(0, 2 * per)], [(0, per), (1, per)]], [3 * per, per]
        )
    else:
        scatter = functools.partial(
            lax.psum_scatter, axis_name="tiles", scatter_dimension=0, tiled=True
        )
        grad_node_w1, grad_node_w2 = scatter(node_keep), scatter(node_send)
        grad_edge_w1, grad_edge_w2 = scatter(first[0]), scatter(second_keep)
    return (grad_node, grad_edge, grad_edge_w1, grad_edge_w2, grad_node_w1, grad_node_w2)


def solution(mesh):
    split = P(("groups", "tiles"), None)
    return jax.shard_map(
        shards,
        mesh=mesh,
        in_specs=(split,) * 4
        + (P(),) * 10
        + (
            P(("groups", "tiles"), None, None),
            P(("groups", "tiles")),
            P(("groups", "tiles")),
            P("groups"),
        ),
        out_specs=(split,) * 6,
        check_vma=False,
    )
```

```python
import functools

import jax
import jax.numpy as jnp
from jax import lax
from jax.experimental import pallas as pl
from jax.experimental.pallas import tpu as pltpu
from jax.sharding import PartitionSpec as P

NEAR = 64
EPSILON = 1e-05
TILE = 256
LANES = 128
F32 = jnp.float32
BF16 = jnp.bfloat16
MIB = 1024 * 1024

NN = (((1,), (0,)), ((), ()))
NT = (((1,), (1,)), ((), ()))
TN = (((0,), (0,)), ((), ()))


def dot(a, b, dims=NN):
    return lax.dot_general(a, b, dims, preferred_element_type=F32)


def sigmoid(x):
    return 0.5 * jnp.tanh(0.5 * x) + 0.5


def row_mean(x):
    return jnp.sum(x, axis=-1, keepdims=True) * (1.0 / x.shape[-1])


def ones_where(mask):
    return jnp.where(mask, 1.0, 0.0).astype(BF16)


def index_columns(idx_ref, step, tile):
    per = tile // LANES
    parts = []
    for j in range(per):
        row = idx_ref[pl.ds(step * per + j, 1), :]
        parts.append(jnp.transpose(jnp.broadcast_to(row, (LANES, LANES))))
    return jnp.concatenate(parts, axis=0)


def pick_columns(columns, start, stop):
    lane = lax.broadcasted_iota(jnp.int32, columns.shape, 1)
    return [ones_where(columns == lane + at) for at in range(start, stop, LANES)]


def pick_rows(idx_ref, step, tile, width):
    per = tile // LANES
    row = jnp.concatenate([idx_ref[pl.ds(step * per + j, 1), :] for j in range(per)], axis=1)
    return ones_where(lax.broadcasted_iota(jnp.int32, (width, tile), 0) == row)


def norm_forward(out):
    centred = out - row_mean(out)
    inverse = lax.rsqrt(row_mean(centred * centred) + EPSILON)
    return centred, inverse


def norm_backward(scaled, normed, inverse):
    return (
        inverse * (scaled - row_mean(scaled) - normed * row_mean(scaled * normed))
    ).astype(BF16)


def split_halves(bit, total_ref, at, block, first, rows, send_ref, keep_ref, offset):
    half, size = keep_ref.shape[:2]
    for q in range(half):
        there = pl.multiple_of(at + first + (2 * q + 1 - bit) * block, 32)
        here = pl.multiple_of(at + first + (2 * q + bit) * block, 32)
        to = q * size + offset
        send_ref[to : to + rows, :] = total_ref[pl.ds(there, rows), :].astype(BF16)
        keep_ref[q, offset : offset + rows, :] = total_ref[pl.ds(here, rows), :]


def fetch(pairs, sems):
    copies = []
    for at, (source, target) in enumerate(pairs):
        copies.append(pltpu.make_async_copy(source, target, sems.at[at]))
    for copy in copies:
        copy.start()
    return copies


def tile_pairs(source, target, tile):
    return [
        (source.at[pl.ds(at, tile)], target.at[pl.ds(at, tile)])
        for at in range(0, source.shape[0], tile)
    ]


def slot_owner(origin, shape, dim, places):
    row = lax.broadcasted_iota(jnp.int32, shape, dim)
    return lax.div(row, places) ^ origin, lax.rem(row, places)


def bit_slots(bit, shape, places):
    row = lax.broadcasted_iota(jnp.int32, shape, 0)
    column = lax.broadcasted_iota(jnp.int32, shape, 1)
    slot, place = lax.div(column, places), lax.rem(column, places)
    rank = ((slot >> (bit + 1)) << bit) | (slot & (2**bit - 1))
    return ((slot >> bit) & 1 == 1) & (rank * places + place == row)


def slots_out(bit, slots, places):
    rows = slots.shape[0]
    return dot(ones_where(bit_slots(bit, (rows // 2, rows), places)), slots).astype(BF16)


def slots_in(bit, slots, got, places):
    rows = slots.shape[0]
    row = lax.broadcasted_iota(jnp.int32, (rows, rows), 0)
    column = lax.broadcasted_iota(jnp.int32, (rows, rows), 1)
    kept = (row == column) & ((lax.div(column, places) >> bit) & 1 == 0)
    moved = ones_where(bit_slots(bit, (rows // 2, rows), places))
    return (dot(ones_where(kept), slots) + dot(moved, got, TN)).astype(BF16)


def outgoing_kernel(
    fast, index_hbm, node_hbm, slots_ref, send_ref, head_ref, tail_ref, index_ref, node_ref, sems
):
    for copy in fetch([(index_hbm, index_ref), (node_hbm, node_ref)], sems):
        copy.wait()
    places, tiles = index_ref.shape[1], index_ref.shape[2]
    nodes, latent = node_ref.shape
    origin = lax.axis_index("tiles") if fast else 0
    place = lax.broadcasted_iota(jnp.int32, (nodes, tiles), 0)
    owner, at = slot_owner(origin, (places * tiles, tiles), 0, places)
    column = lax.broadcasted_iota(jnp.int32, (places * tiles, tiles), 1)
    slots = jnp.zeros((places * tiles, latent), F32)
    for j in range(places):
        picks = ones_where(place == index_ref[0, j : j + 1, :])
        listed = dot(picks, node_ref[...], TN).astype(BF16)
        slots += dot(ones_where((owner == column) & (at == j)), listed)
    slots = slots.astype(BF16)
    slots_ref[...] = slots
    send_ref[...] = slots_out(0, slots, places) if fast else jnp.zeros_like(send_ref)
    head_ref[...] = node_ref[:NEAR, :]
    tail_ref[...] = node_ref[nodes - NEAR :, :]


def shuffle_kernel(bit, places, slots_ref, got_ref, moved_ref, send_ref):
    slots = slots_in(bit, slots_ref[...], got_ref[...], places)
    moved_ref[...] = slots
    send_ref[...] = slots_out(bit + 1, slots, places)


def table_index(raw, origin, places, nodes):
    far = raw - (nodes + 2 * NEAR)
    owner = lax.div(far, places) ^ origin
    far = nodes + 2 * NEAR + owner * places + lax.rem(far, places)
    rim = jnp.where(raw < NEAR, raw + nodes, raw)
    own = jnp.where((raw >= NEAR) & (raw < NEAR + nodes), raw - NEAR, rim)
    return jnp.where(raw >= nodes + 2 * NEAR, far, own)


def weights_kernel(
    places, fast,
    node_hbm, w1_hbm, sender_hbm, receiver_hbm,
    w1_ref, node_ref, receiver_ref, moved_ref, weights,
    sender_ref, sems,
):
    latent = node_ref.shape[1]
    nodes = node_ref.shape[0]
    copies = fetch(
        [
            (node_hbm, node_ref), (w1_hbm, w1_ref), (sender_hbm, sender_ref),
            (receiver_hbm, receiver_ref),
        ],
        sems,
    )
    for copy in copies:
        copy.wait()
    origin = lax.axis_index("tiles") if fast else 0
    moved_ref[...] = table_index(sender_ref[...], origin, places, nodes)
    weights[:latent, :] = w1_ref[:latent, :]
    weights[latent : latent + nodes, :] = dot(
        node_ref[...], w1_ref[latent : 2 * latent, :]
    ).astype(BF16)
    weights[latent + nodes :, :] = dot(node_ref[...], w1_ref[2 * latent :, :]).astype(BF16)


def prepare_kernel(
    first, b1_hbm, edge_hbm, moved_ref, receiver_ref, weights, edge_ref, partial_ref,
    b1_ref, sems,
):
    edges, latent = edge_ref.shape
    nodes = weights.shape[0] - latent >> 1
    start = pl.ds(first * TILE, edges)
    for copy in fetch([(b1_hbm, b1_ref), (edge_hbm.at[start], edge_ref)], sems):
        copy.wait()
    for step in range(edges // TILE):
        tile = slice(step * TILE, (step + 1) * TILE)
        senders = pick_columns(index_columns(moved_ref, first + step, TILE), 0, nodes)
        receivers = pick_columns(index_columns(receiver_ref, first + step, TILE), 0, nodes)
        inputs = jnp.concatenate([edge_ref[tile, :]] + senders + receivers, axis=1)
        partial_ref[tile, :] = dot(inputs, weights[...]) + b1_ref[...]


def forward_kernel(
    tiles, places, fast,
    w2_hbm, nw1_hbm, nw2_hbm, ncot_hbm,
    b2_hbm, gain_hbm, nb1_hbm, nb2_hbm, ngain_hbm, count_hbm,
    lower_ref, upper_ref, slots_ref, got_ref, early_ref, later_ref,
    w1_ref, node_ref, receiver_ref, moved_ref,
    w2_ref, gain_ref,
    hidden_ref, slope_ref, normed_ref, inverse_ref, table_ref, dsum_ref, base_ref,
    gsend_ref, gkeep_ref,
    weights, summed, grads, nw1_ref, nw2_ref, ncot_ref,
    b2_ref, nb1_ref, nb2_ref, ngain_ref, count_ref, sems,
):
    here = lax.axis_index("tiles")
    edges, latent = hidden_ref.shape
    nodes = node_ref.shape[0]
    rows = table_ref.shape[0]
    steps = edges // TILE

    early = fetch(
        [(count_hbm, count_ref), (b2_hbm, b2_ref), (gain_hbm, gain_ref), (w2_hbm, w2_ref)], sems
    )
    late = fetch(
        [
            (nw1_hbm, nw1_ref), (nw2_hbm, nw2_ref), (ncot_hbm, ncot_ref),
            (nb1_hbm, nb1_ref), (nb2_hbm, nb2_ref), (ngain_hbm, ngain_ref),
        ],
        sems.at[pl.ds(len(early), 6)],
    )

    table_ref[:nodes, :] = node_ref[...]
    table_ref[nodes : nodes + NEAR, :] = lower_ref[...]
    table_ref[nodes + NEAR : nodes + 2 * NEAR, :] = upper_ref[...]
    slots = slots_ref[...]
    if fast:
        slots = slots_in(3, slots, got_ref[...], places)
    table_ref[nodes + 2 * NEAR : nodes + 2 * NEAR + places * tiles, :] = slots
    used = nodes + 2 * NEAR + places * tiles
    if used < rows:
        table_ref[used:, :] = jnp.zeros((rows - used, latent), BF16)
    weights[...] = dot(table_ref[nodes:, :], w1_ref[latent : 2 * latent, :]).astype(BF16)
    for copy in early:
        copy.wait()
    live = count_ref[here]

    def activate(step):
        tile = slice(step * TILE, (step + 1) * TILE)
        senders = pick_columns(index_columns(moved_ref, step, TILE), nodes, rows)
        part = early_ref.shape[0]
        if step * TILE < part:
            known = early_ref[tile, :]
        else:
            known = later_ref[step * TILE - part : (step + 1) * TILE - part, :]
        preact = known + dot(jnp.concatenate(senders, axis=1), weights[...])
        sig = sigmoid(preact)
        slope_ref[tile, :] = (sig * (1.0 + preact * (1.0 - sig))).astype(BF16)
        hidden_ref[tile, :] = (preact * sig).astype(BF16)

    def normalize(step):
        tile = slice(step * TILE, (step + 1) * TILE)
        centred, inverse = norm_forward(dot(hidden_ref[tile, :], w2_ref[...]) + b2_ref[...])
        position = step * TILE + lax.broadcasted_iota(jnp.int32, inverse.shape, 0)
        inverse = jnp.where(position < live, inverse, 0.0)
        normed = centred * inverse
        normed_ref[tile, :] = normed
        inverse_ref[tile, :] = jnp.broadcast_to(inverse, (TILE, LANES))
        update = (normed * gain_ref[...]).astype(BF16)
        part = dot(pick_rows(receiver_ref, step, TILE, nodes), update)
        if step == 0:
            summed[...] = part
        else:
            summed[...] += part

    for step in range(steps + 1):
        if step < steps:
            activate(step)
        if step > 0:
            normalize(step - 1)

    for copy in late:
        copy.wait()
    node_in = jnp.concatenate([node_ref[...], summed[...].astype(BF16)], axis=1)
    preact_n = dot(node_in, nw1_ref[...]) + nb1_ref[...]
    sig_n = sigmoid(preact_n)
    hidden_n = (preact_n * sig_n).astype(BF16)
    centred_n, inverse_n = norm_forward(dot(hidden_n, nw2_ref[...]) + nb2_ref[...])
    cot = ncot_ref[...].astype(F32)
    dout = norm_backward(cot * ngain_ref[...], centred_n * inverse_n, inverse_n)
    slope_n = sig_n * (1.0 + preact_n * (1.0 - sig_n))
    dpre = (dot(dout, nw2_ref[...], NT) * slope_n).astype(BF16)
    grads[: 2 * latent, :] = dot(node_in, dpre, TN)
    grads[2 * latent :, :] = dot(hidden_n, dout, TN)
    base_ref[...] = cot + dot(dpre, nw1_ref[:latent, :], NT)
    dsum_ref[...] = dot(dpre, nw1_ref[latent:, :], NT).astype(BF16)
    if fast:
        bit = lax.rem(here, 2)
        first = 2 * latent // tiles
        split_halves(bit, grads, 0, first, 0, first, gsend_ref, gkeep_ref, 0)
        second = latent // tiles
        split_halves(bit, grads, 2 * latent, second, 0, second, gsend_ref, gkeep_ref, first)
    else:
        gkeep_ref[...] = grads[: 2 * latent, :]
        gsend_ref[...] = grads[2 * latent :, :]


def slope_kernel(
    tiles, fast,
    cot_hbm, receiver_ref, dsum_ref, hidden_ref, slope_ref, normed_ref, inverse_ref, w2_ref, gain_ref,
    cot_ref, dpre_ref, gsend_ref, gkeep_ref,
    grads, dout, sems,
):
    here = lax.axis_index("tiles")
    edges, latent = cot_ref.shape
    nodes = dsum_ref.shape[0]
    copies = fetch(tile_pairs(cot_hbm, cot_ref, edges // 2), sems)
    steps = edges // TILE
    for copy in copies:
        copy.wait()

    def outer(step):
        tile = slice(step * TILE, (step + 1) * TILE)
        receivers = jnp.concatenate(
            pick_columns(index_columns(receiver_ref, step, TILE), 0, nodes), axis=1
        )
        grad_update = cot_ref[tile, :].astype(F32) + dot(receivers, dsum_ref[...])
        inverse = inverse_ref[tile, :1]
        dout[tile, :] = norm_backward(grad_update * gain_ref[...], normed_ref[tile, :], inverse)

    def inner(step):
        tile = slice(step * TILE, (step + 1) * TILE)
        dpre_ref[tile, :] = (
            dot(dout[tile, :], w2_ref[...], NT) * slope_ref[tile, :].astype(F32)
        ).astype(BF16)
        part = dot(hidden_ref[tile, :], dout[tile, :], TN)
        if step == 0:
            grads[...] = part
        else:
            grads[...] += part

    for step in range(steps + 1):
        if step < steps:
            outer(step)
        if step > 0:
            inner(step - 1)

    if fast:
        rows = latent // tiles
        split_halves(lax.rem(here, 2), grads, 0, rows, 0, rows, gsend_ref, gkeep_ref, 0)
    else:
        gkeep_ref[...] = grads[...]
        gsend_ref[...] = jnp.zeros_like(gsend_ref)


def first_kernel(
    tiles, places, fast,
    dpre_ref, early_ref, later_ref, sender_ref, receiver_ref, table_ref, node_ref, w1_ref, base_ref,
    *refs,
):
    out_refs, (grads, sums) = refs[:-2], refs[-2:]
    lower_ref, upper_ref, far_ref, partial_ref = out_refs[:4]
    here = lax.axis_index("tiles")
    edges, latent = dpre_ref.shape
    nodes = node_ref.shape[0]
    rows = table_ref.shape[0]
    early = early_ref.shape[0]

    for step in range(edges // TILE):
        tile = slice(step * TILE, (step + 1) * TILE)
        dpre = dpre_ref[tile, :]
        if step * TILE < early:
            edge = early_ref[tile, :]
        else:
            edge = later_ref[step * TILE - early : (step + 1) * TILE - early, :]
        part = dot(edge, dpre, TN)
        picks = jnp.concatenate(
            [
                pick_rows(sender_ref, step, TILE, rows),
                pick_rows(receiver_ref, step, TILE, nodes),
            ],
            axis=0,
        )
        scattered = dot(picks, dpre)
        if step == 0:
            grads[:latent, :] = part
            sums[...] = scattered
        else:
            grads[:latent, :] += part
            sums[...] += scattered

    by_sender = sums[:rows, :].astype(BF16)
    by_receiver = sums[rows:, :].astype(BF16)
    grads[latent : 2 * latent, :] = dot(table_ref[...], by_sender, TN)
    grads[2 * latent :, :] = dot(node_ref[...], by_receiver, TN)
    back = dot(by_sender, w1_ref[latent : 2 * latent, :], NT)
    far = back[nodes + 2 * NEAR : nodes + 2 * NEAR + places * tiles, :].astype(BF16)
    far_ref[...] = far
    if fast:
        bit = lax.rem(here, 2)
        block = 3 * latent // tiles
        at = 0
        for send_ref, keep_ref in (out_refs[4:6], out_refs[6:8]):
            part = keep_ref.shape[1]
            split_halves(bit, grads, 0, block, at, part, send_ref, keep_ref, 0)
            at += part
        out_refs[4][tiles // 2 * out_refs[5].shape[1] :, :] = slots_out(0, far, places)
    else:
        out_refs[4][...] = grads[...]
    lower_ref[...] = back[nodes : nodes + NEAR, :].astype(BF16)
    upper_ref[...] = back[nodes + NEAR : nodes + 2 * NEAR, :].astype(BF16)
    partial_ref[...] = (
        base_ref[...] + back[:nodes, :] + dot(by_receiver, w1_ref[2 * latent :, :], NT)
    )


def edge_kernel(dpre_ref, cot_ref, w1_ref, out_hbm, out_ref, sems):
    edges, latent = cot_ref.shape
    copies = []
    for step in range(edges // TILE):
        tile = pl.ds(step * TILE, TILE)
        out_ref[tile, :] = (
            cot_ref[tile, :].astype(F32) + dot(dpre_ref[tile, :], w1_ref[:latent, :], NT)
        ).astype(BF16)
        copy = pltpu.make_async_copy(out_ref.at[tile], out_hbm.at[tile], sems.at[step])
        copy.start()
        copies.append(copy)
    for copy in copies:
        copy.wait()


def node_kernel(fast, index_ref, partial_ref, below_ref, above_ref, slots_ref, *refs):
    out_ref = refs[-1]
    places, tiles = index_ref.shape[1], index_ref.shape[2]
    nodes = partial_ref.shape[0]
    origin = lax.axis_index("tiles") if fast else 0
    slots = slots_ref[...]
    if fast:
        got_ref = refs[0]
        slots = slots_in(3, slots, got_ref[got_ref.shape[0] - slots.shape[0] // 2 :, :], places)
    place = lax.broadcasted_iota(jnp.int32, (nodes, tiles), 0)
    owner, at = slot_owner(origin, (tiles, places * tiles), 1, places)
    row = lax.broadcasted_iota(jnp.int32, (tiles, places * tiles), 0)
    total = partial_ref[...]
    for j in range(places):
        picks = ones_where(place == index_ref[0, j : j + 1, :])
        far = dot(ones_where((owner == row) & (at == j)), slots).astype(BF16)
        total = total + dot(picks, far)
    out_ref[:NEAR, :] = (total[:NEAR, :] + below_ref[...].astype(F32)).astype(BF16)
    out_ref[NEAR : nodes - NEAR, :] = total[NEAR : nodes - NEAR, :].astype(BF16)
    out_ref[nodes - NEAR :, :] = (
        total[nodes - NEAR :, :] + above_ref[...].astype(F32)
    ).astype(BF16)


def halve_kernel(shift, count, places, *refs):
    keeps, gots = refs[:count], refs[count : 2 * count]
    rest = refs[2 * count :]
    send_ref, kept_ref = rest[-2:] if not places else rest[-3:-1]
    size = kept_ref.shape[1]
    bit = lax.rem(lax.div(lax.axis_index("tiles"), 2**shift), 2)
    at = 0
    for keep_ref, got_ref in zip(keeps, gots):
        blocks, rows = keep_ref.shape[:2]
        for q in range(blocks // 2):
            there, here = 2 * q + 1 - bit, 2 * q + bit
            got_there = got_ref[pl.ds(pl.multiple_of(there * rows, 32), rows), :].astype(F32)
            got_here = got_ref[pl.ds(pl.multiple_of(here * rows, 32), rows), :].astype(F32)
            to = q * size + at
            send_ref[to : to + rows, :] = (keep_ref[there] + got_there).astype(BF16)
            kept_ref[q, at : at + rows, :] = keep_ref[here] + got_here
        at += rows
    if places:
        slots_ref, moved_ref = rest[0], rest[-1]
        half = slots_ref.shape[0] // 2
        got_ref = gots[0]
        slots = slots_in(shift - 1, slots_ref[...], got_ref[got_ref.shape[0] - half :, :], places)
        moved_ref[...] = slots
        send_ref[send_ref.shape[0] - half :, :] = slots_out(shift, slots, places)


def finish_kernel(count, splits, *refs):
    out_refs = refs[2 * count :]
    rows = [0] * len(out_refs)
    for keep_ref, got_ref, parts in zip(refs[:count], refs[count : 2 * count], splits):
        at = 0
        for which, size in parts:
            first = rows[which]
            out_refs[which][first : first + size, :] = (
                keep_ref[0, at : at + size, :] + got_ref[at : at + size, :].astype(F32)
            )
            at += size
            rows[which] += size


def shaped(shape, dtype):
    return jax.ShapeDtypeStruct(shape, dtype)


def in_hbm(*arrays):
    return [pltpu.with_memory_space_constraint(array, pltpu.HBM) for array in arrays]


def call(kernel, name, out_shape, args, hbm=0, scratch=(), out_specs=None, limit=16):
    vmem = pl.BlockSpec(memory_space=pltpu.VMEM)
    return pl.pallas_call(
        kernel,
        in_specs=[pl.BlockSpec(memory_space=pltpu.HBM)] * hbm + [vmem] * (len(args) - hbm),
        out_specs=out_specs or [vmem] * len(out_shape),
        out_shape=out_shape,
        scratch_shapes=scratch,
        compiler_params=pltpu.CompilerParams(vmem_limit_bytes=limit * MIB),
        name=name,
    )(*in_hbm(*args[:hbm]), *args[hbm:])


def swap(tiles, bit, send):
    return lax.ppermute(send, "tiles", [(i, i ^ bit) for i in range(tiles)])


def halve(shift, keeps, gots, slots=None, places=0):
    half, _, width = keeps[0].shape
    rows = sum(keep.shape[1] for keep in keeps)
    extra = [] if slots is None else [slots]
    sent = half // 2 * rows + sum(slots.shape[0] // 2 for slots in extra)
    return call(
        functools.partial(halve_kernel, shift, len(keeps), places),
        "halve",
        [pltpu.VMEM((sent, width), BF16), pltpu.VMEM((half // 2, rows, width), F32)]
        + [pltpu.VMEM(slots.shape, BF16) for slots in extra],
        [*keeps, *gots, *extra],
    )


def finish(keeps, gots, splits, sizes):
    return call(
        functools.partial(finish_kernel, len(keeps), splits),
        "finish",
        [shaped((size, keeps[0].shape[-1]), F32) for size in sizes],
        [*keeps, *gots],
    )


def after(value, *others):
    return lax.optimization_barrier((value, *others))[0]


def shards(
    node_latent, edge_latent, node_cot, edge_cot,
    edge_w1, edge_b1, edge_w2, edge_b2, edge_gain,
    node_w1, node_b1, node_w2, node_b2, node_gain,
    send_index, edge_sender, edge_receiver, edge_count,
):
    tiles = lax.axis_size("tiles")
    nodes, latent = node_latent.shape
    edges = edge_latent.shape[0]
    places = send_index.shape[2]
    steps = edges // TILE
    used = nodes + 2 * NEAR + places * tiles
    rows = -(-used // LANES) * LANES
    fast = tiles == 16
    half = tiles // 2
    upward = [(i, i + 1) for i in range(tiles - 1)]
    downward = [(i + 1, i) for i in range(tiles - 1)]
    sender = edge_sender.reshape(edges // LANES, LANES)
    receiver = edge_receiver.reshape(edges // LANES, LANES)
    listed = jnp.swapaxes(send_index, 1, 2)
    row = lambda vector: vector.reshape(1, -1)
    vmem = pltpu.VMEM

    if fast:
        grad_shapes = lambda count: [
            vmem((count // 2, latent), BF16),
            vmem((half, count // tiles, latent), F32),
        ]
    else:
        grad_shapes = lambda count: [shaped((latent, latent), F32), shaped((count, latent), F32)]

    outgoing, send, head, tail = call(
        functools.partial(outgoing_kernel, fast),
        "outgoing",
        [
            vmem((tiles * places, latent), BF16) if fast else shaped((tiles * places, latent), BF16),
            vmem((tiles * places // 2, latent), BF16),
            vmem((NEAR, latent), BF16),
            vmem((NEAR, latent), BF16),
        ],
        [listed, node_latent],
        hbm=2,
        scratch=[vmem(listed.shape, jnp.int32), vmem((nodes, latent), BF16), pltpu.SemaphoreType.DMA((2,))],
    )
    lower = lax.ppermute(tail, "tiles", upward)
    upper = lax.ppermute(head, "tiles", downward)
    w1_kept, node_kept, receiver_kept, moved, weights = call(
        functools.partial(weights_kernel, places, fast),
        "weights",
        [
            vmem(edge_w1.shape, BF16), vmem((nodes, latent), BF16),
            vmem(receiver.shape, jnp.int32), vmem(sender.shape, jnp.int32),
            vmem((latent + 2 * nodes, latent), BF16),
        ],
        [node_latent, edge_w1, after(sender, send), receiver],
        hbm=4,
        scratch=[vmem(sender.shape, jnp.int32), pltpu.SemaphoreType.DMA((4,))],
    )

    def prepare(first, moved):
        return call(
            functools.partial(prepare_kernel, first),
            "prepare",
            [vmem((edges // 2, latent), BF16), vmem((edges // 2, latent), F32)],
            [row(edge_b1), edge_latent, moved, receiver_kept, weights],
            hbm=2,
            scratch=[vmem((1, latent), F32), pltpu.SemaphoreType.DMA((2,))],
        )

    def shuffle(bit, slots, got):
        return call(
            functools.partial(shuffle_kernel, bit, places),
            "shuffle",
            [vmem(slots.shape, BF16), vmem(got.shape, BF16)],
            [slots, got],
        )

    if fast:
        got = swap(tiles, 1, send)
        slots, send = shuffle(0, after(outgoing, moved), got)
        got = swap(tiles, 2, send)
        edge_early, early = prepare(0, after(moved, send))
        slots, send = shuffle(1, after(slots, early), got)
        got = swap(tiles, 4, send)
        edge_later, later = prepare(steps // 2, after(moved, send))
        slots, send = shuffle(2, after(slots, later), got)
        got = swap(tiles, 8, send)
    else:
        edge_early, early = prepare(0, moved)
        edge_later, later = prepare(steps // 2, moved)
        slots = lax.all_to_all(outgoing, "tiles", split_axis=0, concat_axis=0, tiled=True)
        got = slots

    (
        w2_kept, gain_kept,
        hidden, slope, normed, inverse, table, dsum, base, node_send, node_keep,
    ) = call(
        functools.partial(forward_kernel, tiles, places, fast),
        "forward",
        [
            vmem(edge_w2.shape, BF16), vmem((1, latent), F32),
            vmem((edges, latent), BF16), vmem((edges, latent), BF16), vmem((edges, latent), F32),
            vmem((edges, LANES), F32), vmem((rows, latent), BF16),
            vmem((nodes, latent), BF16), vmem((nodes, latent), F32),
        ] + grad_shapes(3 * latent if fast else 2 * latent),
        [
            edge_w2, node_w1, node_w2, node_cot,
            row(edge_b2), row(edge_gain), row(node_b1), row(node_b2), row(node_gain), edge_count,
            lower, upper, slots, got, early, later, w1_kept, node_kept, receiver_kept, moved,
        ],
        hbm=10,
        scratch=[
            vmem((rows - nodes, latent), BF16), vmem((nodes, latent), F32),
            vmem((3 * latent, latent), F32), vmem(node_w1.shape, BF16), vmem(node_w2.shape, BF16),
            vmem((nodes, latent), BF16),
        ] + [vmem((1, latent), F32)] * 4 + [
            pltpu.SMEM(edge_count.shape, jnp.int32), pltpu.SemaphoreType.DMA((10,)),
        ],
    )

    cot_kept, dpre, second_send, second_keep = call(
        functools.partial(slope_kernel, tiles, fast),
        "slope",
        [vmem((edges, latent), BF16), vmem((edges, latent), BF16)] + grad_shapes(latent),
        [edge_cot, receiver_kept, dsum, hidden, slope, normed, inverse, w2_kept, gain_kept],
        hbm=1,
        scratch=[
            vmem((latent, latent), F32), vmem((edges, latent), BF16), pltpu.SemaphoreType.DMA((2,)),
        ],
    )
    if fast:
        send, chain = halve(1, [node_keep], [swap(tiles, 1, node_send)])
        dpre = after(dpre, send)
        got = swap(tiles, 2, send)
        got_second = swap(tiles, 1, second_send)

    per = latent // tiles
    to_lower, to_upper, to_far, partial, *first = call(
        functools.partial(first_kernel, tiles, places, fast),
        "first",
        [
            vmem((NEAR, latent), BF16),
            vmem((NEAR, latent), BF16),
            vmem((tiles * places, latent), BF16) if fast else shaped((tiles * places, latent), BF16),
            vmem((nodes, latent), F32),
        ] + (
            [
                vmem((2 * half * per + tiles * places // 2, latent), BF16),
                vmem((half, 2 * per, latent), F32),
                vmem((half * per, latent), BF16), vmem((half, per, latent), F32),
            ]
            if fast else [shaped((3 * latent, latent), F32)]
        ),
        [dpre, edge_early, edge_later, moved, receiver_kept, table, node_kept, w1_kept, base],
        scratch=[vmem((3 * latent, latent), F32), vmem((rows + nodes, latent), F32)],
    )

    (grad_edge,) = call(
        edge_kernel,
        "edge",
        [shaped((edges, latent), BF16)],
        [after(dpre, partial), cot_kept, w1_kept],
        out_specs=[pl.BlockSpec(memory_space=pltpu.HBM)],
        scratch=[vmem((edges, latent), BF16), pltpu.SemaphoreType.DMA((steps,))],
    )

    if fast:
        send_a, keep_a, send_b, keep_b = first
        send_a, chain_a, slots = halve(
            1, [after(keep_a, grad_edge)], [swap(tiles, 1, send_a)], to_far, places
        )
        got_a = swap(tiles, 2, send_a)
        send_b, chain_b = halve(
            1, [after(keep_b, send_a), second_keep], [swap(tiles, 1, send_b), got_second]
        )
        got_b = swap(tiles, 2, send_b)
        to_lower, to_upper = lax.optimization_barrier((to_lower, to_upper, send_b))[:2]
        send, chain = halve(2, [after(chain, send_b)], [got])
        got = swap(tiles, 4, send)

    above = lax.ppermute(to_lower, "tiles", downward)
    below = lax.ppermute(to_upper, "tiles", upward)
    if fast:
        send, chain = halve(3, [chain], [got])
        got = swap(tiles, 8, send)
        send_a, chain_a, slots = halve(2, [after(chain_a, send)], [got_a], slots, places)
        got_a = swap(tiles, 4, send_a)
        send_a, chain_a, slots = halve(3, [chain_a], [got_a], slots, places)
        got_a = swap(tiles, 8, send_a)
        returned = [slots, got_a]
        send_b, chain_b = halve(2, [after(chain_b, send_a)], [got_b])
        got_b = swap(tiles, 4, send_b)
        grad_node_w1, grad_node_w2 = finish(
            [chain], [got], [[(0, 2 * per), (1, per)]], [2 * per, per]
        )
        send_b, chain_b = halve(3, [chain_b], [got_b])
        got_b = swap(tiles, 8, send_b)
        grad_edge_w1, grad_edge_w2 = finish(
            [chain_a, chain_b], [got_a, got_b], [[(0, 2 * per)], [(0, per), (1, per)]], [3 * per, per]
        )
    else:
        returned = [lax.all_to_all(to_far, "tiles", split_axis=0, concat_axis=0, tiled=True)]
        scatter = functools.partial(
            lax.psum_scatter, axis_name="tiles", scatter_dimension=0, tiled=True
        )
        grad_node_w1, grad_node_w2 = scatter(node_keep), scatter(node_send)
        grad_edge_w1, grad_edge_w2 = scatter(first[0]), scatter(second_keep)
    (grad_node,) = call(
        functools.partial(node_kernel, fast),
        "node",
        [shaped((nodes, latent), BF16)],
        [listed, partial, below, above, *returned],
    )
    return (grad_node, grad_edge, grad_edge_w1, grad_edge_w2, grad_node_w1, grad_node_w2)


def solution(mesh):
    split = P(("groups", "tiles"), None)
    return jax.shard_map(
        shards,
        mesh=mesh,
        in_specs=(split,) * 4
        + (P(),) * 10
        + (
            P(("groups", "tiles"), None, None),
            P(("groups", "tiles")),
            P(("groups", "tiles")),
            P("groups"),
        ),
        out_specs=(split,) * 6,
        check_vma=False,
    )
```

```python
import functools

import jax
import jax.numpy as jnp
from jax import lax
from jax.experimental import pallas as pl
from jax.experimental.pallas import tpu as pltpu
from jax.sharding import PartitionSpec as P

NEAR = 64
EPSILON = 1e-05
TILE = 256
LANES = 128
F32 = jnp.float32
BF16 = jnp.bfloat16
MIB = 1024 * 1024
AHEAD = 10**10

NN = (((1,), (0,)), ((), ()))
NT = (((1,), (1,)), ((), ()))
TN = (((0,), (0,)), ((), ()))


def dot(a, b, dims=NN):
    return lax.dot_general(a, b, dims, preferred_element_type=F32)


def sigmoid(x):
    return 0.5 * jnp.tanh(0.5 * x) + 0.5


def row_mean(x):
    return jnp.sum(x, axis=-1, keepdims=True) * (1.0 / x.shape[-1])


def ones_where(mask):
    return jnp.where(mask, 1.0, 0.0).astype(BF16)


def index_columns(idx_ref, step, tile):
    per = tile // LANES
    parts = []
    for j in range(per):
        row = idx_ref[pl.ds(step * per + j, 1), :]
        parts.append(jnp.transpose(jnp.broadcast_to(row, (LANES, LANES))))
    return jnp.concatenate(parts, axis=0)


def pick_columns(columns, start, stop):
    lane = lax.broadcasted_iota(jnp.int32, columns.shape, 1)
    return [ones_where(columns == lane + at) for at in range(start, stop, LANES)]


def pick_rows(idx_ref, step, tile, width):
    per = tile // LANES
    row = jnp.concatenate([idx_ref[pl.ds(step * per + j, 1), :] for j in range(per)], axis=1)
    return ones_where(lax.broadcasted_iota(jnp.int32, (width, tile), 0) == row)


def norm_forward(out):
    centred = out - row_mean(out)
    inverse = lax.rsqrt(row_mean(centred * centred) + EPSILON)
    return centred, inverse


def norm_backward(scaled, normed, inverse):
    return (
        inverse * (scaled - row_mean(scaled) - normed * row_mean(scaled * normed))
    ).astype(BF16)


def split_halves(bit, total_ref, at, block, first, rows, send_ref, keep_ref, offset):
    half, size = keep_ref.shape[:2]
    for q in range(half):
        there = pl.multiple_of(at + first + (2 * q + 1 - bit) * block, 32)
        here = pl.multiple_of(at + first + (2 * q + bit) * block, 32)
        to = q * size + offset
        send_ref[to : to + rows, :] = total_ref[pl.ds(there, rows), :].astype(BF16)
        keep_ref[q, offset : offset + rows, :] = total_ref[pl.ds(here, rows), :]


def fetch(pairs, sems):
    copies = []
    for at, (source, target) in enumerate(pairs):
        copies.append(pltpu.make_async_copy(source, target, sems.at[at]))
    for copy in copies:
        copy.start()
    return copies


def tile_pairs(source, target, tile):
    return [
        (source.at[pl.ds(at, tile)], target.at[pl.ds(at, tile)])
        for at in range(0, source.shape[0], tile)
    ]


def slot_owner(origin, shape, dim, places):
    row = lax.broadcasted_iota(jnp.int32, shape, dim)
    return lax.div(row, places) ^ origin, lax.rem(row, places)


def bit_slots(bit, shape, places):
    row = lax.broadcasted_iota(jnp.int32, shape, 0)
    column = lax.broadcasted_iota(jnp.int32, shape, 1)
    slot, place = lax.div(column, places), lax.rem(column, places)
    rank = ((slot >> (bit + 1)) << bit) | (slot & (2**bit - 1))
    return ((slot >> bit) & 1 == 1) & (rank * places + place == row)


def slots_out(bit, slots, places):
    rows = slots.shape[0]
    return dot(ones_where(bit_slots(bit, (rows // 2, rows), places)), slots).astype(BF16)


def slots_in(bit, slots, got, places):
    rows = slots.shape[0]
    row = lax.broadcasted_iota(jnp.int32, (rows, rows), 0)
    column = lax.broadcasted_iota(jnp.int32, (rows, rows), 1)
    kept = (row == column) & ((lax.div(column, places) >> bit) & 1 == 0)
    moved = ones_where(bit_slots(bit, (rows // 2, rows), places))
    return (dot(ones_where(kept), slots) + dot(moved, got, TN)).astype(BF16)


def outgoing_kernel(
    fast, index_hbm, node_hbm, slots_ref, send_ref, head_ref, tail_ref, index_ref, node_ref, sems
):
    for copy in fetch([(index_hbm, index_ref), (node_hbm, node_ref)], sems):
        copy.wait()
    places, tiles = index_ref.shape[1], index_ref.shape[2]
    nodes, latent = node_ref.shape
    origin = lax.axis_index("tiles") if fast else 0
    place = lax.broadcasted_iota(jnp.int32, (nodes, tiles), 0)
    owner, at = slot_owner(origin, (places * tiles, tiles), 0, places)
    column = lax.broadcasted_iota(jnp.int32, (places * tiles, tiles), 1)
    slots = jnp.zeros((places * tiles, latent), F32)
    for j in range(places):
        picks = ones_where(place == index_ref[0, j : j + 1, :])
        listed = dot(picks, node_ref[...], TN).astype(BF16)
        slots += dot(ones_where((owner == column) & (at == j)), listed)
    slots = slots.astype(BF16)
    slots_ref[...] = slots
    send_ref[...] = slots_out(3, slots, places) if fast else jnp.zeros_like(send_ref)
    head_ref[...] = node_ref[:NEAR, :]
    tail_ref[...] = node_ref[nodes - NEAR :, :]


def shuffle_kernel(bit, places, slots_ref, got_ref, moved_ref, send_ref):
    slots = slots_in(bit, slots_ref[...], got_ref[...], places)
    moved_ref[...] = slots
    send_ref[...] = slots_out(bit - 1, slots, places)


def table_index(raw, origin, places, nodes):
    far = raw - (nodes + 2 * NEAR)
    owner = lax.div(far, places) ^ origin
    far = nodes + 2 * NEAR + owner * places + lax.rem(far, places)
    rim = jnp.where(raw < NEAR, raw + nodes, raw)
    own = jnp.where((raw >= NEAR) & (raw < NEAR + nodes), raw - NEAR, rim)
    return jnp.where(raw >= nodes + 2 * NEAR, far, own)


def weights_kernel(
    places, fast,
    node_hbm, w1_hbm, sender_hbm, receiver_hbm,
    w1_ref, node_ref, receiver_ref, moved_ref, weights,
    sender_ref, sems,
):
    latent = node_ref.shape[1]
    nodes = node_ref.shape[0]
    copies = fetch(
        [
            (node_hbm, node_ref), (w1_hbm, w1_ref), (sender_hbm, sender_ref),
            (receiver_hbm, receiver_ref),
        ],
        sems,
    )
    for copy in copies:
        copy.wait()
    origin = lax.axis_index("tiles") if fast else 0
    moved_ref[...] = table_index(sender_ref[...], origin, places, nodes)
    weights[:latent, :] = w1_ref[:latent, :]
    weights[latent : latent + nodes, :] = dot(
        node_ref[...], w1_ref[latent : 2 * latent, :]
    ).astype(BF16)
    weights[latent + nodes :, :] = dot(node_ref[...], w1_ref[2 * latent :, :]).astype(BF16)


def prepare_kernel(
    first, b1_hbm, edge_hbm, moved_ref, receiver_ref, weights, edge_ref, partial_ref,
    b1_ref, sems,
):
    edges, latent = edge_ref.shape
    nodes = weights.shape[0] - latent >> 1
    start = pl.ds(first * TILE, edges)
    for copy in fetch([(b1_hbm, b1_ref), (edge_hbm.at[start], edge_ref)], sems):
        copy.wait()
    for step in range(edges // TILE):
        tile = slice(step * TILE, (step + 1) * TILE)
        senders = pick_columns(index_columns(moved_ref, first + step, TILE), 0, nodes)
        receivers = pick_columns(index_columns(receiver_ref, first + step, TILE), 0, nodes)
        inputs = jnp.concatenate([edge_ref[tile, :]] + senders + receivers, axis=1)
        partial_ref[tile, :] = dot(inputs, weights[...]) + b1_ref[...]


def forward_kernel(
    tiles, places, fast,
    w2_hbm, nw1_hbm, nw2_hbm, ncot_hbm,
    b2_hbm, gain_hbm, nb1_hbm, nb2_hbm, ngain_hbm, count_hbm,
    lower_ref, upper_ref, slots_ref, got_ref, early_ref, later_ref,
    w1_ref, node_ref, receiver_ref, moved_ref,
    w2_ref, gain_ref,
    hidden_ref, slope_ref, normed_ref, inverse_ref, table_ref, dsum_ref, base_ref,
    gsend_ref, gkeep_ref,
    weights, summed, grads, nw1_ref, nw2_ref, ncot_ref,
    b2_ref, nb1_ref, nb2_ref, ngain_ref, count_ref, sems,
):
    here = lax.axis_index("tiles")
    edges, latent = hidden_ref.shape
    nodes = node_ref.shape[0]
    rows = table_ref.shape[0]
    steps = edges // TILE

    early = fetch(
        [(count_hbm, count_ref), (b2_hbm, b2_ref), (gain_hbm, gain_ref), (w2_hbm, w2_ref)], sems
    )
    late = fetch(
        [
            (nw1_hbm, nw1_ref), (nw2_hbm, nw2_ref), (ncot_hbm, ncot_ref),
            (nb1_hbm, nb1_ref), (nb2_hbm, nb2_ref), (ngain_hbm, ngain_ref),
        ],
        sems.at[pl.ds(len(early), 6)],
    )

    table_ref[:nodes, :] = node_ref[...]
    table_ref[nodes : nodes + NEAR, :] = lower_ref[...]
    table_ref[nodes + NEAR : nodes + 2 * NEAR, :] = upper_ref[...]
    slots = slots_ref[...]
    if fast:
        slots = slots_in(0, slots, got_ref[...], places)
    table_ref[nodes + 2 * NEAR : nodes + 2 * NEAR + places * tiles, :] = slots
    used = nodes + 2 * NEAR + places * tiles
    if used < rows:
        table_ref[used:, :] = jnp.zeros((rows - used, latent), BF16)
    weights[...] = dot(table_ref[nodes:, :], w1_ref[latent : 2 * latent, :]).astype(BF16)
    for copy in early:
        copy.wait()
    live = count_ref[here]

    def activate(step):
        tile = slice(step * TILE, (step + 1) * TILE)
        senders = pick_columns(index_columns(moved_ref, step, TILE), nodes, rows)
        part = early_ref.shape[0]
        if step * TILE < part:
            known = early_ref[tile, :]
        else:
            known = later_ref[step * TILE - part : (step + 1) * TILE - part, :]
        preact = known + dot(jnp.concatenate(senders, axis=1), weights[...])
        sig = sigmoid(preact)
        slope_ref[tile, :] = (sig * (1.0 + preact * (1.0 - sig))).astype(BF16)
        hidden_ref[tile, :] = (preact * sig).astype(BF16)

    def normalize(step):
        tile = slice(step * TILE, (step + 1) * TILE)
        centred, inverse = norm_forward(dot(hidden_ref[tile, :], w2_ref[...]) + b2_ref[...])
        position = step * TILE + lax.broadcasted_iota(jnp.int32, inverse.shape, 0)
        inverse = jnp.where(position < live, inverse, 0.0)
        normed = centred * inverse
        normed_ref[tile, :] = normed
        inverse_ref[tile, :] = jnp.broadcast_to(inverse, (TILE, LANES))
        update = (normed * gain_ref[...]).astype(BF16)
        part = dot(pick_rows(receiver_ref, step, TILE, nodes), update)
        if step == 0:
            summed[...] = part
        else:
            summed[...] += part

    for step in range(steps + 1):
        if step < steps:
            activate(step)
        if step > 0:
            normalize(step - 1)

    for copy in late:
        copy.wait()
    node_in = jnp.concatenate([node_ref[...], summed[...].astype(BF16)], axis=1)
    preact_n = dot(node_in, nw1_ref[...]) + nb1_ref[...]
    sig_n = sigmoid(preact_n)
    hidden_n = (preact_n * sig_n).astype(BF16)
    centred_n, inverse_n = norm_forward(dot(hidden_n, nw2_ref[...]) + nb2_ref[...])
    cot = ncot_ref[...].astype(F32)
    dout = norm_backward(cot * ngain_ref[...], centred_n * inverse_n, inverse_n)
    slope_n = sig_n * (1.0 + preact_n * (1.0 - sig_n))
    dpre = (dot(dout, nw2_ref[...], NT) * slope_n).astype(BF16)
    grads[: 2 * latent, :] = dot(node_in, dpre, TN)
    grads[2 * latent :, :] = dot(hidden_n, dout, TN)
    base_ref[...] = cot + dot(dpre, nw1_ref[:latent, :], NT)
    dsum_ref[...] = dot(dpre, nw1_ref[latent:, :], NT).astype(BF16)
    if fast:
        bit = lax.rem(here, 2)
        first = 2 * latent // tiles
        split_halves(bit, grads, 0, first, 0, first, gsend_ref, gkeep_ref, 0)
        second = latent // tiles
        split_halves(bit, grads, 2 * latent, second, 0, second, gsend_ref, gkeep_ref, first)
    else:
        gkeep_ref[...] = grads[: 2 * latent, :]
        gsend_ref[...] = grads[2 * latent :, :]


def slope_kernel(
    tiles, fast,
    cot_hbm, receiver_ref, dsum_ref, hidden_ref, slope_ref, normed_ref, inverse_ref, w2_ref, gain_ref,
    cot_ref, dpre_ref, gsend_ref, gkeep_ref,
    grads, dout, sems,
):
    here = lax.axis_index("tiles")
    edges, latent = cot_ref.shape
    nodes = dsum_ref.shape[0]
    copies = fetch(tile_pairs(cot_hbm, cot_ref, edges // 2), sems)
    steps = edges // TILE
    for copy in copies:
        copy.wait()

    def outer(step):
        tile = slice(step * TILE, (step + 1) * TILE)
        receivers = jnp.concatenate(
            pick_columns(index_columns(receiver_ref, step, TILE), 0, nodes), axis=1
        )
        grad_update = cot_ref[tile, :].astype(F32) + dot(receivers, dsum_ref[...])
        inverse = inverse_ref[tile, :1]
        dout[tile, :] = norm_backward(grad_update * gain_ref[...], normed_ref[tile, :], inverse)

    def inner(step):
        tile = slice(step * TILE, (step + 1) * TILE)
        dpre_ref[tile, :] = (
            dot(dout[tile, :], w2_ref[...], NT) * slope_ref[tile, :].astype(F32)
        ).astype(BF16)
        part = dot(hidden_ref[tile, :], dout[tile, :], TN)
        if step == 0:
            grads[...] = part
        else:
            grads[...] += part

    for step in range(steps + 1):
        if step < steps:
            outer(step)
        if step > 0:
            inner(step - 1)

    if fast:
        rows = latent // tiles
        split_halves(lax.rem(here, 2), grads, 0, rows, 0, rows, gsend_ref, gkeep_ref, 0)
    else:
        gkeep_ref[...] = grads[...]
        gsend_ref[...] = jnp.zeros_like(gsend_ref)


def first_kernel(
    tiles, places, fast,
    dpre_ref, early_ref, later_ref, sender_ref, receiver_ref, table_ref, node_ref, w1_ref, base_ref,
    *refs,
):
    out_refs, (grads, sums) = refs[:-2], refs[-2:]
    lower_ref, upper_ref, far_ref, partial_ref = out_refs[:4]
    here = lax.axis_index("tiles")
    edges, latent = dpre_ref.shape
    nodes = node_ref.shape[0]
    rows = table_ref.shape[0]
    early = early_ref.shape[0]

    for step in range(edges // TILE):
        tile = slice(step * TILE, (step + 1) * TILE)
        dpre = dpre_ref[tile, :]
        if step * TILE < early:
            edge = early_ref[tile, :]
        else:
            edge = later_ref[step * TILE - early : (step + 1) * TILE - early, :]
        part = dot(edge, dpre, TN)
        picks = jnp.concatenate(
            [
                pick_rows(sender_ref, step, TILE, rows),
                pick_rows(receiver_ref, step, TILE, nodes),
            ],
            axis=0,
        )
        scattered = dot(picks, dpre)
        if step == 0:
            grads[:latent, :] = part
            sums[...] = scattered
        else:
            grads[:latent, :] += part
            sums[...] += scattered

    by_sender = sums[:rows, :].astype(BF16)
    by_receiver = sums[rows:, :].astype(BF16)
    grads[latent : 2 * latent, :] = dot(table_ref[...], by_sender, TN)
    grads[2 * latent :, :] = dot(node_ref[...], by_receiver, TN)
    back = dot(by_sender, w1_ref[latent : 2 * latent, :], NT)
    far = back[nodes + 2 * NEAR : nodes + 2 * NEAR + places * tiles, :].astype(BF16)
    far_ref[...] = far
    if fast:
        bit = lax.rem(here, 2)
        block = 3 * latent // tiles
        at = 0
        for send_ref, keep_ref in (out_refs[4:6], out_refs[6:8]):
            part = keep_ref.shape[1]
            split_halves(bit, grads, 0, block, at, part, send_ref, keep_ref, 0)
            at += part
        out_refs[4][tiles // 2 * out_refs[5].shape[1] :, :] = slots_out(0, far, places)
    else:
        out_refs[4][...] = grads[...]
    lower_ref[...] = back[nodes : nodes + NEAR, :].astype(BF16)
    upper_ref[...] = back[nodes + NEAR : nodes + 2 * NEAR, :].astype(BF16)
    partial_ref[...] = (
        base_ref[...] + back[:nodes, :] + dot(by_receiver, w1_ref[2 * latent :, :], NT)
    )


def edge_kernel(dpre_ref, cot_ref, w1_ref, out_hbm, out_ref, sems):
    edges, latent = cot_ref.shape
    copies = []
    for step in range(edges // TILE):
        tile = pl.ds(step * TILE, TILE)
        out_ref[tile, :] = (
            cot_ref[tile, :].astype(F32) + dot(dpre_ref[tile, :], w1_ref[:latent, :], NT)
        ).astype(BF16)
        copy = pltpu.make_async_copy(out_ref.at[tile], out_hbm.at[tile], sems.at[step])
        copy.start()
        copies.append(copy)
    for copy in copies:
        copy.wait()


def node_kernel(fast, index_ref, partial_ref, below_ref, above_ref, slots_ref, *refs):
    out_ref = refs[-1]
    places, tiles = index_ref.shape[1], index_ref.shape[2]
    nodes = partial_ref.shape[0]
    origin = lax.axis_index("tiles") if fast else 0
    slots = slots_ref[...]
    if fast:
        got_ref = refs[0]
        slots = slots_in(3, slots, got_ref[got_ref.shape[0] - slots.shape[0] // 2 :, :], places)
    place = lax.broadcasted_iota(jnp.int32, (nodes, tiles), 0)
    owner, at = slot_owner(origin, (tiles, places * tiles), 1, places)
    row = lax.broadcasted_iota(jnp.int32, (tiles, places * tiles), 0)
    total = partial_ref[...]
    for j in range(places):
        picks = ones_where(place == index_ref[0, j : j + 1, :])
        far = dot(ones_where((owner == row) & (at == j)), slots).astype(BF16)
        total = total + dot(picks, far)
    out_ref[:NEAR, :] = (total[:NEAR, :] + below_ref[...].astype(F32)).astype(BF16)
    out_ref[NEAR : nodes - NEAR, :] = total[NEAR : nodes - NEAR, :].astype(BF16)
    out_ref[nodes - NEAR :, :] = (
        total[nodes - NEAR :, :] + above_ref[...].astype(F32)
    ).astype(BF16)


def halve_kernel(shift, count, places, *refs):
    keeps, gots = refs[:count], refs[count : 2 * count]
    rest = refs[2 * count :]
    send_ref, kept_ref = rest[-2:] if not places else rest[-3:-1]
    size = kept_ref.shape[1]
    bit = lax.rem(lax.div(lax.axis_index("tiles"), 2**shift), 2)
    at = 0
    for keep_ref, got_ref in zip(keeps, gots):
        blocks, rows = keep_ref.shape[:2]
        for q in range(blocks // 2):
            there, here = 2 * q + 1 - bit, 2 * q + bit
            got_there = got_ref[pl.ds(pl.multiple_of(there * rows, 32), rows), :].astype(F32)
            got_here = got_ref[pl.ds(pl.multiple_of(here * rows, 32), rows), :].astype(F32)
            to = q * size + at
            send_ref[to : to + rows, :] = (keep_ref[there] + got_there).astype(BF16)
            kept_ref[q, at : at + rows, :] = keep_ref[here] + got_here
        at += rows
    if places:
        slots_ref, moved_ref = rest[0], rest[-1]
        half = slots_ref.shape[0] // 2
        got_ref = gots[0]
        slots = slots_in(shift - 1, slots_ref[...], got_ref[got_ref.shape[0] - half :, :], places)
        moved_ref[...] = slots
        send_ref[send_ref.shape[0] - half :, :] = slots_out(shift, slots, places)


def finish_kernel(count, splits, *refs):
    out_refs = refs[2 * count :]
    rows = [0] * len(out_refs)
    for keep_ref, got_ref, parts in zip(refs[:count], refs[count : 2 * count], splits):
        at = 0
        for which, size in parts:
            first = rows[which]
            out_refs[which][first : first + size, :] = (
                keep_ref[0, at : at + size, :] + got_ref[at : at + size, :].astype(F32)
            )
            at += size
            rows[which] += size


def shaped(shape, dtype):
    return jax.ShapeDtypeStruct(shape, dtype)


def in_hbm(*arrays):
    return [pltpu.with_memory_space_constraint(array, pltpu.HBM) for array in arrays]


def call(kernel, name, out_shape, args, hbm=0, scratch=(), out_specs=None, flops=0):
    vmem = pl.BlockSpec(memory_space=pltpu.VMEM)
    return pl.pallas_call(
        kernel,
        in_specs=[pl.BlockSpec(memory_space=pltpu.HBM)] * hbm + [vmem] * (len(args) - hbm),
        out_specs=out_specs or [vmem] * len(out_shape),
        out_shape=out_shape,
        scratch_shapes=scratch,
        compiler_params=pltpu.CompilerParams(vmem_limit_bytes=16 * MIB),
        cost_estimate=pl.CostEstimate(flops=flops, bytes_accessed=flops // 100, transcendentals=0),
        name=name,
    )(*in_hbm(*args[:hbm]), *args[hbm:])


def swap(tiles, bit, send):
    return lax.ppermute(send, "tiles", [(i, i ^ bit) for i in range(tiles)])


def halve(shift, keeps, gots, slots=None, places=0, flops=0):
    half, _, width = keeps[0].shape
    rows = sum(keep.shape[1] for keep in keeps)
    extra = [] if slots is None else [slots]
    sent = half // 2 * rows + sum(slots.shape[0] // 2 for slots in extra)
    return call(
        functools.partial(halve_kernel, shift, len(keeps), places),
        "halve",
        [pltpu.VMEM((sent, width), BF16), pltpu.VMEM((half // 2, rows, width), F32)]
        + [pltpu.VMEM(slots.shape, BF16) for slots in extra],
        [*keeps, *gots, *extra],
        flops=flops,
    )


def finish(keeps, gots, splits, sizes):
    return call(
        functools.partial(finish_kernel, len(keeps), splits),
        "finish",
        [shaped((size, keeps[0].shape[-1]), F32) for size in sizes],
        [*keeps, *gots],
    )


def after(value, *others):
    return lax.optimization_barrier((value, *others))[0]


def shards(
    node_latent, edge_latent, node_cot, edge_cot,
    edge_w1, edge_b1, edge_w2, edge_b2, edge_gain,
    node_w1, node_b1, node_w2, node_b2, node_gain,
    send_index, edge_sender, edge_receiver, edge_count,
):
    tiles = lax.axis_size("tiles")
    nodes, latent = node_latent.shape
    edges = edge_latent.shape[0]
    places = send_index.shape[2]
    steps = edges // TILE
    used = nodes + 2 * NEAR + places * tiles
    rows = -(-used // LANES) * LANES
    fast = tiles == 16
    half = tiles // 2
    upward = [(i, i + 1) for i in range(tiles - 1)]
    downward = [(i + 1, i) for i in range(tiles - 1)]
    sender = edge_sender.reshape(edges // LANES, LANES)
    receiver = edge_receiver.reshape(edges // LANES, LANES)
    listed = jnp.swapaxes(send_index, 1, 2)
    row = lambda vector: vector.reshape(1, -1)
    vmem = pltpu.VMEM

    if fast:
        grad_shapes = lambda count: [
            vmem((count // 2, latent), BF16),
            vmem((half, count // tiles, latent), F32),
        ]
    else:
        grad_shapes = lambda count: [shaped((latent, latent), F32), shaped((count, latent), F32)]

    outgoing, send, head, tail = call(
        functools.partial(outgoing_kernel, fast),
        "outgoing",
        [
            vmem((tiles * places, latent), BF16) if fast else shaped((tiles * places, latent), BF16),
            vmem((tiles * places // 2, latent), BF16),
            vmem((NEAR, latent), BF16),
            vmem((NEAR, latent), BF16),
        ],
        [listed, node_latent],
        hbm=2,
        scratch=[vmem(listed.shape, jnp.int32), vmem((nodes, latent), BF16), pltpu.SemaphoreType.DMA((2,))],
    )
    if fast:
        far_got = swap(tiles, 8, send)
    lower = lax.ppermute(tail, "tiles", upward)
    upper = lax.ppermute(head, "tiles", downward)
    w1_kept, node_kept, receiver_kept, moved, weights = call(
        functools.partial(weights_kernel, places, fast),
        "weights",
        [
            vmem(edge_w1.shape, BF16), vmem((nodes, latent), BF16),
            vmem(receiver.shape, jnp.int32), vmem(sender.shape, jnp.int32),
            vmem((latent + 2 * nodes, latent), BF16),
        ],
        [node_latent, edge_w1, after(sender, send), receiver],
        hbm=4,
        scratch=[vmem(sender.shape, jnp.int32), pltpu.SemaphoreType.DMA((4,))],
    )

    def prepare(first, moved):
        return call(
            functools.partial(prepare_kernel, first),
            "prepare",
            [vmem((edges // 2, latent), BF16), vmem((edges // 2, latent), F32)],
            [row(edge_b1), edge_latent, moved, receiver_kept, weights],
            hbm=2,
            scratch=[vmem((1, latent), F32), pltpu.SemaphoreType.DMA((2,))],
        )

    def shuffle(bit, slots, got):
        return call(
            functools.partial(shuffle_kernel, bit, places),
            "shuffle",
            [vmem(slots.shape, BF16), vmem(got.shape, BF16)],
            [slots, got],
        )

    if fast:
        slots, send = shuffle(3, after(outgoing, moved), far_got)
        got = swap(tiles, 4, send)
        edge_early, early = prepare(0, after(moved, send))
        slots, send = shuffle(2, after(slots, early), got)
        got = swap(tiles, 2, send)
        edge_later, later = prepare(steps // 2, after(moved, send))
        slots, send = shuffle(1, after(slots, later), got)
        got = swap(tiles, 1, send)
    else:
        edge_early, early = prepare(0, moved)
        edge_later, later = prepare(steps // 2, moved)
        slots = lax.all_to_all(outgoing, "tiles", split_axis=0, concat_axis=0, tiled=True)
        got = slots

    (
        w2_kept, gain_kept,
        hidden, slope, normed, inverse, table, dsum, base, node_send, node_keep,
    ) = call(
        functools.partial(forward_kernel, tiles, places, fast),
        "forward",
        [
            vmem(edge_w2.shape, BF16), vmem((1, latent), F32),
            vmem((edges, latent), BF16), vmem((edges, latent), BF16), vmem((edges, latent), F32),
            vmem((edges, LANES), F32), vmem((rows, latent), BF16),
            vmem((nodes, latent), BF16), vmem((nodes, latent), F32),
        ] + grad_shapes(3 * latent if fast else 2 * latent),
        [
            edge_w2, node_w1, node_w2, node_cot,
            row(edge_b2), row(edge_gain), row(node_b1), row(node_b2), row(node_gain), edge_count,
            lower, upper, slots, got, early, later, w1_kept, node_kept, receiver_kept, moved,
        ],
        hbm=10,
        scratch=[
            vmem((rows - nodes, latent), BF16), vmem((nodes, latent), F32),
            vmem((3 * latent, latent), F32), vmem(node_w1.shape, BF16), vmem(node_w2.shape, BF16),
            vmem((nodes, latent), BF16),
        ] + [vmem((1, latent), F32)] * 4 + [
            pltpu.SMEM(edge_count.shape, jnp.int32), pltpu.SemaphoreType.DMA((10,)),
        ],
    )

    cot_kept, dpre, second_send, second_keep = call(
        functools.partial(slope_kernel, tiles, fast),
        "slope",
        [vmem((edges, latent), BF16), vmem((edges, latent), BF16)] + grad_shapes(latent),
        [edge_cot, receiver_kept, dsum, hidden, slope, normed, inverse, w2_kept, gain_kept],
        hbm=1,
        scratch=[
            vmem((latent, latent), F32), vmem((edges, latent), BF16), pltpu.SemaphoreType.DMA((2,)),
        ],
    )
    if fast:
        send, chain = halve(1, [after(node_keep, dpre)], [swap(tiles, 1, node_send)])
        dpre = after(dpre, send)
        got = swap(tiles, 2, send)
        got_second = swap(tiles, 1, second_send)

    (grad_edge,) = call(
        edge_kernel,
        "edge",
        [shaped((edges, latent), BF16)],
        [dpre, cot_kept, w1_kept],
        out_specs=[pl.BlockSpec(memory_space=pltpu.HBM)],
        scratch=[vmem((edges, latent), BF16), pltpu.SemaphoreType.DMA((steps,))],
    )
    dpre = after(dpre, grad_edge)

    per = latent // tiles
    to_lower, to_upper, to_far, partial, *first = call(
        functools.partial(first_kernel, tiles, places, fast),
        "first",
        [
            vmem((NEAR, latent), BF16),
            vmem((NEAR, latent), BF16),
            vmem((tiles * places, latent), BF16) if fast else shaped((tiles * places, latent), BF16),
            vmem((nodes, latent), F32),
        ] + (
            [
                vmem((2 * half * per + tiles * places // 2, latent), BF16),
                vmem((half, 2 * per, latent), F32),
                vmem((half * per, latent), BF16), vmem((half, per, latent), F32),
            ]
            if fast else [shaped((3 * latent, latent), F32)]
        ),
        [dpre, edge_early, edge_later, moved, receiver_kept, table, node_kept, w1_kept, base],
        scratch=[vmem((3 * latent, latent), F32), vmem((rows + nodes, latent), F32)],
    )

    if fast:
        send_a, keep_a, send_b, keep_b = first
        send, chain = halve(2, [after(chain, partial)], [got], flops=AHEAD)
        got = swap(tiles, 4, send)
        send_a, chain_a, slots = halve(
            1, [after(keep_a, send)], [swap(tiles, 1, send_a)], to_far, places
        )
        got_a = swap(tiles, 2, send_a)
        send_b, chain_b = halve(
            1, [after(keep_b, send_a), second_keep], [swap(tiles, 1, send_b), got_second]
        )
        got_b = swap(tiles, 2, send_b)
        to_lower, to_upper = lax.optimization_barrier((to_lower, to_upper, send_b))[:2]

    above = lax.ppermute(to_lower, "tiles", downward)
    below = lax.ppermute(to_upper, "tiles", upward)
    if fast:
        send, chain = halve(3, [chain], [got])
        got = swap(tiles, 8, send)
        chain_a = lax.optimization_barrier((chain_a, send, above, below))[0]
        send_a, chain_a, slots = halve(2, [chain_a], [got_a], slots, places, AHEAD)
        got_a = swap(tiles, 4, send_a)
        send_a, chain_a, slots = halve(3, [chain_a], [got_a], slots, places)
        got_a = swap(tiles, 8, send_a)
        send_b, chain_b = halve(2, [after(chain_b, send_a, got)], [got_b])
        got_b = swap(tiles, 4, send_b)
        send_b, chain_b = halve(3, [chain_b], [got_b])
        got_b = swap(tiles, 8, send_b)
        returned = [slots, got_a]
        grad_edge_w1, grad_edge_w2, grad_node_w1, grad_node_w2 = finish(
            [chain, chain_a, chain_b],
            [got, got_a, got_b],
            [[(2, 2 * per), (3, per)], [(0, 2 * per)], [(0, per), (1, per)]],
            [3 * per, per, 2 * per, per],
        )
    else:
        returned = [lax.all_to_all(to_far, "tiles", split_axis=0, concat_axis=0, tiled=True)]
        scatter = functools.partial(
            lax.psum_scatter, axis_name="tiles", scatter_dimension=0, tiled=True
        )
        grad_node_w1, grad_node_w2 = scatter(node_keep), scatter(node_send)
        grad_edge_w1, grad_edge_w2 = scatter(first[0]), scatter(second_keep)
    (grad_node,) = call(
        functools.partial(node_kernel, fast),
        "node",
        [shaped((nodes, latent), BF16)],
        [listed, partial, below, above, *returned],
    )
    return (grad_node, grad_edge, grad_edge_w1, grad_edge_w2, grad_node_w1, grad_node_w2)


def solution(mesh):
    split = P(("groups", "tiles"), None)
    return jax.shard_map(
        shards,
        mesh=mesh,
        in_specs=(split,) * 4
        + (P(),) * 10
        + (
            P(("groups", "tiles"), None, None),
            P(("groups", "tiles")),
            P(("groups", "tiles")),
            P("groups"),
        ),
        out_specs=(split,) * 6,
        check_vma=False,
    )
```

```python
import functools

import jax
import jax.numpy as jnp
from jax import lax
from jax.experimental import pallas as pl
from jax.experimental.pallas import tpu as pltpu
from jax.sharding import PartitionSpec as P

NEAR = 64
EPSILON = 1e-05
TILE = 256
LANES = 128
F32 = jnp.float32
BF16 = jnp.bfloat16
MIB = 1024 * 1024
AHEAD = 10**10

NN = (((1,), (0,)), ((), ()))
NT = (((1,), (1,)), ((), ()))
TN = (((0,), (0,)), ((), ()))


def dot(a, b, dims=NN):
    return lax.dot_general(a, b, dims, preferred_element_type=F32)


def sigmoid(x):
    return 0.5 * jnp.tanh(0.5 * x) + 0.5


def row_mean(x):
    return jnp.sum(x, axis=-1, keepdims=True) * (1.0 / x.shape[-1])


def ones_where(mask):
    return jnp.where(mask, 1.0, 0.0).astype(BF16)


def index_columns(idx_ref, step, tile):
    per = tile // LANES
    parts = []
    for j in range(per):
        row = idx_ref[pl.ds(step * per + j, 1), :]
        parts.append(jnp.transpose(jnp.broadcast_to(row, (LANES, LANES))))
    return jnp.concatenate(parts, axis=0)


def pick_columns(columns, start, stop):
    lane = lax.broadcasted_iota(jnp.int32, columns.shape, 1)
    return [ones_where(columns == lane + at) for at in range(start, stop, LANES)]


def pick_rows(idx_ref, step, tile, width):
    per = tile // LANES
    row = jnp.concatenate([idx_ref[pl.ds(step * per + j, 1), :] for j in range(per)], axis=1)
    return ones_where(lax.broadcasted_iota(jnp.int32, (width, tile), 0) == row)


def norm_forward(out):
    centred = out - row_mean(out)
    inverse = lax.rsqrt(row_mean(centred * centred) + EPSILON)
    return centred, inverse


def norm_backward(scaled, normed, inverse):
    return (
        inverse * (scaled - row_mean(scaled) - normed * row_mean(scaled * normed))
    ).astype(BF16)


def split_halves(bit, total_ref, at, block, first, rows, send_ref, keep_ref, offset):
    half, size = keep_ref.shape[:2]
    for q in range(half):
        there = pl.multiple_of(at + first + (2 * q + 1 - bit) * block, 32)
        here = pl.multiple_of(at + first + (2 * q + bit) * block, 32)
        to = q * size + offset
        send_ref[to : to + rows, :] = total_ref[pl.ds(there, rows), :].astype(BF16)
        keep_ref[q, offset : offset + rows, :] = total_ref[pl.ds(here, rows), :]


def fetch(pairs, sems):
    copies = []
    for at, (source, target) in enumerate(pairs):
        copies.append(pltpu.make_async_copy(source, target, sems.at[at]))
    for copy in copies:
        copy.start()
    return copies


def tile_pairs(source, target, tile):
    return [
        (source.at[pl.ds(at, tile)], target.at[pl.ds(at, tile)])
        for at in range(0, source.shape[0], tile)
    ]


def slot_owner(origin, shape, dim, places):
    row = lax.broadcasted_iota(jnp.int32, shape, dim)
    return lax.div(row, places) ^ origin, lax.rem(row, places)


def bit_slots(bit, shape, places):
    row = lax.broadcasted_iota(jnp.int32, shape, 0)
    column = lax.broadcasted_iota(jnp.int32, shape, 1)
    slot, place = lax.div(column, places), lax.rem(column, places)
    rank = ((slot >> (bit + 1)) << bit) | (slot & (2**bit - 1))
    return ((slot >> bit) & 1 == 1) & (rank * places + place == row)


def slots_out(bit, slots, places):
    rows = slots.shape[0]
    return dot(ones_where(bit_slots(bit, (rows // 2, rows), places)), slots).astype(BF16)


def slots_in(bit, slots, got, places):
    rows = slots.shape[0]
    row = lax.broadcasted_iota(jnp.int32, (rows, rows), 0)
    column = lax.broadcasted_iota(jnp.int32, (rows, rows), 1)
    kept = (row == column) & ((lax.div(column, places) >> bit) & 1 == 0)
    moved = ones_where(bit_slots(bit, (rows // 2, rows), places))
    return (dot(ones_where(kept), slots) + dot(moved, got, TN)).astype(BF16)


def outgoing_kernel(
    index_hbm, node_hbm, slots_ref, head_ref, tail_ref, index_ref, node_ref, sems
):
    for copy in fetch([(index_hbm, index_ref), (node_hbm, node_ref)], sems):
        copy.wait()
    places, tiles = index_ref.shape[1], index_ref.shape[2]
    nodes, latent = node_ref.shape
    place = lax.broadcasted_iota(jnp.int32, (nodes, tiles), 0)
    for j in range(places):
        picks = ones_where(place == index_ref[0, j : j + 1, :])
        slots_ref[:, j, :] = dot(picks, node_ref[...], TN).astype(BF16)
    head_ref[...] = node_ref[:NEAR, :]
    tail_ref[...] = node_ref[nodes - NEAR :, :]


def table_index(raw, origin, places, nodes):
    far = raw - (nodes + 2 * NEAR)
    owner = lax.div(far, places) ^ origin
    far = nodes + 2 * NEAR + owner * places + lax.rem(far, places)
    rim = jnp.where(raw < NEAR, raw + nodes, raw)
    own = jnp.where((raw >= NEAR) & (raw < NEAR + nodes), raw - NEAR, rim)
    return jnp.where(raw >= nodes + 2 * NEAR, far, own)


def prepare_kernel(
    places, fast,
    node_hbm, w1_hbm, sender_hbm, receiver_hbm, b1_hbm, edge_hbm,
    edge_ref, w1_ref, node_ref, receiver_ref, moved_ref, partial_ref,
    weights, sender_ref, b1_ref, sems, edge_sems,
):
    edges, latent = edge_ref.shape
    nodes = node_ref.shape[0]
    copies = fetch(
        [
            (node_hbm, node_ref), (w1_hbm, w1_ref), (sender_hbm, sender_ref),
            (receiver_hbm, receiver_ref), (b1_hbm, b1_ref),
        ],
        sems,
    )
    edge_copies = fetch(tile_pairs(edge_hbm, edge_ref, edges // 2), edge_sems)
    for copy in copies:
        copy.wait()
    origin = lax.axis_index("tiles") if fast else 0
    moved_ref[...] = table_index(sender_ref[...], origin, places, nodes)
    weights[:latent, :] = w1_ref[:latent, :]
    weights[latent : latent + nodes, :] = dot(
        node_ref[...], w1_ref[latent : 2 * latent, :]
    ).astype(BF16)
    weights[latent + nodes :, :] = dot(node_ref[...], w1_ref[2 * latent :, :]).astype(BF16)
    for copy in edge_copies:
        copy.wait()
    for step in range(edges // TILE):
        tile = slice(step * TILE, (step + 1) * TILE)
        senders = pick_columns(index_columns(moved_ref, step, TILE), 0, nodes)
        receivers = pick_columns(index_columns(receiver_ref, step, TILE), 0, nodes)
        inputs = jnp.concatenate([edge_ref[tile, :]] + senders + receivers, axis=1)
        partial_ref[tile, :] = dot(inputs, weights[...]) + b1_ref[...]


def forward_kernel(
    tiles, places, fast,
    w2_hbm, nw1_hbm, nw2_hbm, ncot_hbm,
    b2_hbm, gain_hbm, nb1_hbm, nb2_hbm, ngain_hbm, count_hbm,
    lower_ref, upper_ref, slots_ref, known_ref, w1_ref, node_ref, receiver_ref, moved_ref,
    w2_ref, gain_ref,
    hidden_ref, slope_ref, normed_ref, inverse_ref, table_ref, dsum_ref, base_ref,
    gsend_ref, gkeep_ref,
    weights, summed, grads, nw1_ref, nw2_ref, ncot_ref,
    b2_ref, nb1_ref, nb2_ref, ngain_ref, count_ref, sems,
):
    here = lax.axis_index("tiles")
    edges, latent = hidden_ref.shape
    nodes = node_ref.shape[0]
    rows = table_ref.shape[0]
    steps = edges // TILE

    early = fetch(
        [(count_hbm, count_ref), (b2_hbm, b2_ref), (gain_hbm, gain_ref), (w2_hbm, w2_ref)], sems
    )
    late = fetch(
        [
            (nw1_hbm, nw1_ref), (nw2_hbm, nw2_ref), (ncot_hbm, ncot_ref),
            (nb1_hbm, nb1_ref), (nb2_hbm, nb2_ref), (ngain_hbm, ngain_ref),
        ],
        sems.at[pl.ds(len(early), 6)],
    )

    table_ref[:nodes, :] = node_ref[...]
    table_ref[nodes : nodes + NEAR, :] = lower_ref[...]
    table_ref[nodes + NEAR : nodes + 2 * NEAR, :] = upper_ref[...]
    owner, at = slot_owner(here if fast else 0, (places * tiles, tiles), 0, places)
    source = lax.broadcasted_iota(jnp.int32, (places * tiles, tiles), 1)
    slots = jnp.zeros((places * tiles, latent), F32)
    for j in range(places):
        slots += dot(ones_where((owner == source) & (at == j)), slots_ref[:, j, :])
    table_ref[nodes + 2 * NEAR : nodes + 2 * NEAR + places * tiles, :] = slots.astype(BF16)
    used = nodes + 2 * NEAR + places * tiles
    if used < rows:
        table_ref[used:, :] = jnp.zeros((rows - used, latent), BF16)
    weights[...] = dot(table_ref[nodes:, :], w1_ref[latent : 2 * latent, :]).astype(BF16)
    for copy in early:
        copy.wait()
    live = count_ref[here]

    def activate(step):
        tile = slice(step * TILE, (step + 1) * TILE)
        senders = pick_columns(index_columns(moved_ref, step, TILE), nodes, rows)
        preact = known_ref[tile, :] + dot(jnp.concatenate(senders, axis=1), weights[...])
        sig = sigmoid(preact)
        slope_ref[tile, :] = (sig * (1.0 + preact * (1.0 - sig))).astype(BF16)
        hidden_ref[tile, :] = (preact * sig).astype(BF16)

    def normalize(step):
        tile = slice(step * TILE, (step + 1) * TILE)
        centred, inverse = norm_forward(dot(hidden_ref[tile, :], w2_ref[...]) + b2_ref[...])
        position = step * TILE + lax.broadcasted_iota(jnp.int32, inverse.shape, 0)
        inverse = jnp.where(position < live, inverse, 0.0)
        normed = centred * inverse
        normed_ref[tile, :] = normed
        inverse_ref[tile, :] = jnp.broadcast_to(inverse, (TILE, LANES))
        update = (normed * gain_ref[...]).astype(BF16)
        part = dot(pick_rows(receiver_ref, step, TILE, nodes), update)
        if step == 0:
            summed[...] = part
        else:
            summed[...] += part

    for step in range(steps + 1):
        if step < steps:
            activate(step)
        if step > 0:
            normalize(step - 1)

    for copy in late:
        copy.wait()
    node_in = jnp.concatenate([node_ref[...], summed[...].astype(BF16)], axis=1)
    preact_n = dot(node_in, nw1_ref[...]) + nb1_ref[...]
    sig_n = sigmoid(preact_n)
    hidden_n = (preact_n * sig_n).astype(BF16)
    centred_n, inverse_n = norm_forward(dot(hidden_n, nw2_ref[...]) + nb2_ref[...])
    cot = ncot_ref[...].astype(F32)
    dout = norm_backward(cot * ngain_ref[...], centred_n * inverse_n, inverse_n)
    slope_n = sig_n * (1.0 + preact_n * (1.0 - sig_n))
    dpre = (dot(dout, nw2_ref[...], NT) * slope_n).astype(BF16)
    grads[: 2 * latent, :] = dot(node_in, dpre, TN)
    grads[2 * latent :, :] = dot(hidden_n, dout, TN)
    base_ref[...] = cot + dot(dpre, nw1_ref[:latent, :], NT)
    dsum_ref[...] = dot(dpre, nw1_ref[latent:, :], NT).astype(BF16)
    if fast:
        bit = lax.rem(here, 2)
        first = 2 * latent // tiles
        split_halves(bit, grads, 0, first, 0, first, gsend_ref, gkeep_ref, 0)
        second = latent // tiles
        split_halves(bit, grads, 2 * latent, second, 0, second, gsend_ref, gkeep_ref, first)
    else:
        gkeep_ref[...] = grads[: 2 * latent, :]
        gsend_ref[...] = grads[2 * latent :, :]


def slope_kernel(
    tiles, fast,
    cot_hbm, receiver_ref, dsum_ref, hidden_ref, slope_ref, normed_ref, inverse_ref, w2_ref, gain_ref,
    cot_ref, dpre_ref, gsend_ref, gkeep_ref,
    grads, dout, sems,
):
    here = lax.axis_index("tiles")
    edges, latent = cot_ref.shape
    nodes = dsum_ref.shape[0]
    copies = fetch(tile_pairs(cot_hbm, cot_ref, edges // 2), sems)
    steps = edges // TILE
    for copy in copies:
        copy.wait()

    def outer(step):
        tile = slice(step * TILE, (step + 1) * TILE)
        receivers = jnp.concatenate(
            pick_columns(index_columns(receiver_ref, step, TILE), 0, nodes), axis=1
        )
        grad_update = cot_ref[tile, :].astype(F32) + dot(receivers, dsum_ref[...])
        inverse = inverse_ref[tile, :1]
        dout[tile, :] = norm_backward(grad_update * gain_ref[...], normed_ref[tile, :], inverse)

    def inner(step):
        tile = slice(step * TILE, (step + 1) * TILE)
        dpre_ref[tile, :] = (
            dot(dout[tile, :], w2_ref[...], NT) * slope_ref[tile, :].astype(F32)
        ).astype(BF16)
        part = dot(hidden_ref[tile, :], dout[tile, :], TN)
        if step == 0:
            grads[...] = part
        else:
            grads[...] += part

    for step in range(steps + 1):
        if step < steps:
            outer(step)
        if step > 0:
            inner(step - 1)

    if fast:
        rows = latent // tiles
        split_halves(lax.rem(here, 2), grads, 0, rows, 0, rows, gsend_ref, gkeep_ref, 0)
    else:
        gkeep_ref[...] = grads[...]
        gsend_ref[...] = jnp.zeros_like(gsend_ref)


def first_kernel(
    tiles, places, fast,
    dpre_ref, edge_ref, sender_ref, receiver_ref, table_ref, node_ref, w1_ref, base_ref,
    *refs,
):
    out_refs, (grads, sums) = refs[:-2], refs[-2:]
    lower_ref, upper_ref, far_ref, partial_ref = out_refs[:4]
    here = lax.axis_index("tiles")
    edges, latent = dpre_ref.shape
    nodes = node_ref.shape[0]
    rows = table_ref.shape[0]

    for step in range(edges // TILE):
        tile = slice(step * TILE, (step + 1) * TILE)
        dpre = dpre_ref[tile, :]
        part = dot(edge_ref[tile, :], dpre, TN)
        picks = jnp.concatenate(
            [
                pick_rows(sender_ref, step, TILE, rows),
                pick_rows(receiver_ref, step, TILE, nodes),
            ],
            axis=0,
        )
        scattered = dot(picks, dpre)
        if step == 0:
            grads[:latent, :] = part
            sums[...] = scattered
        else:
            grads[:latent, :] += part
            sums[...] += scattered

    by_sender = sums[:rows, :].astype(BF16)
    by_receiver = sums[rows:, :].astype(BF16)
    grads[latent : 2 * latent, :] = dot(table_ref[...], by_sender, TN)
    grads[2 * latent :, :] = dot(node_ref[...], by_receiver, TN)
    back = dot(by_sender, w1_ref[latent : 2 * latent, :], NT)
    far = back[nodes + 2 * NEAR : nodes + 2 * NEAR + places * tiles, :].astype(BF16)
    far_ref[...] = far
    if fast:
        bit = lax.rem(here, 2)
        block = 3 * latent // tiles
        at = 0
        for send_ref, keep_ref in (out_refs[4:6], out_refs[6:8], out_refs[8:10]):
            part = keep_ref.shape[1]
            split_halves(bit, grads, 0, block, at, part, send_ref, keep_ref, 0)
            at += part
        out_refs[4][tiles // 2 * out_refs[5].shape[1] :, :] = slots_out(0, far, places)
    else:
        out_refs[4][...] = grads[...]
    lower_ref[...] = back[nodes : nodes + NEAR, :].astype(BF16)
    upper_ref[...] = back[nodes + NEAR : nodes + 2 * NEAR, :].astype(BF16)
    partial_ref[...] = (
        base_ref[...] + back[:nodes, :] + dot(by_receiver, w1_ref[2 * latent :, :], NT)
    )


def edge_kernel(dpre_ref, cot_ref, w1_ref, out_hbm, out_ref, sems):
    edges, latent = cot_ref.shape
    copies = []
    for step in range(edges // TILE):
        tile = pl.ds(step * TILE, TILE)
        out_ref[tile, :] = (
            cot_ref[tile, :].astype(F32) + dot(dpre_ref[tile, :], w1_ref[:latent, :], NT)
        ).astype(BF16)
        copy = pltpu.make_async_copy(out_ref.at[tile], out_hbm.at[tile], sems.at[step])
        copy.start()
        copies.append(copy)
    for copy in copies:
        copy.wait()


def node_kernel(fast, index_ref, partial_ref, below_ref, above_ref, slots_ref, *refs):
    out_ref = refs[-1]
    places, tiles = index_ref.shape[1], index_ref.shape[2]
    nodes = partial_ref.shape[0]
    origin = lax.axis_index("tiles") if fast else 0
    slots = slots_ref[...]
    if fast:
        got_ref = refs[0]
        slots = slots_in(3, slots, got_ref[got_ref.shape[0] - slots.shape[0] // 2 :, :], places)
    place = lax.broadcasted_iota(jnp.int32, (nodes, tiles), 0)
    owner, at = slot_owner(origin, (tiles, places * tiles), 1, places)
    row = lax.broadcasted_iota(jnp.int32, (tiles, places * tiles), 0)
    total = partial_ref[...]
    for j in range(places):
        picks = ones_where(place == index_ref[0, j : j + 1, :])
        far = dot(ones_where((owner == row) & (at == j)), slots).astype(BF16)
        total = total + dot(picks, far)
    out_ref[:NEAR, :] = (total[:NEAR, :] + below_ref[...].astype(F32)).astype(BF16)
    out_ref[NEAR : nodes - NEAR, :] = total[NEAR : nodes - NEAR, :].astype(BF16)
    out_ref[nodes - NEAR :, :] = (
        total[nodes - NEAR :, :] + above_ref[...].astype(F32)
    ).astype(BF16)


def halve_kernel(shift, count, places, *refs):
    keeps, gots = refs[:count], refs[count : 2 * count]
    rest = refs[2 * count :]
    send_ref, kept_ref = rest[-2:] if not places else rest[-3:-1]
    size = kept_ref.shape[1]
    bit = lax.rem(lax.div(lax.axis_index("tiles"), 2**shift), 2)
    at = 0
    for keep_ref, got_ref in zip(keeps, gots):
        blocks, rows = keep_ref.shape[:2]
        for q in range(blocks // 2):
            there, here = 2 * q + 1 - bit, 2 * q + bit
            got_there = got_ref[pl.ds(pl.multiple_of(there * rows, 32), rows), :].astype(F32)
            got_here = got_ref[pl.ds(pl.multiple_of(here * rows, 32), rows), :].astype(F32)
            to = q * size + at
            send_ref[to : to + rows, :] = (keep_ref[there] + got_there).astype(BF16)
            kept_ref[q, at : at + rows, :] = keep_ref[here] + got_here
        at += rows
    if places:
        slots_ref, moved_ref = rest[0], rest[-1]
        half = slots_ref.shape[0] // 2
        got_ref = gots[0]
        slots = slots_in(shift - 1, slots_ref[...], got_ref[got_ref.shape[0] - half :, :], places)
        moved_ref[...] = slots
        send_ref[send_ref.shape[0] - half :, :] = slots_out(shift, slots, places)


def finish_kernel(count, splits, *refs):
    out_refs = refs[2 * count :]
    rows = [0] * len(out_refs)
    for keep_ref, got_ref, parts in zip(refs[:count], refs[count : 2 * count], splits):
        at = 0
        for which, size in parts:
            first = rows[which]
            out_refs[which][first : first + size, :] = (
                keep_ref[0, at : at + size, :] + got_ref[at : at + size, :].astype(F32)
            )
            at += size
            rows[which] += size


def shaped(shape, dtype):
    return jax.ShapeDtypeStruct(shape, dtype)


def in_hbm(*arrays):
    return [pltpu.with_memory_space_constraint(array, pltpu.HBM) for array in arrays]


def call(kernel, name, out_shape, args, hbm=0, scratch=(), out_specs=None, flops=0):
    vmem = pl.BlockSpec(memory_space=pltpu.VMEM)
    return pl.pallas_call(
        kernel,
        in_specs=[pl.BlockSpec(memory_space=pltpu.HBM)] * hbm + [vmem] * (len(args) - hbm),
        out_specs=out_specs or [vmem] * len(out_shape),
        out_shape=out_shape,
        scratch_shapes=scratch,
        compiler_params=pltpu.CompilerParams(vmem_limit_bytes=16 * MIB),
        cost_estimate=pl.CostEstimate(flops=flops, bytes_accessed=flops // 100, transcendentals=0),
        name=name,
    )(*in_hbm(*args[:hbm]), *args[hbm:])


def swap(tiles, bit, send):
    return lax.ppermute(send, "tiles", [(i, i ^ bit) for i in range(tiles)])


def halve(shift, keeps, gots, slots=None, places=0, flops=0):
    half, _, width = keeps[0].shape
    rows = sum(keep.shape[1] for keep in keeps)
    extra = [] if slots is None else [slots]
    sent = half // 2 * rows + sum(slots.shape[0] // 2 for slots in extra)
    return call(
        functools.partial(halve_kernel, shift, len(keeps), places),
        "halve",
        [pltpu.VMEM((sent, width), BF16), pltpu.VMEM((half // 2, rows, width), F32)]
        + [pltpu.VMEM(slots.shape, BF16) for slots in extra],
        [*keeps, *gots, *extra],
        flops=flops,
    )


def finish(keeps, gots, splits, sizes):
    return call(
        functools.partial(finish_kernel, len(keeps), splits),
        "finish",
        [shaped((size, keeps[0].shape[-1]), F32) for size in sizes],
        [*keeps, *gots],
    )


def after(value, *others):
    return lax.optimization_barrier((value, *others))[0]


def shards(
    node_latent, edge_latent, node_cot, edge_cot,
    edge_w1, edge_b1, edge_w2, edge_b2, edge_gain,
    node_w1, node_b1, node_w2, node_b2, node_gain,
    send_index, edge_sender, edge_receiver, edge_count,
):
    tiles = lax.axis_size("tiles")
    nodes, latent = node_latent.shape
    edges = edge_latent.shape[0]
    places = send_index.shape[2]
    steps = edges // TILE
    used = nodes + 2 * NEAR + places * tiles
    rows = -(-used // LANES) * LANES
    fast = tiles == 16
    half = tiles // 2
    upward = [(i, i + 1) for i in range(tiles - 1)]
    downward = [(i + 1, i) for i in range(tiles - 1)]
    sender = edge_sender.reshape(edges // LANES, LANES)
    receiver = edge_receiver.reshape(edges // LANES, LANES)
    listed = jnp.swapaxes(send_index, 1, 2)
    row = lambda vector: vector.reshape(1, -1)
    vmem = pltpu.VMEM

    if fast:
        grad_shapes = lambda count: [
            vmem((count // 2, latent), BF16),
            vmem((half, count // tiles, latent), F32),
        ]
    else:
        grad_shapes = lambda count: [shaped((latent, latent), F32), shaped((count, latent), F32)]

    outgoing, head, tail = call(
        outgoing_kernel,
        "outgoing",
        [
            shaped((tiles, places, latent), BF16),
            vmem((NEAR, latent), BF16),
            vmem((NEAR, latent), BF16),
        ],
        [listed, node_latent],
        hbm=2,
        scratch=[vmem(listed.shape, jnp.int32), vmem((nodes, latent), BF16), pltpu.SemaphoreType.DMA((2,))],
    )
    lower = lax.ppermute(tail, "tiles", upward)
    upper = lax.ppermute(head, "tiles", downward)
    slots = lax.all_to_all(outgoing, "tiles", split_axis=0, concat_axis=0, tiled=True)
    edge_kept, w1_kept, node_kept, receiver_kept, moved, preact = call(
        functools.partial(prepare_kernel, places, fast),
        "prepare",
        [
            vmem((edges, latent), BF16), vmem(edge_w1.shape, BF16), vmem((nodes, latent), BF16),
            vmem(receiver.shape, jnp.int32), vmem(sender.shape, jnp.int32),
            vmem((edges, latent), F32),
        ],
        [node_latent, edge_w1, after(sender, outgoing), receiver, row(edge_b1), edge_latent],
        hbm=6,
        scratch=[
            vmem((latent + 2 * nodes, latent), BF16), vmem(sender.shape, jnp.int32),
            vmem((1, latent), F32), pltpu.SemaphoreType.DMA((5,)), pltpu.SemaphoreType.DMA((2,)),
        ],
        flops=AHEAD,
    )

    (
        w2_kept, gain_kept,
        hidden, slope, normed, inverse, table, dsum, base, node_send, node_keep,
    ) = call(
        functools.partial(forward_kernel, tiles, places, fast),
        "forward",
        [
            vmem(edge_w2.shape, BF16), vmem((1, latent), F32),
            vmem((edges, latent), BF16), vmem((edges, latent), BF16), vmem((edges, latent), F32),
            vmem((edges, LANES), F32), vmem((rows, latent), BF16),
            vmem((nodes, latent), BF16), vmem((nodes, latent), F32),
        ] + grad_shapes(3 * latent if fast else 2 * latent),
        [
            edge_w2, node_w1, node_w2, node_cot,
            row(edge_b2), row(edge_gain), row(node_b1), row(node_b2), row(node_gain), edge_count,
            lower, upper, slots, preact, w1_kept, node_kept, receiver_kept, moved,
        ],
        hbm=10,
        scratch=[
            vmem((rows - nodes, latent), BF16), vmem((nodes, latent), F32),
            vmem((3 * latent, latent), F32), vmem(node_w1.shape, BF16), vmem(node_w2.shape, BF16),
            vmem((nodes, latent), BF16),
        ] + [vmem((1, latent), F32)] * 4 + [
            pltpu.SMEM(edge_count.shape, jnp.int32), pltpu.SemaphoreType.DMA((10,)),
        ],
    )

    if fast:
        send, chain = halve(1, [node_keep], [swap(tiles, 1, node_send)])
        dsum = after(dsum, send)
        got = swap(tiles, 2, send)
    cot_kept, dpre, second_send, second_keep = call(
        functools.partial(slope_kernel, tiles, fast),
        "slope",
        [vmem((edges, latent), BF16), vmem((edges, latent), BF16)] + grad_shapes(latent),
        [edge_cot, receiver_kept, dsum, hidden, slope, normed, inverse, w2_kept, gain_kept],
        hbm=1,
        scratch=[
            vmem((latent, latent), F32), vmem((edges, latent), BF16), pltpu.SemaphoreType.DMA((2,)),
        ],
    )
    if fast:
        got_second = swap(tiles, 1, second_send)

    per = latent // tiles
    to_lower, to_upper, to_far, partial, *first = call(
        functools.partial(first_kernel, tiles, places, fast),
        "first",
        [
            vmem((NEAR, latent), BF16),
            vmem((NEAR, latent), BF16),
            vmem((tiles * places, latent), BF16) if fast else shaped((tiles * places, latent), BF16),
            vmem((nodes, latent), F32),
        ] + (
            [
                vmem((half * per + tiles * places // 2, latent), BF16),
                vmem((half, per, latent), F32),
                vmem((half * per, latent), BF16), vmem((half, per, latent), F32),
                vmem((half * per, latent), BF16), vmem((half, per, latent), F32),
            ]
            if fast else [shaped((3 * latent, latent), F32)]
        ),
        [dpre, edge_kept, moved, receiver_kept, table, node_kept, w1_kept, base],
        scratch=[vmem((3 * latent, latent), F32), vmem((rows + nodes, latent), F32)],
    )

    (grad_edge,) = call(
        edge_kernel,
        "edge",
        [shaped((edges, latent), BF16)],
        [after(dpre, partial), cot_kept, w1_kept],
        out_specs=[pl.BlockSpec(memory_space=pltpu.HBM)],
        scratch=[vmem((edges, latent), BF16), pltpu.SemaphoreType.DMA((steps,))],
    )

    if fast:
        send_a, keep_a, send_more, keep_more, send_b, keep_b = first
        send, chain = halve(2, [after(chain, grad_edge)], [got])
        got = swap(tiles, 4, send)
        send_a, chain_a, slots = halve(
            1,
            [after(keep_a, send), keep_more],
            [swap(tiles, 1, send_a), swap(tiles, 1, send_more)],
            to_far,
            places,
     )
        got_a = swap(tiles, 2, send_a)
        send_b, chain_b = halve(
            1, [after(keep_b, send_a), second_keep], [swap(tiles, 1, send_b), got_second]
     )
        got_b = swap(tiles, 2, send_b)

        to_lower, to_upper = lax.optimization_barrier((to_lower, to_upper, send_b))[:2]
        above = lax.ppermute(to_lower, "tiles", downward)
        below = lax.ppermute(to_upper, "tiles", upward)
        send, chain = halve(3, [after(chain, above, below)], [got])
        got = swap(tiles, 8, send)
        send_a, chain_a, slots = halve(2, [after(chain_a, send)], [got_a], slots, places)
        got_a = swap(tiles, 4, send_a)
        send_b, chain_b = halve(2, [after(chain_b, send_a)], [got_b], flops=AHEAD)
        got_b = swap(tiles, 4, send_b)
        chain_a = lax.optimization_barrier((chain_a, send_b, got))[0]
        send_a, chain_a, slots = halve(3, [chain_a], [got_a], slots, places, AHEAD)
        got_a = swap(tiles, 8, send_a)
        chain_b = after(chain_b, send_a)
        send_b, chain_b = halve(3, [chain_b], [got_b], flops=AHEAD)
        got_b = swap(tiles, 8, send_b)
        returned = [slots, got_a]
        grad_edge_w1, grad_edge_w2, grad_node_w1, grad_node_w2 = finish(
            [chain, chain_a, chain_b],
            [got, got_a, got_b],
            [[(2, 2 * per), (3, per)], [(0, 2 * per)], [(0, per), (1, per)]],
            [3 * per, per, 2 * per, per],
        )
    else:
        above = lax.ppermute(to_lower, "tiles", downward)
        below = lax.ppermute(to_upper, "tiles", upward)
        returned = [lax.all_to_all(to_far, "tiles", split_axis=0, concat_axis=0, tiled=True)]
        scatter = functools.partial(
            lax.psum_scatter, axis_name="tiles", scatter_dimension=0, tiled=True
        )
        grad_node_w1, grad_node_w2 = scatter(node_keep), scatter(node_send)
        grad_edge_w1, grad_edge_w2 = scatter(first[0]), scatter(second_keep)
    (grad_node,) = call(
        functools.partial(node_kernel, fast),
        "node",
        [shaped((nodes, latent), BF16)],
        [listed, partial, below, above, *returned],
    )
    return (grad_node, grad_edge, grad_edge_w1, grad_edge_w2, grad_node_w1, grad_node_w2)


def solution(mesh):
    split = P(("groups", "tiles"), None)
    return jax.shard_map(
        shards,
        mesh=mesh,
        in_specs=(split,) * 4
        + (P(),) * 10
        + (
            P(("groups", "tiles"), None, None),
            P(("groups", "tiles")),
            P(("groups", "tiles")),
            P("groups"),
        ),
        out_specs=(split,) * 6,
        check_vma=False,
    )
```

```python
import functools

import jax
import jax.numpy as jnp
from jax import lax
from jax.experimental import pallas as pl
from jax.experimental.pallas import tpu as pltpu
from jax.sharding import PartitionSpec as P

NEAR = 64
EPSILON = 1e-05
TILE = 256
LANES = 128
F32 = jnp.float32
BF16 = jnp.bfloat16
MIB = 1024 * 1024
AHEAD = 10**10

NN = (((1,), (0,)), ((), ()))
NT = (((1,), (1,)), ((), ()))
TN = (((0,), (0,)), ((), ()))


def dot(a, b, dims=NN):
    return lax.dot_general(a, b, dims, preferred_element_type=F32)


def sigmoid(x):
    return 0.5 * jnp.tanh(0.5 * x) + 0.5


def row_mean(x):
    return jnp.sum(x, axis=-1, keepdims=True) * (1.0 / x.shape[-1])


def ones_where(mask):
    return jnp.where(mask, 1.0, 0.0).astype(BF16)


def index_columns(idx_ref, step, tile):
    per = tile // LANES
    parts = []
    for j in range(per):
        row = idx_ref[pl.ds(step * per + j, 1), :]
        parts.append(jnp.transpose(jnp.broadcast_to(row, (LANES, LANES))))
    return jnp.concatenate(parts, axis=0)


def pick_columns(columns, start, stop):
    lane = lax.broadcasted_iota(jnp.int32, columns.shape, 1)
    return [ones_where(columns == lane + at) for at in range(start, stop, LANES)]


def pick_rows(idx_ref, step, tile, width):
    per = tile // LANES
    row = jnp.concatenate([idx_ref[pl.ds(step * per + j, 1), :] for j in range(per)], axis=1)
    return ones_where(lax.broadcasted_iota(jnp.int32, (width, tile), 0) == row)


def norm_forward(out):
    centred = out - row_mean(out)
    inverse = lax.rsqrt(row_mean(centred * centred) + EPSILON)
    return centred, inverse


def norm_backward(scaled, normed, inverse):
    return (
        inverse * (scaled - row_mean(scaled) - normed * row_mean(scaled * normed))
    ).astype(BF16)


def split_halves(bit, total_ref, at, block, first, rows, send_ref, keep_ref, offset):
    half, size = keep_ref.shape[:2]
    for q in range(half):
        there = pl.multiple_of(at + first + (2 * q + 1 - bit) * block, 32)
        here = pl.multiple_of(at + first + (2 * q + bit) * block, 32)
        to = q * size + offset
        send_ref[to : to + rows, :] = total_ref[pl.ds(there, rows), :].astype(BF16)
        keep_ref[q, offset : offset + rows, :] = total_ref[pl.ds(here, rows), :]


def fetch(pairs, sems):
    copies = []
    for at, (source, target) in enumerate(pairs):
        copies.append(pltpu.make_async_copy(source, target, sems.at[at]))
    for copy in copies:
        copy.start()
    return copies


def tile_pairs(source, target, tile):
    return [
        (source.at[pl.ds(at, tile)], target.at[pl.ds(at, tile)])
        for at in range(0, source.shape[0], tile)
    ]


def slot_owner(origin, shape, dim, places):
    row = lax.broadcasted_iota(jnp.int32, shape, dim)
    return lax.div(row, places) ^ origin, lax.rem(row, places)


def bit_slots(bit, shape, places):
    row = lax.broadcasted_iota(jnp.int32, shape, 0)
    column = lax.broadcasted_iota(jnp.int32, shape, 1)
    slot, place = lax.div(column, places), lax.rem(column, places)
    rank = ((slot >> (bit + 1)) << bit) | (slot & (2**bit - 1))
    return ((slot >> bit) & 1 == 1) & (rank * places + place == row)


def slots_out(bit, slots, places):
    rows = slots.shape[0]
    return dot(ones_where(bit_slots(bit, (rows // 2, rows), places)), slots).astype(BF16)


def slots_in(bit, slots, got, places):
    rows = slots.shape[0]
    row = lax.broadcasted_iota(jnp.int32, (rows, rows), 0)
    column = lax.broadcasted_iota(jnp.int32, (rows, rows), 1)
    kept = (row == column) & ((lax.div(column, places) >> bit) & 1 == 0)
    moved = ones_where(bit_slots(bit, (rows // 2, rows), places))
    return (dot(ones_where(kept), slots) + dot(moved, got, TN)).astype(BF16)


def outgoing_kernel(
    index_hbm, node_hbm, slots_ref, inner_ref, outer_ref, index_ref, node_ref, sems
):
    for copy in fetch([(index_hbm, index_ref), (node_hbm, node_ref)], sems):
        copy.wait()
    places, tiles = index_ref.shape[1], index_ref.shape[2]
    nodes, latent = node_ref.shape
    place = lax.broadcasted_iota(jnp.int32, (nodes, tiles), 0)
    for j in range(places):
        picks = ones_where(place == index_ref[0, j : j + 1, :])
        slots_ref[:, j, :] = dot(picks, node_ref[...], TN).astype(BF16)
    odd = lax.rem(lax.axis_index("tiles"), 2)
    inner_ref[...] = node_ref[pl.ds(pl.multiple_of((1 - odd) * (nodes - NEAR), NEAR), NEAR), :]
    outer_ref[...] = node_ref[pl.ds(pl.multiple_of(odd * (nodes - NEAR), NEAR), NEAR), :]


def table_index(raw, tiles, places, nodes):
    far = raw - (nodes + 2 * NEAR)
    far = nodes + 2 * NEAR + lax.rem(far, places) * tiles + lax.div(far, places)
    rim = jnp.where(raw < NEAR, raw + nodes, raw)
    own = jnp.where((raw >= NEAR) & (raw < NEAR + nodes), raw - NEAR, rim)
    return jnp.where(raw >= nodes + 2 * NEAR, far, own)


def prepare_kernel(
    tiles, places,
    node_hbm, w1_hbm, sender_hbm, receiver_hbm, b1_hbm, edge_hbm,
    node_ref, receiver_ref, moved_ref, partial_ref,
    edge_ref, w1_ref, weights, sender_ref, b1_ref, sems, edge_sems,
):
    edges, latent = edge_ref.shape
    nodes = node_ref.shape[0]
    copies = fetch(
        [
            (node_hbm, node_ref), (w1_hbm, w1_ref), (sender_hbm, sender_ref),
            (receiver_hbm, receiver_ref), (b1_hbm, b1_ref),
        ],
        sems,
    )
    edge_copies = fetch(tile_pairs(edge_hbm, edge_ref, edges // 2), edge_sems)
    for copy in copies:
        copy.wait()
    moved_ref[...] = table_index(sender_ref[...], tiles, places, nodes)
    weights[:latent, :] = w1_ref[:latent, :]
    weights[latent : latent + nodes, :] = dot(
        node_ref[...], w1_ref[latent : 2 * latent, :]
    ).astype(BF16)
    weights[latent + nodes :, :] = dot(node_ref[...], w1_ref[2 * latent :, :]).astype(BF16)
    for copy in edge_copies:
        copy.wait()
    for step in range(edges // TILE):
        tile = slice(step * TILE, (step + 1) * TILE)
        senders = pick_columns(index_columns(moved_ref, step, TILE), 0, nodes)
        receivers = pick_columns(index_columns(receiver_ref, step, TILE), 0, nodes)
        inputs = jnp.concatenate([edge_ref[tile, :]] + senders + receivers, axis=1)
        partial_ref[tile, :] = dot(inputs, weights[...]) + b1_ref[...]


def forward_kernel(
    tiles, places, fast,
    w1_hbm, edge_hbm, w2_hbm, nw1_hbm, nw2_hbm, ncot_hbm,
    b2_hbm, gain_hbm, nb1_hbm, nb2_hbm, ngain_hbm, count_hbm,
    inner_ref, outer_ref, far_ref, known_ref, node_ref, receiver_ref, moved_ref,
    w1_ref, edge_ref, w2_ref, gain_ref,
    hidden_ref, slope_ref, normed_ref, inverse_ref, table_ref, dsum_ref, base_ref,
    gsend_ref, gkeep_ref,
    weights, summed, grads, nw1_ref, nw2_ref, ncot_ref,
    b2_ref, nb1_ref, nb2_ref, ngain_ref, count_ref, sems,
):
    here = lax.axis_index("tiles")
    edges, latent = hidden_ref.shape
    nodes = node_ref.shape[0]
    rows = table_ref.shape[0]
    steps = edges // TILE

    early = fetch(
        [
            (w1_hbm, w1_ref), (count_hbm, count_ref), (b2_hbm, b2_ref), (gain_hbm, gain_ref),
            (w2_hbm, w2_ref),
        ],
        sems,
    )
    late = fetch(
        [
            (nw1_hbm, nw1_ref), (nw2_hbm, nw2_ref), (ncot_hbm, ncot_ref),
            (nb1_hbm, nb1_ref), (nb2_hbm, nb2_ref), (ngain_hbm, ngain_ref), (edge_hbm, edge_ref),
        ],
        sems.at[pl.ds(len(early), 7)],
    )

    table_ref[:nodes, :] = node_ref[...]
    odd = lax.rem(here, 2)
    table_ref[pl.ds(pl.multiple_of(nodes + (1 - odd) * NEAR, NEAR), NEAR), :] = inner_ref[...]
    table_ref[pl.ds(pl.multiple_of(nodes + odd * NEAR, NEAR), NEAR), :] = outer_ref[...]
    for j in range(places):
        at = nodes + 2 * NEAR + j * tiles
        table_ref[at : at + tiles, :] = far_ref[:, j, :]
    used = nodes + 2 * NEAR + places * tiles
    if used < rows:
        table_ref[used:, :] = jnp.zeros((rows - used, latent), BF16)
    for copy in early:
        copy.wait()
    weights[...] = dot(table_ref[nodes:, :], w1_ref[latent : 2 * latent, :]).astype(BF16)
    live = count_ref[here]

    def activate(step):
        tile = slice(step * TILE, (step + 1) * TILE)
        senders = pick_columns(index_columns(moved_ref, step, TILE), nodes, rows)
        preact = known_ref[tile, :] + dot(jnp.concatenate(senders, axis=1), weights[...])
        sig = sigmoid(preact)
        slope_ref[tile, :] = (sig * (1.0 + preact * (1.0 - sig))).astype(BF16)
        hidden_ref[tile, :] = (preact * sig).astype(BF16)

    def normalize(step):
        tile = slice(step * TILE, (step + 1) * TILE)
        centred, inverse = norm_forward(dot(hidden_ref[tile, :], w2_ref[...]) + b2_ref[...])
        position = step * TILE + lax.broadcasted_iota(jnp.int32, inverse.shape, 0)
        inverse = jnp.where(position < live, inverse, 0.0)
        normed = centred * inverse
        normed_ref[tile, :] = normed
        inverse_ref[tile, :] = jnp.broadcast_to(inverse, (TILE, LANES))
        update = (normed * gain_ref[...]).astype(BF16)
        part = dot(pick_rows(receiver_ref, step, TILE, nodes), update)
        if step == 0:
            summed[...] = part
        else:
            summed[...] += part

    for step in range(steps + 1):
        if step < steps:
            activate(step)
        if step > 0:
            normalize(step - 1)

    for copy in late:
        copy.wait()
    node_in = jnp.concatenate([node_ref[...], summed[...].astype(BF16)], axis=1)
    preact_n = dot(node_in, nw1_ref[...]) + nb1_ref[...]
    sig_n = sigmoid(preact_n)
    hidden_n = (preact_n * sig_n).astype(BF16)
    centred_n, inverse_n = norm_forward(dot(hidden_n, nw2_ref[...]) + nb2_ref[...])
    cot = ncot_ref[...].astype(F32)
    dout = norm_backward(cot * ngain_ref[...], centred_n * inverse_n, inverse_n)
    slope_n = sig_n * (1.0 + preact_n * (1.0 - sig_n))
    dpre = (dot(dout, nw2_ref[...], NT) * slope_n).astype(BF16)
    grads[: 2 * latent, :] = dot(node_in, dpre, TN)
    grads[2 * latent :, :] = dot(hidden_n, dout, TN)
    base_ref[...] = cot + dot(dpre, nw1_ref[:latent, :], NT)
    dsum_ref[...] = dot(dpre, nw1_ref[latent:, :], NT).astype(BF16)
    if fast:
        bit = lax.rem(here, 2)
        first = 2 * latent // tiles
        split_halves(bit, grads, 0, first, 0, first, gsend_ref, gkeep_ref, 0)
        second = latent // tiles
        split_halves(bit, grads, 2 * latent, second, 0, second, gsend_ref, gkeep_ref, first)
    else:
        gkeep_ref[...] = grads[: 2 * latent, :]
        gsend_ref[...] = grads[2 * latent :, :]


def slope_kernel(
    tiles, fast, start, last,
    cot_hbm, receiver_ref, dsum_ref, hidden_ref, slope_ref, normed_ref, inverse_ref, w2_ref, gain_ref,
    *refs,
):
    cot_ref, dpre_ref, *out_refs, grads, dout, sem = refs[0 if start == 0 else 1 :]
    here = lax.axis_index("tiles")
    edges, latent = cot_ref.shape
    nodes = dsum_ref.shape[0]
    copy = pltpu.make_async_copy(cot_hbm.at[pl.ds(start, edges)], cot_ref, sem)
    copy.start()
    steps = edges // TILE
    grads[...] = jnp.zeros_like(grads) if start == 0 else refs[0][...]
    copy.wait()

    def outer(step):
        tile = slice(step * TILE, (step + 1) * TILE)
        whole = slice(start + step * TILE, start + (step + 1) * TILE)
        receivers = jnp.concatenate(
            pick_columns(index_columns(receiver_ref, start // TILE + step, TILE), 0, nodes), axis=1
        )
        grad_update = cot_ref[tile, :].astype(F32) + dot(receivers, dsum_ref[...])
        inverse = inverse_ref[whole, :1]
        dout[tile, :] = norm_backward(grad_update * gain_ref[...], normed_ref[whole, :], inverse)

    def inner(step):
        tile = slice(step * TILE, (step + 1) * TILE)
        whole = slice(start + step * TILE, start + (step + 1) * TILE)
        dpre_ref[tile, :] = (
            dot(dout[tile, :], w2_ref[...], NT) * slope_ref[whole, :].astype(F32)
        ).astype(BF16)
        grads[...] += dot(hidden_ref[whole, :], dout[tile, :], TN)

    for step in range(steps + 1):
        if step < steps:
            outer(step)
        if step > 0:
            inner(step - 1)

    if not last:
        out_refs[0][...] = grads[...]
    elif fast:
        rows = latent // tiles
        split_halves(lax.rem(here, 2), grads, 0, rows, 0, rows, *out_refs, 0)
    else:
        out_refs[0][...] = jnp.zeros_like(out_refs[0])
        out_refs[1][...] = grads[...]


def first_kernel(
    tiles, places, fast,
    dpre_a_ref, dpre_b_ref, edge_ref, sender_ref, receiver_ref, table_ref, node_ref, w1_ref, base_ref,
    *refs,
):
    out_refs, (grads, sums, rims) = refs[:-3], refs[-3:]
    inner_ref, outer_ref, far_ref, partial_ref = out_refs[:4]
    here = lax.axis_index("tiles")
    edges, latent = edge_ref.shape
    early = dpre_a_ref.shape[0]
    nodes = node_ref.shape[0]
    rows = table_ref.shape[0]

    for step in range(edges // TILE):
        tile = slice(step * TILE, (step + 1) * TILE)
        if step * TILE < early:
            dpre = dpre_a_ref[tile, :]
        else:
            dpre = dpre_b_ref[step * TILE - early : (step + 1) * TILE - early, :]
        part = dot(edge_ref[tile, :], dpre, TN)
        picks = jnp.concatenate(
            [
                pick_rows(sender_ref, step, TILE, rows),
                pick_rows(receiver_ref, step, TILE, nodes),
            ],
            axis=0,
        )
        scattered = dot(picks, dpre)
        if step == 0:
            grads[:latent, :] = part
            sums[...] = scattered
        else:
            grads[:latent, :] += part
            sums[...] += scattered

    by_sender = sums[:rows, :].astype(BF16)
    by_receiver = sums[rows:, :].astype(BF16)
    grads[latent : 2 * latent, :] = dot(table_ref[...], by_sender, TN)
    grads[2 * latent :, :] = dot(node_ref[...], by_receiver, TN)
    back = dot(by_sender, w1_ref[latent : 2 * latent, :], NT)
    far = back[nodes + 2 * NEAR : nodes + 2 * NEAR + places * tiles, :].astype(BF16)
    owner, at = slot_owner(here if fast else 0, (places * tiles, places * tiles), 0, places)
    column = lax.broadcasted_iota(jnp.int32, (places * tiles, places * tiles), 1)
    far = dot(ones_where(at * tiles + owner == column), far).astype(BF16)
    far_ref[...] = far
    if fast:
        bit = lax.rem(here, 2)
        block = 3 * latent // tiles
        at = 0
        for send_ref, keep_ref in (out_refs[4:6], out_refs[6:8], out_refs[8:10]):
            part = keep_ref.shape[1]
            split_halves(bit, grads, 0, block, at, part, send_ref, keep_ref, 0)
            at += part
        out_refs[4][tiles // 2 * out_refs[5].shape[1] :, :] = slots_out(0, far, places)
    else:
        out_refs[4][...] = grads[...]
    rims[...] = back[nodes : nodes + 2 * NEAR, :]
    odd = lax.rem(here, 2)
    inner_ref[...] = rims[pl.ds(pl.multiple_of((1 - odd) * NEAR, NEAR), NEAR), :].astype(BF16)
    outer_ref[...] = rims[pl.ds(pl.multiple_of(odd * NEAR, NEAR), NEAR), :].astype(BF16)
    partial_ref[...] = (
        base_ref[...] + back[:nodes, :] + dot(by_receiver, w1_ref[2 * latent :, :], NT)
    )


def edge_kernel(dpre_a_ref, dpre_b_ref, cot_a_ref, cot_b_ref, w1_ref, out_hbm, out_ref, sems):
    early, latent = cot_a_ref.shape
    copies = []
    for dpre_ref, cot_ref, base in ((dpre_a_ref, cot_a_ref, 0), (dpre_b_ref, cot_b_ref, early)):
        for at in range(0, early, TILE):
            part = slice(at, at + TILE)
            tile = pl.ds(base + at, TILE)
            out_ref[tile, :] = (
                cot_ref[part, :].astype(F32) + dot(dpre_ref[part, :], w1_ref[:latent, :], NT)
            ).astype(BF16)
            copy = pltpu.make_async_copy(
                out_ref.at[tile], out_hbm.at[tile], sems.at[(base + at) // TILE]
            )
            copy.start()
            copies.append(copy)
    for copy in copies:
        copy.wait()


def node_kernel(fast, index_ref, partial_ref, inner_ref, outer_ref, slots_ref, *refs):
    out_ref, sums = refs[-2:]
    places, tiles = index_ref.shape[1], index_ref.shape[2]
    nodes = partial_ref.shape[0]
    origin = lax.axis_index("tiles") if fast else 0
    slots = slots_ref[...]
    if fast:
        got_ref = refs[0]
        slots = slots_in(3, slots, got_ref[got_ref.shape[0] - slots.shape[0] // 2 :, :], places)
    place = lax.broadcasted_iota(jnp.int32, (nodes, tiles), 0)
    owner, at = slot_owner(origin, (tiles, places * tiles), 1, places)
    row = lax.broadcasted_iota(jnp.int32, (tiles, places * tiles), 0)
    total = partial_ref[...]
    for j in range(places):
        picks = ones_where(place == index_ref[0, j : j + 1, :])
        far = dot(ones_where((owner == row) & (at == j)), slots).astype(BF16)
        total = total + dot(picks, far)
    sums[...] = total
    odd = lax.rem(lax.axis_index("tiles"), 2)
    inner_at = pl.ds(pl.multiple_of((1 - odd) * (nodes - NEAR), NEAR), NEAR)
    outer_at = pl.ds(pl.multiple_of(odd * (nodes - NEAR), NEAR), NEAR)
    sums[inner_at, :] += inner_ref[...].astype(F32)
    sums[outer_at, :] += outer_ref[...].astype(F32)
    out_ref[...] = sums[...].astype(BF16)


def halve_kernel(shift, count, places, *refs):
    keeps, gots = refs[:count], refs[count : 2 * count]
    rest = refs[2 * count :]
    send_ref, kept_ref = rest[-2:] if not places else rest[-3:-1]
    size = kept_ref.shape[1]
    bit = lax.rem(lax.div(lax.axis_index("tiles"), 2**shift), 2)
    at = 0
    for keep_ref, got_ref in zip(keeps, gots):
        blocks, rows = keep_ref.shape[:2]
        for q in range(blocks // 2):
            there, here = 2 * q + 1 - bit, 2 * q + bit
            got_there = got_ref[pl.ds(pl.multiple_of(there * rows, 32), rows), :].astype(F32)
            got_here = got_ref[pl.ds(pl.multiple_of(here * rows, 32), rows), :].astype(F32)
            to = q * size + at
            send_ref[to : to + rows, :] = (keep_ref[there] + got_there).astype(BF16)
            kept_ref[q, at : at + rows, :] = keep_ref[here] + got_here
        at += rows
    if places:
        slots_ref, moved_ref = rest[0], rest[-1]
        half = slots_ref.shape[0] // 2
        got_ref = gots[0]
        slots = slots_in(shift - 1, slots_ref[...], got_ref[got_ref.shape[0] - half :, :], places)
        moved_ref[...] = slots
        send_ref[send_ref.shape[0] - half :, :] = slots_out(shift, slots, places)


def finish_kernel(count, splits, *refs):
    out_refs = refs[2 * count :]
    rows = [0] * len(out_refs)
    for keep_ref, got_ref, parts in zip(refs[:count], refs[count : 2 * count], splits):
        at = 0
        for which, size in parts:
            first = rows[which]
            out_refs[which][first : first + size, :] = (
                keep_ref[0, at : at + size, :] + got_ref[at : at + size, :].astype(F32)
            )
            at += size
            rows[which] += size


def shaped(shape, dtype):
    return jax.ShapeDtypeStruct(shape, dtype)


def in_hbm(*arrays):
    return [pltpu.with_memory_space_constraint(array, pltpu.HBM) for array in arrays]


def call(kernel, name, out_shape, args, hbm=0, scratch=(), out_specs=None, flops=0):
    vmem = pl.BlockSpec(memory_space=pltpu.VMEM)
    return pl.pallas_call(
        kernel,
        in_specs=[pl.BlockSpec(memory_space=pltpu.HBM)] * hbm + [vmem] * (len(args) - hbm),
        out_specs=out_specs or [vmem] * len(out_shape),
        out_shape=out_shape,
        scratch_shapes=scratch,
        compiler_params=pltpu.CompilerParams(vmem_limit_bytes=16 * MIB),
        cost_estimate=pl.CostEstimate(flops=flops, bytes_accessed=flops // 100, transcendentals=0),
        name=name,
    )(*in_hbm(*args[:hbm]), *args[hbm:])


def swap(tiles, bit, send):
    return lax.ppermute(send, "tiles", [(i, i ^ bit) for i in range(tiles)])


def halve(shift, keeps, gots, slots=None, places=0, flops=0):
    half, _, width = keeps[0].shape
    rows = sum(keep.shape[1] for keep in keeps)
    extra = [] if slots is None else [slots]
    sent = half // 2 * rows + sum(slots.shape[0] // 2 for slots in extra)
    return call(
        functools.partial(halve_kernel, shift, len(keeps), places),
        "halve",
        [pltpu.VMEM((sent, width), BF16), pltpu.VMEM((half // 2, rows, width), F32)]
        + [pltpu.VMEM(slots.shape, BF16) for slots in extra],
        [*keeps, *gots, *extra],
        flops=flops,
    )


def finish(keeps, gots, splits, sizes):
    return call(
        functools.partial(finish_kernel, len(keeps), splits),
        "finish",
        [shaped((size, keeps[0].shape[-1]), F32) for size in sizes],
        [*keeps, *gots],
    )


def after(value, *others):
    return lax.optimization_barrier((value, *others))[0]


def shards(
    node_latent, edge_latent, node_cot, edge_cot,
    edge_w1, edge_b1, edge_w2, edge_b2, edge_gain,
    node_w1, node_b1, node_w2, node_b2, node_gain,
    send_index, edge_sender, edge_receiver, edge_count,
):
    tiles = lax.axis_size("tiles")
    nodes, latent = node_latent.shape
    edges = edge_latent.shape[0]
    places = send_index.shape[2]
    steps = edges // TILE
    used = nodes + 2 * NEAR + places * tiles
    rows = -(-used // LANES) * LANES
    fast = tiles == 16
    half = tiles // 2
    inside = [(i, i ^ 1) for i in range(tiles)]
    across = [(i, i + 1 if i % 2 else i - 1) for i in range(1, tiles - 1)]
    sender = edge_sender.reshape(edges // LANES, LANES)
    receiver = edge_receiver.reshape(edges // LANES, LANES)
    listed = jnp.swapaxes(send_index, 1, 2)
    row = lambda vector: vector.reshape(1, -1)
    vmem = pltpu.VMEM

    if fast:
        grad_shapes = lambda count: [
            vmem((count // 2, latent), BF16),
            vmem((half, count // tiles, latent), F32),
        ]
    else:
        grad_shapes = lambda count: [shaped((latent, latent), F32), shaped((count, latent), F32)]

    outgoing, inner, outer = call(
        outgoing_kernel,
        "outgoing",
        [
            shaped((tiles, places, latent), BF16),
            vmem((NEAR, latent), BF16),
            vmem((NEAR, latent), BF16),
        ],
        [listed, node_latent],
        hbm=2,
        scratch=[vmem(listed.shape, jnp.int32), vmem((nodes, latent), BF16), pltpu.SemaphoreType.DMA((2,))],
    )
    inner = lax.ppermute(inner, "tiles", inside)
    outer = lax.ppermute(outer, "tiles", across)
    slots = lax.all_to_all(outgoing, "tiles", split_axis=0, concat_axis=0, tiled=True)
    node_kept, receiver_kept, moved, preact = call(
        functools.partial(prepare_kernel, tiles, places),
        "prepare",
        [
            vmem((nodes, latent), BF16),
            vmem(receiver.shape, jnp.int32), vmem(sender.shape, jnp.int32),
            vmem((edges, latent), F32),
        ],
        [node_latent, edge_w1, after(sender, outgoing), receiver, row(edge_b1), edge_latent],
        hbm=6,
        scratch=[
            vmem((edges, latent), BF16), vmem(edge_w1.shape, BF16),
            vmem((latent + 2 * nodes, latent), BF16), vmem(sender.shape, jnp.int32),
            vmem((1, latent), F32), pltpu.SemaphoreType.DMA((5,)), pltpu.SemaphoreType.DMA((2,)),
        ],
        flops=AHEAD,
    )

    (
        w1_kept, edge_kept, w2_kept, gain_kept,
        hidden, slope, normed, inverse, table, dsum, base, node_send, node_keep,
    ) = call(
        functools.partial(forward_kernel, tiles, places, fast),
        "forward",
        [
            vmem(edge_w1.shape, BF16), vmem((edges, latent), BF16),
            vmem(edge_w2.shape, BF16), vmem((1, latent), F32),
            vmem((edges, latent), BF16), vmem((edges, latent), BF16), vmem((edges, latent), F32),
            vmem((edges, LANES), F32), vmem((rows, latent), BF16),
            vmem((nodes, latent), BF16), vmem((nodes, latent), F32),
        ] + grad_shapes(3 * latent if fast else 2 * latent),
        [
            edge_w1, edge_latent, edge_w2, node_w1, node_w2, node_cot,
            row(edge_b2), row(edge_gain), row(node_b1), row(node_b2), row(node_gain), edge_count,
            inner, outer, slots, preact, node_kept, receiver_kept, moved,
        ],
        hbm=12,
        scratch=[
            vmem((rows - nodes, latent), BF16), vmem((nodes, latent), F32),
            vmem((3 * latent, latent), F32), vmem(node_w1.shape, BF16), vmem(node_w2.shape, BF16),
            vmem((nodes, latent), BF16),
        ] + [vmem((1, latent), F32)] * 4 + [
            pltpu.SMEM(edge_count.shape, jnp.int32), pltpu.SemaphoreType.DMA((12,)),
        ],
    )

    early = edges // 2

    def slope_call(start, last, dsum, outs, more):
        return call(
            functools.partial(slope_kernel, tiles, fast, start, last),
            "slope",
            [vmem((early, latent), BF16), vmem((early, latent), BF16)] + outs,
            [edge_cot, receiver_kept, dsum, hidden, slope, normed, inverse, w2_kept, gain_kept] + more,
            hbm=1,
            scratch=[
                vmem((latent, latent), F32), vmem((early, latent), BF16), pltpu.SemaphoreType.DMA,
            ],
        )

    cot_a, dpre_a, grads = slope_call(0, False, dsum, [vmem((latent, latent), F32)], [])
    if fast:
        send, chain = halve(1, [after(node_keep, grads)], [swap(tiles, 1, node_send)])
        dsum = after(dsum, send)
        got = swap(tiles, 2, send)
    cot_b, dpre_b, second_send, second_keep = slope_call(
        early, True, dsum, grad_shapes(latent), [grads]
    )
    if fast:
        got_second = swap(tiles, 1, second_send)

    per = latent // tiles
    to_inner, to_outer, to_far, partial, *first = call(
        functools.partial(first_kernel, tiles, places, fast),
        "first",
        [
            vmem((NEAR, latent), BF16),
            vmem((NEAR, latent), BF16),
            vmem((tiles * places, latent), BF16) if fast else shaped((tiles * places, latent), BF16),
            vmem((nodes, latent), F32),
        ] + (
            [
                vmem((half * per + tiles * places // 2, latent), BF16),
                vmem((half, per, latent), F32),
                vmem((half * per, latent), BF16), vmem((half, per, latent), F32),
                vmem((half * per, latent), BF16), vmem((half, per, latent), F32),
            ]
            if fast else [shaped((3 * latent, latent), F32)]
        ),
        [dpre_a, dpre_b, edge_kept, moved, receiver_kept, table, node_kept, w1_kept, base],
        scratch=[
            vmem((3 * latent, latent), F32), vmem((rows + nodes, latent), F32),
            vmem((2 * NEAR, latent), F32),
        ],
    )

    (grad_edge,) = call(
        edge_kernel,
        "edge",
        [shaped((edges, latent), BF16)],
        [after(dpre_a, partial), dpre_b, cot_a, cot_b, w1_kept],
        out_specs=[pl.BlockSpec(memory_space=pltpu.HBM)],
        scratch=[vmem((edges, latent), BF16), pltpu.SemaphoreType.DMA((steps,))],
    )

    if fast:
        send_a, keep_a, send_more, keep_more, send_b, keep_b = first
        send_a, chain_a, slots = halve(
            1,
            [after(keep_a, grad_edge), keep_more],
            [swap(tiles, 1, send_a), swap(tiles, 1, send_more)],
            to_far,
            places,
     )
        got_a = swap(tiles, 2, send_a)
        send_b, chain_b = halve(
            1, [after(keep_b, send_a), second_keep], [swap(tiles, 1, send_b), got_second]
     )
        got_b = swap(tiles, 2, send_b)
        send, chain = halve(2, [after(chain, send_b)], [got])
        got = swap(tiles, 4, send)
        to_inner, to_outer = lax.optimization_barrier((to_inner, to_outer, send))[:2]
        inner = lax.ppermute(to_inner, "tiles", inside)
        outer = lax.ppermute(to_outer, "tiles", across)
        send, chain = halve(3, [after(chain, inner, outer)], [got])
        got = swap(tiles, 8, send)
        send_a, chain_a, slots = halve(2, [after(chain_a, send)], [got_a], slots, places)
        got_a = swap(tiles, 4, send_a)
        send_b, chain_b = halve(2, [after(chain_b, send_a)], [got_b], flops=AHEAD)
        got_b = swap(tiles, 4, send_b)
        chain_a = lax.optimization_barrier((chain_a, send_b, got))[0]
        send_a, chain_a, slots = halve(3, [chain_a], [got_a], slots, places, AHEAD)
        got_a = swap(tiles, 8, send_a)
        chain_b = after(chain_b, send_a)
        send_b, chain_b = halve(3, [chain_b], [got_b], flops=AHEAD)
        got_b = swap(tiles, 8, send_b)
        returned = [slots, got_a]
        grad_edge_w1, grad_edge_w2, grad_node_w1, grad_node_w2 = finish(
            [chain, chain_a, chain_b],
            [got, got_a, got_b],
            [[(2, 2 * per), (3, per)], [(0, 2 * per)], [(0, per), (1, per)]],
            [3 * per, per, 2 * per, per],
        )
    else:
        inner = lax.ppermute(to_inner, "tiles", inside)
        outer = lax.ppermute(to_outer, "tiles", across)
        returned = [lax.all_to_all(to_far, "tiles", split_axis=0, concat_axis=0, tiled=True)]
        scatter = functools.partial(
            lax.psum_scatter, axis_name="tiles", scatter_dimension=0, tiled=True
        )
        grad_node_w1, grad_node_w2 = scatter(node_keep), scatter(node_send)
        grad_edge_w1, grad_edge_w2 = scatter(first[0]), scatter(second_keep)
    (grad_node,) = call(
        functools.partial(node_kernel, fast),
        "node",
        [shaped((nodes, latent), BF16)],
        [listed, partial, inner, outer, *returned],
        scratch=[vmem((nodes, latent), F32)],
    )
    return (grad_node, grad_edge, grad_edge_w1, grad_edge_w2, grad_node_w1, grad_node_w2)


def solution(mesh):
    split = P(("groups", "tiles"), None)
    return jax.shard_map(
        shards,
        mesh=mesh,
        in_specs=(split,) * 4
        + (P(),) * 10
        + (
            P(("groups", "tiles"), None, None),
            P(("groups", "tiles")),
            P(("groups", "tiles")),
            P("groups"),
        ),
        out_specs=(split,) * 6,
        check_vma=False,
    )
```

```python
import functools

import jax
import jax.numpy as jnp
from jax import lax
from jax.experimental import pallas as pl
from jax.experimental.pallas import tpu as pltpu
from jax.sharding import PartitionSpec as P

NEAR = 64
EPSILON = 1e-05
TILE = 256
LANES = 128
F32 = jnp.float32
BF16 = jnp.bfloat16
MIB = 1024 * 1024
AHEAD = 10**10

NN = (((1,), (0,)), ((), ()))
NT = (((1,), (1,)), ((), ()))
TN = (((0,), (0,)), ((), ()))


def dot(a, b, dims=NN):
    return lax.dot_general(a, b, dims, preferred_element_type=F32)


def sigmoid(x):
    return 0.5 * jnp.tanh(0.5 * x) + 0.5


def row_mean(x):
    return jnp.sum(x, axis=-1, keepdims=True) * (1.0 / x.shape[-1])


def ones_where(mask):
    return jnp.where(mask, 1.0, 0.0).astype(BF16)


def index_columns(idx_ref, step, tile):
    per = tile // LANES
    parts = []
    for j in range(per):
        row = idx_ref[pl.ds(step * per + j, 1), :]
        parts.append(jnp.transpose(jnp.broadcast_to(row, (LANES, LANES))))
    return jnp.concatenate(parts, axis=0)


def pick_columns(columns, start, stop):
    lane = lax.broadcasted_iota(jnp.int32, columns.shape, 1)
    return [ones_where(columns == lane + at) for at in range(start, stop, LANES)]


def pick_rows(idx_ref, step, tile, width):
    per = tile // LANES
    row = jnp.concatenate([idx_ref[pl.ds(step * per + j, 1), :] for j in range(per)], axis=1)
    return ones_where(lax.broadcasted_iota(jnp.int32, (width, tile), 0) == row)


def norm_forward(out):
    centred = out - row_mean(out)
    inverse = lax.rsqrt(row_mean(centred * centred) + EPSILON)
    return centred, inverse


def norm_backward(scaled, normed, inverse):
    return (
        inverse * (scaled - row_mean(scaled) - normed * row_mean(scaled * normed))
    ).astype(BF16)


def split_halves(bit, total_ref, at, block, first, rows, send_ref, keep_ref, offset):
    half, size = keep_ref.shape[:2]
    for q in range(half):
        there = pl.multiple_of(at + first + (2 * q + 1 - bit) * block, 32)
        here = pl.multiple_of(at + first + (2 * q + bit) * block, 32)
        to = q * size + offset
        send_ref[to : to + rows, :] = total_ref[pl.ds(there, rows), :].astype(BF16)
        keep_ref[q, offset : offset + rows, :] = total_ref[pl.ds(here, rows), :]


def fetch(pairs, sems):
    copies = []
    for at, (source, target) in enumerate(pairs):
        copies.append(pltpu.make_async_copy(source, target, sems.at[at]))
    for copy in copies:
        copy.start()
    return copies


def tile_pairs(source, target, tile):
    return [
        (source.at[pl.ds(at, tile)], target.at[pl.ds(at, tile)])
        for at in range(0, source.shape[0], tile)
    ]


def slot_owner(origin, shape, dim, places):
    row = lax.broadcasted_iota(jnp.int32, shape, dim)
    return lax.div(row, places) ^ origin, lax.rem(row, places)


def bit_slots(bit, shape, places):
    row = lax.broadcasted_iota(jnp.int32, shape, 0)
    column = lax.broadcasted_iota(jnp.int32, shape, 1)
    slot, place = lax.div(column, places), lax.rem(column, places)
    rank = ((slot >> (bit + 1)) << bit) | (slot & (2**bit - 1))
    return ((slot >> bit) & 1 == 1) & (rank * places + place == row)


def slots_out(bit, slots, places):
    rows = slots.shape[0]
    return dot(ones_where(bit_slots(bit, (rows // 2, rows), places)), slots).astype(BF16)


def slots_in(bit, slots, got, places):
    rows = slots.shape[0]
    row = lax.broadcasted_iota(jnp.int32, (rows, rows), 0)
    column = lax.broadcasted_iota(jnp.int32, (rows, rows), 1)
    kept = (row == column) & ((lax.div(column, places) >> bit) & 1 == 0)
    moved = ones_where(bit_slots(bit, (rows // 2, rows), places))
    return (dot(ones_where(kept), slots) + dot(moved, got, TN)).astype(BF16)


def outgoing_kernel(
    index_hbm, node_hbm, w1_hbm, edge_hbm,
    slots_ref, inner_ref, outer_ref, node_ref, w1_ref, edge_ref,
    index_ref, sems,
):
    copies = fetch(
        [
            (index_hbm, index_ref), (node_hbm, node_ref), (w1_hbm, w1_ref), (edge_hbm, edge_ref),
        ],
        sems,
    )
    copies[0].wait()
    copies[1].wait()
    places, tiles = index_ref.shape[1], index_ref.shape[2]
    nodes, latent = node_ref.shape
    place = lax.broadcasted_iota(jnp.int32, (nodes, tiles), 0)
    for j in range(places):
        picks = ones_where(place == index_ref[0, j : j + 1, :])
        slots_ref[:, j, :] = dot(picks, node_ref[...], TN).astype(BF16)
    odd = lax.rem(lax.axis_index("tiles"), 2)
    inner_ref[...] = node_ref[pl.ds(pl.multiple_of((1 - odd) * (nodes - NEAR), NEAR), NEAR), :]
    outer_ref[...] = node_ref[pl.ds(pl.multiple_of(odd * (nodes - NEAR), NEAR), NEAR), :]
    copies[2].wait()
    copies[3].wait()


def table_index(raw, tiles, places, nodes):
    far = raw - (nodes + 2 * NEAR)
    far = nodes + 2 * NEAR + lax.rem(far, places) * tiles + lax.div(far, places)
    rim = jnp.where(raw < NEAR, raw + nodes, raw)
    own = jnp.where((raw >= NEAR) & (raw < NEAR + nodes), raw - NEAR, rim)
    return jnp.where(raw >= nodes + 2 * NEAR, far, own)


def prepare_kernel(
    tiles, places,
    sender_hbm, receiver_hbm, b1_hbm, node_ref, w1_ref, edge_ref,
    receiver_ref, moved_ref, partial_ref,
    weights, sender_ref, b1_ref, sems,
):
    edges, latent = edge_ref.shape
    nodes = node_ref.shape[0]
    copies = fetch(
        [(sender_hbm, sender_ref), (receiver_hbm, receiver_ref), (b1_hbm, b1_ref)], sems
    )
    weights[:latent, :] = w1_ref[:latent, :]
    weights[latent : latent + nodes, :] = dot(
        node_ref[...], w1_ref[latent : 2 * latent, :]
    ).astype(BF16)
    weights[latent + nodes :, :] = dot(node_ref[...], w1_ref[2 * latent :, :]).astype(BF16)
    for copy in copies:
        copy.wait()
    moved_ref[...] = table_index(sender_ref[...], tiles, places, nodes)
    for step in range(edges // TILE):
        tile = slice(step * TILE, (step + 1) * TILE)
        senders = pick_columns(index_columns(moved_ref, step, TILE), 0, nodes)
        receivers = pick_columns(index_columns(receiver_ref, step, TILE), 0, nodes)
        inputs = jnp.concatenate([edge_ref[tile, :]] + senders + receivers, axis=1)
        partial_ref[tile, :] = dot(inputs, weights[...]) + b1_ref[...]


def forward_kernel(
    tiles, places, fast,
    w1_hbm, edge_hbm, cot_hbm, w2_hbm, nw1_hbm, nw2_hbm, ncot_hbm,
    b2_hbm, gain_hbm, nb1_hbm, nb2_hbm, ngain_hbm, count_hbm,
    inner_ref, outer_ref, far_ref, known_ref, node_ref, receiver_ref, moved_ref,
    w1_ref, edge_ref, cot_ref, w2_ref, gain_ref,
    hidden_ref, slope_ref, normed_ref, inverse_ref, table_ref, dsum_ref, base_ref,
    gsend_ref, gkeep_ref,
    weights, summed, grads, nw1_ref, nw2_ref, ncot_ref,
    b2_ref, nb1_ref, nb2_ref, ngain_ref, count_ref, sems,
):
    here = lax.axis_index("tiles")
    edges, latent = hidden_ref.shape
    nodes = node_ref.shape[0]
    rows = table_ref.shape[0]
    steps = edges // TILE

    senders_part = pl.ds(latent, latent)
    early = fetch(
        [
            (w1_hbm.at[senders_part], w1_ref.at[senders_part]), (count_hbm, count_ref),
            (b2_hbm, b2_ref), (gain_hbm, gain_ref), (w2_hbm, w2_ref),
        ],
        sems,
    )
    edges_part, receivers_part = pl.ds(0, latent), pl.ds(2 * latent, latent)
    late = fetch(
        [
            (nw1_hbm, nw1_ref), (nw2_hbm, nw2_ref), (ncot_hbm, ncot_ref),
            (nb1_hbm, nb1_ref), (nb2_hbm, nb2_ref), (ngain_hbm, ngain_ref),
            (cot_hbm, cot_ref), (edge_hbm, edge_ref),
            (w1_hbm.at[edges_part], w1_ref.at[edges_part]),
            (w1_hbm.at[receivers_part], w1_ref.at[receivers_part]),
        ],
        sems.at[pl.ds(len(early), 10)],
    )

    table_ref[:nodes, :] = node_ref[...]
    odd = lax.rem(here, 2)
    table_ref[pl.ds(pl.multiple_of(nodes + (1 - odd) * NEAR, NEAR), NEAR), :] = inner_ref[...]
    table_ref[pl.ds(pl.multiple_of(nodes + odd * NEAR, NEAR), NEAR), :] = outer_ref[...]
    for j in range(places):
        at = nodes + 2 * NEAR + j * tiles
        table_ref[at : at + tiles, :] = far_ref[:, j, :]
    used = nodes + 2 * NEAR + places * tiles
    if used < rows:
        table_ref[used:, :] = jnp.zeros((rows - used, latent), BF16)
    early[0].wait()
    weights[...] = dot(table_ref[nodes:, :], w1_ref[latent : 2 * latent, :]).astype(BF16)
    for copy in early[1:]:
        copy.wait()
    live = count_ref[here]

    def activate(step):
        tile = slice(step * TILE, (step + 1) * TILE)
        senders = pick_columns(index_columns(moved_ref, step, TILE), nodes, rows)
        preact = known_ref[tile, :] + dot(jnp.concatenate(senders, axis=1), weights[...])
        sig = sigmoid(preact)
        slope_ref[tile, :] = (sig * (1.0 + preact * (1.0 - sig))).astype(BF16)
        hidden_ref[tile, :] = (preact * sig).astype(BF16)

    def normalize(step):
        tile = slice(step * TILE, (step + 1) * TILE)
        centred, inverse = norm_forward(dot(hidden_ref[tile, :], w2_ref[...]) + b2_ref[...])
        position = step * TILE + lax.broadcasted_iota(jnp.int32, inverse.shape, 0)
        inverse = jnp.where(position < live, inverse, 0.0)
        normed = centred * inverse
        normed_ref[tile, :] = normed
        inverse_ref[tile, :] = jnp.broadcast_to(inverse, (TILE, LANES))
        update = (normed * gain_ref[...]).astype(BF16)
        part = dot(pick_rows(receiver_ref, step, TILE, nodes), update)
        if step == 0:
            summed[...] = part
        else:
            summed[...] += part

    for step in range(steps + 1):
        if step < steps:
            activate(step)
        if step > 0:
            normalize(step - 1)

    for copy in late:
        copy.wait()
    node_in = jnp.concatenate([node_ref[...], summed[...].astype(BF16)], axis=1)
    preact_n = dot(node_in, nw1_ref[...]) + nb1_ref[...]
    sig_n = sigmoid(preact_n)
    hidden_n = (preact_n * sig_n).astype(BF16)
    centred_n, inverse_n = norm_forward(dot(hidden_n, nw2_ref[...]) + nb2_ref[...])
    cot = ncot_ref[...].astype(F32)
    dout = norm_backward(cot * ngain_ref[...], centred_n * inverse_n, inverse_n)
    slope_n = sig_n * (1.0 + preact_n * (1.0 - sig_n))
    dpre = (dot(dout, nw2_ref[...], NT) * slope_n).astype(BF16)
    grads[: 2 * latent, :] = dot(node_in, dpre, TN)
    grads[2 * latent :, :] = dot(hidden_n, dout, TN)
    base_ref[...] = cot + dot(dpre, nw1_ref[:latent, :], NT)
    dsum_ref[...] = dot(dpre, nw1_ref[latent:, :], NT).astype(BF16)
    if fast:
        bit = lax.rem(here, 2)
        first = 2 * latent // tiles
        split_halves(bit, grads, 0, first, 0, first, gsend_ref, gkeep_ref, 0)
        second = latent // tiles
        split_halves(bit, grads, 2 * latent, second, 0, second, gsend_ref, gkeep_ref, first)
    else:
        gkeep_ref[...] = grads[: 2 * latent, :]
        gsend_ref[...] = grads[2 * latent :, :]


def slope_kernel(
    tiles, fast, start, last,
    cot_ref, receiver_ref, dsum_ref, hidden_ref, slope_ref, normed_ref, inverse_ref, w2_ref, gain_ref,
    *refs,
):
    dpre_ref, *out_refs, grads, dout = refs[0 if start == 0 else 1 :]
    here = lax.axis_index("tiles")
    edges, latent = dpre_ref.shape
    nodes = dsum_ref.shape[0]
    steps = edges // TILE
    grads[...] = jnp.zeros_like(grads) if start == 0 else refs[0][...]

    def outer(step):
        tile = slice(step * TILE, (step + 1) * TILE)
        whole = slice(start + step * TILE, start + (step + 1) * TILE)
        receivers = jnp.concatenate(
            pick_columns(index_columns(receiver_ref, start // TILE + step, TILE), 0, nodes), axis=1
        )
        grad_update = cot_ref[whole, :].astype(F32) + dot(receivers, dsum_ref[...])
        inverse = inverse_ref[whole, :1]
        dout[tile, :] = norm_backward(grad_update * gain_ref[...], normed_ref[whole, :], inverse)

    def inner(step):
        tile = slice(step * TILE, (step + 1) * TILE)
        whole = slice(start + step * TILE, start + (step + 1) * TILE)
        dpre_ref[tile, :] = (
            dot(dout[tile, :], w2_ref[...], NT) * slope_ref[whole, :].astype(F32)
        ).astype(BF16)
        grads[...] += dot(hidden_ref[whole, :], dout[tile, :], TN)

    for step in range(steps + 1):
        if step < steps:
            outer(step)
        if step > 0:
            inner(step - 1)

    if not last:
        out_refs[0][...] = grads[...]
    elif fast:
        rows = latent // tiles
        split_halves(lax.rem(here, 2), grads, 0, rows, 0, rows, *out_refs, 0)
    else:
        out_refs[0][...] = jnp.zeros_like(out_refs[0])
        out_refs[1][...] = grads[...]


def first_kernel(
    tiles, places, fast,
    dpre_a_ref, dpre_b_ref, edge_ref, sender_ref, receiver_ref, table_ref, node_ref, w1_ref, base_ref,
    *refs,
):
    out_refs, (grads, sums, rims) = refs[:-3], refs[-3:]
    inner_ref, outer_ref, far_ref, partial_ref = out_refs[:4]
    here = lax.axis_index("tiles")
    edges, latent = edge_ref.shape
    early = dpre_a_ref.shape[0]
    nodes = node_ref.shape[0]
    rows = table_ref.shape[0]

    for step in range(edges // TILE):
        tile = slice(step * TILE, (step + 1) * TILE)
        if step * TILE < early:
            dpre = dpre_a_ref[tile, :]
        else:
            dpre = dpre_b_ref[step * TILE - early : (step + 1) * TILE - early, :]
        part = dot(edge_ref[tile, :], dpre, TN)
        picks = jnp.concatenate(
            [
                pick_rows(sender_ref, step, TILE, rows),
                pick_rows(receiver_ref, step, TILE, nodes),
            ],
            axis=0,
        )
        scattered = dot(picks, dpre)
        if step == 0:
            grads[:latent, :] = part
            sums[...] = scattered
        else:
            grads[:latent, :] += part
            sums[...] += scattered

    by_sender = sums[:rows, :].astype(BF16)
    by_receiver = sums[rows:, :].astype(BF16)
    grads[latent : 2 * latent, :] = dot(table_ref[...], by_sender, TN)
    grads[2 * latent :, :] = dot(node_ref[...], by_receiver, TN)
    back = dot(by_sender, w1_ref[latent : 2 * latent, :], NT)
    far = back[nodes + 2 * NEAR : nodes + 2 * NEAR + places * tiles, :].astype(BF16)
    owner, at = slot_owner(here if fast else 0, (places * tiles, places * tiles), 0, places)
    column = lax.broadcasted_iota(jnp.int32, (places * tiles, places * tiles), 1)
    far = dot(ones_where(at * tiles + owner == column), far).astype(BF16)
    far_ref[...] = far
    if fast:
        bit = lax.rem(here, 2)
        block = 3 * latent // tiles
        at = 0
        for send_ref, keep_ref in (out_refs[4:6], out_refs[6:8], out_refs[8:10]):
            part = keep_ref.shape[1]
            split_halves(bit, grads, 0, block, at, part, send_ref, keep_ref, 0)
            at += part
        out_refs[4][tiles // 2 * out_refs[5].shape[1] :, :] = slots_out(0, far, places)
    else:
        out_refs[4][...] = grads[...]
    rims[...] = back[nodes : nodes + 2 * NEAR, :]
    odd = lax.rem(here, 2)
    inner_ref[...] = rims[pl.ds(pl.multiple_of((1 - odd) * NEAR, NEAR), NEAR), :].astype(BF16)
    outer_ref[...] = rims[pl.ds(pl.multiple_of(odd * NEAR, NEAR), NEAR), :].astype(BF16)
    partial_ref[...] = (
        base_ref[...] + back[:nodes, :] + dot(by_receiver, w1_ref[2 * latent :, :], NT)
    )


def edge_kernel(dpre_a_ref, dpre_b_ref, cot_ref, w1_ref, out_hbm, out_ref, sems):
    early, latent = dpre_a_ref.shape
    copies = []
    for dpre_ref, base in ((dpre_a_ref, 0), (dpre_b_ref, early)):
        for at in range(0, early, TILE):
            part = slice(at, at + TILE)
            tile = pl.ds(base + at, TILE)
            out_ref[tile, :] = (
                cot_ref[tile, :].astype(F32) + dot(dpre_ref[part, :], w1_ref[:latent, :], NT)
            ).astype(BF16)
            copy = pltpu.make_async_copy(
                out_ref.at[tile], out_hbm.at[tile], sems.at[(base + at) // TILE]
            )
            copy.start()
            copies.append(copy)
    for copy in copies:
        copy.wait()


def node_kernel(fast, index_ref, partial_ref, inner_ref, outer_ref, slots_ref, *refs):
    out_ref, sums = refs[-2:]
    places, tiles = index_ref.shape[1], index_ref.shape[2]
    nodes = partial_ref.shape[0]
    origin = lax.axis_index("tiles") if fast else 0
    slots = slots_ref[...]
    if fast:
        got_ref = refs[0]
        slots = slots_in(3, slots, got_ref[got_ref.shape[0] - slots.shape[0] // 2 :, :], places)
    place = lax.broadcasted_iota(jnp.int32, (nodes, tiles), 0)
    owner, at = slot_owner(origin, (tiles, places * tiles), 1, places)
    row = lax.broadcasted_iota(jnp.int32, (tiles, places * tiles), 0)
    total = partial_ref[...]
    for j in range(places):
        picks = ones_where(place == index_ref[0, j : j + 1, :])
        far = dot(ones_where((owner == row) & (at == j)), slots).astype(BF16)
        total = total + dot(picks, far)
    sums[...] = total
    odd = lax.rem(lax.axis_index("tiles"), 2)
    inner_at = pl.ds(pl.multiple_of((1 - odd) * (nodes - NEAR), NEAR), NEAR)
    outer_at = pl.ds(pl.multiple_of(odd * (nodes - NEAR), NEAR), NEAR)
    sums[inner_at, :] += inner_ref[...].astype(F32)
    sums[outer_at, :] += outer_ref[...].astype(F32)
    out_ref[...] = sums[...].astype(BF16)


def halve_kernel(shift, count, places, *refs):
    keeps, gots = refs[:count], refs[count : 2 * count]
    rest = refs[2 * count :]
    send_ref, kept_ref = rest[-2:] if not places else rest[-3:-1]
    size = kept_ref.shape[1]
    bit = lax.rem(lax.div(lax.axis_index("tiles"), 2**shift), 2)
    at = 0
    for keep_ref, got_ref in zip(keeps, gots):
        blocks, rows = keep_ref.shape[:2]
        for q in range(blocks // 2):
            there, here = 2 * q + 1 - bit, 2 * q + bit
            got_there = got_ref[pl.ds(pl.multiple_of(there * rows, 32), rows), :].astype(F32)
            got_here = got_ref[pl.ds(pl.multiple_of(here * rows, 32), rows), :].astype(F32)
            to = q * size + at
            send_ref[to : to + rows, :] = (keep_ref[there] + got_there).astype(BF16)
            kept_ref[q, at : at + rows, :] = keep_ref[here] + got_here
        at += rows
    if places:
        slots_ref, moved_ref = rest[0], rest[-1]
        half = slots_ref.shape[0] // 2
        got_ref = gots[0]
        slots = slots_in(shift - 1, slots_ref[...], got_ref[got_ref.shape[0] - half :, :], places)
        moved_ref[...] = slots
        send_ref[send_ref.shape[0] - half :, :] = slots_out(shift, slots, places)


def finish_kernel(count, splits, *refs):
    out_refs = refs[2 * count :]
    rows = [0] * len(out_refs)
    for keep_ref, got_ref, parts in zip(refs[:count], refs[count : 2 * count], splits):
        at = 0
        for which, size in parts:
            first = rows[which]
            out_refs[which][first : first + size, :] = (
                keep_ref[0, at : at + size, :] + got_ref[at : at + size, :].astype(F32)
            )
            at += size
            rows[which] += size


def shaped(shape, dtype):
    return jax.ShapeDtypeStruct(shape, dtype)


def in_hbm(*arrays):
    return [pltpu.with_memory_space_constraint(array, pltpu.HBM) for array in arrays]


def call(kernel, name, out_shape, args, hbm=0, scratch=(), out_specs=None, flops=0):
    vmem = pl.BlockSpec(memory_space=pltpu.VMEM)
    return pl.pallas_call(
        kernel,
        in_specs=[pl.BlockSpec(memory_space=pltpu.HBM)] * hbm + [vmem] * (len(args) - hbm),
        out_specs=out_specs or [vmem] * len(out_shape),
        out_shape=out_shape,
        scratch_shapes=scratch,
        compiler_params=pltpu.CompilerParams(vmem_limit_bytes=16 * MIB),
        cost_estimate=pl.CostEstimate(flops=flops, bytes_accessed=flops // 100, transcendentals=0),
        name=name,
    )(*in_hbm(*args[:hbm]), *args[hbm:])


def swap(tiles, bit, send):
    return lax.ppermute(send, "tiles", [(i, i ^ bit) for i in range(tiles)])


def halve(shift, keeps, gots, slots=None, places=0, flops=0):
    half, _, width = keeps[0].shape
    rows = sum(keep.shape[1] for keep in keeps)
    extra = [] if slots is None else [slots]
    sent = half // 2 * rows + sum(slots.shape[0] // 2 for slots in extra)
    return call(
        functools.partial(halve_kernel, shift, len(keeps), places),
        "halve",
        [pltpu.VMEM((sent, width), BF16), pltpu.VMEM((half // 2, rows, width), F32)]
        + [pltpu.VMEM(slots.shape, BF16) for slots in extra],
        [*keeps, *gots, *extra],
        flops=flops,
    )


def finish(keeps, gots, splits, sizes):
    return call(
        functools.partial(finish_kernel, len(keeps), splits),
        "finish",
        [shaped((size, keeps[0].shape[-1]), F32) for size in sizes],
        [*keeps, *gots],
    )


def after(value, *others):
    return lax.optimization_barrier((value, *others))[0]


def shards(
    node_latent, edge_latent, node_cot, edge_cot,
    edge_w1, edge_b1, edge_w2, edge_b2, edge_gain,
    node_w1, node_b1, node_w2, node_b2, node_gain,
    send_index, edge_sender, edge_receiver, edge_count,
):
    tiles = lax.axis_size("tiles")
    nodes, latent = node_latent.shape
    edges = edge_latent.shape[0]
    places = send_index.shape[2]
    steps = edges // TILE
    used = nodes + 2 * NEAR + places * tiles
    rows = -(-used // LANES) * LANES
    fast = tiles == 16
    half = tiles // 2
    inside = [(i, i ^ 1) for i in range(tiles)]
    across = [(i, i + 1 if i % 2 else i - 1) for i in range(1, tiles - 1)]
    sender = edge_sender.reshape(edges // LANES, LANES)
    receiver = edge_receiver.reshape(edges // LANES, LANES)
    listed = jnp.swapaxes(send_index, 1, 2)
    row = lambda vector: vector.reshape(1, -1)
    vmem = pltpu.VMEM

    if fast:
        grad_shapes = lambda count: [
            vmem((count // 2, latent), BF16),
            vmem((half, count // tiles, latent), F32),
        ]
    else:
        grad_shapes = lambda count: [shaped((latent, latent), F32), shaped((count, latent), F32)]

    outgoing, inner, outer, node_kept, w1_early, edge_early = call(
        outgoing_kernel,
        "outgoing",
        [
            shaped((tiles, places, latent), BF16),
            vmem((NEAR, latent), BF16),
            vmem((NEAR, latent), BF16),
            vmem((nodes, latent), BF16),
            vmem(edge_w1.shape, BF16),
            vmem((edges, latent), BF16),
        ],
        [listed, node_latent, edge_w1, edge_latent],
        hbm=4,
        scratch=[vmem(listed.shape, jnp.int32), pltpu.SemaphoreType.DMA((4,))],
    )
    inner = lax.ppermute(inner, "tiles", inside)
    outer = lax.ppermute(outer, "tiles", across)
    slots = lax.all_to_all(outgoing, "tiles", split_axis=0, concat_axis=0, tiled=True)
    receiver_kept, moved, preact = call(
        functools.partial(prepare_kernel, tiles, places),
        "prepare",
        [
            vmem(receiver.shape, jnp.int32), vmem(sender.shape, jnp.int32),
            vmem((edges, latent), F32),
        ],
        [sender, receiver, row(edge_b1), node_kept, w1_early, edge_early],
        hbm=3,
        scratch=[
            vmem((latent + 2 * nodes, latent), BF16), vmem(sender.shape, jnp.int32),
            vmem((1, latent), F32), pltpu.SemaphoreType.DMA((3,)),
        ],
        flops=AHEAD,
    )

    (
        w1_kept, edge_kept, cot_kept, w2_kept, gain_kept,
        hidden, slope, normed, inverse, table, dsum, base, node_send, node_keep,
    ) = call(
        functools.partial(forward_kernel, tiles, places, fast),
        "forward",
        [
            vmem(edge_w1.shape, BF16), vmem((edges, latent), BF16), vmem((edges, latent), BF16),
            vmem(edge_w2.shape, BF16), vmem((1, latent), F32),
            vmem((edges, latent), BF16), vmem((edges, latent), BF16), vmem((edges, latent), F32),
            vmem((edges, LANES), F32), vmem((rows, latent), BF16),
            vmem((nodes, latent), BF16), vmem((nodes, latent), F32),
        ] + grad_shapes(3 * latent if fast else 2 * latent),
        [
            edge_w1, edge_latent, edge_cot, edge_w2, node_w1, node_w2, node_cot,
            row(edge_b2), row(edge_gain), row(node_b1), row(node_b2), row(node_gain), edge_count,
            inner, outer, slots, preact, node_kept, receiver_kept, moved,
        ],
        hbm=13,
        scratch=[
            vmem((rows - nodes, latent), BF16), vmem((nodes, latent), F32),
            vmem((3 * latent, latent), F32), vmem(node_w1.shape, BF16), vmem(node_w2.shape, BF16),
            vmem((nodes, latent), BF16),
        ] + [vmem((1, latent), F32)] * 4 + [
            pltpu.SMEM(edge_count.shape, jnp.int32), pltpu.SemaphoreType.DMA((15,)),
        ],
    )

    early = edges // 2

    def slope_call(start, last, dsum, outs, more):
        return call(
            functools.partial(slope_kernel, tiles, fast, start, last),
            "slope",
            [vmem((early, latent), BF16)] + outs,
            [cot_kept, receiver_kept, dsum, hidden, slope, normed, inverse, w2_kept, gain_kept] + more,
            scratch=[vmem((latent, latent), F32), vmem((early, latent), BF16)],
        )

    dpre_a, grads = slope_call(0, False, dsum, [vmem((latent, latent), F32)], [])
    if fast:
        send, chain = halve(1, [after(node_keep, grads)], [swap(tiles, 1, node_send)])
        dsum = after(dsum, send)
        got = swap(tiles, 2, send)
    dpre_b, second_send, second_keep = slope_call(
        early, True, dsum, grad_shapes(latent), [grads]
    )
    if fast:
        got_second = swap(tiles, 1, second_send)

    per = latent // tiles
    to_inner, to_outer, to_far, partial, *first = call(
        functools.partial(first_kernel, tiles, places, fast),
        "first",
        [
            vmem((NEAR, latent), BF16),
            vmem((NEAR, latent), BF16),
            vmem((tiles * places, latent), BF16) if fast else shaped((tiles * places, latent), BF16),
            vmem((nodes, latent), F32),
        ] + (
            [
                vmem((half * per + tiles * places // 2, latent), BF16),
                vmem((half, per, latent), F32),
                vmem((half * per, latent), BF16), vmem((half, per, latent), F32),
                vmem((half * per, latent), BF16), vmem((half, per, latent), F32),
            ]
            if fast else [shaped((3 * latent, latent), F32)]
        ),
        [dpre_a, dpre_b, edge_kept, moved, receiver_kept, table, node_kept, w1_kept, base],
        scratch=[
            vmem((3 * latent, latent), F32), vmem((rows + nodes, latent), F32),
            vmem((2 * NEAR, latent), F32),
        ],
    )

    (grad_edge,) = call(
        edge_kernel,
        "edge",
        [shaped((edges, latent), BF16)],
        [after(dpre_a, partial), dpre_b, cot_kept, w1_kept],
        out_specs=[pl.BlockSpec(memory_space=pltpu.HBM)],
        scratch=[vmem((edges, latent), BF16), pltpu.SemaphoreType.DMA((steps,))],
    )

    if fast:
        send_a, keep_a, send_more, keep_more, send_b, keep_b = first
        send_a, chain_a, slots = halve(
            1,
            [after(keep_a, grad_edge), keep_more],
            [swap(tiles, 1, send_a), swap(tiles, 1, send_more)],
            to_far,
            places,
     )
        got_a = swap(tiles, 2, send_a)
        send_b, chain_b = halve(
            1, [after(keep_b, send_a), second_keep], [swap(tiles, 1, send_b), got_second]
     )
        got_b = swap(tiles, 2, send_b)
        send, chain = halve(2, [after(chain, send_b)], [got])
        got = swap(tiles, 4, send)
        send, chain = halve(3, [chain], [got])
        got = swap(tiles, 8, send)
        send_a, chain_a, slots = halve(2, [after(chain_a, send)], [got_a], slots, places)
        got_a = swap(tiles, 4, send_a)
        send_b, chain_b = halve(2, [after(chain_b, send_a)], [got_b], flops=AHEAD)
        got_b = swap(tiles, 4, send_b)
        to_inner, to_outer = lax.optimization_barrier((to_inner, to_outer, send_b))[:2]
        inner = lax.ppermute(to_inner, "tiles", inside)
        outer = lax.ppermute(to_outer, "tiles", across)
        chain_a = lax.optimization_barrier((chain_a, send_b, got))[0]
        send_a, chain_a, slots = halve(3, [chain_a], [got_a], slots, places, AHEAD)
        got_a = swap(tiles, 8, send_a)
        chain_b = after(chain_b, send_a)
        send_b, chain_b = halve(3, [chain_b], [got_b], flops=AHEAD)
        got_b = swap(tiles, 8, send_b)
        returned = [slots, got_a]
        grad_edge_w1, grad_edge_w2, grad_node_w1, grad_node_w2 = finish(
            [chain, chain_a, chain_b],
            [got, got_a, got_b],
            [[(2, 2 * per), (3, per)], [(0, 2 * per)], [(0, per), (1, per)]],
            [3 * per, per, 2 * per, per],
        )
    else:
        inner = lax.ppermute(to_inner, "tiles", inside)
        outer = lax.ppermute(to_outer, "tiles", across)
        returned = [lax.all_to_all(to_far, "tiles", split_axis=0, concat_axis=0, tiled=True)]
        scatter = functools.partial(
            lax.psum_scatter, axis_name="tiles", scatter_dimension=0, tiled=True
        )
        grad_node_w1, grad_node_w2 = scatter(node_keep), scatter(node_send)
        grad_edge_w1, grad_edge_w2 = scatter(first[0]), scatter(second_keep)
    (grad_node,) = call(
        functools.partial(node_kernel, fast),
        "node",
        [shaped((nodes, latent), BF16)],
        [listed, partial, inner, outer, *returned],
        scratch=[vmem((nodes, latent), F32)],
    )
    return (grad_node, grad_edge, grad_edge_w1, grad_edge_w2, grad_node_w1, grad_node_w2)


def solution(mesh):
    split = P(("groups", "tiles"), None)
    return jax.shard_map(
        shards,
        mesh=mesh,
        in_specs=(split,) * 4
        + (P(),) * 10
        + (
            P(("groups", "tiles"), None, None),
            P(("groups", "tiles")),
            P(("groups", "tiles")),
            P("groups"),
        ),
        out_specs=(split,) * 6,
        check_vma=False,
    )
```

```python
import functools

import jax
import jax.numpy as jnp
from jax import lax
from jax.experimental import pallas as pl
from jax.experimental.pallas import tpu as pltpu
from jax.sharding import PartitionSpec as P

NEAR = 64
EPSILON = 1e-05
TILE = 256
LANES = 128
F32 = jnp.float32
BF16 = jnp.bfloat16
MIB = 1024 * 1024
AHEAD = 10**10

NN = (((1,), (0,)), ((), ()))
NT = (((1,), (1,)), ((), ()))
TN = (((0,), (0,)), ((), ()))


def dot(a, b, dims=NN):
    return lax.dot_general(a, b, dims, preferred_element_type=F32)


def sigmoid(x):
    return 0.5 * jnp.tanh(0.5 * x) + 0.5


def row_mean(x):
    return jnp.sum(x, axis=-1, keepdims=True) * (1.0 / x.shape[-1])


def ones_where(mask):
    return jnp.where(mask, 1.0, 0.0).astype(BF16)


def index_columns(idx_ref, step, tile):
    per = tile // LANES
    parts = []
    for j in range(per):
        row = idx_ref[pl.ds(step * per + j, 1), :]
        parts.append(jnp.transpose(jnp.broadcast_to(row, (LANES, LANES))))
    return jnp.concatenate(parts, axis=0)


def pick_columns(columns, start, stop):
    lane = lax.broadcasted_iota(jnp.int32, columns.shape, 1)
    return [ones_where(columns == lane + at) for at in range(start, stop, LANES)]


def pick_rows(idx_ref, step, tile, width):
    per = tile // LANES
    row = jnp.concatenate([idx_ref[pl.ds(step * per + j, 1), :] for j in range(per)], axis=1)
    return ones_where(lax.broadcasted_iota(jnp.int32, (width, tile), 0) == row)


def norm_forward(out):
    centred = out - row_mean(out)
    inverse = lax.rsqrt(row_mean(centred * centred) + EPSILON)
    return centred, inverse


def norm_backward(scaled, normed, inverse):
    return (
        inverse * (scaled - row_mean(scaled) - normed * row_mean(scaled * normed))
    ).astype(BF16)


def split_halves(bit, total_ref, at, block, first, rows, send_ref, keep_ref, offset, x_last=False):
    half, size = keep_ref.shape[:2]
    for to in range(half):
        q = 2 * to % half + 2 * to // half if x_last else to
        to = to * size + offset
        there = pl.multiple_of(at + first + (2 * q + 1 - bit) * block, 32)
        here = pl.multiple_of(at + first + (2 * q + bit) * block, 32)
        send_ref[to : to + rows, :] = total_ref[pl.ds(there, rows), :].astype(BF16)
        keep_ref[to // size, offset : offset + rows, :] = total_ref[pl.ds(here, rows), :]


def fetch(pairs, sems):
    copies = []
    for at, (source, target) in enumerate(pairs):
        copies.append(pltpu.make_async_copy(source, target, sems.at[at]))
    for copy in copies:
        copy.start()
    return copies


def tile_pairs(source, target, tile):
    return [
        (source.at[pl.ds(at, tile)], target.at[pl.ds(at, tile)])
        for at in range(0, source.shape[0], tile)
    ]


def slot_owner(origin, shape, dim, places):
    row = lax.broadcasted_iota(jnp.int32, shape, dim)
    return lax.div(row, places) ^ origin, lax.rem(row, places)


def bit_slots(bit, shape, places):
    row = lax.broadcasted_iota(jnp.int32, shape, 0)
    column = lax.broadcasted_iota(jnp.int32, shape, 1)
    slot, place = lax.div(column, places), lax.rem(column, places)
    rank = ((slot >> (bit + 1)) << bit) | (slot & (2**bit - 1))
    return ((slot >> bit) & 1 == 1) & (rank * places + place == row)


def slots_out(bit, slots, places):
    rows = slots.shape[0]
    return dot(ones_where(bit_slots(bit, (rows // 2, rows), places)), slots).astype(BF16)


def slots_in(bit, slots, got, places):
    rows = slots.shape[0]
    row = lax.broadcasted_iota(jnp.int32, (rows, rows), 0)
    column = lax.broadcasted_iota(jnp.int32, (rows, rows), 1)
    kept = (row == column) & ((lax.div(column, places) >> bit) & 1 == 0)
    moved = ones_where(bit_slots(bit, (rows // 2, rows), places))
    return (dot(ones_where(kept), slots) + dot(moved, got, TN)).astype(BF16)


def outgoing_kernel(
    index_hbm, node_hbm, slots_ref, inner_ref, outer_ref, index_ref, node_ref, sems
):
    for copy in fetch([(index_hbm, index_ref), (node_hbm, node_ref)], sems):
        copy.wait()
    places, tiles = index_ref.shape[1], index_ref.shape[2]
    nodes, latent = node_ref.shape
    place = lax.broadcasted_iota(jnp.int32, (nodes, tiles), 0)
    for j in range(places):
        picks = ones_where(place == index_ref[0, j : j + 1, :])
        slots_ref[:, j, :] = dot(picks, node_ref[...], TN).astype(BF16)
    odd = lax.rem(lax.axis_index("tiles"), 2)
    inner_ref[...] = node_ref[pl.ds(pl.multiple_of((1 - odd) * (nodes - NEAR), NEAR), NEAR), :]
    outer_ref[...] = node_ref[pl.ds(pl.multiple_of(odd * (nodes - NEAR), NEAR), NEAR), :]


def table_index(raw, tiles, places, nodes):
    far = raw - (nodes + 2 * NEAR)
    far = nodes + 2 * NEAR + lax.rem(far, places) * tiles + lax.div(far, places)
    rim = jnp.where(raw < NEAR, raw + nodes, raw)
    own = jnp.where((raw >= NEAR) & (raw < NEAR + nodes), raw - NEAR, rim)
    return jnp.where(raw >= nodes + 2 * NEAR, far, own)


def prepare_kernel(
    tiles, places,
    node_hbm, w1_hbm, sender_hbm, receiver_hbm, b1_hbm, edge_hbm,
    node_ref, receiver_ref, moved_ref, partial_ref,
    edge_ref, w1_ref, weights, sender_ref, b1_ref, sems, edge_sems,
):
    edges, latent = edge_ref.shape
    nodes = node_ref.shape[0]
    copies = fetch(
        [
            (node_hbm, node_ref), (w1_hbm, w1_ref), (sender_hbm, sender_ref),
            (receiver_hbm, receiver_ref), (b1_hbm, b1_ref),
        ],
        sems,
    )
    edge_copies = fetch(tile_pairs(edge_hbm, edge_ref, edges // 2), edge_sems)
    for copy in copies:
        copy.wait()
    moved_ref[...] = table_index(sender_ref[...], tiles, places, nodes)
    weights[:latent, :] = w1_ref[:latent, :]
    weights[latent : latent + nodes, :] = dot(
        node_ref[...], w1_ref[latent : 2 * latent, :]
    ).astype(BF16)
    weights[latent + nodes :, :] = dot(node_ref[...], w1_ref[2 * latent :, :]).astype(BF16)
    for copy in edge_copies:
        copy.wait()
    for step in range(edges // TILE):
        tile = slice(step * TILE, (step + 1) * TILE)
        senders = pick_columns(index_columns(moved_ref, step, TILE), 0, nodes)
        receivers = pick_columns(index_columns(receiver_ref, step, TILE), 0, nodes)
        inputs = jnp.concatenate([edge_ref[tile, :]] + senders + receivers, axis=1)
        partial_ref[tile, :] = dot(inputs, weights[...]) + b1_ref[...]


def forward_kernel(
    tiles, places, fast,
    w1_hbm, edge_hbm, cot_hbm, w2_hbm, nw1_hbm, nw2_hbm, ncot_hbm,
    b2_hbm, gain_hbm, nb1_hbm, nb2_hbm, ngain_hbm, count_hbm,
    inner_ref, outer_ref, far_ref, known_ref, node_ref, receiver_ref, moved_ref,
    w1_ref, edge_ref, cot_ref, w2_ref, gain_ref,
    hidden_ref, slope_ref, normed_ref, inverse_ref, table_ref, dsum_ref, base_ref,
    gsend_ref, gkeep_ref,
    weights, summed, grads, nw1_ref, nw2_ref, ncot_ref,
    b2_ref, nb1_ref, nb2_ref, ngain_ref, count_ref, sems,
):
    here = lax.axis_index("tiles")
    edges, latent = hidden_ref.shape
    nodes = node_ref.shape[0]
    rows = table_ref.shape[0]
    steps = edges // TILE

    senders_part = pl.ds(latent, latent)
    early = fetch(
        [
            (w1_hbm.at[senders_part], w1_ref.at[senders_part]), (count_hbm, count_ref),
            (b2_hbm, b2_ref), (gain_hbm, gain_ref), (w2_hbm, w2_ref),
        ],
        sems,
    )
    edges_part, receivers_part = pl.ds(0, latent), pl.ds(2 * latent, latent)
    late = fetch(
        [
            (nw1_hbm, nw1_ref), (nw2_hbm, nw2_ref), (ncot_hbm, ncot_ref),
            (nb1_hbm, nb1_ref), (nb2_hbm, nb2_ref), (ngain_hbm, ngain_ref),
            (cot_hbm, cot_ref), (edge_hbm, edge_ref),
            (w1_hbm.at[edges_part], w1_ref.at[edges_part]),
            (w1_hbm.at[receivers_part], w1_ref.at[receivers_part]),
        ],
        sems.at[pl.ds(len(early), 10)],
    )

    table_ref[:nodes, :] = node_ref[...]
    odd = lax.rem(here, 2)
    table_ref[pl.ds(pl.multiple_of(nodes + (1 - odd) * NEAR, NEAR), NEAR), :] = inner_ref[...]
    table_ref[pl.ds(pl.multiple_of(nodes + odd * NEAR, NEAR), NEAR), :] = outer_ref[...]
    for j in range(places):
        at = nodes + 2 * NEAR + j * tiles
        table_ref[at : at + tiles, :] = far_ref[:, j, :]
    used = nodes + 2 * NEAR + places * tiles
    if used < rows:
        table_ref[used:, :] = jnp.zeros((rows - used, latent), BF16)
    early[0].wait()
    weights[...] = dot(table_ref[nodes:, :], w1_ref[latent : 2 * latent, :]).astype(BF16)
    for copy in early[1:]:
        copy.wait()
    live = count_ref[here]

    def activate(step):
        tile = slice(step * TILE, (step + 1) * TILE)
        senders = pick_columns(index_columns(moved_ref, step, TILE), nodes, rows)
        preact = known_ref[tile, :] + dot(jnp.concatenate(senders, axis=1), weights[...])
        sig = sigmoid(preact)
        slope_ref[tile, :] = (sig * (1.0 + preact * (1.0 - sig))).astype(BF16)
        hidden_ref[tile, :] = (preact * sig).astype(BF16)

    def normalize(step):
        tile = slice(step * TILE, (step + 1) * TILE)
        centred, inverse = norm_forward(dot(hidden_ref[tile, :], w2_ref[...]) + b2_ref[...])
        position = step * TILE + lax.broadcasted_iota(jnp.int32, inverse.shape, 0)
        inverse = jnp.where(position < live, inverse, 0.0)
        normed = centred * inverse
        normed_ref[tile, :] = normed
        inverse_ref[tile, :] = jnp.broadcast_to(inverse, (TILE, LANES))
        update = (normed * gain_ref[...]).astype(BF16)
        part = dot(pick_rows(receiver_ref, step, TILE, nodes), update)
        if step == 0:
            summed[...] = part
        else:
            summed[...] += part

    for step in range(steps + 1):
        if step < steps:
            activate(step)
        if step > 0:
            normalize(step - 1)

    for copy in late:
        copy.wait()
    node_in = jnp.concatenate([node_ref[...], summed[...].astype(BF16)], axis=1)
    preact_n = dot(node_in, nw1_ref[...]) + nb1_ref[...]
    sig_n = sigmoid(preact_n)
    hidden_n = (preact_n * sig_n).astype(BF16)
    centred_n, inverse_n = norm_forward(dot(hidden_n, nw2_ref[...]) + nb2_ref[...])
    cot = ncot_ref[...].astype(F32)
    dout = norm_backward(cot * ngain_ref[...], centred_n * inverse_n, inverse_n)
    slope_n = sig_n * (1.0 + preact_n * (1.0 - sig_n))
    dpre = (dot(dout, nw2_ref[...], NT) * slope_n).astype(BF16)
    grads[: 2 * latent, :] = dot(node_in, dpre, TN)
    grads[2 * latent :, :] = dot(hidden_n, dout, TN)
    base_ref[...] = cot + dot(dpre, nw1_ref[:latent, :], NT)
    dsum_ref[...] = dot(dpre, nw1_ref[latent:, :], NT).astype(BF16)
    if fast:
        bit = lax.rem(here, 2)
        first = 2 * latent // tiles
        split_halves(bit, grads, 0, first, 0, first, gsend_ref, gkeep_ref, 0, True)
        second = latent // tiles
        split_halves(bit, grads, 2 * latent, second, 0, second, gsend_ref, gkeep_ref, first, True)
    else:
        gkeep_ref[...] = grads[: 2 * latent, :]
        gsend_ref[...] = grads[2 * latent :, :]


def slope_kernel(
    tiles, fast, start, last,
    cot_ref, receiver_ref, dsum_ref, hidden_ref, slope_ref, normed_ref, inverse_ref, w2_ref, gain_ref,
    *refs,
):
    dpre_ref, *out_refs, grads, dout = refs[0 if start == 0 else 1 :]
    here = lax.axis_index("tiles")
    edges, latent = dpre_ref.shape
    nodes = dsum_ref.shape[0]
    steps = edges // TILE
    grads[...] = jnp.zeros_like(grads) if start == 0 else refs[0][...]

    def outer(step):
        tile = slice(step * TILE, (step + 1) * TILE)
        whole = slice(start + step * TILE, start + (step + 1) * TILE)
        receivers = jnp.concatenate(
            pick_columns(index_columns(receiver_ref, start // TILE + step, TILE), 0, nodes), axis=1
        )
        grad_update = cot_ref[whole, :].astype(F32) + dot(receivers, dsum_ref[...])
        inverse = inverse_ref[whole, :1]
        dout[tile, :] = norm_backward(grad_update * gain_ref[...], normed_ref[whole, :], inverse)

    def inner(step):
        tile = slice(step * TILE, (step + 1) * TILE)
        whole = slice(start + step * TILE, start + (step + 1) * TILE)
        dpre_ref[tile, :] = (
            dot(dout[tile, :], w2_ref[...], NT) * slope_ref[whole, :].astype(F32)
        ).astype(BF16)
        grads[...] += dot(hidden_ref[whole, :], dout[tile, :], TN)

    for step in range(steps + 1):
        if step < steps:
            outer(step)
        if step > 0:
            inner(step - 1)

    if not last:
        out_refs[0][...] = grads[...]
    elif fast:
        rows = latent // tiles
        split_halves(lax.rem(here, 2), grads, 0, rows, 0, rows, *out_refs, 0)
    else:
        out_refs[0][...] = jnp.zeros_like(out_refs[0])
        out_refs[1][...] = grads[...]


def first_kernel(
    tiles, places, fast,
    dpre_a_ref, dpre_b_ref, edge_ref, sender_ref, receiver_ref, table_ref, node_ref, w1_ref, base_ref,
    *refs,
):
    out_refs, (grads, sums, rims) = refs[:-3], refs[-3:]
    inner_ref, outer_ref, far_ref, partial_ref = out_refs[:4]
    here = lax.axis_index("tiles")
    edges, latent = edge_ref.shape
    early = dpre_a_ref.shape[0]
    nodes = node_ref.shape[0]
    rows = table_ref.shape[0]

    for step in range(edges // TILE):
        tile = slice(step * TILE, (step + 1) * TILE)
        if step * TILE < early:
            dpre = dpre_a_ref[tile, :]
        else:
            dpre = dpre_b_ref[step * TILE - early : (step + 1) * TILE - early, :]
        part = dot(edge_ref[tile, :], dpre, TN)
        picks = jnp.concatenate(
            [
                pick_rows(sender_ref, step, TILE, rows),
                pick_rows(receiver_ref, step, TILE, nodes),
            ],
            axis=0,
        )
        scattered = dot(picks, dpre)
        if step == 0:
            grads[:latent, :] = part
            sums[...] = scattered
        else:
            grads[:latent, :] += part
            sums[...] += scattered

    by_sender = sums[:rows, :].astype(BF16)
    by_receiver = sums[rows:, :].astype(BF16)
    grads[latent : 2 * latent, :] = dot(table_ref[...], by_sender, TN)
    grads[2 * latent :, :] = dot(node_ref[...], by_receiver, TN)
    back = dot(by_sender, w1_ref[latent : 2 * latent, :], NT)
    far = back[nodes + 2 * NEAR : nodes + 2 * NEAR + places * tiles, :].astype(BF16)
    owner, at = slot_owner(here if fast else 0, (places * tiles, places * tiles), 0, places)
    column = lax.broadcasted_iota(jnp.int32, (places * tiles, places * tiles), 1)
    far = dot(ones_where(at * tiles + owner == column), far).astype(BF16)
    far_ref[...] = far
    if fast:
        bit = lax.rem(here, 2)
        block = 3 * latent // tiles
        at = 0
        for send_ref, keep_ref in (out_refs[4:6], out_refs[6:8], out_refs[8:10]):
            part = keep_ref.shape[1]
            split_halves(bit, grads, 0, block, at, part, send_ref, keep_ref, 0)
            at += part
        out_refs[4][tiles // 2 * out_refs[5].shape[1] :, :] = slots_out(0, far, places)
    else:
        out_refs[4][...] = grads[...]
    rims[...] = back[nodes : nodes + 2 * NEAR, :]
    odd = lax.rem(here, 2)
    inner_ref[...] = rims[pl.ds(pl.multiple_of((1 - odd) * NEAR, NEAR), NEAR), :].astype(BF16)
    outer_ref[...] = rims[pl.ds(pl.multiple_of(odd * NEAR, NEAR), NEAR), :].astype(BF16)
    partial_ref[...] = (
        base_ref[...] + back[:nodes, :] + dot(by_receiver, w1_ref[2 * latent :, :], NT)
    )


def edge_kernel(dpre_a_ref, dpre_b_ref, cot_ref, w1_ref, out_hbm, out_ref, sems):
    early, latent = dpre_a_ref.shape
    copies = []
    for dpre_ref, base in ((dpre_a_ref, 0), (dpre_b_ref, early)):
        for at in range(0, early, TILE):
            part = slice(at, at + TILE)
            tile = pl.ds(base + at, TILE)
            out_ref[tile, :] = (
                cot_ref[tile, :].astype(F32) + dot(dpre_ref[part, :], w1_ref[:latent, :], NT)
            ).astype(BF16)
            copy = pltpu.make_async_copy(
                out_ref.at[tile], out_hbm.at[tile], sems.at[(base + at) // TILE]
            )
            copy.start()
            copies.append(copy)
    for copy in copies:
        copy.wait()


def node_kernel(fast, index_ref, partial_ref, inner_ref, outer_ref, slots_ref, *refs):
    out_ref, sums = refs[-2:]
    places, tiles = index_ref.shape[1], index_ref.shape[2]
    nodes = partial_ref.shape[0]
    origin = lax.axis_index("tiles") if fast else 0
    slots = slots_ref[...]
    if fast:
        got_ref = refs[0]
        slots = slots_in(3, slots, got_ref[got_ref.shape[0] - slots.shape[0] // 2 :, :], places)
    place = lax.broadcasted_iota(jnp.int32, (nodes, tiles), 0)
    owner, at = slot_owner(origin, (tiles, places * tiles), 1, places)
    row = lax.broadcasted_iota(jnp.int32, (tiles, places * tiles), 0)
    total = partial_ref[...]
    for j in range(places):
        picks = ones_where(place == index_ref[0, j : j + 1, :])
        far = dot(ones_where((owner == row) & (at == j)), slots).astype(BF16)
        total = total + dot(picks, far)
    sums[...] = total
    odd = lax.rem(lax.axis_index("tiles"), 2)
    inner_at = pl.ds(pl.multiple_of((1 - odd) * (nodes - NEAR), NEAR), NEAR)
    outer_at = pl.ds(pl.multiple_of(odd * (nodes - NEAR), NEAR), NEAR)
    sums[inner_at, :] += inner_ref[...].astype(F32)
    sums[outer_at, :] += outer_ref[...].astype(F32)
    out_ref[...] = sums[...].astype(BF16)


def halve_kernel(shift, count, places, *refs):
    keeps, gots = refs[:count], refs[count : 2 * count]
    rest = refs[2 * count :]
    send_ref, kept_ref = rest[-2:] if not places else rest[-3:-1]
    size = kept_ref.shape[1]
    bit = lax.rem(lax.div(lax.axis_index("tiles"), 2**shift), 2)
    at = 0
    for keep_ref, got_ref in zip(keeps, gots):
        blocks, rows = keep_ref.shape[:2]
        for q in range(blocks // 2):
            there, here = 2 * q + 1 - bit, 2 * q + bit
            got_there = got_ref[pl.ds(pl.multiple_of(there * rows, 32), rows), :].astype(F32)
            got_here = got_ref[pl.ds(pl.multiple_of(here * rows, 32), rows), :].astype(F32)
            to = q * size + at
            send_ref[to : to + rows, :] = (keep_ref[there] + got_there).astype(BF16)
            kept_ref[q, at : at + rows, :] = keep_ref[here] + got_here
        at += rows
    if places:
        slots_ref, moved_ref = rest[0], rest[-1]
        half = slots_ref.shape[0] // 2
        got_ref = gots[0]
        slots = slots_in(shift - 1, slots_ref[...], got_ref[got_ref.shape[0] - half :, :], places)
        moved_ref[...] = slots
        send_ref[send_ref.shape[0] - half :, :] = slots_out(shift, slots, places)


def finish_kernel(count, splits, *refs):
    out_refs = refs[2 * count :]
    rows = [0] * len(out_refs)
    for keep_ref, got_ref, parts in zip(refs[:count], refs[count : 2 * count], splits):
        at = 0
        for which, size in parts:
            first = rows[which]
            out_refs[which][first : first + size, :] = (
                keep_ref[0, at : at + size, :] + got_ref[at : at + size, :].astype(F32)
            )
            at += size
            rows[which] += size


def shaped(shape, dtype):
    return jax.ShapeDtypeStruct(shape, dtype)


def in_hbm(*arrays):
    return [pltpu.with_memory_space_constraint(array, pltpu.HBM) for array in arrays]


def call(kernel, name, out_shape, args, hbm=0, scratch=(), out_specs=None, flops=0):
    vmem = pl.BlockSpec(memory_space=pltpu.VMEM)
    return pl.pallas_call(
        kernel,
        in_specs=[pl.BlockSpec(memory_space=pltpu.HBM)] * hbm + [vmem] * (len(args) - hbm),
        out_specs=out_specs or [vmem] * len(out_shape),
        out_shape=out_shape,
        scratch_shapes=scratch,
        compiler_params=pltpu.CompilerParams(vmem_limit_bytes=16 * MIB),
        cost_estimate=pl.CostEstimate(flops=flops, bytes_accessed=flops // 100, transcendentals=0),
        name=name,
    )(*in_hbm(*args[:hbm]), *args[hbm:])


def swap(tiles, bit, send):
    return lax.ppermute(send, "tiles", [(i, i ^ bit) for i in range(tiles)])


def halve(shift, keeps, gots, slots=None, places=0, flops=0):
    half, _, width = keeps[0].shape
    rows = sum(keep.shape[1] for keep in keeps)
    extra = [] if slots is None else [slots]
    sent = half // 2 * rows + sum(slots.shape[0] // 2 for slots in extra)
    return call(
        functools.partial(halve_kernel, shift, len(keeps), places),
        "halve",
        [pltpu.VMEM((sent, width), BF16), pltpu.VMEM((half // 2, rows, width), F32)]
        + [pltpu.VMEM(slots.shape, BF16) for slots in extra],
        [*keeps, *gots, *extra],
        flops=flops,
    )


def finish(keeps, gots, splits, sizes):
    return call(
        functools.partial(finish_kernel, len(keeps), splits),
        "finish",
        [shaped((size, keeps[0].shape[-1]), F32) for size in sizes],
        [*keeps, *gots],
    )


def after(value, *others):
    return lax.optimization_barrier((value, *others))[0]


def shards(
    node_latent, edge_latent, node_cot, edge_cot,
    edge_w1, edge_b1, edge_w2, edge_b2, edge_gain,
    node_w1, node_b1, node_w2, node_b2, node_gain,
    send_index, edge_sender, edge_receiver, edge_count,
):
    tiles = lax.axis_size("tiles")
    nodes, latent = node_latent.shape
    edges = edge_latent.shape[0]
    places = send_index.shape[2]
    steps = edges // TILE
    used = nodes + 2 * NEAR + places * tiles
    rows = -(-used // LANES) * LANES
    fast = tiles == 16
    half = tiles // 2
    inside = [(i, i ^ 1) for i in range(tiles)]
    across = [(i, i + 1 if i % 2 else i - 1) for i in range(1, tiles - 1)]
    sender = edge_sender.reshape(edges // LANES, LANES)
    receiver = edge_receiver.reshape(edges // LANES, LANES)
    listed = jnp.swapaxes(send_index, 1, 2)
    row = lambda vector: vector.reshape(1, -1)
    vmem = pltpu.VMEM

    if fast:
        grad_shapes = lambda count: [
            vmem((count // 2, latent), BF16),
            vmem((half, count // tiles, latent), F32),
        ]
    else:
        grad_shapes = lambda count: [shaped((latent, latent), F32), shaped((count, latent), F32)]

    outgoing, inner, outer = call(
        outgoing_kernel,
        "outgoing",
        [
            shaped((tiles, places, latent), BF16),
            vmem((NEAR, latent), BF16),
            vmem((NEAR, latent), BF16),
        ],
        [listed, node_latent],
        hbm=2,
        scratch=[vmem(listed.shape, jnp.int32), vmem((nodes, latent), BF16), pltpu.SemaphoreType.DMA((2,))],
    )
    inner = lax.ppermute(inner, "tiles", inside)
    outer = lax.ppermute(outer, "tiles", across)
    slots = lax.all_to_all(outgoing, "tiles", split_axis=0, concat_axis=0, tiled=True)
    node_kept, receiver_kept, moved, preact = call(
        functools.partial(prepare_kernel, tiles, places),
        "prepare",
        [
            vmem((nodes, latent), BF16),
            vmem(receiver.shape, jnp.int32), vmem(sender.shape, jnp.int32),
            vmem((edges, latent), F32),
        ],
        [node_latent, edge_w1, after(sender, outgoing), receiver, row(edge_b1), edge_latent],
        hbm=6,
        scratch=[
            vmem((edges, latent), BF16), vmem(edge_w1.shape, BF16),
            vmem((latent + 2 * nodes, latent), BF16), vmem(sender.shape, jnp.int32),
            vmem((1, latent), F32), pltpu.SemaphoreType.DMA((5,)), pltpu.SemaphoreType.DMA((2,)),
        ],
        flops=AHEAD,
    )

    (
        w1_kept, edge_kept, cot_kept, w2_kept, gain_kept,
        hidden, slope, normed, inverse, table, dsum, base, node_send, node_keep,
    ) = call(
        functools.partial(forward_kernel, tiles, places, fast),
        "forward",
        [
            vmem(edge_w1.shape, BF16), vmem((edges, latent), BF16), vmem((edges, latent), BF16),
            vmem(edge_w2.shape, BF16), vmem((1, latent), F32),
            vmem((edges, latent), BF16), vmem((edges, latent), BF16), vmem((edges, latent), F32),
            vmem((edges, LANES), F32), vmem((rows, latent), BF16),
            vmem((nodes, latent), BF16), vmem((nodes, latent), F32),
        ] + grad_shapes(3 * latent if fast else 2 * latent),
        [
            edge_w1, edge_latent, edge_cot, edge_w2, node_w1, node_w2, node_cot,
            row(edge_b2), row(edge_gain), row(node_b1), row(node_b2), row(node_gain), edge_count,
            inner, outer, slots, preact, node_kept, receiver_kept, moved,
        ],
        hbm=13,
        scratch=[
            vmem((rows - nodes, latent), BF16), vmem((nodes, latent), F32),
            vmem((3 * latent, latent), F32), vmem(node_w1.shape, BF16), vmem(node_w2.shape, BF16),
            vmem((nodes, latent), BF16),
        ] + [vmem((1, latent), F32)] * 4 + [
            pltpu.SMEM(edge_count.shape, jnp.int32), pltpu.SemaphoreType.DMA((15,)),
        ],
    )

    early = edges // 2

    def slope_call(start, last, dsum, outs, more):
        return call(
            functools.partial(slope_kernel, tiles, fast, start, last),
            "slope",
            [vmem((early, latent), BF16)] + outs,
            [cot_kept, receiver_kept, dsum, hidden, slope, normed, inverse, w2_kept, gain_kept] + more,
            scratch=[vmem((latent, latent), F32), vmem((early, latent), BF16)],
        )

    dpre_a, grads = slope_call(0, False, dsum, [vmem((latent, latent), F32)], [])
    if fast:
        send, chain = halve(2, [after(node_keep, grads)], [swap(tiles, 1, node_send)])
        dsum = after(dsum, send)
        got = swap(tiles, 4, send)
    dpre_b, second_send, second_keep = slope_call(
        early, True, dsum, grad_shapes(latent), [grads]
    )
    if fast:
        got_second = swap(tiles, 1, second_send)

    per = latent // tiles
    to_inner, to_outer, to_far, partial, *first = call(
        functools.partial(first_kernel, tiles, places, fast),
        "first",
        [
            vmem((NEAR, latent), BF16),
            vmem((NEAR, latent), BF16),
            vmem((tiles * places, latent), BF16) if fast else shaped((tiles * places, latent), BF16),
            vmem((nodes, latent), F32),
        ] + (
            [
                vmem((half * per + tiles * places // 2, latent), BF16),
                vmem((half, per, latent), F32),
                vmem((half * per, latent), BF16), vmem((half, per, latent), F32),
                vmem((half * per, latent), BF16), vmem((half, per, latent), F32),
            ]
            if fast else [shaped((3 * latent, latent), F32)]
        ),
        [dpre_a, dpre_b, edge_kept, moved, receiver_kept, table, node_kept, w1_kept, base],
        scratch=[
            vmem((3 * latent, latent), F32), vmem((rows + nodes, latent), F32),
            vmem((2 * NEAR, latent), F32),
        ],
    )

    (grad_edge,) = call(
        edge_kernel,
        "edge",
        [shaped((edges, latent), BF16)],
        [after(dpre_a, partial), dpre_b, cot_kept, w1_kept],
        out_specs=[pl.BlockSpec(memory_space=pltpu.HBM)],
        scratch=[vmem((edges, latent), BF16), pltpu.SemaphoreType.DMA((steps,))],
    )

    if fast:
        send_a, keep_a, send_more, keep_more, send_b, keep_b = first
        send_a, chain_a, slots = halve(
            1,
            [after(keep_a, grad_edge), keep_more],
            [swap(tiles, 1, send_a), swap(tiles, 1, send_more)],
            to_far,
            places,
     )
        got_a = swap(tiles, 2, send_a)
        send_b, chain_b = halve(
            1, [after(keep_b, send_a), second_keep], [swap(tiles, 1, send_b), got_second]
     )
        got_b = swap(tiles, 2, send_b)
        send, chain = halve(3, [after(chain, send_b)], [got], flops=AHEAD)
        got = swap(tiles, 8, send)
        to_inner, to_outer = lax.optimization_barrier((to_inner, to_outer, send))[:2]
        inner = lax.ppermute(to_inner, "tiles", inside)
        outer = lax.ppermute(to_outer, "tiles", across)
        send_a, chain_a, slots = halve(2, [after(chain_a, send)], [got_a], slots, places)
        got_a = swap(tiles, 4, send_a)
        send_b, chain_b = halve(2, [after(chain_b, send_a, inner, outer)], [got_b])
        got_b = swap(tiles, 4, send_b)
        send, chain = halve(1, [after(chain, send_b)], [got])
        got = swap(tiles, 2, send)
        chain_a = after(chain_a, send)
        send_a, chain_a, slots = halve(3, [chain_a], [got_a], slots, places, AHEAD)
        got_a = swap(tiles, 8, send_a)
        chain_b = after(chain_b, send_a)
        send_b, chain_b = halve(3, [chain_b], [got_b], flops=AHEAD)
        got_b = swap(tiles, 8, send_b)
        returned = [slots, got_a]
        grad_edge_w1, grad_edge_w2, grad_node_w1, grad_node_w2 = finish(
            [chain, chain_a, chain_b],
            [got, got_a, got_b],
            [[(2, 2 * per), (3, per)], [(0, 2 * per)], [(0, per), (1, per)]],
            [3 * per, per, 2 * per, per],
        )
    else:
        inner = lax.ppermute(to_inner, "tiles", inside)
        outer = lax.ppermute(to_outer, "tiles", across)
        returned = [lax.all_to_all(to_far, "tiles", split_axis=0, concat_axis=0, tiled=True)]
        scatter = functools.partial(
            lax.psum_scatter, axis_name="tiles", scatter_dimension=0, tiled=True
        )
        grad_node_w1, grad_node_w2 = scatter(node_keep), scatter(node_send)
        grad_edge_w1, grad_edge_w2 = scatter(first[0]), scatter(second_keep)
    (grad_node,) = call(
        functools.partial(node_kernel, fast),
        "node",
        [shaped((nodes, latent), BF16)],
        [listed, partial, inner, outer, *returned],
        scratch=[vmem((nodes, latent), F32)],
    )
    return (grad_node, grad_edge, grad_edge_w1, grad_edge_w2, grad_node_w1, grad_node_w2)


def solution(mesh):
    split = P(("groups", "tiles"), None)
    return jax.shard_map(
        shards,
        mesh=mesh,
        in_specs=(split,) * 4
        + (P(),) * 10
        + (
            P(("groups", "tiles"), None, None),
            P(("groups", "tiles")),
            P(("groups", "tiles")),
            P("groups"),
        ),
        out_specs=(split,) * 6,
        check_vma=False,
    )
```

```python
import functools

import jax
import jax.numpy as jnp
from jax import lax
from jax.experimental import pallas as pl
from jax.experimental.pallas import tpu as pltpu
from jax.sharding import PartitionSpec as P

NEAR = 64
EPSILON = 1e-05
TILE = 256
LANES = 128
F32 = jnp.float32
BF16 = jnp.bfloat16
MIB = 1024 * 1024
AHEAD = 10**10

NN = (((1,), (0,)), ((), ()))
NT = (((1,), (1,)), ((), ()))
TN = (((0,), (0,)), ((), ()))


def dot(a, b, dims=NN):
    return lax.dot_general(a, b, dims, preferred_element_type=F32)


def sigmoid(x):
    return 0.5 * jnp.tanh(0.5 * x) + 0.5


def row_mean(x):
    return jnp.sum(x, axis=-1, keepdims=True) * (1.0 / x.shape[-1])


def ones_where(mask):
    return jnp.where(mask, 1.0, 0.0).astype(BF16)


def index_columns(idx_ref, step, tile):
    per = tile // LANES
    parts = []
    for j in range(per):
        row = idx_ref[pl.ds(step * per + j, 1), :]
        parts.append(jnp.transpose(jnp.broadcast_to(row, (LANES, LANES))))
    return jnp.concatenate(parts, axis=0)


def pick_columns(columns, start, stop):
    lane = lax.broadcasted_iota(jnp.int32, columns.shape, 1)
    return [ones_where(columns == lane + at) for at in range(start, stop, LANES)]


def pick_rows(idx_ref, step, tile, width):
    per = tile // LANES
    row = jnp.concatenate([idx_ref[pl.ds(step * per + j, 1), :] for j in range(per)], axis=1)
    return ones_where(lax.broadcasted_iota(jnp.int32, (width, tile), 0) == row)


def norm_forward(out):
    centred = out - row_mean(out)
    inverse = lax.rsqrt(row_mean(centred * centred) + EPSILON)
    return centred, inverse


def norm_backward(scaled, normed, inverse):
    return (
        inverse * (scaled - row_mean(scaled) - normed * row_mean(scaled * normed))
    ).astype(BF16)


def split_halves(bit, total_ref, at, block, first, rows, send_ref, keep_ref, offset, x_last=False):
    half, size = keep_ref.shape[:2]
    for to in range(half):
        q = 2 * to % half + 2 * to // half if x_last else to
        to = to * size + offset
        there = pl.multiple_of(at + first + (2 * q + 1 - bit) * block, 32)
        here = pl.multiple_of(at + first + (2 * q + bit) * block, 32)
        send_ref[to : to + rows, :] = total_ref[pl.ds(there, rows), :].astype(BF16)
        keep_ref[to // size, offset : offset + rows, :] = total_ref[pl.ds(here, rows), :]


def fetch(pairs, sems):
    copies = []
    for at, (source, target) in enumerate(pairs):
        copies.append(pltpu.make_async_copy(source, target, sems.at[at]))
    for copy in copies:
        copy.start()
    return copies


def tile_pairs(source, target, tile):
    return [
        (source.at[pl.ds(at, tile)], target.at[pl.ds(at, tile)])
        for at in range(0, source.shape[0], tile)
    ]


def slot_owner(origin, shape, dim, places):
    row = lax.broadcasted_iota(jnp.int32, shape, dim)
    return lax.div(row, places) ^ origin, lax.rem(row, places)


def bit_slots(bit, shape, places):
    row = lax.broadcasted_iota(jnp.int32, shape, 0)
    column = lax.broadcasted_iota(jnp.int32, shape, 1)
    slot, place = lax.div(column, places), lax.rem(column, places)
    rank = ((slot >> (bit + 1)) << bit) | (slot & (2**bit - 1))
    return ((slot >> bit) & 1 == 1) & (rank * places + place == row)


def slots_out(bit, slots, places):
    rows = slots.shape[0]
    return dot(ones_where(bit_slots(bit, (rows // 2, rows), places)), slots).astype(BF16)


def slots_in(bit, slots, got, places):
    rows = slots.shape[0]
    row = lax.broadcasted_iota(jnp.int32, (rows, rows), 0)
    column = lax.broadcasted_iota(jnp.int32, (rows, rows), 1)
    kept = (row == column) & ((lax.div(column, places) >> bit) & 1 == 0)
    moved = ones_where(bit_slots(bit, (rows // 2, rows), places))
    return (dot(ones_where(kept), slots) + dot(moved, got, TN)).astype(BF16)


def outgoing_kernel(
    index_hbm, node_hbm, slots_ref, inner_ref, outer_ref, index_ref, node_ref, sems
):
    for copy in fetch([(index_hbm, index_ref), (node_hbm, node_ref)], sems):
        copy.wait()
    places, tiles = index_ref.shape[1], index_ref.shape[2]
    nodes, latent = node_ref.shape
    place = lax.broadcasted_iota(jnp.int32, (nodes, tiles), 0)
    for j in range(places):
        picks = ones_where(place == index_ref[0, j : j + 1, :])
        slots_ref[:, j, :] = dot(picks, node_ref[...], TN).astype(BF16)
    odd = lax.rem(lax.axis_index("tiles"), 2)
    inner_ref[...] = node_ref[pl.ds(pl.multiple_of((1 - odd) * (nodes - NEAR), NEAR), NEAR), :]
    outer_ref[...] = node_ref[pl.ds(pl.multiple_of(odd * (nodes - NEAR), NEAR), NEAR), :]


def table_index(raw, tiles, places, nodes):
    far = raw - (nodes + 2 * NEAR)
    far = nodes + 2 * NEAR + lax.rem(far, places) * tiles + lax.div(far, places)
    rim = jnp.where(raw < NEAR, raw + nodes, raw)
    own = jnp.where((raw >= NEAR) & (raw < NEAR + nodes), raw - NEAR, rim)
    return jnp.where(raw >= nodes + 2 * NEAR, far, own)


def prepare_kernel(
    tiles, places,
    node_hbm, w1_hbm, sender_hbm, receiver_hbm, b1_hbm, edge_hbm,
    node_ref, receiver_ref, moved_ref, partial_ref,
    edge_ref, w1_ref, weights, sender_ref, b1_ref, sems, edge_sems,
):
    edges, latent = edge_ref.shape
    nodes = node_ref.shape[0]
    copies = fetch(
        [
            (node_hbm, node_ref), (w1_hbm, w1_ref), (sender_hbm, sender_ref),
            (receiver_hbm, receiver_ref), (b1_hbm, b1_ref),
        ],
        sems,
    )
    edge_copies = fetch(tile_pairs(edge_hbm, edge_ref, edges // 2), edge_sems)
    for copy in copies:
        copy.wait()
    moved_ref[...] = table_index(sender_ref[...], tiles, places, nodes)
    weights[:latent, :] = w1_ref[:latent, :]
    weights[latent : latent + nodes, :] = dot(
        node_ref[...], w1_ref[latent : 2 * latent, :]
    ).astype(BF16)
    weights[latent + nodes :, :] = dot(node_ref[...], w1_ref[2 * latent :, :]).astype(BF16)
    for copy in edge_copies:
        copy.wait()
    for step in range(edges // TILE):
        tile = slice(step * TILE, (step + 1) * TILE)
        senders = pick_columns(index_columns(moved_ref, step, TILE), 0, nodes)
        receivers = pick_columns(index_columns(receiver_ref, step, TILE), 0, nodes)
        inputs = jnp.concatenate([edge_ref[tile, :]] + senders + receivers, axis=1)
        partial_ref[tile, :] = dot(inputs, weights[...]) + b1_ref[...]


def forward_kernel(
    tiles, places, fast,
    w1_hbm, edge_hbm, cot_hbm, w2_hbm, nw1_hbm, nw2_hbm, ncot_hbm,
    b2_hbm, gain_hbm, nb1_hbm, nb2_hbm, ngain_hbm, count_hbm,
    inner_ref, outer_ref, far_ref, known_ref, node_ref, receiver_ref, moved_ref,
    w1_ref, edge_ref, cot_ref, w2_ref, gain_ref,
    hidden_ref, slope_ref, normed_ref, inverse_ref, table_ref, dsum_ref, base_ref,
    gsend_ref, gkeep_ref,
    weights, summed, grads, nw1_ref, nw2_ref, ncot_ref,
    b2_ref, nb1_ref, nb2_ref, ngain_ref, count_ref, sems,
):
    here = lax.axis_index("tiles")
    edges, latent = hidden_ref.shape
    nodes = node_ref.shape[0]
    rows = table_ref.shape[0]
    steps = edges // TILE

    senders_part = pl.ds(latent, latent)
    early = fetch(
        [
            (w1_hbm.at[senders_part], w1_ref.at[senders_part]), (count_hbm, count_ref),
            (b2_hbm, b2_ref), (gain_hbm, gain_ref), (w2_hbm, w2_ref),
        ],
        sems,
    )
    edges_part, receivers_part = pl.ds(0, latent), pl.ds(2 * latent, latent)
    late = fetch(
        [
            (nw1_hbm, nw1_ref), (nw2_hbm, nw2_ref), (ncot_hbm, ncot_ref),
            (nb1_hbm, nb1_ref), (nb2_hbm, nb2_ref), (ngain_hbm, ngain_ref),
            (cot_hbm, cot_ref), (edge_hbm, edge_ref),
            (w1_hbm.at[edges_part], w1_ref.at[edges_part]),
            (w1_hbm.at[receivers_part], w1_ref.at[receivers_part]),
        ],
        sems.at[pl.ds(len(early), 10)],
    )

    table_ref[:nodes, :] = node_ref[...]
    odd = lax.rem(here, 2)
    table_ref[pl.ds(pl.multiple_of(nodes + (1 - odd) * NEAR, NEAR), NEAR), :] = inner_ref[...]
    table_ref[pl.ds(pl.multiple_of(nodes + odd * NEAR, NEAR), NEAR), :] = outer_ref[...]
    for j in range(places):
        at = nodes + 2 * NEAR + j * tiles
        table_ref[at : at + tiles, :] = far_ref[:, j, :]
    used = nodes + 2 * NEAR + places * tiles
    if used < rows:
        table_ref[used:, :] = jnp.zeros((rows - used, latent), BF16)
    early[0].wait()
    weights[...] = dot(table_ref[nodes:, :], w1_ref[latent : 2 * latent, :]).astype(BF16)
    for copy in early[1:]:
        copy.wait()
    live = count_ref[here]

    def activate(step):
        tile = slice(step * TILE, (step + 1) * TILE)
        senders = pick_columns(index_columns(moved_ref, step, TILE), nodes, rows)
        preact = known_ref[tile, :] + dot(jnp.concatenate(senders, axis=1), weights[...])
        sig = sigmoid(preact)
        slope_ref[tile, :] = (sig * (1.0 + preact * (1.0 - sig))).astype(BF16)
        hidden_ref[tile, :] = (preact * sig).astype(BF16)

    def normalize(step):
        tile = slice(step * TILE, (step + 1) * TILE)
        centred, inverse = norm_forward(dot(hidden_ref[tile, :], w2_ref[...]) + b2_ref[...])
        position = step * TILE + lax.broadcasted_iota(jnp.int32, inverse.shape, 0)
        inverse = jnp.where(position < live, inverse, 0.0)
        normed = centred * inverse
        normed_ref[tile, :] = normed
        inverse_ref[tile, :] = jnp.broadcast_to(inverse, (TILE, LANES))
        update = (normed * gain_ref[...]).astype(BF16)
        part = dot(pick_rows(receiver_ref, step, TILE, nodes), update)
        if step == 0:
            summed[...] = part
        else:
            summed[...] += part

    for step in range(steps + 1):
        if step < steps:
            activate(step)
        if step > 0:
            normalize(step - 1)

    for copy in late:
        copy.wait()
    node_in = jnp.concatenate([node_ref[...], summed[...].astype(BF16)], axis=1)
    preact_n = dot(node_in, nw1_ref[...]) + nb1_ref[...]
    sig_n = sigmoid(preact_n)
    hidden_n = (preact_n * sig_n).astype(BF16)
    centred_n, inverse_n = norm_forward(dot(hidden_n, nw2_ref[...]) + nb2_ref[...])
    cot = ncot_ref[...].astype(F32)
    dout = norm_backward(cot * ngain_ref[...], centred_n * inverse_n, inverse_n)
    slope_n = sig_n * (1.0 + preact_n * (1.0 - sig_n))
    dpre = (dot(dout, nw2_ref[...], NT) * slope_n).astype(BF16)
    grads[: 2 * latent, :] = dot(node_in, dpre, TN)
    grads[2 * latent :, :] = dot(hidden_n, dout, TN)
    base_ref[...] = cot + dot(dpre, nw1_ref[:latent, :], NT)
    dsum_ref[...] = dot(dpre, nw1_ref[latent:, :], NT).astype(BF16)
    if fast:
        bit = lax.rem(here, 2)
        first = 2 * latent // tiles
        split_halves(bit, grads, 0, first, 0, first, gsend_ref, gkeep_ref, 0, True)
        second = latent // tiles
        split_halves(bit, grads, 2 * latent, second, 0, second, gsend_ref, gkeep_ref, first, True)
    else:
        gkeep_ref[...] = grads[: 2 * latent, :]
        gsend_ref[...] = grads[2 * latent :, :]


def slope_kernel(
    tiles, fast, start, last,
    cot_ref, receiver_ref, dsum_ref, hidden_ref, slope_ref, normed_ref, inverse_ref, w2_ref, gain_ref,
    *refs,
):
    dpre_ref, *out_refs, grads, dout = refs[0 if start == 0 else 1 :]
    here = lax.axis_index("tiles")
    edges, latent = dpre_ref.shape
    nodes = dsum_ref.shape[0]
    steps = edges // TILE
    grads[...] = jnp.zeros_like(grads) if start == 0 else refs[0][...]

    def outer(step):
        tile = slice(step * TILE, (step + 1) * TILE)
        whole = slice(start + step * TILE, start + (step + 1) * TILE)
        receivers = jnp.concatenate(
            pick_columns(index_columns(receiver_ref, start // TILE + step, TILE), 0, nodes), axis=1
        )
        grad_update = cot_ref[whole, :].astype(F32) + dot(receivers, dsum_ref[...])
        inverse = inverse_ref[whole, :1]
        dout[tile, :] = norm_backward(grad_update * gain_ref[...], normed_ref[whole, :], inverse)

    def inner(step):
        tile = slice(step * TILE, (step + 1) * TILE)
        whole = slice(start + step * TILE, start + (step + 1) * TILE)
        dpre_ref[tile, :] = (
            dot(dout[tile, :], w2_ref[...], NT) * slope_ref[whole, :].astype(F32)
        ).astype(BF16)
        grads[...] += dot(hidden_ref[whole, :], dout[tile, :], TN)

    for step in range(steps + 1):
        if step < steps:
            outer(step)
        if step > 0:
            inner(step - 1)

    if not last:
        out_refs[0][...] = grads[...]
    elif fast:
        rows = latent // tiles
        split_halves(lax.rem(here, 2), grads, 0, rows, 0, rows, *out_refs, 0)
    else:
        out_refs[0][...] = jnp.zeros_like(out_refs[0])
        out_refs[1][...] = grads[...]


def first_kernel(
    tiles, places, fast,
    dpre_a_ref, dpre_b_ref, edge_ref, sender_ref, receiver_ref, table_ref, node_ref, w1_ref, base_ref,
    *refs,
):
    out_refs, (grads, sums, rims) = refs[:-3], refs[-3:]
    inner_ref, outer_ref, far_ref, partial_ref = out_refs[:4]
    here = lax.axis_index("tiles")
    edges, latent = edge_ref.shape
    early = dpre_a_ref.shape[0]
    nodes = node_ref.shape[0]
    rows = table_ref.shape[0]

    for step in range(edges // TILE):
        tile = slice(step * TILE, (step + 1) * TILE)
        if step * TILE < early:
            dpre = dpre_a_ref[tile, :]
        else:
            dpre = dpre_b_ref[step * TILE - early : (step + 1) * TILE - early, :]
        part = dot(edge_ref[tile, :], dpre, TN)
        picks = jnp.concatenate(
            [
                pick_rows(sender_ref, step, TILE, rows),
                pick_rows(receiver_ref, step, TILE, nodes),
            ],
            axis=0,
        )
        scattered = dot(picks, dpre)
        if step == 0:
            grads[:latent, :] = part
            sums[...] = scattered
        else:
            grads[:latent, :] += part
            sums[...] += scattered

    by_sender = sums[:rows, :].astype(BF16)
    by_receiver = sums[rows:, :].astype(BF16)
    grads[latent : 2 * latent, :] = dot(table_ref[...], by_sender, TN)
    grads[2 * latent :, :] = dot(node_ref[...], by_receiver, TN)
    back = dot(by_sender, w1_ref[latent : 2 * latent, :], NT)
    rims[...] = back[nodes : nodes + 2 * NEAR, :]
    odd = lax.rem(here, 2)
    inner = rims[pl.ds(pl.multiple_of((1 - odd) * NEAR, NEAR), NEAR), :].astype(BF16)
    inner_ref[...] = inner
    outer_ref[...] = rims[pl.ds(pl.multiple_of(odd * NEAR, NEAR), NEAR), :].astype(BF16)
    far = back[nodes + 2 * NEAR : nodes + 2 * NEAR + places * tiles, :].astype(BF16)
    owner, at = slot_owner(here if fast else 0, (places * tiles, places * tiles), 0, places)
    column = lax.broadcasted_iota(jnp.int32, (places * tiles, places * tiles), 1)
    far = dot(ones_where(at * tiles + owner == column), far).astype(BF16)
    far_ref[...] = far
    if fast:
        bit = lax.rem(here, 2)
        block = 3 * latent // tiles
        at = 0
        for send_ref, keep_ref in (out_refs[4:6], out_refs[6:8], out_refs[8:10]):
            part = keep_ref.shape[1]
            split_halves(bit, grads, 0, block, at, part, send_ref, keep_ref, 0)
            at += part
        out_refs[4][tiles // 2 * out_refs[5].shape[1] :, :] = slots_out(0, far, places)
        out_refs[8][tiles // 2 * out_refs[9].shape[1] :, :] = inner
    else:
        out_refs[4][...] = grads[...]
    partial_ref[...] = (
        base_ref[...] + back[:nodes, :] + dot(by_receiver, w1_ref[2 * latent :, :], NT)
    )


def edge_kernel(dpre_a_ref, dpre_b_ref, cot_ref, w1_ref, out_hbm, out_ref, sems):
    early, latent = dpre_a_ref.shape
    copies = []
    for dpre_ref, base in ((dpre_a_ref, 0), (dpre_b_ref, early)):
        for at in range(0, early, TILE):
            part = slice(at, at + TILE)
            tile = pl.ds(base + at, TILE)
            out_ref[tile, :] = (
                cot_ref[tile, :].astype(F32) + dot(dpre_ref[part, :], w1_ref[:latent, :], NT)
            ).astype(BF16)
            copy = pltpu.make_async_copy(
                out_ref.at[tile], out_hbm.at[tile], sems.at[(base + at) // TILE]
            )
            copy.start()
            copies.append(copy)
    for copy in copies:
        copy.wait()


def node_kernel(fast, index_ref, partial_ref, inner_ref, outer_ref, slots_ref, *refs):
    out_ref, sums = refs[-2:]
    places, tiles = index_ref.shape[1], index_ref.shape[2]
    nodes = partial_ref.shape[0]
    origin = lax.axis_index("tiles") if fast else 0
    slots = slots_ref[...]
    if fast:
        got_ref = refs[0]
        slots = slots_in(3, slots, got_ref[got_ref.shape[0] - slots.shape[0] // 2 :, :], places)
    place = lax.broadcasted_iota(jnp.int32, (nodes, tiles), 0)
    owner, at = slot_owner(origin, (tiles, places * tiles), 1, places)
    row = lax.broadcasted_iota(jnp.int32, (tiles, places * tiles), 0)
    total = partial_ref[...]
    for j in range(places):
        picks = ones_where(place == index_ref[0, j : j + 1, :])
        far = dot(ones_where((owner == row) & (at == j)), slots).astype(BF16)
        total = total + dot(picks, far)
    sums[...] = total
    odd = lax.rem(lax.axis_index("tiles"), 2)
    inner_at = pl.ds(pl.multiple_of((1 - odd) * (nodes - NEAR), NEAR), NEAR)
    outer_at = pl.ds(pl.multiple_of(odd * (nodes - NEAR), NEAR), NEAR)
    sums[inner_at, :] += inner_ref[inner_ref.shape[0] - NEAR :, :].astype(F32)
    sums[outer_at, :] += outer_ref[...].astype(F32)
    out_ref[...] = sums[...].astype(BF16)


def halve_kernel(shift, count, places, *refs):
    keeps, gots = refs[:count], refs[count : 2 * count]
    rest = refs[2 * count :]
    send_ref, kept_ref = rest[-2:] if not places else rest[-3:-1]
    size = kept_ref.shape[1]
    bit = lax.rem(lax.div(lax.axis_index("tiles"), 2**shift), 2)
    at = 0
    for keep_ref, got_ref in zip(keeps, gots):
        blocks, rows = keep_ref.shape[:2]
        for q in range(blocks // 2):
            there, here = 2 * q + 1 - bit, 2 * q + bit
            got_there = got_ref[pl.ds(pl.multiple_of(there * rows, 32), rows), :].astype(F32)
            got_here = got_ref[pl.ds(pl.multiple_of(here * rows, 32), rows), :].astype(F32)
            to = q * size + at
            send_ref[to : to + rows, :] = (keep_ref[there] + got_there).astype(BF16)
            kept_ref[q, at : at + rows, :] = keep_ref[here] + got_here
        at += rows
    if places:
        slots_ref, moved_ref = rest[0], rest[-1]
        half = slots_ref.shape[0] // 2
        got_ref = gots[0]
        slots = slots_in(shift - 1, slots_ref[...], got_ref[got_ref.shape[0] - half :, :], places)
        moved_ref[...] = slots
        send_ref[send_ref.shape[0] - half :, :] = slots_out(shift, slots, places)


def finish_kernel(count, splits, *refs):
    out_refs = refs[2 * count :]
    rows = [0] * len(out_refs)
    for keep_ref, got_ref, parts in zip(refs[:count], refs[count : 2 * count], splits):
        at = 0
        for which, size in parts:
            first = rows[which]
            out_refs[which][first : first + size, :] = (
                keep_ref[0, at : at + size, :] + got_ref[at : at + size, :].astype(F32)
            )
            at += size
            rows[which] += size


def shaped(shape, dtype):
    return jax.ShapeDtypeStruct(shape, dtype)


def in_hbm(*arrays):
    return [pltpu.with_memory_space_constraint(array, pltpu.HBM) for array in arrays]


def call(kernel, name, out_shape, args, hbm=0, scratch=(), out_specs=None, flops=0):
    vmem = pl.BlockSpec(memory_space=pltpu.VMEM)
    return pl.pallas_call(
        kernel,
        in_specs=[pl.BlockSpec(memory_space=pltpu.HBM)] * hbm + [vmem] * (len(args) - hbm),
        out_specs=out_specs or [vmem] * len(out_shape),
        out_shape=out_shape,
        scratch_shapes=scratch,
        compiler_params=pltpu.CompilerParams(vmem_limit_bytes=16 * MIB),
        cost_estimate=pl.CostEstimate(flops=flops, bytes_accessed=flops // 100, transcendentals=0),
        name=name,
    )(*in_hbm(*args[:hbm]), *args[hbm:])


def swap(tiles, bit, send):
    return lax.ppermute(send, "tiles", [(i, i ^ bit) for i in range(tiles)])


def halve(shift, keeps, gots, slots=None, places=0, flops=0):
    half, _, width = keeps[0].shape
    rows = sum(keep.shape[1] for keep in keeps)
    extra = [] if slots is None else [slots]
    sent = half // 2 * rows + sum(slots.shape[0] // 2 for slots in extra)
    return call(
        functools.partial(halve_kernel, shift, len(keeps), places),
        "halve",
        [pltpu.VMEM((sent, width), BF16), pltpu.VMEM((half // 2, rows, width), F32)]
        + [pltpu.VMEM(slots.shape, BF16) for slots in extra],
        [*keeps, *gots, *extra],
        flops=flops,
    )


def finish(keeps, gots, splits, sizes):
    return call(
        functools.partial(finish_kernel, len(keeps), splits),
        "finish",
        [shaped((size, keeps[0].shape[-1]), F32) for size in sizes],
        [*keeps, *gots],
    )


def after(value, *others):
    return lax.optimization_barrier((value, *others))[0]


def shards(
    node_latent, edge_latent, node_cot, edge_cot,
    edge_w1, edge_b1, edge_w2, edge_b2, edge_gain,
    node_w1, node_b1, node_w2, node_b2, node_gain,
    send_index, edge_sender, edge_receiver, edge_count,
):
    tiles = lax.axis_size("tiles")
    nodes, latent = node_latent.shape
    edges = edge_latent.shape[0]
    places = send_index.shape[2]
    steps = edges // TILE
    used = nodes + 2 * NEAR + places * tiles
    rows = -(-used // LANES) * LANES
    fast = tiles == 16
    half = tiles // 2
    inside = [(i, i ^ 1) for i in range(tiles)]
    across = [(i, i + 1 if i % 2 else i - 1) for i in range(1, tiles - 1)]
    sender = edge_sender.reshape(edges // LANES, LANES)
    receiver = edge_receiver.reshape(edges // LANES, LANES)
    listed = jnp.swapaxes(send_index, 1, 2)
    row = lambda vector: vector.reshape(1, -1)
    vmem = pltpu.VMEM

    if fast:
        grad_shapes = lambda count: [
            vmem((count // 2, latent), BF16),
            vmem((half, count // tiles, latent), F32),
        ]
    else:
        grad_shapes = lambda count: [shaped((latent, latent), F32), shaped((count, latent), F32)]

    outgoing, inner, outer = call(
        outgoing_kernel,
        "outgoing",
        [
            shaped((tiles, places, latent), BF16),
            vmem((NEAR, latent), BF16),
            vmem((NEAR, latent), BF16),
        ],
        [listed, node_latent],
        hbm=2,
        scratch=[vmem(listed.shape, jnp.int32), vmem((nodes, latent), BF16), pltpu.SemaphoreType.DMA((2,))],
    )
    inner = lax.ppermute(inner, "tiles", inside)
    outer = lax.ppermute(outer, "tiles", across)
    slots = lax.all_to_all(outgoing, "tiles", split_axis=0, concat_axis=0, tiled=True)
    node_kept, receiver_kept, moved, preact = call(
        functools.partial(prepare_kernel, tiles, places),
        "prepare",
        [
            vmem((nodes, latent), BF16),
            vmem(receiver.shape, jnp.int32), vmem(sender.shape, jnp.int32),
            vmem((edges, latent), F32),
        ],
        [node_latent, edge_w1, after(sender, outgoing), receiver, row(edge_b1), edge_latent],
        hbm=6,
        scratch=[
            vmem((edges, latent), BF16), vmem(edge_w1.shape, BF16),
            vmem((latent + 2 * nodes, latent), BF16), vmem(sender.shape, jnp.int32),
            vmem((1, latent), F32), pltpu.SemaphoreType.DMA((5,)), pltpu.SemaphoreType.DMA((2,)),
        ],
        flops=AHEAD,
    )

    (
        w1_kept, edge_kept, cot_kept, w2_kept, gain_kept,
        hidden, slope, normed, inverse, table, dsum, base, node_send, node_keep,
    ) = call(
        functools.partial(forward_kernel, tiles, places, fast),
        "forward",
        [
            vmem(edge_w1.shape, BF16), vmem((edges, latent), BF16), vmem((edges, latent), BF16),
            vmem(edge_w2.shape, BF16), vmem((1, latent), F32),
            vmem((edges, latent), BF16), vmem((edges, latent), BF16), vmem((edges, latent), F32),
            vmem((edges, LANES), F32), vmem((rows, latent), BF16),
            vmem((nodes, latent), BF16), vmem((nodes, latent), F32),
        ] + grad_shapes(3 * latent if fast else 2 * latent),
        [
            edge_w1, edge_latent, edge_cot, edge_w2, node_w1, node_w2, node_cot,
            row(edge_b2), row(edge_gain), row(node_b1), row(node_b2), row(node_gain), edge_count,
            inner, outer, slots, preact, node_kept, receiver_kept, moved,
        ],
        hbm=13,
        scratch=[
            vmem((rows - nodes, latent), BF16), vmem((nodes, latent), F32),
            vmem((3 * latent, latent), F32), vmem(node_w1.shape, BF16), vmem(node_w2.shape, BF16),
            vmem((nodes, latent), BF16),
        ] + [vmem((1, latent), F32)] * 4 + [
            pltpu.SMEM(edge_count.shape, jnp.int32), pltpu.SemaphoreType.DMA((15,)),
        ],
    )

    early = edges // 2

    def slope_call(start, last, dsum, outs, more):
        return call(
            functools.partial(slope_kernel, tiles, fast, start, last),
            "slope",
            [vmem((early, latent), BF16)] + outs,
            [cot_kept, receiver_kept, dsum, hidden, slope, normed, inverse, w2_kept, gain_kept] + more,
            scratch=[vmem((latent, latent), F32), vmem((early, latent), BF16)],
        )

    dpre_a, grads = slope_call(0, False, dsum, [vmem((latent, latent), F32)], [])
    if fast:
        send, chain = halve(2, [after(node_keep, grads)], [swap(tiles, 1, node_send)])
        dsum = after(dsum, send)
        got = swap(tiles, 4, send)
    dpre_b, second_send, second_keep = slope_call(
        early, True, dsum, grad_shapes(latent), [grads]
    )
    if fast:
        got_second = swap(tiles, 1, second_send)

    per = latent // tiles
    to_inner, to_outer, to_far, partial, *first = call(
        functools.partial(first_kernel, tiles, places, fast),
        "first",
        [
            vmem((NEAR, latent), BF16),
            vmem((NEAR, latent), BF16),
            vmem((tiles * places, latent), BF16) if fast else shaped((tiles * places, latent), BF16),
            vmem((nodes, latent), F32),
        ] + (
            [
                vmem((half * per + tiles * places // 2, latent), BF16),
                vmem((half, per, latent), F32),
                vmem((half * per, latent), BF16), vmem((half, per, latent), F32),
                vmem((half * per + NEAR, latent), BF16), vmem((half, per, latent), F32),
            ]
            if fast else [shaped((3 * latent, latent), F32)]
        ),
        [dpre_a, dpre_b, edge_kept, moved, receiver_kept, table, node_kept, w1_kept, base],
        scratch=[
            vmem((3 * latent, latent), F32), vmem((rows + nodes, latent), F32),
            vmem((2 * NEAR, latent), F32),
        ],
    )

    def edge_call(dpre_a):
        return call(
            edge_kernel,
            "edge",
            [shaped((edges, latent), BF16)],
            [dpre_a, dpre_b, cot_kept, w1_kept],
            out_specs=[pl.BlockSpec(memory_space=pltpu.HBM)],
            scratch=[vmem((edges, latent), BF16), pltpu.SemaphoreType.DMA((steps,))],
        )[0]

    if fast:
        send_a, keep_a, send_more, keep_more, send_b, keep_b = first
        send_a, send_more, send_b, to_outer = lax.optimization_barrier(
            (send_a, send_more, send_b, to_outer, got_second)
        )[:4]
        inner = swap(tiles, 1, send_b)
        outer = lax.ppermute(to_outer, "tiles", across)
        send_a, chain_a, slots = halve(
            1,
            [keep_a, keep_more],
            [swap(tiles, 1, send_a), swap(tiles, 1, send_more)],
            to_far,
            places,
     )
        got_a = swap(tiles, 2, send_a)
        send_b, chain_b = halve(
            1, [after(keep_b, send_a), second_keep], [inner, got_second]
     )
        got_b = swap(tiles, 2, send_b)
        grad_edge = edge_call(after(dpre_a, send_b))
        send, chain = halve(3, [after(chain, grad_edge, outer)], [got], flops=AHEAD)
        got = swap(tiles, 8, send)
        send_a, chain_a, slots = halve(2, [after(chain_a, send)], [got_a], slots, places)
        got_a = swap(tiles, 4, send_a)
        send_b, chain_b = halve(2, [after(chain_b, send_a)], [got_b])
        got_b = swap(tiles, 4, send_b)
        send, chain = halve(1, [after(chain, send_b)], [got])
        got = swap(tiles, 2, send)
        chain_a = after(chain_a, send)
        send_a, chain_a, slots = halve(3, [chain_a], [got_a], slots, places, AHEAD)
        got_a = swap(tiles, 8, send_a)
        chain_b = after(chain_b, send_a)
        send_b, chain_b = halve(3, [chain_b], [got_b], flops=AHEAD)
        got_b = swap(tiles, 8, send_b)
        returned = [slots, got_a]
        grad_edge_w1, grad_edge_w2, grad_node_w1, grad_node_w2 = finish(
            [chain, chain_a, chain_b],
            [got, got_a, got_b],
            [[(2, 2 * per), (3, per)], [(0, 2 * per)], [(0, per), (1, per)]],
            [3 * per, per, 2 * per, per],
        )
    else:
        grad_edge = edge_call(dpre_a)
        inner = lax.ppermute(to_inner, "tiles", inside)
        outer = lax.ppermute(to_outer, "tiles", across)
        returned = [lax.all_to_all(to_far, "tiles", split_axis=0, concat_axis=0, tiled=True)]
        scatter = functools.partial(
            lax.psum_scatter, axis_name="tiles", scatter_dimension=0, tiled=True
        )
        grad_node_w1, grad_node_w2 = scatter(node_keep), scatter(node_send)
        grad_edge_w1, grad_edge_w2 = scatter(first[0]), scatter(second_keep)
    (grad_node,) = call(
        functools.partial(node_kernel, fast),
        "node",
        [shaped((nodes, latent), BF16)],
        [listed, partial, inner, outer, *returned],
        scratch=[vmem((nodes, latent), F32)],
    )
    return (grad_node, grad_edge, grad_edge_w1, grad_edge_w2, grad_node_w1, grad_node_w2)


def solution(mesh):
    split = P(("groups", "tiles"), None)
    return jax.shard_map(
        shards,
        mesh=mesh,
        in_specs=(split,) * 4
        + (P(),) * 10
        + (
            P(("groups", "tiles"), None, None),
            P(("groups", "tiles")),
            P(("groups", "tiles")),
            P("groups"),
        ),
        out_specs=(split,) * 6,
        check_vma=False,
    )
```

```python
import functools

import jax
import jax.numpy as jnp
from jax import lax
from jax.experimental import pallas as pl
from jax.experimental.pallas import tpu as pltpu
from jax.sharding import PartitionSpec as P

NEAR = 64
EPSILON = 1e-05
TILE = 256
LANES = 128
F32 = jnp.float32
BF16 = jnp.bfloat16
MIB = 1024 * 1024
AHEAD = 10**10

NN = (((1,), (0,)), ((), ()))
NT = (((1,), (1,)), ((), ()))
TN = (((0,), (0,)), ((), ()))


def dot(a, b, dims=NN):
    return lax.dot_general(a, b, dims, preferred_element_type=F32)


def sigmoid(x):
    return 0.5 * jnp.tanh(0.5 * x) + 0.5


def row_mean(x):
    return jnp.sum(x, axis=-1, keepdims=True) * (1.0 / x.shape[-1])


def ones_where(mask):
    return jnp.where(mask, 1.0, 0.0).astype(BF16)


def index_columns(idx_ref, step, tile):
    per = tile // LANES
    parts = []
    for j in range(per):
        row = idx_ref[pl.ds(step * per + j, 1), :]
        parts.append(jnp.transpose(jnp.broadcast_to(row, (LANES, LANES))))
    return jnp.concatenate(parts, axis=0)


def pick_columns(columns, start, stop):
    lane = lax.broadcasted_iota(jnp.int32, columns.shape, 1)
    return [ones_where(columns == lane + at) for at in range(start, stop, LANES)]


def pick_rows(idx_ref, step, tile, width):
    per = tile // LANES
    row = jnp.concatenate([idx_ref[pl.ds(step * per + j, 1), :] for j in range(per)], axis=1)
    return ones_where(lax.broadcasted_iota(jnp.int32, (width, tile), 0) == row)


def norm_forward(out):
    centred = out - row_mean(out)
    inverse = lax.rsqrt(row_mean(centred * centred) + EPSILON)
    return centred, inverse


def norm_backward(scaled, normed, inverse):
    return (
        inverse * (scaled - row_mean(scaled) - normed * row_mean(scaled * normed))
    ).astype(BF16)


def split_halves(bit, total_ref, at, block, first, rows, send_ref, keep_ref, offset, x_last=False):
    half, size = keep_ref.shape[:2]
    for to in range(half):
        q = 2 * to % half + 2 * to // half if x_last else to
        to = to * size + offset
        there = pl.multiple_of(at + first + (2 * q + 1 - bit) * block, 32)
        here = pl.multiple_of(at + first + (2 * q + bit) * block, 32)
        send_ref[to : to + rows, :] = total_ref[pl.ds(there, rows), :].astype(BF16)
        keep_ref[to // size, offset : offset + rows, :] = total_ref[pl.ds(here, rows), :]


def fetch(pairs, sems):
    copies = []
    for at, (source, target) in enumerate(pairs):
        copies.append(pltpu.make_async_copy(source, target, sems.at[at]))
    for copy in copies:
        copy.start()
    return copies


def tile_pairs(source, target, tile):
    return [
        (source.at[pl.ds(at, tile)], target.at[pl.ds(at, tile)])
        for at in range(0, source.shape[0], tile)
    ]


def slot_owner(origin, shape, dim, places):
    row = lax.broadcasted_iota(jnp.int32, shape, dim)
    return lax.div(row, places) ^ origin, lax.rem(row, places)


def bit_slots(bit, shape, places):
    row = lax.broadcasted_iota(jnp.int32, shape, 0)
    column = lax.broadcasted_iota(jnp.int32, shape, 1)
    slot, place = lax.div(column, places), lax.rem(column, places)
    rank = ((slot >> (bit + 1)) << bit) | (slot & (2**bit - 1))
    return ((slot >> bit) & 1 == 1) & (rank * places + place == row)


def slots_out(bit, slots, places):
    rows = slots.shape[0]
    return dot(ones_where(bit_slots(bit, (rows // 2, rows), places)), slots).astype(BF16)


def slots_in(bit, slots, got, places):
    rows = slots.shape[0]
    row = lax.broadcasted_iota(jnp.int32, (rows, rows), 0)
    column = lax.broadcasted_iota(jnp.int32, (rows, rows), 1)
    kept = (row == column) & ((lax.div(column, places) >> bit) & 1 == 0)
    moved = ones_where(bit_slots(bit, (rows // 2, rows), places))
    return (dot(ones_where(kept), slots) + dot(moved, got, TN)).astype(BF16)


def outgoing_kernel(
    index_hbm, node_hbm, slots_ref, inner_ref, outer_ref, index_ref, node_ref, sems
):
    for copy in fetch([(index_hbm, index_ref), (node_hbm, node_ref)], sems):
        copy.wait()
    places, tiles = index_ref.shape[1], index_ref.shape[2]
    nodes, latent = node_ref.shape
    place = lax.broadcasted_iota(jnp.int32, (nodes, tiles), 0)
    for j in range(places):
        picks = ones_where(place == index_ref[0, j : j + 1, :])
        slots_ref[:, j, :] = dot(picks, node_ref[...], TN).astype(BF16)
    odd = lax.rem(lax.axis_index("tiles"), 2)
    inner_ref[...] = node_ref[pl.ds(pl.multiple_of((1 - odd) * (nodes - NEAR), NEAR), NEAR), :]
    outer_ref[...] = node_ref[pl.ds(pl.multiple_of(odd * (nodes - NEAR), NEAR), NEAR), :]


def table_index(raw, tiles, places, nodes):
    far = raw - (nodes + 2 * NEAR)
    far = nodes + 2 * NEAR + lax.rem(far, places) * tiles + lax.div(far, places)
    rim = jnp.where(raw < NEAR, raw + nodes, raw)
    own = jnp.where((raw >= NEAR) & (raw < NEAR + nodes), raw - NEAR, rim)
    return jnp.where(raw >= nodes + 2 * NEAR, far, own)


def prepare_kernel(
    tiles, places,
    node_hbm, w1_hbm, sender_hbm, receiver_hbm, b1_hbm, edge_hbm,
    node_ref, receiver_ref, moved_ref, partial_ref,
    edge_ref, w1_ref, weights, sender_ref, b1_ref, sems, edge_sems,
):
    edges, latent = edge_ref.shape
    nodes = node_ref.shape[0]
    copies = fetch(
        [
            (node_hbm, node_ref), (w1_hbm, w1_ref), (sender_hbm, sender_ref),
            (receiver_hbm, receiver_ref), (b1_hbm, b1_ref),
        ],
        sems,
    )
    edge_copies = fetch(tile_pairs(edge_hbm, edge_ref, edges // 2), edge_sems)
    for copy in copies:
        copy.wait()
    moved_ref[...] = table_index(sender_ref[...], tiles, places, nodes)
    weights[:latent, :] = w1_ref[:latent, :]
    weights[latent : latent + nodes, :] = dot(
        node_ref[...], w1_ref[latent : 2 * latent, :]
    ).astype(BF16)
    weights[latent + nodes :, :] = dot(node_ref[...], w1_ref[2 * latent :, :]).astype(BF16)
    for copy in edge_copies:
        copy.wait()
    for step in range(edges // TILE):
        tile = slice(step * TILE, (step + 1) * TILE)
        senders = pick_columns(index_columns(moved_ref, step, TILE), 0, nodes)
        receivers = pick_columns(index_columns(receiver_ref, step, TILE), 0, nodes)
        inputs = jnp.concatenate([edge_ref[tile, :]] + senders + receivers, axis=1)
        partial_ref[tile, :] = dot(inputs, weights[...]) + b1_ref[...]


def forward_kernel(
    tiles, places, fast,
    w1_hbm, edge_hbm, cot_hbm, w2_hbm, nw1_hbm, nw2_hbm, ncot_hbm,
    b2_hbm, gain_hbm, nb1_hbm, nb2_hbm, ngain_hbm, count_hbm,
    inner_ref, outer_ref, far_ref, known_ref, node_ref, receiver_ref, moved_ref,
    w1_ref, edge_ref, cot_ref, w2_ref, gain_ref,
    hidden_ref, slope_ref, normed_ref, inverse_ref, table_ref, dsum_ref, base_ref,
    gsend_ref, gkeep_ref,
    weights, summed, grads, nw1_ref, nw2_ref, ncot_ref,
    b2_ref, nb1_ref, nb2_ref, ngain_ref, count_ref, sems,
):
    here = lax.axis_index("tiles")
    edges, latent = hidden_ref.shape
    nodes = node_ref.shape[0]
    rows = table_ref.shape[0]
    steps = edges // TILE

    senders_part = pl.ds(latent, latent)
    early = fetch(
        [
            (w1_hbm.at[senders_part], w1_ref.at[senders_part]), (count_hbm, count_ref),
            (b2_hbm, b2_ref), (gain_hbm, gain_ref), (w2_hbm, w2_ref),
        ],
        sems,
    )
    edges_part, receivers_part = pl.ds(0, latent), pl.ds(2 * latent, latent)
    late = fetch(
        [
            (nw1_hbm, nw1_ref), (nw2_hbm, nw2_ref), (ncot_hbm, ncot_ref),
            (nb1_hbm, nb1_ref), (nb2_hbm, nb2_ref), (ngain_hbm, ngain_ref),
            (cot_hbm, cot_ref), (edge_hbm, edge_ref),
            (w1_hbm.at[edges_part], w1_ref.at[edges_part]),
            (w1_hbm.at[receivers_part], w1_ref.at[receivers_part]),
        ],
        sems.at[pl.ds(len(early), 10)],
    )

    table_ref[:nodes, :] = node_ref[...]
    odd = lax.rem(here, 2)
    table_ref[pl.ds(pl.multiple_of(nodes + (1 - odd) * NEAR, NEAR), NEAR), :] = inner_ref[...]
    table_ref[pl.ds(pl.multiple_of(nodes + odd * NEAR, NEAR), NEAR), :] = outer_ref[...]
    for j in range(places):
        at = nodes + 2 * NEAR + j * tiles
        table_ref[at : at + tiles, :] = far_ref[:, j, :]
    used = nodes + 2 * NEAR + places * tiles
    if used < rows:
        table_ref[used:, :] = jnp.zeros((rows - used, latent), BF16)
    early[0].wait()
    weights[...] = dot(table_ref[nodes:, :], w1_ref[latent : 2 * latent, :]).astype(BF16)
    for copy in early[1:]:
        copy.wait()
    live = count_ref[here]

    def activate(step):
        tile = slice(step * TILE, (step + 1) * TILE)
        senders = pick_columns(index_columns(moved_ref, step, TILE), nodes, rows)
        preact = known_ref[tile, :] + dot(jnp.concatenate(senders, axis=1), weights[...])
        sig = sigmoid(preact)
        slope_ref[tile, :] = (sig * (1.0 + preact * (1.0 - sig))).astype(BF16)
        hidden_ref[tile, :] = (preact * sig).astype(BF16)

    def normalize(step):
        tile = slice(step * TILE, (step + 1) * TILE)
        centred, inverse = norm_forward(dot(hidden_ref[tile, :], w2_ref[...]) + b2_ref[...])
        position = step * TILE + lax.broadcasted_iota(jnp.int32, inverse.shape, 0)
        inverse = jnp.where(position < live, inverse, 0.0)
        normed = centred * inverse
        normed_ref[tile, :] = normed
        inverse_ref[tile, :] = jnp.broadcast_to(inverse, (TILE, LANES))
        update = (normed * gain_ref[...]).astype(BF16)
        part = dot(pick_rows(receiver_ref, step, TILE, nodes), update)
        if step == 0:
            summed[...] = part
        else:
            summed[...] += part

    for step in range(steps + 1):
        if step < steps:
            activate(step)
        if step > 0:
            normalize(step - 1)

    for copy in late:
        copy.wait()
    node_in = jnp.concatenate([node_ref[...], summed[...].astype(BF16)], axis=1)
    preact_n = dot(node_in, nw1_ref[...]) + nb1_ref[...]
    sig_n = sigmoid(preact_n)
    hidden_n = (preact_n * sig_n).astype(BF16)
    centred_n, inverse_n = norm_forward(dot(hidden_n, nw2_ref[...]) + nb2_ref[...])
    cot = ncot_ref[...].astype(F32)
    dout = norm_backward(cot * ngain_ref[...], centred_n * inverse_n, inverse_n)
    slope_n = sig_n * (1.0 + preact_n * (1.0 - sig_n))
    dpre = (dot(dout, nw2_ref[...], NT) * slope_n).astype(BF16)
    grads[: 2 * latent, :] = dot(node_in, dpre, TN)
    grads[2 * latent :, :] = dot(hidden_n, dout, TN)
    base_ref[...] = cot + dot(dpre, nw1_ref[:latent, :], NT)
    dsum_ref[...] = dot(dpre, nw1_ref[latent:, :], NT).astype(BF16)
    if fast:
        bit = lax.rem(here, 2)
        first = 2 * latent // tiles
        split_halves(bit, grads, 0, first, 0, first, gsend_ref, gkeep_ref, 0, True)
        second = latent // tiles
        split_halves(bit, grads, 2 * latent, second, 0, second, gsend_ref, gkeep_ref, first, True)
    else:
        gkeep_ref[...] = grads[: 2 * latent, :]
        gsend_ref[...] = grads[2 * latent :, :]


def slope_kernel(
    tiles, fast, start, last,
    cot_ref, receiver_ref, dsum_ref, hidden_ref, slope_ref, normed_ref, inverse_ref, w2_ref, gain_ref,
    *refs,
):
    dpre_ref, *out_refs, grads, dout = refs[0 if start == 0 else 1 :]
    here = lax.axis_index("tiles")
    edges, latent = dpre_ref.shape
    nodes = dsum_ref.shape[0]
    steps = edges // TILE
    grads[...] = jnp.zeros_like(grads) if start == 0 else refs[0][...]

    def outer(step):
        tile = slice(step * TILE, (step + 1) * TILE)
        whole = slice(start + step * TILE, start + (step + 1) * TILE)
        receivers = jnp.concatenate(
            pick_columns(index_columns(receiver_ref, start // TILE + step, TILE), 0, nodes), axis=1
        )
        grad_update = cot_ref[whole, :].astype(F32) + dot(receivers, dsum_ref[...])
        inverse = inverse_ref[whole, :1]
        dout[tile, :] = norm_backward(grad_update * gain_ref[...], normed_ref[whole, :], inverse)

    def inner(step):
        tile = slice(step * TILE, (step + 1) * TILE)
        whole = slice(start + step * TILE, start + (step + 1) * TILE)
        dpre_ref[tile, :] = (
            dot(dout[tile, :], w2_ref[...], NT) * slope_ref[whole, :].astype(F32)
        ).astype(BF16)
        grads[...] += dot(hidden_ref[whole, :], dout[tile, :], TN)

    for step in range(steps + 1):
        if step < steps:
            outer(step)
        if step > 0:
            inner(step - 1)

    if not last:
        out_refs[0][...] = grads[...]
    elif fast:
        rows = latent // tiles
        split_halves(lax.rem(here, 2), grads, 0, rows, 0, rows, *out_refs, 0)
    else:
        out_refs[0][...] = jnp.zeros_like(out_refs[0])
        out_refs[1][...] = grads[...]


def first_kernel(
    tiles, places, fast,
    dpre_a_ref, dpre_b_ref, edge_ref, sender_ref, receiver_ref, table_ref, node_ref, w1_ref,
    *refs,
):
    out_refs, (grads, sums, rims) = refs[:-3], refs[-3:]
    inner_ref, outer_ref, far_ref, sums_ref = out_refs[:4]
    here = lax.axis_index("tiles")
    edges, latent = edge_ref.shape
    early = dpre_a_ref.shape[0]
    nodes = node_ref.shape[0]
    rows = table_ref.shape[0]

    for step in range(edges // TILE):
        tile = slice(step * TILE, (step + 1) * TILE)
        if step * TILE < early:
            dpre = dpre_a_ref[tile, :]
        else:
            dpre = dpre_b_ref[step * TILE - early : (step + 1) * TILE - early, :]
        part = dot(edge_ref[tile, :], dpre, TN)
        picks = jnp.concatenate(
            [
                pick_rows(sender_ref, step, TILE, rows),
                pick_rows(receiver_ref, step, TILE, nodes),
            ],
            axis=0,
        )
        scattered = dot(picks, dpre)
        if step == 0:
            grads[:latent, :] = part
            sums[...] = scattered
        else:
            grads[:latent, :] += part
            sums[...] += scattered

    by_sender = sums[:rows, :].astype(BF16)
    by_receiver = sums[rows:, :].astype(BF16)
    grads[latent : 2 * latent, :] = dot(table_ref[...], by_sender, TN)
    grads[2 * latent :, :] = dot(node_ref[...], by_receiver, TN)
    back = dot(by_sender[nodes:, :], w1_ref[latent : 2 * latent, :], NT)
    rims[...] = back[: 2 * NEAR, :]
    odd = lax.rem(here, 2)
    inner = rims[pl.ds(pl.multiple_of((1 - odd) * NEAR, NEAR), NEAR), :].astype(BF16)
    inner_ref[...] = inner
    outer_ref[...] = rims[pl.ds(pl.multiple_of(odd * NEAR, NEAR), NEAR), :].astype(BF16)
    far = back[2 * NEAR : 2 * NEAR + places * tiles, :].astype(BF16)
    owner, at = slot_owner(here if fast else 0, (places * tiles, places * tiles), 0, places)
    column = lax.broadcasted_iota(jnp.int32, (places * tiles, places * tiles), 1)
    far = dot(ones_where(at * tiles + owner == column), far).astype(BF16)
    far_ref[...] = far
    if fast:
        bit = lax.rem(here, 2)
        block = 3 * latent // tiles
        at = 0
        for send_ref, keep_ref in (out_refs[4:6], out_refs[6:8], out_refs[8:10]):
            part = keep_ref.shape[1]
            split_halves(bit, grads, 0, block, at, part, send_ref, keep_ref, 0)
            at += part
        out_refs[4][tiles // 2 * out_refs[5].shape[1] :, :] = slots_out(0, far, places)
        out_refs[8][tiles // 2 * out_refs[9].shape[1] :, :] = inner
    else:
        out_refs[4][...] = grads[...]
    sums_ref[:nodes, :] = by_sender[:nodes, :]
    sums_ref[nodes:, :] = by_receiver


def edge_kernel(
    dpre_a_ref, dpre_b_ref, cot_ref, w1_ref, base_ref, sums_ref, out_hbm, partial_ref, out_ref, sems
):
    early, latent = dpre_a_ref.shape
    copies = []
    for dpre_ref, base in ((dpre_a_ref, 0), (dpre_b_ref, early)):
        for at in range(0, early, TILE):
            part = slice(at, at + TILE)
            tile = pl.ds(base + at, TILE)
            out_ref[tile, :] = (
                cot_ref[tile, :].astype(F32) + dot(dpre_ref[part, :], w1_ref[:latent, :], NT)
            ).astype(BF16)
            copy = pltpu.make_async_copy(
                out_ref.at[tile], out_hbm.at[tile], sems.at[(base + at) // TILE]
            )
            copy.start()
            copies.append(copy)
    nodes = base_ref.shape[0]
    partial_ref[...] = (
        base_ref[...]
        + dot(sums_ref[:nodes, :], w1_ref[latent : 2 * latent, :], NT)
        + dot(sums_ref[nodes:, :], w1_ref[2 * latent :, :], NT)
    )
    for copy in copies:
        copy.wait()


def add_rims(total, inner_ref, outer_ref, sums_ref):
    nodes = total.shape[0]
    odd = lax.rem(lax.axis_index("tiles"), 2)
    inner_at = pl.ds(pl.multiple_of((1 - odd) * (nodes - NEAR), NEAR), NEAR)
    outer_at = pl.ds(pl.multiple_of(odd * (nodes - NEAR), NEAR), NEAR)
    sums_ref[...] = total
    sums_ref[inner_at, :] += inner_ref[inner_ref.shape[0] - NEAR :, :].astype(F32)
    sums_ref[outer_at, :] += outer_ref[...].astype(F32)


def slot_picks(origin, index_ref, nodes):
    places, tiles = index_ref.shape[1], index_ref.shape[2]
    place = lax.broadcasted_iota(jnp.int32, (nodes, tiles), 0)
    owner, at = slot_owner(origin, (tiles, places * tiles), 1, places)
    row = lax.broadcasted_iota(jnp.int32, (tiles, places * tiles), 0)
    picks = jnp.zeros((nodes, places * tiles), F32)
    for j in range(places):
        listed = ones_where(place == index_ref[0, j : j + 1, :])
        picks += dot(listed, ones_where((owner == row) & (at == j)))
    return picks.astype(BF16)


def settle_kernel(
    index_ref, partial_ref, inner_ref, outer_ref, slots_ref, sums_ref, picks_ref
):
    places = index_ref.shape[1]
    rows = slots_ref.shape[0]
    picks = slot_picks(lax.axis_index("tiles"), index_ref, partial_ref.shape[0])
    column = lax.broadcasted_iota(jnp.int32, picks.shape, 1)
    here = ones_where((picks > 0) & ((lax.div(column, places) >> 3) & 1 == 0))
    moved = ones_where(bit_slots(3, (rows // 2, rows), places))
    picks_ref[...] = dot(picks, moved, NT).astype(BF16)
    add_rims(partial_ref[...] + dot(here, slots_ref[...]), inner_ref, outer_ref, sums_ref)


def last_kernel(sums_ref, picks_ref, got_ref, out_ref):
    rows = picks_ref.shape[1]
    got = got_ref[got_ref.shape[0] - rows :, :]
    out_ref[...] = (sums_ref[...] + dot(picks_ref[...], got)).astype(BF16)


def node_kernel(index_ref, partial_ref, inner_ref, outer_ref, slots_ref, out_ref, sums_ref):
    picks = slot_picks(0, index_ref, partial_ref.shape[0])
    add_rims(partial_ref[...] + dot(picks, slots_ref[...]), inner_ref, outer_ref, sums_ref)
    out_ref[...] = sums_ref[...].astype(BF16)


def halve_kernel(shift, count, places, *refs):
    keeps, gots = refs[:count], refs[count : 2 * count]
    rest = refs[2 * count :]
    send_ref, kept_ref = rest[-2:] if not places else rest[-3:-1]
    size = kept_ref.shape[1]
    bit = lax.rem(lax.div(lax.axis_index("tiles"), 2**shift), 2)
    at = 0
    for keep_ref, got_ref in zip(keeps, gots):
        blocks, rows = keep_ref.shape[:2]
        for q in range(blocks // 2):
            there, here = 2 * q + 1 - bit, 2 * q + bit
            got_there = got_ref[pl.ds(pl.multiple_of(there * rows, 32), rows), :].astype(F32)
            got_here = got_ref[pl.ds(pl.multiple_of(here * rows, 32), rows), :].astype(F32)
            to = q * size + at
            send_ref[to : to + rows, :] = (keep_ref[there] + got_there).astype(BF16)
            kept_ref[q, at : at + rows, :] = keep_ref[here] + got_here
        at += rows
    if places:
        slots_ref, moved_ref = rest[0], rest[-1]
        half = slots_ref.shape[0] // 2
        got_ref = gots[0]
        slots = slots_in(shift - 1, slots_ref[...], got_ref[got_ref.shape[0] - half :, :], places)
        moved_ref[...] = slots
        send_ref[send_ref.shape[0] - half :, :] = slots_out(shift, slots, places)


def finish_kernel(count, splits, *refs):
    out_refs = refs[2 * count :]
    rows = [0] * len(out_refs)
    for keep_ref, got_ref, parts in zip(refs[:count], refs[count : 2 * count], splits):
        at = 0
        for which, size in parts:
            first = rows[which]
            out_refs[which][first : first + size, :] = (
                keep_ref[0, at : at + size, :] + got_ref[at : at + size, :].astype(F32)
            )
            at += size
            rows[which] += size


def shaped(shape, dtype):
    return jax.ShapeDtypeStruct(shape, dtype)


def in_hbm(*arrays):
    return [pltpu.with_memory_space_constraint(array, pltpu.HBM) for array in arrays]


def call(kernel, name, out_shape, args, hbm=0, scratch=(), out_specs=None, flops=0):
    vmem = pl.BlockSpec(memory_space=pltpu.VMEM)
    return pl.pallas_call(
        kernel,
        in_specs=[pl.BlockSpec(memory_space=pltpu.HBM)] * hbm + [vmem] * (len(args) - hbm),
        out_specs=out_specs or [vmem] * len(out_shape),
        out_shape=out_shape,
        scratch_shapes=scratch,
        compiler_params=pltpu.CompilerParams(vmem_limit_bytes=16 * MIB),
        cost_estimate=pl.CostEstimate(flops=flops, bytes_accessed=flops // 100, transcendentals=0),
        name=name,
    )(*in_hbm(*args[:hbm]), *args[hbm:])


def swap(tiles, bit, send):
    return lax.ppermute(send, "tiles", [(i, i ^ bit) for i in range(tiles)])


def halve(shift, keeps, gots, slots=None, places=0, flops=0):
    half, _, width = keeps[0].shape
    rows = sum(keep.shape[1] for keep in keeps)
    extra = [] if slots is None else [slots]
    sent = half // 2 * rows + sum(slots.shape[0] // 2 for slots in extra)
    return call(
        functools.partial(halve_kernel, shift, len(keeps), places),
        "halve",
        [pltpu.VMEM((sent, width), BF16), pltpu.VMEM((half // 2, rows, width), F32)]
        + [pltpu.VMEM(slots.shape, BF16) for slots in extra],
        [*keeps, *gots, *extra],
        flops=flops,
    )


def finish(keeps, gots, splits, sizes):
    return call(
        functools.partial(finish_kernel, len(keeps), splits),
        "finish",
        [shaped((size, keeps[0].shape[-1]), F32) for size in sizes],
        [*keeps, *gots],
    )


def after(value, *others):
    return lax.optimization_barrier((value, *others))[0]


def shards(
    node_latent, edge_latent, node_cot, edge_cot,
    edge_w1, edge_b1, edge_w2, edge_b2, edge_gain,
    node_w1, node_b1, node_w2, node_b2, node_gain,
    send_index, edge_sender, edge_receiver, edge_count,
):
    tiles = lax.axis_size("tiles")
    nodes, latent = node_latent.shape
    edges = edge_latent.shape[0]
    places = send_index.shape[2]
    steps = edges // TILE
    used = nodes + 2 * NEAR + places * tiles
    rows = -(-used // LANES) * LANES
    fast = tiles == 16
    half = tiles // 2
    inside = [(i, i ^ 1) for i in range(tiles)]
    across = [(i, i + 1 if i % 2 else i - 1) for i in range(1, tiles - 1)]
    sender = edge_sender.reshape(edges // LANES, LANES)
    receiver = edge_receiver.reshape(edges // LANES, LANES)
    listed = jnp.swapaxes(send_index, 1, 2)
    row = lambda vector: vector.reshape(1, -1)
    vmem = pltpu.VMEM

    if fast:
        grad_shapes = lambda count: [
            vmem((count // 2, latent), BF16),
            vmem((half, count // tiles, latent), F32),
        ]
    else:
        grad_shapes = lambda count: [shaped((latent, latent), F32), shaped((count, latent), F32)]

    outgoing, inner, outer = call(
        outgoing_kernel,
        "outgoing",
        [
            shaped((tiles, places, latent), BF16),
            vmem((NEAR, latent), BF16),
            vmem((NEAR, latent), BF16),
        ],
        [listed, node_latent],
        hbm=2,
        scratch=[vmem(listed.shape, jnp.int32), vmem((nodes, latent), BF16), pltpu.SemaphoreType.DMA((2,))],
    )
    inner = lax.ppermute(inner, "tiles", inside)
    outer = lax.ppermute(outer, "tiles", across)
    slots = lax.all_to_all(outgoing, "tiles", split_axis=0, concat_axis=0, tiled=True)
    node_kept, receiver_kept, moved, preact = call(
        functools.partial(prepare_kernel, tiles, places),
        "prepare",
        [
            vmem((nodes, latent), BF16),
            vmem(receiver.shape, jnp.int32), vmem(sender.shape, jnp.int32),
            vmem((edges, latent), F32),
        ],
        [node_latent, edge_w1, after(sender, outgoing), receiver, row(edge_b1), edge_latent],
        hbm=6,
        scratch=[
            vmem((edges, latent), BF16), vmem(edge_w1.shape, BF16),
            vmem((latent + 2 * nodes, latent), BF16), vmem(sender.shape, jnp.int32),
            vmem((1, latent), F32), pltpu.SemaphoreType.DMA((5,)), pltpu.SemaphoreType.DMA((2,)),
        ],
        flops=AHEAD,
    )

    (
        w1_kept, edge_kept, cot_kept, w2_kept, gain_kept,
        hidden, slope, normed, inverse, table, dsum, base, node_send, node_keep,
    ) = call(
        functools.partial(forward_kernel, tiles, places, fast),
        "forward",
        [
            vmem(edge_w1.shape, BF16), vmem((edges, latent), BF16), vmem((edges, latent), BF16),
            vmem(edge_w2.shape, BF16), vmem((1, latent), F32),
            vmem((edges, latent), BF16), vmem((edges, latent), BF16), vmem((edges, latent), F32),
            vmem((edges, LANES), F32), vmem((rows, latent), BF16),
            vmem((nodes, latent), BF16), vmem((nodes, latent), F32),
        ] + grad_shapes(3 * latent if fast else 2 * latent),
        [
            edge_w1, edge_latent, edge_cot, edge_w2, node_w1, node_w2, node_cot,
            row(edge_b2), row(edge_gain), row(node_b1), row(node_b2), row(node_gain), edge_count,
            inner, outer, slots, preact, node_kept, receiver_kept, moved,
        ],
        hbm=13,
        scratch=[
            vmem((rows - nodes, latent), BF16), vmem((nodes, latent), F32),
            vmem((3 * latent, latent), F32), vmem(node_w1.shape, BF16), vmem(node_w2.shape, BF16),
            vmem((nodes, latent), BF16),
        ] + [vmem((1, latent), F32)] * 4 + [
            pltpu.SMEM(edge_count.shape, jnp.int32), pltpu.SemaphoreType.DMA((15,)),
        ],
    )

    early = edges // 2

    def slope_call(start, last, dsum, outs, more):
        return call(
            functools.partial(slope_kernel, tiles, fast, start, last),
            "slope",
            [vmem((early, latent), BF16)] + outs,
            [cot_kept, receiver_kept, dsum, hidden, slope, normed, inverse, w2_kept, gain_kept] + more,
            scratch=[vmem((latent, latent), F32), vmem((early, latent), BF16)],
        )

    dpre_a, grads = slope_call(0, False, dsum, [vmem((latent, latent), F32)], [])
    if fast:
        send, chain = halve(2, [after(node_keep, grads)], [swap(tiles, 1, node_send)])
        dsum = after(dsum, send)
        got = swap(tiles, 4, send)
    dpre_b, second_send, second_keep = slope_call(
        early, True, dsum, grad_shapes(latent), [grads]
    )
    if fast:
        got_second = swap(tiles, 1, second_send)

    per = latent // tiles
    to_inner, to_outer, to_far, sums, *first = call(
        functools.partial(first_kernel, tiles, places, fast),
        "first",
        [
            vmem((NEAR, latent), BF16),
            vmem((NEAR, latent), BF16),
            vmem((tiles * places, latent), BF16) if fast else shaped((tiles * places, latent), BF16),
            vmem((2 * nodes, latent), BF16),
        ] + (
            [
                vmem((half * per + tiles * places // 2, latent), BF16),
                vmem((half, per, latent), F32),
                vmem((half * per, latent), BF16), vmem((half, per, latent), F32),
                vmem((half * per + NEAR, latent), BF16), vmem((half, per, latent), F32),
            ]
            if fast else [shaped((3 * latent, latent), F32)]
        ),
        [dpre_a, dpre_b, edge_kept, moved, receiver_kept, table, node_kept, w1_kept],
        scratch=[
            vmem((3 * latent, latent), F32), vmem((rows + nodes, latent), F32),
            vmem((2 * NEAR, latent), F32),
        ],
    )

    def edge_call(dpre_a):
        return call(
            edge_kernel,
            "edge",
            [shaped((edges, latent), BF16), vmem((nodes, latent), F32)],
            [dpre_a, dpre_b, cot_kept, w1_kept, base, sums],
            out_specs=[
                pl.BlockSpec(memory_space=pltpu.HBM), pl.BlockSpec(memory_space=pltpu.VMEM),
            ],
            scratch=[vmem((edges, latent), BF16), pltpu.SemaphoreType.DMA((steps,))],
        )

    if fast:
        send_a, keep_a, send_more, keep_more, send_b, keep_b = first
        send_a, send_more, send_b, to_outer = lax.optimization_barrier(
            (send_a, send_more, send_b, to_outer, got_second)
        )[:4]
        inner = swap(tiles, 1, send_b)
        outer = lax.ppermute(to_outer, "tiles", across)
        send_a, chain_a, slots = halve(
            1,
            [keep_a, keep_more],
            [swap(tiles, 1, send_a), swap(tiles, 1, send_more)],
            to_far,
            places,
     )
        got_a = swap(tiles, 2, send_a)
        send_b, chain_b = halve(
            1, [after(keep_b, send_a), second_keep], [inner, got_second]
     )
        got_b = swap(tiles, 2, send_b)
        grad_edge, partial = edge_call(after(dpre_a, send_b))
        send, chain = halve(3, [after(chain, grad_edge, outer)], [got], flops=AHEAD)
        got = swap(tiles, 8, send)
        send_a, chain_a, slots = halve(2, [after(chain_a, send)], [got_a], slots, places)
        got_a = swap(tiles, 4, send_a)
        send_b, chain_b = halve(2, [after(chain_b, send_a)], [got_b])
        got_b = swap(tiles, 4, send_b)
        send, chain = halve(1, [after(chain, send_b)], [got])
        got = swap(tiles, 2, send)
        chain_a = after(chain_a, send)
        send_a, chain_a, slots = halve(3, [chain_a], [got_a], slots, places, AHEAD)
        got_a = swap(tiles, 8, send_a)
        chain_b = after(chain_b, send_a)
        send_b, chain_b = halve(3, [chain_b], [got_b], flops=AHEAD)
        got_b = swap(tiles, 8, send_b)
        node_sums, picks = call(
            settle_kernel,
            "settle",
            [vmem((nodes, latent), F32), vmem((nodes, places * half), BF16)],
            [listed, partial, inner, outer, slots],
        )
        (grad_node,) = call(
            last_kernel, "last", [shaped((nodes, latent), BF16)], [node_sums, picks, got_a]
        )
        grad_edge_w1, grad_edge_w2, grad_node_w1, grad_node_w2 = finish(
            [chain, chain_a, chain_b],
            [got, got_a, got_b],
            [[(2, 2 * per), (3, per)], [(0, 2 * per)], [(0, per), (1, per)]],
            [3 * per, per, 2 * per, per],
        )
    else:
        grad_edge, partial = edge_call(dpre_a)
        inner = lax.ppermute(to_inner, "tiles", inside)
        outer = lax.ppermute(to_outer, "tiles", across)
        returned = lax.all_to_all(to_far, "tiles", split_axis=0, concat_axis=0, tiled=True)
        (grad_node,) = call(
            node_kernel,
            "node",
            [shaped((nodes, latent), BF16)],
            [listed, partial, inner, outer, returned],
            scratch=[vmem((nodes, latent), F32)],
        )
        scatter = functools.partial(
            lax.psum_scatter, axis_name="tiles", scatter_dimension=0, tiled=True
        )
        grad_node_w1, grad_node_w2 = scatter(node_keep), scatter(node_send)
        grad_edge_w1, grad_edge_w2 = scatter(first[0]), scatter(second_keep)
    return (grad_node, grad_edge, grad_edge_w1, grad_edge_w2, grad_node_w1, grad_node_w2)


def solution(mesh):
    split = P(("groups", "tiles"), None)
    return jax.shard_map(
        shards,
        mesh=mesh,
        in_specs=(split,) * 4
        + (P(),) * 10
        + (
            P(("groups", "tiles"), None, None),
            P(("groups", "tiles")),
            P(("groups", "tiles")),
            P("groups"),
        ),
        out_specs=(split,) * 6,
        check_vma=False,
    )
```

```python
import functools

import jax
import jax.numpy as jnp
from jax import lax
from jax.experimental import pallas as pl
from jax.experimental.pallas import tpu as pltpu
from jax.sharding import PartitionSpec as P

NEAR = 64
EPSILON = 1e-05
TILE = 384
LANES = 128
F32 = jnp.float32
BF16 = jnp.bfloat16
MIB = 1024 * 1024
AHEAD = 10**10

NN = (((1,), (0,)), ((), ()))
NT = (((1,), (1,)), ((), ()))
TN = (((0,), (0,)), ((), ()))


def dot(a, b, dims=NN):
    return lax.dot_general(a, b, dims, preferred_element_type=F32)


def sigmoid(x):
    return 0.5 * jnp.tanh(0.5 * x) + 0.5


def row_mean(x):
    return jnp.sum(x, axis=-1, keepdims=True) * (1.0 / x.shape[-1])


def ones_where(mask):
    return jnp.where(mask, 1.0, 0.0).astype(BF16)


def index_columns(idx_ref, step, tile):
    per = tile // LANES
    parts = []
    for j in range(per):
        row = idx_ref[pl.ds(step * per + j, 1), :]
        parts.append(jnp.transpose(jnp.broadcast_to(row, (LANES, LANES))))
    return jnp.concatenate(parts, axis=0)


def pick_columns(columns, start, stop):
    lane = lax.broadcasted_iota(jnp.int32, columns.shape, 1)
    return [ones_where(columns == lane + at) for at in range(start, stop, LANES)]


def pick_rows(idx_ref, step, tile, width):
    per = tile // LANES
    row = jnp.concatenate([idx_ref[pl.ds(step * per + j, 1), :] for j in range(per)], axis=1)
    return ones_where(lax.broadcasted_iota(jnp.int32, (width, tile), 0) == row)


def norm_forward(out):
    centred = out - row_mean(out)
    inverse = lax.rsqrt(row_mean(centred * centred) + EPSILON)
    return centred, inverse


def norm_backward(scaled, normed, inverse):
    return (
        inverse * (scaled - row_mean(scaled) - normed * row_mean(scaled * normed))
    ).astype(BF16)


def split_halves(bit, total_ref, at, block, first, rows, send_ref, keep_ref, offset, x_last=False):
    half, size = keep_ref.shape[:2]
    for to in range(half):
        q = 2 * to % half + 2 * to // half if x_last else to
        to = to * size + offset
        there = pl.multiple_of(at + first + (2 * q + 1 - bit) * block, 32)
        here = pl.multiple_of(at + first + (2 * q + bit) * block, 32)
        send_ref[to : to + rows, :] = total_ref[pl.ds(there, rows), :].astype(BF16)
        keep_ref[to // size, offset : offset + rows, :] = total_ref[pl.ds(here, rows), :]


def fetch(pairs, sems):
    copies = []
    for at, (source, target) in enumerate(pairs):
        copies.append(pltpu.make_async_copy(source, target, sems.at[at]))
    for copy in copies:
        copy.start()
    return copies


def tile_pairs(source, target, tile):
    return [
        (source.at[pl.ds(at, tile)], target.at[pl.ds(at, tile)])
        for at in range(0, source.shape[0], tile)
    ]


def slot_owner(origin, shape, dim, places):
    row = lax.broadcasted_iota(jnp.int32, shape, dim)
    return lax.div(row, places) ^ origin, lax.rem(row, places)


def bit_slots(bit, shape, places):
    row = lax.broadcasted_iota(jnp.int32, shape, 0)
    column = lax.broadcasted_iota(jnp.int32, shape, 1)
    slot, place = lax.div(column, places), lax.rem(column, places)
    rank = ((slot >> (bit + 1)) << bit) | (slot & (2**bit - 1))
    return ((slot >> bit) & 1 == 1) & (rank * places + place == row)


def slots_out(bit, slots, places):
    rows = slots.shape[0]
    return dot(ones_where(bit_slots(bit, (rows // 2, rows), places)), slots).astype(BF16)


def slots_in(bit, slots, got, places):
    rows = slots.shape[0]
    row = lax.broadcasted_iota(jnp.int32, (rows, rows), 0)
    column = lax.broadcasted_iota(jnp.int32, (rows, rows), 1)
    kept = (row == column) & ((lax.div(column, places) >> bit) & 1 == 0)
    moved = ones_where(bit_slots(bit, (rows // 2, rows), places))
    return (dot(ones_where(kept), slots) + dot(moved, got, TN)).astype(BF16)


def outgoing_kernel(
    index_hbm, node_hbm, slots_ref, inner_ref, outer_ref, index_ref, node_ref, sems
):
    for copy in fetch([(index_hbm, index_ref), (node_hbm, node_ref)], sems):
        copy.wait()
    places, tiles = index_ref.shape[1], index_ref.shape[2]
    nodes, latent = node_ref.shape
    place = lax.broadcasted_iota(jnp.int32, (nodes, tiles), 0)
    for j in range(places):
        picks = ones_where(place == index_ref[0, j : j + 1, :])
        slots_ref[:, j, :] = dot(picks, node_ref[...], TN).astype(BF16)
    odd = lax.rem(lax.axis_index("tiles"), 2)
    inner_ref[...] = node_ref[pl.ds(pl.multiple_of((1 - odd) * (nodes - NEAR), NEAR), NEAR), :]
    outer_ref[...] = node_ref[pl.ds(pl.multiple_of(odd * (nodes - NEAR), NEAR), NEAR), :]


def table_index(raw, tiles, places, nodes):
    far = raw - (nodes + 2 * NEAR)
    far = nodes + 2 * NEAR + lax.rem(far, places) * tiles + lax.div(far, places)
    rim = jnp.where(raw < NEAR, raw + nodes, raw)
    own = jnp.where((raw >= NEAR) & (raw < NEAR + nodes), raw - NEAR, rim)
    return jnp.where(raw >= nodes + 2 * NEAR, far, own)


def prepare_kernel(
    tiles, places,
    node_hbm, w1_hbm, sender_hbm, receiver_hbm, b1_hbm, edge_hbm,
    node_ref, receiver_ref, moved_ref, partial_ref,
    edge_ref, w1_ref, weights, sender_ref, b1_ref, sems, edge_sems,
):
    edges, latent = edge_ref.shape
    nodes = node_ref.shape[0]
    copies = fetch(
        [
            (node_hbm, node_ref), (w1_hbm.at[pl.ds(latent, 2 * latent)], w1_ref),
            (sender_hbm, sender_ref), (receiver_hbm, receiver_ref), (b1_hbm, b1_ref),
        ],
        sems,
    )
    edge_copies = fetch(
        [(w1_hbm.at[pl.ds(0, latent)], weights.at[pl.ds(0, latent)]), (edge_hbm, edge_ref)],
        edge_sems,
    )
    for copy in copies:
        copy.wait()
    moved_ref[...] = table_index(sender_ref[...], tiles, places, nodes)
    weights[latent : latent + nodes, :] = dot(
        node_ref[...], w1_ref[:latent, :]
    ).astype(BF16)
    weights[latent + nodes :, :] = dot(node_ref[...], w1_ref[latent:, :]).astype(BF16)
    for copy in edge_copies:
        copy.wait()
    for step in range(edges // TILE):
        tile = slice(step * TILE, (step + 1) * TILE)
        senders = pick_columns(index_columns(moved_ref, step, TILE), 0, nodes)
        receivers = pick_columns(index_columns(receiver_ref, step, TILE), 0, nodes)
        inputs = jnp.concatenate([edge_ref[tile, :]] + senders + receivers, axis=1)
        partial_ref[tile, :] = dot(inputs, weights[...]) + b1_ref[...]


def forward_kernel(
    tiles, places, fast,
    w1_hbm, edge_hbm, cot_hbm, w2_hbm, nw1_hbm, nw2_hbm, ncot_hbm,
    b2_hbm, gain_hbm, nb1_hbm, nb2_hbm, ngain_hbm, count_hbm,
    inner_ref, outer_ref, far_ref, known_ref, node_ref, receiver_ref, moved_ref,
    w1_ref, edge_ref, cot_ref, w2_ref, gain_ref,
    hidden_ref, slope_ref, normed_ref, inverse_ref, table_ref, dsum_ref, base_ref,
    gsend_ref, gkeep_ref,
    weights, summed, grads, nw1_ref, nw2_ref, ncot_ref,
    b2_ref, nb1_ref, nb2_ref, ngain_ref, count_ref, sems,
):
    here = lax.axis_index("tiles")
    edges, latent = hidden_ref.shape
    nodes = node_ref.shape[0]
    rows = table_ref.shape[0]
    steps = edges // TILE

    senders_part = pl.ds(latent, latent)
    early = fetch(
        [
            (w1_hbm.at[senders_part], w1_ref.at[senders_part]), (count_hbm, count_ref),
            (b2_hbm, b2_ref), (gain_hbm, gain_ref), (w2_hbm, w2_ref),
        ],
        sems,
    )
    edges_part, receivers_part = pl.ds(0, latent), pl.ds(2 * latent, latent)
    late = fetch(
        [
            (nw1_hbm, nw1_ref), (nw2_hbm, nw2_ref), (ncot_hbm, ncot_ref),
            (nb1_hbm, nb1_ref), (nb2_hbm, nb2_ref), (ngain_hbm, ngain_ref),
            (cot_hbm, cot_ref), (edge_hbm, edge_ref),
            (w1_hbm.at[edges_part], w1_ref.at[edges_part]),
            (w1_hbm.at[receivers_part], w1_ref.at[receivers_part]),
        ],
        sems.at[pl.ds(len(early), 10)],
    )

    table_ref[:nodes, :] = node_ref[...]
    odd = lax.rem(here, 2)
    table_ref[pl.ds(pl.multiple_of(nodes + (1 - odd) * NEAR, NEAR), NEAR), :] = inner_ref[...]
    table_ref[pl.ds(pl.multiple_of(nodes + odd * NEAR, NEAR), NEAR), :] = outer_ref[...]
    for j in range(places):
        at = nodes + 2 * NEAR + j * tiles
        table_ref[at : at + tiles, :] = far_ref[:, j, :]
    used = nodes + 2 * NEAR + places * tiles
    if used < rows:
        table_ref[used:, :] = jnp.zeros((rows - used, latent), BF16)
    early[0].wait()
    weights[...] = dot(table_ref[nodes:, :], w1_ref[latent : 2 * latent, :]).astype(BF16)
    for copy in early[1:]:
        copy.wait()
    live = count_ref[here]

    def activate(step):
        tile = slice(step * TILE, (step + 1) * TILE)
        senders = pick_columns(index_columns(moved_ref, step, TILE), nodes, rows)
        preact = known_ref[tile, :] + dot(jnp.concatenate(senders, axis=1), weights[...])
        sig = sigmoid(preact)
        slope_ref[tile, :] = (sig * (1.0 + preact * (1.0 - sig))).astype(BF16)
        hidden_ref[tile, :] = (preact * sig).astype(BF16)

    def normalize(step):
        tile = slice(step * TILE, (step + 1) * TILE)
        centred, inverse = norm_forward(dot(hidden_ref[tile, :], w2_ref[...]) + b2_ref[...])
        position = step * TILE + lax.broadcasted_iota(jnp.int32, inverse.shape, 0)
        inverse = jnp.where(position < live, inverse, 0.0)
        normed = centred * inverse
        normed_ref[tile, :] = normed
        inverse_ref[tile, :] = jnp.broadcast_to(inverse, (TILE, LANES))
        update = (normed * gain_ref[...]).astype(BF16)
        part = dot(pick_rows(receiver_ref, step, TILE, nodes), update)
        if step == 0:
            summed[...] = part
        else:
            summed[...] += part

    for step in range(steps + 1):
        if step < steps:
            activate(step)
        if step > 0:
            normalize(step - 1)

    for copy in late:
        copy.wait()
    node_in = jnp.concatenate([node_ref[...], summed[...].astype(BF16)], axis=1)
    preact_n = dot(node_in, nw1_ref[...]) + nb1_ref[...]
    sig_n = sigmoid(preact_n)
    hidden_n = (preact_n * sig_n).astype(BF16)
    centred_n, inverse_n = norm_forward(dot(hidden_n, nw2_ref[...]) + nb2_ref[...])
    cot = ncot_ref[...].astype(F32)
    dout = norm_backward(cot * ngain_ref[...], centred_n * inverse_n, inverse_n)
    slope_n = sig_n * (1.0 + preact_n * (1.0 - sig_n))
    dpre = (dot(dout, nw2_ref[...], NT) * slope_n).astype(BF16)
    grads[: 2 * latent, :] = dot(node_in, dpre, TN)
    grads[2 * latent :, :] = dot(hidden_n, dout, TN)
    base_ref[...] = cot + dot(dpre, nw1_ref[:latent, :], NT)
    dsum_ref[...] = dot(dpre, nw1_ref[latent:, :], NT).astype(BF16)
    if fast:
        bit = lax.rem(here, 2)
        first = 2 * latent // tiles
        split_halves(bit, grads, 0, first, 0, first, gsend_ref, gkeep_ref, 0, True)
        second = latent // tiles
        split_halves(bit, grads, 2 * latent, second, 0, second, gsend_ref, gkeep_ref, first, True)
    else:
        gkeep_ref[...] = grads[: 2 * latent, :]
        gsend_ref[...] = grads[2 * latent :, :]


def slope_kernel(
    tiles, fast, start, last,
    cot_ref, receiver_ref, dsum_ref, hidden_ref, slope_ref, normed_ref, inverse_ref, w2_ref, gain_ref,
    *refs,
):
    dpre_ref, *out_refs, grads, dout = refs[0 if start == 0 else 1 :]
    here = lax.axis_index("tiles")
    edges, latent = dpre_ref.shape
    nodes = dsum_ref.shape[0]
    steps = edges // TILE
    grads[...] = jnp.zeros_like(grads) if start == 0 else refs[0][...]

    def outer(step):
        tile = slice(step * TILE, (step + 1) * TILE)
        whole = slice(start + step * TILE, start + (step + 1) * TILE)
        receivers = jnp.concatenate(
            pick_columns(index_columns(receiver_ref, start // TILE + step, TILE), 0, nodes), axis=1
        )
        grad_update = cot_ref[whole, :].astype(F32) + dot(receivers, dsum_ref[...])
        inverse = inverse_ref[whole, :1]
        dout[tile, :] = norm_backward(grad_update * gain_ref[...], normed_ref[whole, :], inverse)

    def inner(step):
        tile = slice(step * TILE, (step + 1) * TILE)
        whole = slice(start + step * TILE, start + (step + 1) * TILE)
        dpre_ref[tile, :] = (
            dot(dout[tile, :], w2_ref[...], NT) * slope_ref[whole, :].astype(F32)
        ).astype(BF16)
        grads[...] += dot(hidden_ref[whole, :], dout[tile, :], TN)

    for step in range(steps + 1):
        if step < steps:
            outer(step)
        if step > 0:
            inner(step - 1)

    if not last:
        out_refs[0][...] = grads[...]
    elif fast:
        rows = latent // tiles
        split_halves(lax.rem(here, 2), grads, 0, rows, 0, rows, *out_refs, 0)
    else:
        out_refs[0][...] = jnp.zeros_like(out_refs[0])
        out_refs[1][...] = grads[...]


def first_kernel(
    tiles, places, fast,
    dpre_a_ref, dpre_b_ref, edge_ref, sender_ref, receiver_ref, table_ref, node_ref, w1_ref,
    *refs,
):
    out_refs, (grads, sums, rims) = refs[:-3], refs[-3:]
    inner_ref, outer_ref, far_ref, sums_ref = out_refs[:4]
    here = lax.axis_index("tiles")
    edges, latent = edge_ref.shape
    early = dpre_a_ref.shape[0]
    nodes = node_ref.shape[0]
    rows = table_ref.shape[0]

    for step in range(edges // TILE):
        tile = slice(step * TILE, (step + 1) * TILE)
        if step * TILE < early:
            dpre = dpre_a_ref[tile, :]
        else:
            dpre = dpre_b_ref[step * TILE - early : (step + 1) * TILE - early, :]
        part = dot(edge_ref[tile, :], dpre, TN)
        picks = jnp.concatenate(
            [
                pick_rows(sender_ref, step, TILE, rows),
                pick_rows(receiver_ref, step, TILE, nodes),
            ],
            axis=0,
        )
        scattered = dot(picks, dpre)
        if step == 0:
            grads[:latent, :] = part
            sums[...] = scattered
        else:
            grads[:latent, :] += part
            sums[...] += scattered

    by_sender = sums[:rows, :].astype(BF16)
    by_receiver = sums[rows:, :].astype(BF16)
    grads[latent : 2 * latent, :] = dot(table_ref[...], by_sender, TN)
    grads[2 * latent :, :] = dot(node_ref[...], by_receiver, TN)
    back = dot(by_sender[nodes:, :], w1_ref[latent : 2 * latent, :], NT)
    rims[...] = back[: 2 * NEAR, :]
    odd = lax.rem(here, 2)
    inner = rims[pl.ds(pl.multiple_of((1 - odd) * NEAR, NEAR), NEAR), :].astype(BF16)
    inner_ref[...] = inner
    outer_ref[...] = rims[pl.ds(pl.multiple_of(odd * NEAR, NEAR), NEAR), :].astype(BF16)
    far = back[2 * NEAR : 2 * NEAR + places * tiles, :].astype(BF16)
    owner, at = slot_owner(here if fast else 0, (places * tiles, places * tiles), 0, places)
    column = lax.broadcasted_iota(jnp.int32, (places * tiles, places * tiles), 1)
    far = dot(ones_where(at * tiles + owner == column), far).astype(BF16)
    far_ref[...] = far
    if fast:
        bit = lax.rem(here, 2)
        block = 3 * latent // tiles
        at = 0
        for send_ref, keep_ref in (out_refs[4:6], out_refs[6:8], out_refs[8:10]):
            part = keep_ref.shape[1]
            split_halves(bit, grads, 0, block, at, part, send_ref, keep_ref, 0)
            at += part
        out_refs[4][tiles // 2 * out_refs[5].shape[1] :, :] = slots_out(0, far, places)
        out_refs[8][tiles // 2 * out_refs[9].shape[1] :, :] = inner
    else:
        out_refs[4][...] = grads[...]
    sums_ref[:nodes, :] = by_sender[:nodes, :]
    sums_ref[nodes:, :] = by_receiver


def edge_kernel(
    dpre_a_ref, dpre_b_ref, cot_ref, w1_ref, base_ref, sums_ref, out_hbm, partial_ref, out_ref, sems
):
    early, latent = dpre_a_ref.shape
    copies = []
    for dpre_ref, base in ((dpre_a_ref, 0), (dpre_b_ref, early)):
        for at in range(0, early, TILE):
            part = slice(at, at + TILE)
            tile = pl.ds(base + at, TILE)
            out_ref[tile, :] = (
                cot_ref[tile, :].astype(F32) + dot(dpre_ref[part, :], w1_ref[:latent, :], NT)
            ).astype(BF16)
            copy = pltpu.make_async_copy(
                out_ref.at[tile], out_hbm.at[tile], sems.at[(base + at) // TILE]
            )
            copy.start()
            copies.append(copy)
    nodes = base_ref.shape[0]
    partial_ref[...] = (
        base_ref[...]
        + dot(sums_ref[:nodes, :], w1_ref[latent : 2 * latent, :], NT)
        + dot(sums_ref[nodes:, :], w1_ref[2 * latent :, :], NT)
    )
    for copy in copies:
        copy.wait()


def add_rims(total, inner_ref, outer_ref, sums_ref):
    nodes = total.shape[0]
    odd = lax.rem(lax.axis_index("tiles"), 2)
    inner_at = pl.ds(pl.multiple_of((1 - odd) * (nodes - NEAR), NEAR), NEAR)
    outer_at = pl.ds(pl.multiple_of(odd * (nodes - NEAR), NEAR), NEAR)
    sums_ref[...] = total
    sums_ref[inner_at, :] += inner_ref[inner_ref.shape[0] - NEAR :, :].astype(F32)
    sums_ref[outer_at, :] += outer_ref[...].astype(F32)


def slot_picks(origin, index_ref, nodes):
    places, tiles = index_ref.shape[1], index_ref.shape[2]
    place = lax.broadcasted_iota(jnp.int32, (nodes, tiles), 0)
    owner, at = slot_owner(origin, (tiles, places * tiles), 1, places)
    row = lax.broadcasted_iota(jnp.int32, (tiles, places * tiles), 0)
    picks = jnp.zeros((nodes, places * tiles), F32)
    for j in range(places):
        listed = ones_where(place == index_ref[0, j : j + 1, :])
        picks += dot(listed, ones_where((owner == row) & (at == j)))
    return picks.astype(BF16)


def settle_kernel(
    index_ref, partial_ref, inner_ref, outer_ref, slots_ref, sums_ref, picks_ref
):
    places = index_ref.shape[1]
    rows = slots_ref.shape[0]
    picks = slot_picks(lax.axis_index("tiles"), index_ref, partial_ref.shape[0])
    column = lax.broadcasted_iota(jnp.int32, picks.shape, 1)
    here = ones_where((picks > 0) & ((lax.div(column, places) >> 3) & 1 == 0))
    moved = ones_where(bit_slots(3, (rows // 2, rows), places))
    picks_ref[...] = dot(picks, moved, NT).astype(BF16)
    add_rims(partial_ref[...] + dot(here, slots_ref[...]), inner_ref, outer_ref, sums_ref)


def last_kernel(sums_ref, picks_ref, got_ref, out_ref):
    rows = picks_ref.shape[1]
    got = got_ref[got_ref.shape[0] - rows :, :]
    out_ref[...] = (sums_ref[...] + dot(picks_ref[...], got)).astype(BF16)


def node_kernel(index_ref, partial_ref, inner_ref, outer_ref, slots_ref, out_ref, sums_ref):
    picks = slot_picks(0, index_ref, partial_ref.shape[0])
    add_rims(partial_ref[...] + dot(picks, slots_ref[...]), inner_ref, outer_ref, sums_ref)
    out_ref[...] = sums_ref[...].astype(BF16)


def halve_kernel(shift, count, places, *refs):
    keeps, gots = refs[:count], refs[count : 2 * count]
    rest = refs[2 * count :]
    send_ref, kept_ref = rest[-2:] if not places else rest[-3:-1]
    size = kept_ref.shape[1]
    bit = lax.rem(lax.div(lax.axis_index("tiles"), 2**shift), 2)
    at = 0
    for keep_ref, got_ref in zip(keeps, gots):
        blocks, rows = keep_ref.shape[:2]
        for q in range(blocks // 2):
            there, here = 2 * q + 1 - bit, 2 * q + bit
            got_there = got_ref[pl.ds(pl.multiple_of(there * rows, 32), rows), :].astype(F32)
            got_here = got_ref[pl.ds(pl.multiple_of(here * rows, 32), rows), :].astype(F32)
            to = q * size + at
            send_ref[to : to + rows, :] = (keep_ref[there] + got_there).astype(BF16)
            kept_ref[q, at : at + rows, :] = keep_ref[here] + got_here
        at += rows
    if places:
        slots_ref, moved_ref = rest[0], rest[-1]
        half = slots_ref.shape[0] // 2
        got_ref = gots[0]
        slots = slots_in(shift - 1, slots_ref[...], got_ref[got_ref.shape[0] - half :, :], places)
        moved_ref[...] = slots
        send_ref[send_ref.shape[0] - half :, :] = slots_out(shift, slots, places)


def finish_kernel(count, splits, *refs):
    out_refs = refs[2 * count :]
    rows = [0] * len(out_refs)
    for keep_ref, got_ref, parts in zip(refs[:count], refs[count : 2 * count], splits):
        at = 0
        for which, size in parts:
            first = rows[which]
            out_refs[which][first : first + size, :] = (
                keep_ref[0, at : at + size, :] + got_ref[at : at + size, :].astype(F32)
            )
            at += size
            rows[which] += size


def shaped(shape, dtype):
    return jax.ShapeDtypeStruct(shape, dtype)


def in_hbm(*arrays):
    return [pltpu.with_memory_space_constraint(array, pltpu.HBM) for array in arrays]


def call(kernel, name, out_shape, args, hbm=0, scratch=(), out_specs=None, flops=0):
    vmem = pl.BlockSpec(memory_space=pltpu.VMEM)
    return pl.pallas_call(
        kernel,
        in_specs=[pl.BlockSpec(memory_space=pltpu.HBM)] * hbm + [vmem] * (len(args) - hbm),
        out_specs=out_specs or [vmem] * len(out_shape),
        out_shape=out_shape,
        scratch_shapes=scratch,
        compiler_params=pltpu.CompilerParams(vmem_limit_bytes=16 * MIB),
        cost_estimate=pl.CostEstimate(flops=flops, bytes_accessed=flops // 100, transcendentals=0),
        name=name,
    )(*in_hbm(*args[:hbm]), *args[hbm:])


def swap(tiles, bit, send):
    return lax.ppermute(send, "tiles", [(i, i ^ bit) for i in range(tiles)])


def halve(shift, keeps, gots, slots=None, places=0, flops=0):
    half, _, width = keeps[0].shape
    rows = sum(keep.shape[1] for keep in keeps)
    extra = [] if slots is None else [slots]
    sent = half // 2 * rows + sum(slots.shape[0] // 2 for slots in extra)
    return call(
        functools.partial(halve_kernel, shift, len(keeps), places),
        "halve",
        [pltpu.VMEM((sent, width), BF16), pltpu.VMEM((half // 2, rows, width), F32)]
        + [pltpu.VMEM(slots.shape, BF16) for slots in extra],
        [*keeps, *gots, *extra],
        flops=flops,
    )


def finish(keeps, gots, splits, sizes):
    return call(
        functools.partial(finish_kernel, len(keeps), splits),
        "finish",
        [shaped((size, keeps[0].shape[-1]), F32) for size in sizes],
        [*keeps, *gots],
    )


def after(value, *others):
    return lax.optimization_barrier((value, *others))[0]


def shards(
    node_latent, edge_latent, node_cot, edge_cot,
    edge_w1, edge_b1, edge_w2, edge_b2, edge_gain,
    node_w1, node_b1, node_w2, node_b2, node_gain,
    send_index, edge_sender, edge_receiver, edge_count,
):
    tiles = lax.axis_size("tiles")
    nodes, latent = node_latent.shape
    edges = edge_latent.shape[0]
    places = send_index.shape[2]
    steps = edges // TILE
    used = nodes + 2 * NEAR + places * tiles
    rows = -(-used // LANES) * LANES
    fast = tiles == 16
    half = tiles // 2
    inside = [(i, i ^ 1) for i in range(tiles)]
    across = [(i, i + 1 if i % 2 else i - 1) for i in range(1, tiles - 1)]
    sender = edge_sender.reshape(edges // LANES, LANES)
    receiver = edge_receiver.reshape(edges // LANES, LANES)
    listed = jnp.swapaxes(send_index, 1, 2)
    row = lambda vector: vector.reshape(1, -1)
    vmem = pltpu.VMEM

    if fast:
        grad_shapes = lambda count: [
            vmem((count // 2, latent), BF16),
            vmem((half, count // tiles, latent), F32),
        ]
    else:
        grad_shapes = lambda count: [shaped((latent, latent), F32), shaped((count, latent), F32)]

    outgoing, inner, outer = call(
        outgoing_kernel,
        "outgoing",
        [
            shaped((tiles, places, latent), BF16),
            vmem((NEAR, latent), BF16),
            vmem((NEAR, latent), BF16),
        ],
        [listed, node_latent],
        hbm=2,
        scratch=[vmem(listed.shape, jnp.int32), vmem((nodes, latent), BF16), pltpu.SemaphoreType.DMA((2,))],
    )
    inner = lax.ppermute(inner, "tiles", inside)
    outer = lax.ppermute(outer, "tiles", across)
    slots = lax.all_to_all(outgoing, "tiles", split_axis=0, concat_axis=0, tiled=True)
    node_kept, receiver_kept, moved, preact = call(
        functools.partial(prepare_kernel, tiles, places),
        "prepare",
        [
            vmem((nodes, latent), BF16),
            vmem(receiver.shape, jnp.int32), vmem(sender.shape, jnp.int32),
            vmem((edges, latent), F32),
        ],
        [node_latent, edge_w1, after(sender, outgoing), receiver, row(edge_b1), edge_latent],
        hbm=6,
        scratch=[
            vmem((edges, latent), BF16), vmem((2 * latent, latent), BF16),
            vmem((latent + 2 * nodes, latent), BF16), vmem(sender.shape, jnp.int32),
            vmem((1, latent), F32), pltpu.SemaphoreType.DMA((5,)), pltpu.SemaphoreType.DMA((2,)),
        ],
        flops=AHEAD,
    )

    (
        w1_kept, edge_kept, cot_kept, w2_kept, gain_kept,
        hidden, slope, normed, inverse, table, dsum, base, node_send, node_keep,
    ) = call(
        functools.partial(forward_kernel, tiles, places, fast),
        "forward",
        [
            vmem(edge_w1.shape, BF16), vmem((edges, latent), BF16), vmem((edges, latent), BF16),
            vmem(edge_w2.shape, BF16), vmem((1, latent), F32),
            vmem((edges, latent), BF16), vmem((edges, latent), BF16), vmem((edges, latent), F32),
            vmem((edges, LANES), F32), vmem((rows, latent), BF16),
            vmem((nodes, latent), BF16), vmem((nodes, latent), F32),
        ] + grad_shapes(3 * latent if fast else 2 * latent),
        [
            edge_w1, edge_latent, edge_cot, edge_w2, node_w1, node_w2, node_cot,
            row(edge_b2), row(edge_gain), row(node_b1), row(node_b2), row(node_gain), edge_count,
            inner, outer, slots, preact, node_kept, receiver_kept, moved,
        ],
        hbm=13,
        scratch=[
            vmem((rows - nodes, latent), BF16), vmem((nodes, latent), F32),
            vmem((3 * latent, latent), F32), vmem(node_w1.shape, BF16), vmem(node_w2.shape, BF16),
            vmem((nodes, latent), BF16),
        ] + [vmem((1, latent), F32)] * 4 + [
            pltpu.SMEM(edge_count.shape, jnp.int32), pltpu.SemaphoreType.DMA((15,)),
        ],
    )

    early = edges // 2

    def slope_call(start, last, dsum, outs, more):
        return call(
            functools.partial(slope_kernel, tiles, fast, start, last),
            "slope",
            [vmem((early, latent), BF16)] + outs,
            [cot_kept, receiver_kept, dsum, hidden, slope, normed, inverse, w2_kept, gain_kept] + more,
            scratch=[vmem((latent, latent), F32), vmem((early, latent), BF16)],
        )

    dpre_a, grads = slope_call(0, False, dsum, [vmem((latent, latent), F32)], [])
    if fast:
        send, chain = halve(2, [after(node_keep, grads)], [swap(tiles, 1, node_send)])
        dsum = after(dsum, send)
        got = swap(tiles, 4, send)
    dpre_b, second_send, second_keep = slope_call(
        early, True, dsum, grad_shapes(latent), [grads]
    )
    if fast:
        got_second = swap(tiles, 1, second_send)

    per = latent // tiles
    to_inner, to_outer, to_far, sums, *first = call(
        functools.partial(first_kernel, tiles, places, fast),
        "first",
        [
            vmem((NEAR, latent), BF16),
            vmem((NEAR, latent), BF16),
            vmem((tiles * places, latent), BF16) if fast else shaped((tiles * places, latent), BF16),
            vmem((2 * nodes, latent), BF16),
        ] + (
            [
                vmem((half * per + tiles * places // 2, latent), BF16),
                vmem((half, per, latent), F32),
                vmem((half * per, latent), BF16), vmem((half, per, latent), F32),
                vmem((half * per + NEAR, latent), BF16), vmem((half, per, latent), F32),
            ]
            if fast else [shaped((3 * latent, latent), F32)]
        ),
        [dpre_a, dpre_b, edge_kept, moved, receiver_kept, table, node_kept, w1_kept],
        scratch=[
            vmem((3 * latent, latent), F32), vmem((rows + nodes, latent), F32),
            vmem((2 * NEAR, latent), F32),
        ],
    )

    def edge_call(dpre_a):
        return call(
            edge_kernel,
            "edge",
            [shaped((edges, latent), BF16), vmem((nodes, latent), F32)],
            [dpre_a, dpre_b, cot_kept, w1_kept, base, sums],
            out_specs=[
                pl.BlockSpec(memory_space=pltpu.HBM), pl.BlockSpec(memory_space=pltpu.VMEM),
            ],
            scratch=[vmem((edges, latent), BF16), pltpu.SemaphoreType.DMA((steps,))],
        )

    if fast:
        send_a, keep_a, send_more, keep_more, send_b, keep_b = first
        send_a, send_more, send_b, to_outer = lax.optimization_barrier(
            (send_a, send_more, send_b, to_outer, got_second)
        )[:4]
        inner = swap(tiles, 1, send_b)
        outer = lax.ppermute(to_outer, "tiles", across)
        send_a, chain_a, slots = halve(
            1,
            [keep_a, keep_more],
            [swap(tiles, 1, send_a), swap(tiles, 1, send_more)],
            to_far,
            places,
     )
        got_a = swap(tiles, 2, send_a)
        send_b, chain_b = halve(
            1, [after(keep_b, send_a), second_keep], [inner, got_second]
     )
        got_b = swap(tiles, 2, send_b)
        grad_edge, partial = edge_call(after(dpre_a, send_b))
        send, chain = halve(3, [after(chain, grad_edge, outer)], [got], flops=AHEAD)
        got = swap(tiles, 8, send)
        send_a, chain_a, slots = halve(2, [after(chain_a, send)], [got_a], slots, places)
        got_a = swap(tiles, 4, send_a)
        send_b, chain_b = halve(2, [after(chain_b, send_a)], [got_b])
        got_b = swap(tiles, 4, send_b)
        send, chain = halve(1, [after(chain, send_b)], [got])
        got = swap(tiles, 2, send)
        chain_a = after(chain_a, send)
        send_a, chain_a, slots = halve(3, [chain_a], [got_a], slots, places, AHEAD)
        got_a = swap(tiles, 8, send_a)
        chain_b = after(chain_b, send_a)
        send_b, chain_b = halve(3, [chain_b], [got_b], flops=AHEAD)
        got_b = swap(tiles, 8, send_b)
        node_sums, picks = call(
            settle_kernel,
            "settle",
            [vmem((nodes, latent), F32), vmem((nodes, places * half), BF16)],
            [listed, partial, inner, outer, slots],
        )
        (grad_node,) = call(
            last_kernel, "last", [shaped((nodes, latent), BF16)], [node_sums, picks, got_a]
        )
        grad_edge_w1, grad_edge_w2, grad_node_w1, grad_node_w2 = finish(
            [chain, chain_a, chain_b],
            [got, got_a, got_b],
            [[(2, 2 * per), (3, per)], [(0, 2 * per)], [(0, per), (1, per)]],
            [3 * per, per, 2 * per, per],
        )
    else:
        grad_edge, partial = edge_call(dpre_a)
        inner = lax.ppermute(to_inner, "tiles", inside)
        outer = lax.ppermute(to_outer, "tiles", across)
        returned = lax.all_to_all(to_far, "tiles", split_axis=0, concat_axis=0, tiled=True)
        (grad_node,) = call(
            node_kernel,
            "node",
            [shaped((nodes, latent), BF16)],
            [listed, partial, inner, outer, returned],
            scratch=[vmem((nodes, latent), F32)],
        )
        scatter = functools.partial(
            lax.psum_scatter, axis_name="tiles", scatter_dimension=0, tiled=True
        )
        grad_node_w1, grad_node_w2 = scatter(node_keep), scatter(node_send)
        grad_edge_w1, grad_edge_w2 = scatter(first[0]), scatter(second_keep)
    return (grad_node, grad_edge, grad_edge_w1, grad_edge_w2, grad_node_w1, grad_node_w2)


def solution(mesh):
    split = P(("groups", "tiles"), None)
    return jax.shard_map(
        shards,
        mesh=mesh,
        in_specs=(split,) * 4
        + (P(),) * 10
        + (
            P(("groups", "tiles"), None, None),
            P(("groups", "tiles")),
            P(("groups", "tiles")),
            P("groups"),
        ),
        out_specs=(split,) * 6,
        check_vma=False,
    )
```

```python
import functools

import jax
import jax.numpy as jnp
from jax import lax
from jax.experimental import pallas as pl
from jax.experimental.pallas import tpu as pltpu
from jax.sharding import PartitionSpec as P

NEAR = 64
EPSILON = 1e-05
TILE = 256
LANES = 128
F32 = jnp.float32
BF16 = jnp.bfloat16
MIB = 1024 * 1024
AHEAD = 10**10

NN = (((1,), (0,)), ((), ()))
NT = (((1,), (1,)), ((), ()))
TN = (((0,), (0,)), ((), ()))


def dot(a, b, dims=NN):
    return lax.dot_general(a, b, dims, preferred_element_type=F32)


def sigmoid(x):
    return 0.5 * jnp.tanh(0.5 * x) + 0.5


def row_mean(x):
    return jnp.sum(x, axis=-1, keepdims=True) * (1.0 / x.shape[-1])


def ones_where(mask):
    return jnp.where(mask, 1.0, 0.0).astype(BF16)


def index_columns(idx_ref, step, tile):
    per = tile // LANES
    parts = []
    for j in range(per):
        row = idx_ref[pl.ds(step * per + j, 1), :]
        parts.append(jnp.transpose(jnp.broadcast_to(row, (LANES, LANES))))
    return jnp.concatenate(parts, axis=0)


def pick_columns(columns, start, stop):
    lane = lax.broadcasted_iota(jnp.int32, columns.shape, 1)
    return [ones_where(columns == lane + at) for at in range(start, stop, LANES)]


def pick_rows(idx_ref, step, tile, width):
    per = tile // LANES
    row = jnp.concatenate([idx_ref[pl.ds(step * per + j, 1), :] for j in range(per)], axis=1)
    return ones_where(lax.broadcasted_iota(jnp.int32, (width, tile), 0) == row)


def norm_forward(out):
    centred = out - row_mean(out)
    inverse = lax.rsqrt(row_mean(centred * centred) + EPSILON)
    return centred, inverse


def norm_backward(scaled, normed, inverse):
    return (
        inverse * (scaled - row_mean(scaled) - normed * row_mean(scaled * normed))
    ).astype(BF16)


def split_halves(bit, total_ref, at, block, first, rows, send_ref, keep_ref, offset, x_last=False):
    half, size = keep_ref.shape[:2]
    for to in range(half):
        q = 2 * to % half + 2 * to // half if x_last else to
        to = to * size + offset
        there = pl.multiple_of(at + first + (2 * q + 1 - bit) * block, 32)
        here = pl.multiple_of(at + first + (2 * q + bit) * block, 32)
        send_ref[to : to + rows, :] = total_ref[pl.ds(there, rows), :].astype(BF16)
        keep_ref[to // size, offset : offset + rows, :] = total_ref[pl.ds(here, rows), :]


def fetch(pairs, sems):
    copies = []
    for at, (source, target) in enumerate(pairs):
        copies.append(pltpu.make_async_copy(source, target, sems.at[at]))
    for copy in copies:
        copy.start()
    return copies


def tile_pairs(source, target, tile):
    return [
        (source.at[pl.ds(at, tile)], target.at[pl.ds(at, tile)])
        for at in range(0, source.shape[0], tile)
    ]


def slot_owner(origin, shape, dim, places):
    row = lax.broadcasted_iota(jnp.int32, shape, dim)
    return lax.div(row, places) ^ origin, lax.rem(row, places)


def bit_slots(bit, shape, places):
    row = lax.broadcasted_iota(jnp.int32, shape, 0)
    column = lax.broadcasted_iota(jnp.int32, shape, 1)
    slot, place = lax.div(column, places), lax.rem(column, places)
    rank = ((slot >> (bit + 1)) << bit) | (slot & (2**bit - 1))
    return ((slot >> bit) & 1 == 1) & (rank * places + place == row)


def slots_out(bit, slots, places):
    rows = slots.shape[0]
    return dot(ones_where(bit_slots(bit, (rows // 2, rows), places)), slots).astype(BF16)


def slots_in(bit, slots, got, places):
    rows = slots.shape[0]
    row = lax.broadcasted_iota(jnp.int32, (rows, rows), 0)
    column = lax.broadcasted_iota(jnp.int32, (rows, rows), 1)
    kept = (row == column) & ((lax.div(column, places) >> bit) & 1 == 0)
    moved = ones_where(bit_slots(bit, (rows // 2, rows), places))
    return (dot(ones_where(kept), slots) + dot(moved, got, TN)).astype(BF16)


def outgoing_kernel(
    index_hbm, node_hbm, slots_ref, inner_ref, outer_ref, index_ref, node_ref, sems
):
    for copy in fetch([(index_hbm, index_ref), (node_hbm, node_ref)], sems):
        copy.wait()
    places, tiles = index_ref.shape[1], index_ref.shape[2]
    nodes, latent = node_ref.shape
    place = lax.broadcasted_iota(jnp.int32, (nodes, tiles), 0)
    for j in range(places):
        picks = ones_where(place == index_ref[0, j : j + 1, :])
        slots_ref[:, j, :] = dot(picks, node_ref[...], TN).astype(BF16)
    odd = lax.rem(lax.axis_index("tiles"), 2)
    inner_ref[...] = node_ref[pl.ds(pl.multiple_of((1 - odd) * (nodes - NEAR), NEAR), NEAR), :]
    outer_ref[...] = node_ref[pl.ds(pl.multiple_of(odd * (nodes - NEAR), NEAR), NEAR), :]


def table_index(raw, tiles, places, nodes):
    far = raw - (nodes + 2 * NEAR)
    far = nodes + 2 * NEAR + lax.rem(far, places) * tiles + lax.div(far, places)
    rim = jnp.where(raw < NEAR, raw + nodes, raw)
    own = jnp.where((raw >= NEAR) & (raw < NEAR + nodes), raw - NEAR, rim)
    return jnp.where(raw >= nodes + 2 * NEAR, far, own)


def prepare_kernel(
    tiles, places,
    node_hbm, w1_hbm, sender_hbm, receiver_hbm, b1_hbm, edge_hbm,
    node_ref, receiver_ref, moved_ref, partial_ref,
    edge_ref, w1_ref, weights, sender_ref, b1_ref, sems, edge_sems,
):
    edges, latent = edge_ref.shape
    nodes = node_ref.shape[0]
    copies = fetch(
        [
            (node_hbm, node_ref), (w1_hbm, w1_ref), (sender_hbm, sender_ref),
            (receiver_hbm, receiver_ref), (b1_hbm, b1_ref),
        ],
        sems,
    )
    edge_copies = fetch(tile_pairs(edge_hbm, edge_ref, edges // 2), edge_sems)
    for copy in copies:
        copy.wait()
    moved_ref[...] = table_index(sender_ref[...], tiles, places, nodes)
    weights[:latent, :] = w1_ref[:latent, :]
    weights[latent : latent + nodes, :] = dot(
        node_ref[...], w1_ref[latent : 2 * latent, :]
    ).astype(BF16)
    weights[latent + nodes :, :] = dot(node_ref[...], w1_ref[2 * latent :, :]).astype(BF16)
    for copy in edge_copies:
        copy.wait()
    for step in range(edges // TILE):
        tile = slice(step * TILE, (step + 1) * TILE)
        senders = pick_columns(index_columns(moved_ref, step, TILE), 0, nodes)
        receivers = pick_columns(index_columns(receiver_ref, step, TILE), 0, nodes)
        inputs = jnp.concatenate([edge_ref[tile, :]] + senders + receivers, axis=1)
        partial_ref[tile, :] = dot(inputs, weights[...]) + b1_ref[...]


def forward_kernel(
    tiles, places, fast,
    w1_hbm, edge_hbm, cot_hbm, w2_hbm, nw1_hbm, nw2_hbm, ncot_hbm,
    b2_hbm, gain_hbm, nb1_hbm, nb2_hbm, ngain_hbm, count_hbm,
    inner_ref, outer_ref, far_ref, known_ref, node_ref, receiver_ref, moved_ref,
    w1_ref, edge_ref, cot_ref, w2_ref, gain_ref,
    hidden_ref, slope_ref, normed_ref, inverse_ref, table_ref, dsum_ref, base_ref,
    gsend_ref, gkeep_ref,
    weights, summed, grads, nw1_ref, nw2_ref, ncot_ref,
    b2_ref, nb1_ref, nb2_ref, ngain_ref, count_ref, sems,
):
    here = lax.axis_index("tiles")
    edges, latent = hidden_ref.shape
    nodes = node_ref.shape[0]
    rows = table_ref.shape[0]
    steps = edges // TILE

    senders_part = pl.ds(latent, latent)
    early = fetch(
        [
            (w1_hbm.at[senders_part], w1_ref.at[senders_part]), (count_hbm, count_ref),
            (b2_hbm, b2_ref), (gain_hbm, gain_ref), (w2_hbm, w2_ref),
        ],
        sems,
    )
    edges_part, receivers_part = pl.ds(0, latent), pl.ds(2 * latent, latent)
    late = fetch(
        [
            (nw1_hbm, nw1_ref), (nw2_hbm, nw2_ref), (ncot_hbm, ncot_ref),
            (nb1_hbm, nb1_ref), (nb2_hbm, nb2_ref), (ngain_hbm, ngain_ref),
            (cot_hbm, cot_ref), (edge_hbm, edge_ref),
            (w1_hbm.at[edges_part], w1_ref.at[edges_part]),
            (w1_hbm.at[receivers_part], w1_ref.at[receivers_part]),
        ],
        sems.at[pl.ds(len(early), 10)],
    )

    table_ref[:nodes, :] = node_ref[...]
    odd = lax.rem(here, 2)
    table_ref[pl.ds(pl.multiple_of(nodes + (1 - odd) * NEAR, NEAR), NEAR), :] = inner_ref[...]
    table_ref[pl.ds(pl.multiple_of(nodes + odd * NEAR, NEAR), NEAR), :] = outer_ref[...]
    for j in range(places):
        at = nodes + 2 * NEAR + j * tiles
        table_ref[at : at + tiles, :] = far_ref[:, j, :]
    used = nodes + 2 * NEAR + places * tiles
    if used < rows:
        table_ref[used:, :] = jnp.zeros((rows - used, latent), BF16)
    early[0].wait()
    weights[...] = dot(table_ref[nodes:, :], w1_ref[latent : 2 * latent, :]).astype(BF16)
    for copy in early[1:]:
        copy.wait()
    live = count_ref[here]

    def activate(step):
        tile = slice(step * TILE, (step + 1) * TILE)
        senders = pick_columns(index_columns(moved_ref, step, TILE), nodes, rows)
        preact = known_ref[tile, :] + dot(jnp.concatenate(senders, axis=1), weights[...])
        sig = sigmoid(preact)
        slope_ref[tile, :] = (sig * (1.0 + preact * (1.0 - sig))).astype(BF16)
        hidden_ref[tile, :] = (preact * sig).astype(BF16)

    def normalize(step):
        tile = slice(step * TILE, (step + 1) * TILE)
        centred, inverse = norm_forward(dot(hidden_ref[tile, :], w2_ref[...]) + b2_ref[...])
        position = step * TILE + lax.broadcasted_iota(jnp.int32, inverse.shape, 0)
        inverse = jnp.where(position < live, inverse, 0.0)
        normed = centred * inverse
        normed_ref[tile, :] = normed
        inverse_ref[tile, :] = jnp.broadcast_to(inverse, (TILE, LANES))
        update = (normed * gain_ref[...]).astype(BF16)
        part = dot(pick_rows(receiver_ref, step, TILE, nodes), update)
        if step == 0:
            summed[...] = part
        else:
            summed[...] += part

    for step in range(steps + 2):
        if step < steps:
            activate(step)
        if step > 1:
            normalize(step - 2)

    for copy in late:
        copy.wait()
    node_in = jnp.concatenate([node_ref[...], summed[...].astype(BF16)], axis=1)
    preact_n = dot(node_in, nw1_ref[...]) + nb1_ref[...]
    sig_n = sigmoid(preact_n)
    hidden_n = (preact_n * sig_n).astype(BF16)
    centred_n, inverse_n = norm_forward(dot(hidden_n, nw2_ref[...]) + nb2_ref[...])
    cot = ncot_ref[...].astype(F32)
    dout = norm_backward(cot * ngain_ref[...], centred_n * inverse_n, inverse_n)
    slope_n = sig_n * (1.0 + preact_n * (1.0 - sig_n))
    dpre = (dot(dout, nw2_ref[...], NT) * slope_n).astype(BF16)
    grads[: 2 * latent, :] = dot(node_in, dpre, TN)
    grads[2 * latent :, :] = dot(hidden_n, dout, TN)
    base_ref[...] = cot + dot(dpre, nw1_ref[:latent, :], NT)
    dsum_ref[...] = dot(dpre, nw1_ref[latent:, :], NT).astype(BF16)
    if fast:
        bit = lax.rem(here, 2)
        first = 2 * latent // tiles
        split_halves(bit, grads, 0, first, 0, first, gsend_ref, gkeep_ref, 0, True)
        second = latent // tiles
        split_halves(bit, grads, 2 * latent, second, 0, second, gsend_ref, gkeep_ref, first, True)
    else:
        gkeep_ref[...] = grads[: 2 * latent, :]
        gsend_ref[...] = grads[2 * latent :, :]


def slope_kernel(
    tiles, fast, start, last,
    cot_ref, receiver_ref, dsum_ref, hidden_ref, slope_ref, normed_ref, inverse_ref, w2_ref, gain_ref,
    *refs,
):
    dpre_ref, *out_refs, grads, dout = refs[0 if start == 0 else 1 :]
    here = lax.axis_index("tiles")
    edges, latent = dpre_ref.shape
    nodes = dsum_ref.shape[0]
    steps = edges // TILE
    grads[...] = jnp.zeros_like(grads) if start == 0 else refs[0][...]

    def outer(step):
        tile = slice(step * TILE, (step + 1) * TILE)
        whole = slice(start + step * TILE, start + (step + 1) * TILE)
        receivers = jnp.concatenate(
            pick_columns(index_columns(receiver_ref, start // TILE + step, TILE), 0, nodes), axis=1
        )
        grad_update = cot_ref[whole, :].astype(F32) + dot(receivers, dsum_ref[...])
        inverse = inverse_ref[whole, :1]
        dout[tile, :] = norm_backward(grad_update * gain_ref[...], normed_ref[whole, :], inverse)

    def inner(step):
        tile = slice(step * TILE, (step + 1) * TILE)
        whole = slice(start + step * TILE, start + (step + 1) * TILE)
        dpre_ref[tile, :] = (
            dot(dout[tile, :], w2_ref[...], NT) * slope_ref[whole, :].astype(F32)
        ).astype(BF16)
        grads[...] += dot(hidden_ref[whole, :], dout[tile, :], TN)

    for step in range(steps + 1):
        if step < steps:
            outer(step)
        if step > 0:
            inner(step - 1)

    if not last:
        out_refs[0][...] = grads[...]
    elif fast:
        rows = latent // tiles
        split_halves(lax.rem(here, 2), grads, 0, rows, 0, rows, *out_refs, 0)
    else:
        out_refs[0][...] = jnp.zeros_like(out_refs[0])
        out_refs[1][...] = grads[...]


def first_kernel(
    tiles, places, fast,
    dpre_a_ref, dpre_b_ref, edge_ref, sender_ref, receiver_ref, table_ref, node_ref, w1_ref,
    *refs,
):
    out_refs, (grads, sums, rims) = refs[:-3], refs[-3:]
    inner_ref, outer_ref, far_ref, sums_ref = out_refs[:4]
    here = lax.axis_index("tiles")
    edges, latent = edge_ref.shape
    early = dpre_a_ref.shape[0]
    nodes = node_ref.shape[0]
    rows = table_ref.shape[0]

    for step in range(edges // TILE):
        tile = slice(step * TILE, (step + 1) * TILE)
        if step * TILE < early:
            dpre = dpre_a_ref[tile, :]
        else:
            dpre = dpre_b_ref[step * TILE - early : (step + 1) * TILE - early, :]
        part = dot(edge_ref[tile, :], dpre, TN)
        picks = jnp.concatenate(
            [
                pick_rows(sender_ref, step, TILE, rows),
                pick_rows(receiver_ref, step, TILE, nodes),
            ],
            axis=0,
        )
        scattered = dot(picks, dpre)
        if step == 0:
            grads[:latent, :] = part
            sums[...] = scattered
        else:
            grads[:latent, :] += part
            sums[...] += scattered

    by_sender = sums[:rows, :].astype(BF16)
    by_receiver = sums[rows:, :].astype(BF16)
    grads[latent : 2 * latent, :] = dot(table_ref[...], by_sender, TN)
    grads[2 * latent :, :] = dot(node_ref[...], by_receiver, TN)
    back = dot(by_sender[nodes:, :], w1_ref[latent : 2 * latent, :], NT)
    rims[...] = back[: 2 * NEAR, :]
    odd = lax.rem(here, 2)
    inner = rims[pl.ds(pl.multiple_of((1 - odd) * NEAR, NEAR), NEAR), :].astype(BF16)
    inner_ref[...] = inner
    outer_ref[...] = rims[pl.ds(pl.multiple_of(odd * NEAR, NEAR), NEAR), :].astype(BF16)
    far = back[2 * NEAR : 2 * NEAR + places * tiles, :].astype(BF16)
    owner, at = slot_owner(here if fast else 0, (places * tiles, places * tiles), 0, places)
    column = lax.broadcasted_iota(jnp.int32, (places * tiles, places * tiles), 1)
    far = dot(ones_where(at * tiles + owner == column), far).astype(BF16)
    far_ref[...] = far
    if fast:
        bit = lax.rem(here, 2)
        block = 3 * latent // tiles
        at = 0
        for send_ref, keep_ref in (out_refs[4:6], out_refs[6:8], out_refs[8:10]):
            part = keep_ref.shape[1]
            split_halves(bit, grads, 0, block, at, part, send_ref, keep_ref, 0)
            at += part
        out_refs[4][tiles // 2 * out_refs[5].shape[1] :, :] = slots_out(0, far, places)
        out_refs[8][tiles // 2 * out_refs[9].shape[1] :, :] = inner
    else:
        out_refs[4][...] = grads[...]
    sums_ref[:nodes, :] = by_sender[:nodes, :]
    sums_ref[nodes:, :] = by_receiver


def edge_kernel(
    dpre_a_ref, dpre_b_ref, cot_ref, w1_ref, base_ref, sums_ref, out_hbm, partial_ref, out_ref, sems
):
    early, latent = dpre_a_ref.shape
    copies = []
    for dpre_ref, base in ((dpre_a_ref, 0), (dpre_b_ref, early)):
        for at in range(0, early, TILE):
            part = slice(at, at + TILE)
            tile = pl.ds(base + at, TILE)
            out_ref[tile, :] = (
                cot_ref[tile, :].astype(F32) + dot(dpre_ref[part, :], w1_ref[:latent, :], NT)
            ).astype(BF16)
            copy = pltpu.make_async_copy(
                out_ref.at[tile], out_hbm.at[tile], sems.at[(base + at) // TILE]
            )
            copy.start()
            copies.append(copy)
    nodes = base_ref.shape[0]
    partial_ref[...] = (
        base_ref[...]
        + dot(sums_ref[:nodes, :], w1_ref[latent : 2 * latent, :], NT)
        + dot(sums_ref[nodes:, :], w1_ref[2 * latent :, :], NT)
    )
    for copy in copies:
        copy.wait()


def add_rims(total, inner_ref, outer_ref, sums_ref):
    nodes = total.shape[0]
    odd = lax.rem(lax.axis_index("tiles"), 2)
    inner_at = pl.ds(pl.multiple_of((1 - odd) * (nodes - NEAR), NEAR), NEAR)
    outer_at = pl.ds(pl.multiple_of(odd * (nodes - NEAR), NEAR), NEAR)
    sums_ref[...] = total
    sums_ref[inner_at, :] += inner_ref[inner_ref.shape[0] - NEAR :, :].astype(F32)
    sums_ref[outer_at, :] += outer_ref[...].astype(F32)


def slot_picks(origin, index_ref, nodes):
    places, tiles = index_ref.shape[1], index_ref.shape[2]
    place = lax.broadcasted_iota(jnp.int32, (nodes, tiles), 0)
    owner, at = slot_owner(origin, (tiles, places * tiles), 1, places)
    row = lax.broadcasted_iota(jnp.int32, (tiles, places * tiles), 0)
    picks = jnp.zeros((nodes, places * tiles), F32)
    for j in range(places):
        listed = ones_where(place == index_ref[0, j : j + 1, :])
        picks += dot(listed, ones_where((owner == row) & (at == j)))
    return picks.astype(BF16)


def settle_kernel(
    index_ref, partial_ref, inner_ref, outer_ref, slots_ref, sums_ref, picks_ref
):
    places = index_ref.shape[1]
    rows = slots_ref.shape[0]
    picks = slot_picks(lax.axis_index("tiles"), index_ref, partial_ref.shape[0])
    column = lax.broadcasted_iota(jnp.int32, picks.shape, 1)
    here = ones_where((picks > 0) & ((lax.div(column, places) >> 3) & 1 == 0))
    moved = ones_where(bit_slots(3, (rows // 2, rows), places))
    picks_ref[...] = dot(picks, moved, NT).astype(BF16)
    add_rims(partial_ref[...] + dot(here, slots_ref[...]), inner_ref, outer_ref, sums_ref)


def last_kernel(sums_ref, picks_ref, got_ref, out_ref):
    rows = picks_ref.shape[1]
    got = got_ref[got_ref.shape[0] - rows :, :]
    out_ref[...] = (sums_ref[...] + dot(picks_ref[...], got)).astype(BF16)


def node_kernel(index_ref, partial_ref, inner_ref, outer_ref, slots_ref, out_ref, sums_ref):
    picks = slot_picks(0, index_ref, partial_ref.shape[0])
    add_rims(partial_ref[...] + dot(picks, slots_ref[...]), inner_ref, outer_ref, sums_ref)
    out_ref[...] = sums_ref[...].astype(BF16)


def halve_kernel(shift, count, places, *refs):
    keeps, gots = refs[:count], refs[count : 2 * count]
    rest = refs[2 * count :]
    send_ref, kept_ref = rest[-2:] if not places else rest[-3:-1]
    size = kept_ref.shape[1]
    bit = lax.rem(lax.div(lax.axis_index("tiles"), 2**shift), 2)
    at = 0
    for keep_ref, got_ref in zip(keeps, gots):
        blocks, rows = keep_ref.shape[:2]
        for q in range(blocks // 2):
            there, here = 2 * q + 1 - bit, 2 * q + bit
            got_there = got_ref[pl.ds(pl.multiple_of(there * rows, 32), rows), :].astype(F32)
            got_here = got_ref[pl.ds(pl.multiple_of(here * rows, 32), rows), :].astype(F32)
            to = q * size + at
            send_ref[to : to + rows, :] = (keep_ref[there] + got_there).astype(BF16)
            kept_ref[q, at : at + rows, :] = keep_ref[here] + got_here
        at += rows
    if places:
        slots_ref, moved_ref = rest[0], rest[-1]
        half = slots_ref.shape[0] // 2
        got_ref = gots[0]
        slots = slots_in(shift - 1, slots_ref[...], got_ref[got_ref.shape[0] - half :, :], places)
        moved_ref[...] = slots
        send_ref[send_ref.shape[0] - half :, :] = slots_out(shift, slots, places)


def finish_kernel(count, splits, *refs):
    out_refs = refs[2 * count :]
    rows = [0] * len(out_refs)
    for keep_ref, got_ref, parts in zip(refs[:count], refs[count : 2 * count], splits):
        at = 0
        for which, size in parts:
            first = rows[which]
            out_refs[which][first : first + size, :] = (
                keep_ref[0, at : at + size, :] + got_ref[at : at + size, :].astype(F32)
            )
            at += size
            rows[which] += size


def shaped(shape, dtype):
    return jax.ShapeDtypeStruct(shape, dtype)


def in_hbm(*arrays):
    return [pltpu.with_memory_space_constraint(array, pltpu.HBM) for array in arrays]


def call(kernel, name, out_shape, args, hbm=0, scratch=(), out_specs=None, flops=0):
    vmem = pl.BlockSpec(memory_space=pltpu.VMEM)
    return pl.pallas_call(
        kernel,
        in_specs=[pl.BlockSpec(memory_space=pltpu.HBM)] * hbm + [vmem] * (len(args) - hbm),
        out_specs=out_specs or [vmem] * len(out_shape),
        out_shape=out_shape,
        scratch_shapes=scratch,
        compiler_params=pltpu.CompilerParams(vmem_limit_bytes=16 * MIB),
        cost_estimate=pl.CostEstimate(flops=flops, bytes_accessed=flops // 100, transcendentals=0),
        name=name,
    )(*in_hbm(*args[:hbm]), *args[hbm:])


def swap(tiles, bit, send):
    return lax.ppermute(send, "tiles", [(i, i ^ bit) for i in range(tiles)])


def halve(shift, keeps, gots, slots=None, places=0, flops=0):
    half, _, width = keeps[0].shape
    rows = sum(keep.shape[1] for keep in keeps)
    extra = [] if slots is None else [slots]
    sent = half // 2 * rows + sum(slots.shape[0] // 2 for slots in extra)
    return call(
        functools.partial(halve_kernel, shift, len(keeps), places),
        "halve",
        [pltpu.VMEM((sent, width), BF16), pltpu.VMEM((half // 2, rows, width), F32)]
        + [pltpu.VMEM(slots.shape, BF16) for slots in extra],
        [*keeps, *gots, *extra],
        flops=flops,
    )


def finish(keeps, gots, splits, sizes):
    return call(
        functools.partial(finish_kernel, len(keeps), splits),
        "finish",
        [shaped((size, keeps[0].shape[-1]), F32) for size in sizes],
        [*keeps, *gots],
    )


def after(value, *others):
    return lax.optimization_barrier((value, *others))[0]


def shards(
    node_latent, edge_latent, node_cot, edge_cot,
    edge_w1, edge_b1, edge_w2, edge_b2, edge_gain,
    node_w1, node_b1, node_w2, node_b2, node_gain,
    send_index, edge_sender, edge_receiver, edge_count,
):
    tiles = lax.axis_size("tiles")
    nodes, latent = node_latent.shape
    edges = edge_latent.shape[0]
    places = send_index.shape[2]
    steps = edges // TILE
    used = nodes + 2 * NEAR + places * tiles
    rows = -(-used // LANES) * LANES
    fast = tiles == 16
    half = tiles // 2
    inside = [(i, i ^ 1) for i in range(tiles)]
    across = [(i, i + 1 if i % 2 else i - 1) for i in range(1, tiles - 1)]
    sender = edge_sender.reshape(edges // LANES, LANES)
    receiver = edge_receiver.reshape(edges // LANES, LANES)
    listed = jnp.swapaxes(send_index, 1, 2)
    row = lambda vector: vector.reshape(1, -1)
    vmem = pltpu.VMEM

    if fast:
        grad_shapes = lambda count: [
            vmem((count // 2, latent), BF16),
            vmem((half, count // tiles, latent), F32),
        ]
    else:
        grad_shapes = lambda count: [shaped((latent, latent), F32), shaped((count, latent), F32)]

    outgoing, inner, outer = call(
        outgoing_kernel,
        "outgoing",
        [
            shaped((tiles, places, latent), BF16),
            vmem((NEAR, latent), BF16),
            vmem((NEAR, latent), BF16),
        ],
        [listed, node_latent],
        hbm=2,
        scratch=[vmem(listed.shape, jnp.int32), vmem((nodes, latent), BF16), pltpu.SemaphoreType.DMA((2,))],
    )
    inner = lax.ppermute(inner, "tiles", inside)
    outer = lax.ppermute(outer, "tiles", across)
    slots = lax.all_to_all(outgoing, "tiles", split_axis=0, concat_axis=0, tiled=True)
    node_kept, receiver_kept, moved, preact = call(
        functools.partial(prepare_kernel, tiles, places),
        "prepare",
        [
            vmem((nodes, latent), BF16),
            vmem(receiver.shape, jnp.int32), vmem(sender.shape, jnp.int32),
            vmem((edges, latent), F32),
        ],
        [node_latent, edge_w1, after(sender, outgoing), receiver, row(edge_b1), edge_latent],
        hbm=6,
        scratch=[
            vmem((edges, latent), BF16), vmem(edge_w1.shape, BF16),
            vmem((latent + 2 * nodes, latent), BF16), vmem(sender.shape, jnp.int32),
            vmem((1, latent), F32), pltpu.SemaphoreType.DMA((5,)), pltpu.SemaphoreType.DMA((2,)),
        ],
        flops=AHEAD,
    )

    (
        w1_kept, edge_kept, cot_kept, w2_kept, gain_kept,
        hidden, slope, normed, inverse, table, dsum, base, node_send, node_keep,
    ) = call(
        functools.partial(forward_kernel, tiles, places, fast),
        "forward",
        [
            vmem(edge_w1.shape, BF16), vmem((edges, latent), BF16), vmem((edges, latent), BF16),
            vmem(edge_w2.shape, BF16), vmem((1, latent), F32),
            vmem((edges, latent), BF16), vmem((edges, latent), BF16), vmem((edges, latent), F32),
            vmem((edges, LANES), F32), vmem((rows, latent), BF16),
            vmem((nodes, latent), BF16), vmem((nodes, latent), F32),
        ] + grad_shapes(3 * latent if fast else 2 * latent),
        [
            edge_w1, edge_latent, edge_cot, edge_w2, node_w1, node_w2, node_cot,
            row(edge_b2), row(edge_gain), row(node_b1), row(node_b2), row(node_gain), edge_count,
            inner, outer, slots, preact, node_kept, receiver_kept, moved,
        ],
        hbm=13,
        scratch=[
            vmem((rows - nodes, latent), BF16), vmem((nodes, latent), F32),
            vmem((3 * latent, latent), F32), vmem(node_w1.shape, BF16), vmem(node_w2.shape, BF16),
            vmem((nodes, latent), BF16),
        ] + [vmem((1, latent), F32)] * 4 + [
            pltpu.SMEM(edge_count.shape, jnp.int32), pltpu.SemaphoreType.DMA((15,)),
        ],
    )

    early = edges // 2

    def slope_call(start, last, dsum, outs, more):
        return call(
            functools.partial(slope_kernel, tiles, fast, start, last),
            "slope",
            [vmem((early, latent), BF16)] + outs,
            [cot_kept, receiver_kept, dsum, hidden, slope, normed, inverse, w2_kept, gain_kept] + more,
            scratch=[vmem((latent, latent), F32), vmem((early, latent), BF16)],
        )

    dpre_a, grads = slope_call(0, False, dsum, [vmem((latent, latent), F32)], [])
    if fast:
        send, chain = halve(2, [after(node_keep, grads)], [swap(tiles, 1, node_send)])
        dsum = after(dsum, send)
        got = swap(tiles, 4, send)
    dpre_b, second_send, second_keep = slope_call(
        early, True, dsum, grad_shapes(latent), [grads]
    )
    if fast:
        got_second = swap(tiles, 1, second_send)

    per = latent // tiles
    to_inner, to_outer, to_far, sums, *first = call(
        functools.partial(first_kernel, tiles, places, fast),
        "first",
        [
            vmem((NEAR, latent), BF16),
            vmem((NEAR, latent), BF16),
            vmem((tiles * places, latent), BF16) if fast else shaped((tiles * places, latent), BF16),
            vmem((2 * nodes, latent), BF16),
        ] + (
            [
                vmem((half * per + tiles * places // 2, latent), BF16),
                vmem((half, per, latent), F32),
                vmem((half * per, latent), BF16), vmem((half, per, latent), F32),
                vmem((half * per + NEAR, latent), BF16), vmem((half, per, latent), F32),
            ]
            if fast else [shaped((3 * latent, latent), F32)]
        ),
        [dpre_a, dpre_b, edge_kept, moved, receiver_kept, table, node_kept, w1_kept],
        scratch=[
            vmem((3 * latent, latent), F32), vmem((rows + nodes, latent), F32),
            vmem((2 * NEAR, latent), F32),
        ],
    )

    def edge_call(dpre_a):
        return call(
            edge_kernel,
            "edge",
            [shaped((edges, latent), BF16), vmem((nodes, latent), F32)],
            [dpre_a, dpre_b, cot_kept, w1_kept, base, sums],
            out_specs=[
                pl.BlockSpec(memory_space=pltpu.HBM), pl.BlockSpec(memory_space=pltpu.VMEM),
            ],
            scratch=[vmem((edges, latent), BF16), pltpu.SemaphoreType.DMA((steps,))],
        )

    if fast:
        send_a, keep_a, send_more, keep_more, send_b, keep_b = first
        send_a, send_more, send_b, to_outer = lax.optimization_barrier(
            (send_a, send_more, send_b, to_outer, got_second)
        )[:4]
        inner = swap(tiles, 1, send_b)
        outer = lax.ppermute(to_outer, "tiles", across)
        send_a, chain_a, slots = halve(
            1,
            [keep_a, keep_more],
            [swap(tiles, 1, send_a), swap(tiles, 1, send_more)],
            to_far,
            places,
     )
        got_a = swap(tiles, 2, send_a)
        send_b, chain_b = halve(
            1, [after(keep_b, send_a), second_keep], [inner, got_second]
     )
        got_b = swap(tiles, 2, send_b)
        grad_edge, partial = edge_call(after(dpre_a, send_b))
        send, chain = halve(3, [after(chain, grad_edge, outer)], [got], flops=AHEAD)
        got = swap(tiles, 8, send)
        send_a, chain_a, slots = halve(2, [after(chain_a, send)], [got_a], slots, places)
        got_a = swap(tiles, 4, send_a)
        send_b, chain_b = halve(2, [after(chain_b, send_a)], [got_b])
        got_b = swap(tiles, 4, send_b)
        send, chain = halve(1, [after(chain, send_b)], [got])
        got = swap(tiles, 2, send)
        chain_a = after(chain_a, send)
        send_a, chain_a, slots = halve(3, [chain_a], [got_a], slots, places, AHEAD)
        got_a = swap(tiles, 8, send_a)
        chain_b = after(chain_b, send_a)
        send_b, chain_b = halve(3, [chain_b], [got_b], flops=AHEAD)
        got_b = swap(tiles, 8, send_b)
        node_sums, picks = call(
            settle_kernel,
            "settle",
            [vmem((nodes, latent), F32), vmem((nodes, places * half), BF16)],
            [listed, partial, inner, outer, slots],
        )
        (grad_node,) = call(
            last_kernel, "last", [shaped((nodes, latent), BF16)], [node_sums, picks, got_a]
        )
        grad_edge_w1, grad_edge_w2, grad_node_w1, grad_node_w2 = finish(
            [chain, chain_a, chain_b],
            [got, got_a, got_b],
            [[(2, 2 * per), (3, per)], [(0, 2 * per)], [(0, per), (1, per)]],
            [3 * per, per, 2 * per, per],
        )
    else:
        grad_edge, partial = edge_call(dpre_a)
        inner = lax.ppermute(to_inner, "tiles", inside)
        outer = lax.ppermute(to_outer, "tiles", across)
        returned = lax.all_to_all(to_far, "tiles", split_axis=0, concat_axis=0, tiled=True)
        (grad_node,) = call(
            node_kernel,
            "node",
            [shaped((nodes, latent), BF16)],
            [listed, partial, inner, outer, returned],
            scratch=[vmem((nodes, latent), F32)],
        )
        scatter = functools.partial(
            lax.psum_scatter, axis_name="tiles", scatter_dimension=0, tiled=True
        )
        grad_node_w1, grad_node_w2 = scatter(node_keep), scatter(node_send)
        grad_edge_w1, grad_edge_w2 = scatter(first[0]), scatter(second_keep)
    return (grad_node, grad_edge, grad_edge_w1, grad_edge_w2, grad_node_w1, grad_node_w2)


def solution(mesh):
    split = P(("groups", "tiles"), None)
    return jax.shard_map(
        shards,
        mesh=mesh,
        in_specs=(split,) * 4
        + (P(),) * 10
        + (
            P(("groups", "tiles"), None, None),
            P(("groups", "tiles")),
            P(("groups", "tiles")),
            P("groups"),
        ),
        out_specs=(split,) * 6,
        check_vma=False,
    )
```
